32 devices in a mesh: dp: 16 (over z, y, core), tensor: 2 (over x).
Axes of the slice: x: 2, y: 2, z: 4, core: 2. Of those that a mesh axis runs over, the one named last changes fastest.
Arguments:
- tokens: bfloat16 [64, 576, 1024], P('dp', 'tensor'), may hold values from -6 to 6
- image_mask: int32 [64], P('dp'), may hold values 0 or 1
- out_grad: bfloat16 [64, 576, 1024], P('dp', 'tensor'), may hold values from -6 to 6
- norm1_gain: bfloat16 [1024], replicated, may hold values from 0.5 to 1.5
- norm1_shift: bfloat16 [1024], replicated, may hold values from -3 to 3
- qkv_weight: bfloat16 [1024, 3, 1024], P('dp', None, 'tensor'), may hold values from -0.1875 to 0.1875
- qv_bias: bfloat16 [2, 1024], P(None, 'tensor'), may hold values from -3 to 3
- out_weight: bfloat16 [1024, 1024], P('dp', 'tensor'), may hold values from -1.5 to 1.5
- out_bias: bfloat16 [1024], replicated, may hold values from -3 to 3
- norm2_gain: bfloat16 [1024], replicated, may hold values from 0.5 to 1.5
- norm2_shift: bfloat16 [1024], replicated, may hold values from -3 to 3
- up_weight: bfloat16 [1024, 4096], P('dp', 'tensor'), may hold values from -0.1875 to 0.1875
- up_bias: bfloat16 [4096], P('tensor'), may hold values from -3 to 3
- down_weight: bfloat16 [1024, 4096], P('dp', 'tensor'), may hold values from -0.09375 to 0.09375
- down_bias: bfloat16 [1024], replicated, may hold values from -3 to 3
Outputs:
- block_out: bfloat16 [64, 576, 1024], P('dp', 'tensor')
- tokens_grad: bfloat16 [64, 576, 1024], P('dp', 'tensor')
- norm1_gain_grad: float32 [1024], replicated
- norm1_shift_grad: float32 [1024], replicated
- qkv_weight_grad: float32 [1024, 3, 1024], P('dp', None, 'tensor')
- qv_bias_grad: float32 [2, 1024], P(None, 'tensor')
- out_weight_grad: float32 [1024, 1024], P('dp', 'tensor')
- out_bias_grad: float32 [1024], replicated
- norm2_gain_grad: float32 [1024], replicated
- norm2_shift_grad: float32 [1024], replicated
- up_weight_grad: float32 [1024, 4096], P('dp', 'tensor')
- up_bias_grad: float32 [4096], P('tensor')
- down_weight_grad: float32 [1024, 4096], P('dp', 'tensor')
- down_bias_grad: float32 [1024], replicated
The draws below stay inside these ranges and needn't reach their ends.
Inputs may be any that keep to these rules, and one draw needn't show every extreme that they name: `image_mask`: 1 marks a real image, 0 a padding image.
All inputs are finite; a program needn't handle non-finite values. No bound on the sum of `image_mask` on one device may be relied on, other than what follows from the above.
Results may differ from the reference program's by a relative error of at most 0.015.
Values may be sent and summed in bfloat16 or wider, within the bound.
No kernel may reach another device: no remote copies, remote signals or barrier semaphores. Data moves between devices by JAX's collectives and lax.ppermute only.
A program may use at most 320 MiB of HBM per device.

```python
import jax
import jax.numpy as jnp
from jax import lax

D = 1024
HEADS = 16
HDIM = 64
FF = 4096
SEQ = 576
MICRO = 2
IMG_DEV = 2
IMAGES = 64


def set_ends(values, key, least, high):
    shape = values.shape
    index_at = [jax.random.randint(jax.random.fold_in(key, axis), (), 0, shape[axis]) for axis in range(len(shape))]
    values = values.at[tuple(index_at)].set(least)
    longest = shape.index(max(shape))
    index_at[longest] = (index_at[longest] + 1) % shape[longest]
    return values.at[tuple(index_at)].set(high)


def with_spikes(entries, rng, source, target, parts, factor):
    owner, partner = [(jnp.arange(entries.shape[position]) // (entries.shape[position] // parts)).reshape([-1 if axis == position else 1 for axis in range(entries.ndim)]) for position in (source, target)]
    chosen = jax.random.permutation(rng, parts)[partner]
    strong = (owner == chosen) | (owner == (partner + parts // 2) % parts)
    return jnp.where(strong, factor * entries, entries)


def steps_of(own_key, dims, split, least, largest):
    factor_of, own = 1.0, jax.random.fold_in(own_key, 6)
    for axis_at, parts in split:
        draws = jnp.exp(jax.random.uniform(jax.random.fold_in(own, axis_at), (parts,), jnp.float32, least / len(split), largest / len(split)))
        factor_of = factor_of * jnp.repeat(draws, dims[axis_at] // parts).reshape([-1 if axis == axis_at else 1 for axis in range(len(dims))])
    return factor_of


def scatter_about(stream_key, dims, scale, reach, split=(), dtype=jnp.bfloat16):
    drawn = jax.random.normal(stream_key, dims, jnp.float32) * scale
    if len(split) > 0:
        drawn = steps_of(stream_key, dims, split, -0.22, 0.18) * drawn
    return jnp.clip(drawn, min=-reach, max=reach).astype(dtype)


def gaussian_with(stream_key, shape, spread, limit, shards, heavy, held_as=jnp.bfloat16):
    drawn = spread * jax.random.normal(stream_key, shape, jnp.float32)
    if shards:
        drawn = drawn * steps_of(stream_key, shape, shards, -0.22, 0.18)
    return jnp.clip(with_spikes(drawn, jax.random.fold_in(stream_key, 3), *heavy), -limit, limit).astype(held_as)


def setup_inputs(seed: int = 0) -> dict:
    seeds = jax.random.split(jax.random.key(seed), 16)
    return {
        "tokens": scatter_about(seeds[0], (IMAGES, SEQ, D), 1.0, 6.0, ((0, 16), (1, 2))),
        "image_mask": set_ends((jax.random.randint(seeds[1], (IMAGES,), 0, 5) < 3).astype(jnp.int32), jax.random.fold_in(seeds[1], 1), 0, 1),
        "out_grad": gaussian_with(seeds[2], (IMAGES, SEQ, D), 1.0, 6.0, ((0, 16), (1, 2)), (0, 2, 16, 2.0)),
        "norm1_gain": jnp.clip(1.0 + 0.1 * jax.random.normal(seeds[3], (D,), jnp.float32), 0.5, 1.5).astype(jnp.bfloat16),
        "norm1_shift": scatter_about(seeds[4], (D,), 0.3, 3.0),
        "qkv_weight": scatter_about(seeds[5], (D, 3, D), D ** -0.5, 0.1875, ((0, 16), (2, 2))),
        "qv_bias": scatter_about(seeds[6], (2, D), 0.3, 3.0, ((1, 2),)),
        "out_weight": scatter_about(seeds[7], (D, D), (D // 64) ** -0.5, 1.5, ((0, 16), (1, 2))),
        "out_bias": scatter_about(seeds[8], (D,), 0.3, 3.0),
        "norm2_gain": jnp.clip(1.0 + 0.1 * jax.random.normal(seeds[9], (D,), jnp.float32), 0.5, 1.5).astype(jnp.bfloat16),
        "norm2_shift": scatter_about(seeds[10], (D,), 0.3, 3.0),
        "up_weight": scatter_about(seeds[11], (D, FF), D ** -0.5, 0.1875, ((0, 16), (1, 2))),
        "up_bias": scatter_about(seeds[12], (FF,), 0.5, 3.0, ((0, 2),)),
        "down_weight": scatter_about(seeds[13], (D, FF), FF ** -0.5, 0.09375, ((0, 16), (1, 2))),
        "down_bias": scatter_about(seeds[14], (D,), 0.3, 3.0),
    }


@jax.custom_vjp
def low(v):
    return lax.optimization_barrier(v.astype(jnp.bfloat16)).astype(jnp.float32)

@jax.custom_vjp
def low_back(v):
    return v

def low_keep(v):
    return (low(v), None)

def low_pass(kept, grad):
    return (grad,)

def back_keep(v):
    return (v, None)

def back_low(kept, grad):
    return (low(grad),)
low.defvjp(low_keep, low_pass)
low_back.defvjp(back_keep, back_low)

def rounded_both(values):
    return low_back(low(values))

def product(left, right, form):
    return jnp.einsum(form, left, right, precision=lax.Precision.HIGHEST)

def normalize(values, gain, shift):
    mean_val = lax.optimization_barrier(jnp.mean(values, axis=-1, keepdims=True))
    centered = values - mean_val
    variance = lax.optimization_barrier(jnp.mean(centered * centered, axis=-1, keepdims=True))
    return centered * lax.rsqrt(variance + 1e-05) * gain + shift

def attend_image(triple):
    queries, key_rows, value_rows = triple
    scores = low_back(product(queries, key_rows, 'qhe,khe->hqk') * HDIM ** (-0.5))
    row_top = lax.optimization_barrier(jnp.max(scores, axis=-1, keepdims=True))
    raw_weights = jnp.exp(scores - row_top)
    probs = low(raw_weights / lax.optimization_barrier(jnp.sum(raw_weights, axis=-1, keepdims=True)))
    return product(probs, value_rows, 'hqk,khe->qhe')

def block(params, block_rows, keep_mask):
    norm1_gain, norm1_shift, qkv_weight, qv_bias, out_weight, out_bias, norm2_gain, norm2_shift, up_weight, up_bias, down_weight, down_bias = params
    images_here = block_rows.shape[0]
    head_shape = (images_here, SEQ, HEADS, HDIM)
    normed = low(normalize(block_rows, norm1_gain, norm1_shift))
    projected = product(normed, qkv_weight, 'gsd,dcf->gscf')
    queries = rounded_both(projected[:, :, 0] + qv_bias[0]).reshape(head_shape)
    key_rows = rounded_both(projected[:, :, 1]).reshape(head_shape)
    value_rows = rounded_both(projected[:, :, 2] + qv_bias[1]).reshape(head_shape)
    context = lax.map(jax.checkpoint(attend_image), (queries, key_rows, value_rows))
    context = rounded_both(context.reshape(images_here, SEQ, D))
    branch = low_back(product(context, out_weight, 'gsf,of->gso') + out_bias)
    middle = block_rows + branch
    second = low(normalize(middle, norm2_gain, norm2_shift))
    hidden = low_back(product(second, up_weight, 'gsd,df->gsf') + up_bias)
    active = low(hidden * jax.nn.sigmoid(1.702 * hidden))
    feed = low_back(product(active, down_weight, 'gsf,of->gso') + down_bias)
    return (middle + feed) * keep_mask[:, None, None]

def reference(tokens, image_mask, out_grad, norm1_gain, norm1_shift, qkv_weight, qv_bias, out_weight, out_bias, norm2_gain, norm2_shift, up_weight, up_bias, down_weight, down_bias):
    params = jax.tree.map(lambda tensor_in: tensor_in.astype(jnp.float32), (norm1_gain, norm1_shift, qkv_weight, qv_bias, out_weight, out_bias, norm2_gain, norm2_shift, up_weight, up_bias, down_weight, down_bias))
    group_size = MICRO * IMG_DEV
    group_count = tokens.shape[0] // group_size
    token_groups = tokens.astype(jnp.float32).reshape(group_count, group_size, SEQ, D)
    grad_groups = out_grad.astype(jnp.float32).reshape(group_count, group_size, SEQ, D)
    keep_groups = image_mask.astype(jnp.float32).reshape(group_count, group_size)

    def advance(carry, item):
        group_tokens, group_keep, group_grad = item

        def forward(params_in, tokens_in):
            return block(params_in, tokens_in, group_keep)
        result, pullback = jax.vjp(forward, params, group_tokens)
        param_grads, token_grads = pullback(group_grad)
        carry = jax.tree.map(lambda summed, latest: summed + latest, carry, param_grads)
        return (carry, (result.astype(jnp.bfloat16), token_grads.astype(jnp.bfloat16)))
    start_sums = jax.tree.map(lambda tensor_in: jnp.zeros(tensor_in.shape, jnp.float32), params)
    totals, (results, token_grads) = lax.scan(advance, start_sums, (token_groups, keep_groups, grad_groups))
    block_out = results.reshape(tokens.shape)
    tokens_grad = token_grads.reshape(tokens.shape)
    return (block_out, tokens_grad, totals[0], totals[1], totals[2], totals[3], totals[4], totals[5], totals[6], totals[7], totals[8], totals[9], totals[10], totals[11])
```

```python
import jax
import jax.numpy as jnp
from jax import lax
from jax.sharding import PartitionSpec as P

HDIM = 64
MICRO = 2


def mixed(form, left, right):
    return jnp.einsum(form, left, right, preferred_element_type=jnp.float32)


def normalize(values, gain, shift):
    mean_val = jnp.mean(values, axis=-1, keepdims=True)
    centered = values - mean_val
    inv_std = lax.rsqrt(jnp.mean(centered * centered, axis=-1, keepdims=True) + 1e-05)
    unit_val = centered * inv_std
    return (unit_val * gain + shift, unit_val, inv_std)


def normalize_back(grad_in, unit_val, inv_std, gain):
    scaled = grad_in * gain
    return inv_std * (
        scaled
        - jnp.mean(scaled, axis=-1, keepdims=True)
        - unit_val * jnp.mean(scaled * unit_val, axis=-1, keepdims=True)
    )


def token_sum(values):
    return jnp.sum(values, axis=(0, 1))


def general_shards(
    tokens,
    image_mask,
    out_grad,
    norm1_gain,
    norm1_shift,
    qkv_weight,
    qv_bias,
    out_weight,
    out_bias,
    norm2_gain,
    norm2_shift,
    up_weight,
    up_bias,
    down_weight,
    down_bias,
):
    images_here = tokens.shape[0] // MICRO
    full_width = norm1_gain.shape[0]
    local_width = qkv_weight.shape[2]
    local_hidden = up_weight.shape[1]
    local_heads = local_width // HDIM
    score_scale = HDIM ** (-0.5)
    gain_one = norm1_gain.astype(jnp.float32)
    shift_one = norm1_shift.astype(jnp.float32)
    gain_two = norm2_gain.astype(jnp.float32)
    shift_two = norm2_shift.astype(jnp.float32)
    bias_pair = qv_bias.astype(jnp.float32)
    grad_qkv = jnp.zeros((full_width, 3, local_width), jnp.float32)
    grad_out = jnp.zeros((full_width, local_width), jnp.float32)
    grad_up = jnp.zeros((full_width, local_hidden), jnp.float32)
    grad_down = jnp.zeros((full_width, local_hidden), jnp.float32)
    grad_gain_one = jnp.zeros((full_width,), jnp.float32)
    grad_shift_one = jnp.zeros((full_width,), jnp.float32)
    grad_gain_two = jnp.zeros((full_width,), jnp.float32)
    grad_shift_two = jnp.zeros((full_width,), jnp.float32)
    grad_out_bias = jnp.zeros((full_width,), jnp.float32)
    grad_down_bias = jnp.zeros((full_width,), jnp.float32)
    grad_pair = jnp.zeros((2, local_width), jnp.float32)
    grad_up_bias = jnp.zeros((local_hidden,), jnp.float32)
    outputs = []
    input_grads = []
    for micro_index in range(MICRO):
        first_image = micro_index * images_here
        block_rows = tokens[first_image : first_image + images_here].astype(jnp.float32)
        keep_mask = image_mask[first_image : first_image + images_here].astype(jnp.float32)[
            :, None, None
        ]
        fwd_weights = (
            lax.all_gather(qkv_weight, "dp", axis=0, tiled=True),
            lax.all_gather(out_weight, "dp", axis=0, tiled=True),
            lax.all_gather(up_weight, "dp", axis=0, tiled=True),
            lax.all_gather(down_weight, "dp", axis=0, tiled=True),
        )
        qkv_full, out_full, up_full, down_full = fwd_weights
        normed, unit_one, inv_one = normalize(block_rows, gain_one, shift_one)
        normed_full = lax.all_gather(normed.astype(jnp.bfloat16), "tensor", axis=1, tiled=True)
        seq_len = normed_full.shape[1]
        head_shape = (images_here, seq_len, local_heads, HDIM)
        projected = mixed("isd,dcf->iscf", normed_full, qkv_full)
        queries = (projected[:, :, 0] + bias_pair[0]).astype(jnp.bfloat16).reshape(head_shape)
        key_rows = projected[:, :, 1].astype(jnp.bfloat16).reshape(head_shape)
        value_rows = (projected[:, :, 2] + bias_pair[1]).astype(jnp.bfloat16).reshape(head_shape)
        scores = mixed("iqhe,ikhe->ihqk", queries, key_rows) * score_scale
        row_top = jnp.max(scores, axis=-1, keepdims=True)
        raw_weights = jnp.exp(scores - row_top)
        row_total = jnp.sum(raw_weights, axis=-1, keepdims=True)
        log_total = row_top + jnp.log(row_total)
        probs = (raw_weights / row_total).astype(jnp.bfloat16)
        context = mixed("ihqk,ikhe->iqhe", probs, value_rows).astype(jnp.bfloat16)
        context = context.reshape(images_here, seq_len, local_width)
        attn_terms = mixed("isf,of->iso", context, out_full)
        branch = lax.psum_scatter(
            attn_terms, "tensor", scatter_dimension=1, tiled=True
        ) + out_bias.astype(jnp.float32)
        middle = block_rows + branch
        second, unit_two, inv_two = normalize(middle, gain_two, shift_two)
        second_full = lax.all_gather(second.astype(jnp.bfloat16), "tensor", axis=1, tiled=True)
        hidden = mixed("isd,df->isf", second_full, up_full) + up_bias.astype(jnp.float32)
        gate_sig = jax.nn.sigmoid(1.702 * hidden)
        active = (hidden * gate_sig).astype(jnp.bfloat16)
        feed_terms = mixed("isf,of->iso", active, down_full)
        feed_out = lax.psum_scatter(
            feed_terms.astype(jnp.bfloat16), "tensor", scatter_dimension=1, tiled=True
        ).astype(jnp.float32) + down_bias.astype(jnp.float32)
        outputs.append(((middle + feed_out) * keep_mask).astype(jnp.bfloat16))
        back_weights = (
            lax.all_gather(qkv_weight, "dp", axis=0, tiled=True),
            lax.all_gather(out_weight, "dp", axis=0, tiled=True),
            lax.all_gather(up_weight, "dp", axis=0, tiled=True),
            lax.all_gather(down_weight, "dp", axis=0, tiled=True),
        )
        qkv_back, out_back, up_back, down_back = back_weights
        grad_final = (
            out_grad[first_image : first_image + images_here].astype(jnp.float32) * keep_mask
        )
        grad_down_bias = grad_down_bias + token_sum(grad_final)
        final_full = lax.all_gather(grad_final.astype(jnp.bfloat16), "tensor", axis=1, tiled=True)
        grad_down = grad_down + mixed("iso,isf->of", final_full, active)
        grad_active = mixed("iso,of->isf", final_full, down_back)
        grad_hidden = (
            grad_active * (gate_sig + 1.702 * hidden * gate_sig * (1.0 - gate_sig))
        ).astype(jnp.bfloat16)
        grad_up_bias = grad_up_bias + token_sum(grad_hidden.astype(jnp.float32))
        grad_up = grad_up + mixed("isd,isf->df", second_full, grad_hidden)
        second_terms = mixed("isf,df->isd", grad_hidden, up_back)
        grad_second = lax.psum_scatter(second_terms, "tensor", scatter_dimension=1, tiled=True)
        grad_gain_two = grad_gain_two + token_sum(grad_second * unit_two)
        grad_shift_two = grad_shift_two + token_sum(grad_second)
        grad_middle = grad_final + normalize_back(grad_second, unit_two, inv_two, gain_two)
        grad_branch = grad_middle.astype(jnp.bfloat16)
        grad_out_bias = grad_out_bias + token_sum(grad_branch.astype(jnp.float32))
        branch_full = lax.all_gather(grad_branch, "tensor", axis=1, tiled=True)
        grad_out = grad_out + mixed("iso,isf->of", branch_full, context)
        grad_context = (
            mixed("iso,of->isf", branch_full, out_back).astype(jnp.bfloat16).reshape(head_shape)
        )
        again = mixed("iqhe,ikhe->ihqk", queries, key_rows) * score_scale
        soft_again = jnp.exp(again - log_total)
        probs_again = soft_again.astype(jnp.bfloat16)
        grad_values = mixed("ihqk,iqhe->ikhe", probs_again, grad_context)
        grad_soft = mixed("iqhe,ikhe->ihqk", grad_context, value_rows)
        grad_scores = (
            soft_again * (grad_soft - jnp.sum(grad_soft * soft_again, axis=-1, keepdims=True))
        ).astype(jnp.bfloat16)
        grad_queries = mixed("ihqk,ikhe->iqhe", grad_scores, key_rows) * score_scale
        grad_keys = mixed("ihqk,iqhe->ikhe", grad_scores, queries) * score_scale
        flat_shape = (images_here, seq_len, local_width)
        grad_projected = jnp.stack(
            (
                grad_queries.reshape(flat_shape),
                grad_keys.reshape(flat_shape),
                grad_values.reshape(flat_shape),
            ),
            axis=2,
        ).astype(jnp.bfloat16)
        pair_terms = grad_projected.astype(jnp.float32)
        grad_pair = grad_pair + jnp.stack(
            (token_sum(pair_terms[:, :, 0]), token_sum(pair_terms[:, :, 2])), axis=0
        )
        grad_qkv = grad_qkv + mixed("isd,iscf->dcf", normed_full, grad_projected)
        normed_terms = mixed("iscf,dcf->isd", grad_projected, qkv_back)
        grad_normed = lax.psum_scatter(
            normed_terms.astype(jnp.bfloat16), "tensor", scatter_dimension=1, tiled=True
        ).astype(jnp.float32)
        grad_gain_one = grad_gain_one + token_sum(grad_normed * unit_one)
        grad_shift_one = grad_shift_one + token_sum(grad_normed)
        grad_tokens = grad_middle + normalize_back(grad_normed, unit_one, inv_one, gain_one)
        input_grads.append(grad_tokens.astype(jnp.bfloat16))
    grad_qkv, grad_out, grad_up, grad_down = (
        lax.psum_scatter(
            grad_qkv.astype(jnp.bfloat16), "dp", scatter_dimension=0, tiled=True
        ).astype(jnp.float32),
        lax.psum_scatter(
            grad_out.astype(jnp.bfloat16), "dp", scatter_dimension=0, tiled=True
        ).astype(jnp.float32),
        lax.psum_scatter(
            grad_up.astype(jnp.bfloat16), "dp", scatter_dimension=0, tiled=True
        ).astype(jnp.float32),
        lax.psum_scatter(
            grad_down.astype(jnp.bfloat16), "dp", scatter_dimension=0, tiled=True
        ).astype(jnp.float32),
    )
    grad_gain_one, grad_shift_one, grad_gain_two, grad_shift_two, grad_out_bias, grad_down_bias = (
        lax.psum(
            (
                grad_gain_one,
                grad_shift_one,
                grad_gain_two,
                grad_shift_two,
                grad_out_bias,
                grad_down_bias,
            ),
            ("dp", "tensor"),
        )
    )
    grad_pair, grad_up_bias = lax.psum((grad_pair, grad_up_bias), "dp")
    block_out = jnp.concatenate(outputs, axis=0)
    tokens_grad = jnp.concatenate(input_grads, axis=0)
    return (
        block_out,
        tokens_grad,
        grad_gain_one,
        grad_shift_one,
        grad_qkv,
        grad_pair,
        grad_out,
        grad_out_bias,
        grad_gain_two,
        grad_shift_two,
        grad_up,
        grad_up_bias,
        grad_down,
        grad_down_bias,
    )


ROWS = 64


def swap(values, axis_name, flip):
    count = lax.axis_size(axis_name)
    return lax.ppermute(values, axis_name, [(place, place ^ flip) for place in range(count)])


def over_core(values):
    return swap(values, "dp", 1)


def over_y(values):
    return swap(values, "dp", 2)


def over_z(values, step):
    return swap(values, "dp", 4 * step)


def over_x(values):
    return swap(values, "tensor", 1)


def gather_pieces(own, x_first):
    base = jnp.concatenate([own] + [over_z(own, step) for step in (1, 2, 3)], axis=0)
    if x_first:
        side = over_x(base)
        near = ((base, side), (over_y(base), over_y(side)))
    else:
        side = over_y(base)
        near = ((base, over_x(base)), (side, over_x(side)))
    far = tuple(tuple(over_core(piece) for piece in pair) for pair in near)
    return (near, far)


def scatter_pieces(pieces, x_first):
    def join(mine, other):
        return (mine.astype(jnp.float32) + other.astype(jnp.float32)).astype(jnp.bfloat16)

    near = [
        [join(pieces[0][y_at][x_at], over_core(pieces[1][y_at][x_at])) for x_at in range(2)]
        for y_at in range(2)
    ]
    if x_first:
        pair = [join(near[y_at][0], over_x(near[y_at][1])) for y_at in range(2)]
        whole = join(pair[0], over_y(pair[1]))
    else:
        pair = [join(near[0][x_at], over_y(near[1][x_at])) for x_at in range(2)]
        whole = join(pair[0], over_x(pair[1]))
    rows = whole.shape[0] // 4
    parts = [whole[:rows]] + [
        over_z(whole[step * rows : (step + 1) * rows], step) for step in (1, 2, 3)
    ]
    parts = [part.astype(jnp.float32) for part in parts]
    return (parts[0] + parts[1]) + (parts[2] + parts[3])


def join_pieces(pieces):
    return jnp.concatenate(
        [jnp.concatenate(pair, axis=1) for half in pieces for pair in half], axis=0
    )


def cut_pieces(values):
    values = values.astype(jnp.bfloat16)
    rows, columns = values.shape[0] // 4, values.shape[1] // 2
    return [
        [
            [
                values[(2 * core + y_at) * rows :][:rows, x_at * columns :][:, :columns]
                for x_at in range(2)
            ]
            for y_at in range(2)
        ]
        for core in range(2)
    ]


def fast_shards(
    tokens,
    image_mask,
    out_grad,
    norm1_gain,
    norm1_shift,
    qkv_weight,
    qv_bias,
    out_weight,
    out_bias,
    norm2_gain,
    norm2_shift,
    up_weight,
    up_bias,
    down_weight,
    down_bias,
):
    f32, bf16 = jnp.float32, jnp.bfloat16
    images, half_len, width = tokens.shape
    mine = images // 2
    half_width = qkv_weight.shape[2]
    half_hidden = up_weight.shape[1]
    heads = width // HDIM
    score_scale = HDIM ** (-0.5)
    me = lax.axis_index("dp")
    side = lax.axis_index("tensor")
    block = jnp.arange(width) // ROWS
    core_rel, y_rel, z_rel = block // 8, (block // 4) % 2, block % 4
    source = ((z_rel * 4 + y_rel * 2 + core_rel) ^ me) * ROWS + jnp.arange(width) % ROWS
    order = (jnp.arange(width)[:, None] == source[None, :]).astype(bf16)

    def arrange(values):
        return jnp.matmul(values, order, preferred_element_type=f32).astype(bf16)

    def restore(values):
        return jnp.einsum("...d,od->...o", values, order, preferred_element_type=f32).astype(bf16)

    def exchange(values):
        keep_part = lax.dynamic_slice_in_dim(values, side * mine, mine, 0)
        send_part = lax.dynamic_slice_in_dim(values, (1 - side) * mine, mine, 0)
        return jnp.stack([keep_part, over_x(send_part)])

    def give_back(values):
        own, other = values[0], over_x(values[1])
        low_part = jnp.where(side == 0, own, other)
        high_part = jnp.where(side == 0, other, own)
        return jnp.concatenate([low_part, high_part], axis=0)

    rows_here = 2 * mine * half_len
    first = jnp.concatenate([qkv_weight.reshape(ROWS, 3 * half_width), out_weight], axis=1)
    first_pieces = gather_pieces(first, True)
    block_rows = arrange(exchange(tokens)).astype(f32).reshape(rows_here, width)
    up_pieces = gather_pieces(up_weight, False)
    down_pieces = gather_pieces(down_weight, True)
    biases = jnp.concatenate([qv_bias.reshape(-1), up_bias])
    biases = jnp.stack([biases, over_x(biases)]).astype(f32)
    bias_q = biases[:, :half_width].reshape(-1)
    bias_v = biases[:, half_width : 2 * half_width].reshape(-1)
    bias_up = biases[:, 2 * half_width :].reshape(-1)
    vectors = jnp.stack([norm1_gain, norm1_shift, norm2_gain, norm2_shift, out_bias, down_bias])
    gain_one, shift_one, gain_two, shift_two, bias_out, bias_down = arrange(vectors).astype(f32)
    keep = image_mask.astype(f32)
    keep = lax.dynamic_slice_in_dim(keep, side * mine, mine, 0)
    keep_rows = jnp.broadcast_to(keep[None, :, None], (2, mine, half_len)).reshape(rows_here, 1)

    first_full = join_pieces(first_pieces)
    first_split = first_full.reshape(width, 2, 2 * width // 1)
    qkv_full = first_split[:, :, : 3 * half_width].reshape(width, 2, 3, half_width)
    out_full = first_split[:, :, 3 * half_width :].reshape(width, width)
    normed, unit_one, inv_one = normalize(block_rows, gain_one, shift_one)
    normed = normed.astype(bf16)
    projected = jnp.einsum("rd,dxcf->rcxf", normed, qkv_full, preferred_element_type=f32)
    projected = projected.reshape(rows_here, 3, width)

    def to_heads(values):
        return (
            values.astype(bf16)
            .reshape(2, mine, half_len, heads, HDIM)
            .transpose(1, 3, 0, 2, 4)
            .reshape(mine, heads, 2 * half_len, HDIM)
        )

    def from_heads(values):
        return (
            values.astype(bf16)
            .reshape(mine, heads, 2, half_len, HDIM)
            .transpose(2, 0, 3, 1, 4)
            .reshape(rows_here, width)
        )

    queries = to_heads(projected[:, 0] + bias_q)
    key_rows = to_heads(projected[:, 1])
    value_rows = to_heads(projected[:, 2] + bias_v)
    scores = mixed("ihqe,ihke->ihqk", queries, key_rows) * score_scale
    row_top = jnp.max(scores, axis=-1, keepdims=True)
    raw_weights = jnp.exp(scores - row_top)
    row_total = jnp.sum(raw_weights, axis=-1, keepdims=True)
    log_total = row_top + jnp.log(row_total)
    probs = (raw_weights / row_total).astype(bf16)
    context = from_heads(mixed("ihqk,ihke->ihqe", probs, value_rows))
    middle = block_rows + mixed("rf,of->ro", context, out_full) + bias_out
    second, unit_two, inv_two = normalize(middle, gain_two, shift_two)
    second = second.astype(bf16)
    up_full = join_pieces(up_pieces)
    hidden = mixed("rd,df->rf", second, up_full) + bias_up
    gate_sig = jax.nn.sigmoid(1.702 * hidden)
    active = (hidden * gate_sig).astype(bf16)
    slope = gate_sig + 1.702 * hidden * gate_sig * (1.0 - gate_sig)
    down_full = join_pieces(down_pieces)
    feed_out = mixed("rf,of->ro", active, down_full) + bias_down
    block_out = ((middle + feed_out) * keep_rows).astype(bf16)
    block_out = give_back(restore(block_out).reshape(2, mine, half_len, width))

    grad_final = arrange(exchange(out_grad)).reshape(rows_here, width).astype(f32) * keep_rows
    final_low = grad_final.astype(bf16)
    grad_down = scatter_pieces(cut_pieces(mixed("ro,rf->of", final_low, active)), True)
    grad_hidden = (mixed("ro,of->rf", final_low, down_full) * slope).astype(bf16)
    grad_up = scatter_pieces(cut_pieces(mixed("rd,rf->df", second, grad_hidden)), False)
    grad_second = mixed("rf,df->rd", grad_hidden, up_full)
    grad_middle = grad_final + normalize_back(grad_second, unit_two, inv_two, gain_two)
    grad_branch = grad_middle.astype(bf16)
    grad_out = mixed("ro,rf->of", grad_branch, context)
    grad_context = to_heads(mixed("ro,of->rf", grad_branch, out_full))
    again = mixed("ihqe,ihke->ihqk", queries, key_rows) * score_scale
    soft_again = jnp.exp(again - log_total)
    probs_again = soft_again.astype(bf16)
    grad_values = mixed("ihqk,ihqe->ihke", probs_again, grad_context)
    grad_soft = mixed("ihqe,ihke->ihqk", grad_context, value_rows)
    grad_scores = (
        soft_again * (grad_soft - jnp.sum(grad_soft * soft_again, axis=-1, keepdims=True))
    ).astype(bf16)
    grad_queries = mixed("ihqk,ihke->ihqe", grad_scores, key_rows) * score_scale
    grad_keys = mixed("ihqk,ihqe->ihke", grad_scores, queries) * score_scale
    grad_projected = jnp.stack(
        [from_heads(grad_queries), from_heads(grad_keys), from_heads(grad_values)], axis=1
    )
    grad_qkv = jnp.einsum(
        "rd,rcxf->dxcf",
        normed,
        grad_projected.reshape(rows_here, 3, 2, half_width),
        preferred_element_type=f32,
    )
    grad_first = jnp.concatenate(
        [
            grad_qkv.reshape(width, 2, 3 * half_width),
            grad_out.reshape(width, 2, half_width),
        ],
        axis=2,
    ).reshape(width, 4 * width)
    grad_first = scatter_pieces(cut_pieces(grad_first), False)
    grad_normed = jnp.einsum(
        "rcxf,dxcf->rd",
        grad_projected.reshape(rows_here, 3, 2, half_width),
        qkv_full,
        preferred_element_type=f32,
    )
    grad_tokens = grad_middle + normalize_back(grad_normed, unit_one, inv_one, gain_one)
    tokens_grad = give_back(
        restore(grad_tokens.astype(bf16)).reshape(2, mine, half_len, width)
    )

    sums = jnp.stack(
        [
            jnp.sum(grad_normed * unit_one, axis=0),
            jnp.sum(grad_normed, axis=0),
            jnp.sum(grad_branch.astype(f32), axis=0),
            jnp.sum(grad_second * unit_two, axis=0),
            jnp.sum(grad_second, axis=0),
            jnp.sum(grad_final, axis=0),
        ]
    )
    sums = jnp.zeros_like(sums).at[:, source].set(sums)
    halves = jnp.stack(
        [
            jnp.sum(grad_projected[:, 0].astype(f32), axis=0).reshape(2, half_width),
            jnp.sum(grad_projected[:, 2].astype(f32), axis=0).reshape(2, half_width),
        ],
        axis=1,
    ).reshape(2, 2 * half_width)
    halves = jnp.concatenate(
        [halves, jnp.sum(grad_hidden.astype(f32), axis=0).reshape(2, half_hidden)], axis=1
    )
    sums = sums + over_x(sums)
    halves = halves[0] + over_x(halves[1])
    small = jnp.concatenate([sums.reshape(-1), halves])
    small = small + over_core(small)
    small = small + over_y(small)
    small = (small + over_z(small, 1)) + (over_z(small, 2) + over_z(small, 3))
    sums = small[: 6 * width].reshape(6, width)
    halves = small[6 * width :]
    return (
        block_out,
        tokens_grad,
        sums[0],
        sums[1],
        grad_first[:, : 3 * half_width].reshape(ROWS, 3, half_width),
        halves[: 2 * half_width].reshape(2, half_width),
        grad_first[:, 3 * half_width :],
        sums[2],
        sums[3],
        sums[4],
        grad_up,
        halves[2 * half_width :],
        grad_down,
        sums[5],
    )


def solution(mesh):
    in_specs = (
        P("dp", "tensor", None),
        P("dp"),
        P("dp", "tensor", None),
        P(),
        P(),
        P("dp", None, "tensor"),
        P(None, "tensor"),
        P("dp", "tensor"),
        P(),
        P(),
        P(),
        P("dp", "tensor"),
        P("tensor"),
        P("dp", "tensor"),
        P(),
    )
    out_specs = (
        P("dp", "tensor", None),
        P("dp", "tensor", None),
        P(),
        P(),
        P("dp", None, "tensor"),
        P(None, "tensor"),
        P("dp", "tensor"),
        P(),
        P(),
        P(),
        P("dp", "tensor"),
        P("tensor"),
        P("dp", "tensor"),
        P(),
    )
    shards = fast_shards if mesh.shape["dp"] == 16 and mesh.shape["tensor"] == 2 else general_shards
    return jax.shard_map(shards, mesh=mesh, in_specs=in_specs, out_specs=out_specs, check_vma=False)
```

```python
import jax
import jax.numpy as jnp
from jax import lax
from jax.experimental import pallas as pl
from jax.experimental.pallas import tpu as pltpu
from jax.sharding import PartitionSpec as P

HDIM = 64
MICRO = 2


def mixed(form, left, right):
    return jnp.einsum(form, left, right, preferred_element_type=jnp.float32)


def normalize(values, gain, shift):
    mean_val = jnp.mean(values, axis=-1, keepdims=True)
    centered = values - mean_val
    inv_std = lax.rsqrt(jnp.mean(centered * centered, axis=-1, keepdims=True) + 1e-05)
    unit_val = centered * inv_std
    return (unit_val * gain + shift, unit_val, inv_std)


def normalize_back(grad_in, unit_val, inv_std, gain):
    scaled = grad_in * gain
    return inv_std * (
        scaled
        - jnp.mean(scaled, axis=-1, keepdims=True)
        - unit_val * jnp.mean(scaled * unit_val, axis=-1, keepdims=True)
    )


def token_sum(values):
    return jnp.sum(values, axis=(0, 1))


def general_shards(
    tokens,
    image_mask,
    out_grad,
    norm1_gain,
    norm1_shift,
    qkv_weight,
    qv_bias,
    out_weight,
    out_bias,
    norm2_gain,
    norm2_shift,
    up_weight,
    up_bias,
    down_weight,
    down_bias,
):
    images_here = tokens.shape[0] // MICRO
    full_width = norm1_gain.shape[0]
    local_width = qkv_weight.shape[2]
    local_hidden = up_weight.shape[1]
    local_heads = local_width // HDIM
    score_scale = HDIM ** (-0.5)
    gain_one = norm1_gain.astype(jnp.float32)
    shift_one = norm1_shift.astype(jnp.float32)
    gain_two = norm2_gain.astype(jnp.float32)
    shift_two = norm2_shift.astype(jnp.float32)
    bias_pair = qv_bias.astype(jnp.float32)
    grad_qkv = jnp.zeros((full_width, 3, local_width), jnp.float32)
    grad_out = jnp.zeros((full_width, local_width), jnp.float32)
    grad_up = jnp.zeros((full_width, local_hidden), jnp.float32)
    grad_down = jnp.zeros((full_width, local_hidden), jnp.float32)
    grad_gain_one = jnp.zeros((full_width,), jnp.float32)
    grad_shift_one = jnp.zeros((full_width,), jnp.float32)
    grad_gain_two = jnp.zeros((full_width,), jnp.float32)
    grad_shift_two = jnp.zeros((full_width,), jnp.float32)
    grad_out_bias = jnp.zeros((full_width,), jnp.float32)
    grad_down_bias = jnp.zeros((full_width,), jnp.float32)
    grad_pair = jnp.zeros((2, local_width), jnp.float32)
    grad_up_bias = jnp.zeros((local_hidden,), jnp.float32)
    outputs = []
    input_grads = []
    for micro_index in range(MICRO):
        first_image = micro_index * images_here
        block_rows = tokens[first_image : first_image + images_here].astype(jnp.float32)
        keep_mask = image_mask[first_image : first_image + images_here].astype(jnp.float32)[
            :, None, None
        ]
        fwd_weights = (
            lax.all_gather(qkv_weight, "dp", axis=0, tiled=True),
            lax.all_gather(out_weight, "dp", axis=0, tiled=True),
            lax.all_gather(up_weight, "dp", axis=0, tiled=True),
            lax.all_gather(down_weight, "dp", axis=0, tiled=True),
        )
        qkv_full, out_full, up_full, down_full = fwd_weights
        normed, unit_one, inv_one = normalize(block_rows, gain_one, shift_one)
        normed_full = lax.all_gather(normed.astype(jnp.bfloat16), "tensor", axis=1, tiled=True)
        seq_len = normed_full.shape[1]
        head_shape = (images_here, seq_len, local_heads, HDIM)
        projected = mixed("isd,dcf->iscf", normed_full, qkv_full)
        queries = (projected[:, :, 0] + bias_pair[0]).astype(jnp.bfloat16).reshape(head_shape)
        key_rows = projected[:, :, 1].astype(jnp.bfloat16).reshape(head_shape)
        value_rows = (projected[:, :, 2] + bias_pair[1]).astype(jnp.bfloat16).reshape(head_shape)
        scores = mixed("iqhe,ikhe->ihqk", queries, key_rows) * score_scale
        row_top = jnp.max(scores, axis=-1, keepdims=True)
        raw_weights = jnp.exp(scores - row_top)
        row_total = jnp.sum(raw_weights, axis=-1, keepdims=True)
        log_total = row_top + jnp.log(row_total)
        probs = (raw_weights / row_total).astype(jnp.bfloat16)
        context = mixed("ihqk,ikhe->iqhe", probs, value_rows).astype(jnp.bfloat16)
        context = context.reshape(images_here, seq_len, local_width)
        attn_terms = mixed("isf,of->iso", context, out_full)
        branch = lax.psum_scatter(
            attn_terms, "tensor", scatter_dimension=1, tiled=True
        ) + out_bias.astype(jnp.float32)
        middle = block_rows + branch
        second, unit_two, inv_two = normalize(middle, gain_two, shift_two)
        second_full = lax.all_gather(second.astype(jnp.bfloat16), "tensor", axis=1, tiled=True)
        hidden = mixed("isd,df->isf", second_full, up_full) + up_bias.astype(jnp.float32)
        gate_sig = jax.nn.sigmoid(1.702 * hidden)
        active = (hidden * gate_sig).astype(jnp.bfloat16)
        feed_terms = mixed("isf,of->iso", active, down_full)
        feed_out = lax.psum_scatter(
            feed_terms.astype(jnp.bfloat16), "tensor", scatter_dimension=1, tiled=True
        ).astype(jnp.float32) + down_bias.astype(jnp.float32)
        outputs.append(((middle + feed_out) * keep_mask).astype(jnp.bfloat16))
        back_weights = (
            lax.all_gather(qkv_weight, "dp", axis=0, tiled=True),
            lax.all_gather(out_weight, "dp", axis=0, tiled=True),
            lax.all_gather(up_weight, "dp", axis=0, tiled=True),
            lax.all_gather(down_weight, "dp", axis=0, tiled=True),
        )
        qkv_back, out_back, up_back, down_back = back_weights
        grad_final = (
            out_grad[first_image : first_image + images_here].astype(jnp.float32) * keep_mask
        )
        grad_down_bias = grad_down_bias + token_sum(grad_final)
        final_full = lax.all_gather(grad_final.astype(jnp.bfloat16), "tensor", axis=1, tiled=True)
        grad_down = grad_down + mixed("iso,isf->of", final_full, active)
        grad_active = mixed("iso,of->isf", final_full, down_back)
        grad_hidden = (
            grad_active * (gate_sig + 1.702 * hidden * gate_sig * (1.0 - gate_sig))
        ).astype(jnp.bfloat16)
        grad_up_bias = grad_up_bias + token_sum(grad_hidden.astype(jnp.float32))
        grad_up = grad_up + mixed("isd,isf->df", second_full, grad_hidden)
        second_terms = mixed("isf,df->isd", grad_hidden, up_back)
        grad_second = lax.psum_scatter(second_terms, "tensor", scatter_dimension=1, tiled=True)
        grad_gain_two = grad_gain_two + token_sum(grad_second * unit_two)
        grad_shift_two = grad_shift_two + token_sum(grad_second)
        grad_middle = grad_final + normalize_back(grad_second, unit_two, inv_two, gain_two)
        grad_branch = grad_middle.astype(jnp.bfloat16)
        grad_out_bias = grad_out_bias + token_sum(grad_branch.astype(jnp.float32))
        branch_full = lax.all_gather(grad_branch, "tensor", axis=1, tiled=True)
        grad_out = grad_out + mixed("iso,isf->of", branch_full, context)
        grad_context = (
            mixed("iso,of->isf", branch_full, out_back).astype(jnp.bfloat16).reshape(head_shape)
        )
        again = mixed("iqhe,ikhe->ihqk", queries, key_rows) * score_scale
        soft_again = jnp.exp(again - log_total)
        probs_again = soft_again.astype(jnp.bfloat16)
        grad_values = mixed("ihqk,iqhe->ikhe", probs_again, grad_context)
        grad_soft = mixed("iqhe,ikhe->ihqk", grad_context, value_rows)
        grad_scores = (
            soft_again * (grad_soft - jnp.sum(grad_soft * soft_again, axis=-1, keepdims=True))
        ).astype(jnp.bfloat16)
        grad_queries = mixed("ihqk,ikhe->iqhe", grad_scores, key_rows) * score_scale
        grad_keys = mixed("ihqk,iqhe->ikhe", grad_scores, queries) * score_scale
        flat_shape = (images_here, seq_len, local_width)
        grad_projected = jnp.stack(
            (
                grad_queries.reshape(flat_shape),
                grad_keys.reshape(flat_shape),
                grad_values.reshape(flat_shape),
            ),
            axis=2,
        ).astype(jnp.bfloat16)
        pair_terms = grad_projected.astype(jnp.float32)
        grad_pair = grad_pair + jnp.stack(
            (token_sum(pair_terms[:, :, 0]), token_sum(pair_terms[:, :, 2])), axis=0
        )
        grad_qkv = grad_qkv + mixed("isd,iscf->dcf", normed_full, grad_projected)
        normed_terms = mixed("iscf,dcf->isd", grad_projected, qkv_back)
        grad_normed = lax.psum_scatter(
            normed_terms.astype(jnp.bfloat16), "tensor", scatter_dimension=1, tiled=True
        ).astype(jnp.float32)
        grad_gain_one = grad_gain_one + token_sum(grad_normed * unit_one)
        grad_shift_one = grad_shift_one + token_sum(grad_normed)
        grad_tokens = grad_middle + normalize_back(grad_normed, unit_one, inv_one, gain_one)
        input_grads.append(grad_tokens.astype(jnp.bfloat16))
    grad_qkv, grad_out, grad_up, grad_down = (
        lax.psum_scatter(
            grad_qkv.astype(jnp.bfloat16), "dp", scatter_dimension=0, tiled=True
        ).astype(jnp.float32),
        lax.psum_scatter(
            grad_out.astype(jnp.bfloat16), "dp", scatter_dimension=0, tiled=True
        ).astype(jnp.float32),
        lax.psum_scatter(
            grad_up.astype(jnp.bfloat16), "dp", scatter_dimension=0, tiled=True
        ).astype(jnp.float32),
        lax.psum_scatter(
            grad_down.astype(jnp.bfloat16), "dp", scatter_dimension=0, tiled=True
        ).astype(jnp.float32),
    )
    grad_gain_one, grad_shift_one, grad_gain_two, grad_shift_two, grad_out_bias, grad_down_bias = (
        lax.psum(
            (
                grad_gain_one,
                grad_shift_one,
                grad_gain_two,
                grad_shift_two,
                grad_out_bias,
                grad_down_bias,
            ),
            ("dp", "tensor"),
        )
    )
    grad_pair, grad_up_bias = lax.psum((grad_pair, grad_up_bias), "dp")
    block_out = jnp.concatenate(outputs, axis=0)
    tokens_grad = jnp.concatenate(input_grads, axis=0)
    return (
        block_out,
        tokens_grad,
        grad_gain_one,
        grad_shift_one,
        grad_qkv,
        grad_pair,
        grad_out,
        grad_out_bias,
        grad_gain_two,
        grad_shift_two,
        grad_up,
        grad_up_bias,
        grad_down,
        grad_down_bias,
    )


ROWS = 64
PART = 256
VMEM_BYTES = 60 * 1024 * 1024
LOG2_E = 1.4426950408889634
BF16 = jnp.bfloat16
F32 = jnp.float32


def swap(values, axis_name, flip):
    count = lax.axis_size(axis_name)
    return lax.ppermute(values, axis_name, [(place, place ^ flip) for place in range(count)])


def over_core(values):
    return swap(values, "dp", 1)


def over_y(values):
    return swap(values, "dp", 2)


def over_z(values, step):
    return swap(values, "dp", 4 * step)


def over_x(values):
    return swap(values, "tensor", 1)


def gather_pieces(own, x_first):
    base = jnp.concatenate([own] + [over_z(own, step) for step in (1, 2, 3)], axis=0)
    if x_first:
        side = over_x(base)
        near = [base, side, over_y(base), over_y(side)]
    else:
        side = over_y(base)
        near = [base, over_x(base), side, over_x(side)]
    return near + [over_core(piece) for piece in near]


def add_low(mine, other):
    return (mine.astype(F32) + other.astype(F32)).astype(BF16)


def scatter_near(near, x_first):
    if x_first:
        pair = [add_low(near[2 * y_at], over_x(near[2 * y_at + 1])) for y_at in range(2)]
        whole_sum = add_low(pair[0], over_y(pair[1]))
    else:
        pair = [add_low(near[x_at], over_y(near[2 + x_at])) for x_at in range(2)]
        whole_sum = add_low(pair[0], over_x(pair[1]))
    parts = [whole_sum[:ROWS]] + [
        over_z(whole_sum[step * ROWS : (step + 1) * ROWS], step) for step in (1, 2, 3)
    ]
    parts = [part.astype(F32) for part in parts]
    return (parts[0] + parts[1]) + (parts[2] + parts[3])


def dot_nn(left, right):
    return lax.dot_general(left, right, (((1,), (0,)), ((), ())), preferred_element_type=F32)


def dot_nt(left, right):
    return lax.dot_general(left, right, (((1,), (1,)), ((), ())), preferred_element_type=F32)


def dot_tn(left, right):
    return lax.dot_general(left, right, (((0,), (0,)), ((), ())), preferred_element_type=F32)


def call(kernel, grid, in_specs, out_specs, out_shape, flops, moved):
    return pl.pallas_call(
        kernel,
        grid=grid,
        in_specs=in_specs,
        out_specs=out_specs,
        out_shape=out_shape,
        compiler_params=pltpu.CompilerParams(vmem_limit_bytes=VMEM_BYTES),
        cost_estimate=pl.CostEstimate(flops=int(flops), bytes_accessed=int(moved), transcendentals=0),
    )


def fixed(*shape, at=None):
    place = at or (0,) * len(shape)
    return pl.BlockSpec(shape, lambda *_: place, pipeline_mode=pl.Buffered(1))


def struct(shape, dtype=BF16):
    return jax.ShapeDtypeStruct(shape, dtype)


def normal_parts(values):
    mean_val = jnp.mean(values, axis=-1, keepdims=True)
    centered = values - mean_val
    inv_std = lax.rsqrt(jnp.mean(centered * centered, axis=-1, keepdims=True) + 1e-05)
    return centered * inv_std, inv_std


def column_sum(values):
    return jnp.sum(values, axis=0, keepdims=True)


def prepare(raw, order, gain, shift, keep, grads, tile=288):
    count, width = raw.shape

    def kernel(raw_ref, grad_ref, keep_ref, order_ref, gain_ref, shift_ref, rows_ref, norm_ref, final_ref, sum_ref):
        rows = dot_nn(raw_ref[...], order_ref[...])
        rows_ref[...] = rows.astype(BF16)
        unit, _ = normal_parts(rows)
        norm_ref[...] = (unit * gain_ref[...] + shift_ref[...]).astype(BF16)
        final = dot_nn(grad_ref[...], order_ref[...]) * keep_ref[...]
        final_ref[...] = final.astype(BF16)

        @pl.when(pl.program_id(0) == 0)
        def _():
            sum_ref[...] = jnp.zeros_like(sum_ref)

        sum_ref[...] += column_sum(final)

    block = pl.BlockSpec((tile, width), lambda i: (i, 0))
    return call(
        kernel,
        (count // tile,),
        [block, block, pl.BlockSpec((tile, 1), lambda i: (i, 0)), fixed(width, width), fixed(1, width), fixed(1, width)],
        [block, block, block, fixed(1, width)],
        [struct((count, width))] * 3 + [struct((1, width), F32)],
        4 * count * width * width,
        12 * count * width,
    )(raw, grads, keep, order, gain, shift)


def project(normed, pieces, bias):
    count, width = normed.shape
    half = width // 2

    def kernel(norm_ref, bias_ref, *refs):
        parts, out_ref = refs[:8], refs[8]
        for x_at in range(2):
            weight = jnp.concatenate([parts[2 * at + x_at][...] for at in range(4)], axis=0)
            columns = slice(x_at * half, (x_at + 1) * half)
            out_ref[0, :, columns] = (
                dot_nn(norm_ref[...], weight) + bias_ref[0, :, columns]
            ).astype(BF16)

    return call(
        kernel,
        (3,),
        [fixed(count, width), pl.BlockSpec((1, 1, width), lambda j: (j, 0, 0))]
        + [pl.BlockSpec((PART, half), lambda j: (0, j))] * 8,
        pl.BlockSpec((1, count, width), lambda j: (j, 0, 0)),
        struct((3, count, width)),
        6 * count * width * width,
        8 * count * width + 6 * width * width,
    )(normed, bias, *pieces)


def attend(projected, lanes=256):
    _, _, images, half_len, width = projected.shape
    length = 2 * half_len
    per_step = lanes // HDIM

    def kernel(proj_ref, out_ref, probs_ref):
        queries, key_rows, value_rows = (proj_ref[at].reshape(length, lanes) for at in range(3))
        outs = []
        for head in range(per_step):
            columns = slice(head * HDIM, (head + 1) * HDIM)
            scores = dot_nt(queries[:, columns], key_rows[:, columns])
            top = jnp.max(scores, axis=-1, keepdims=True)
            raw = jnp.exp2((scores - top) * (LOG2_E * HDIM**-0.5))
            probs = (raw * (1.0 / jnp.sum(raw, axis=-1, keepdims=True))).astype(BF16)
            probs_ref[0, head] = probs
            outs.append(dot_nn(probs, value_rows[:, columns]).astype(BF16))
        out_ref[...] = jnp.concatenate(outs, axis=1).reshape(out_ref.shape)

    heads = width // HDIM
    return call(
        kernel,
        (images, width // lanes),
        [pl.BlockSpec((3, 2, 1, half_len, lanes), lambda i, j: (0, 0, i, 0, j))],
        [
            pl.BlockSpec((2, 1, half_len, lanes), lambda i, j: (0, i, 0, j)),
            pl.BlockSpec((1, per_step, length, length), lambda i, j: (i, j, 0, 0)),
        ],
        [struct((2, images, half_len, width)), struct((images, heads, length, length))],
        16 * images * heads * length * length * HDIM,
        images * heads * length * length * 2,
    )(projected)


def attend_back(projected, grad_context, probs, lanes=256):
    _, _, images, half_len, width = projected.shape
    length = 2 * half_len
    per_step = lanes // HDIM
    scale = HDIM**-0.5

    def kernel(proj_ref, grad_ref, probs_ref, out_ref, sum_ref):
        queries, key_rows, value_rows = (proj_ref[at].reshape(length, lanes) for at in range(3))
        grads = grad_ref[...].reshape(length, lanes)
        found = ([], [], [])
        for head in range(per_step):
            columns = slice(head * HDIM, (head + 1) * HDIM)
            low = probs_ref[0, head]
            found[2].append(dot_tn(low, grads[:, columns]).astype(BF16))
            grad_soft = dot_nt(grads[:, columns], value_rows[:, columns])
            soft = low.astype(F32)
            scaled = soft * grad_soft
            grad_scores = (scaled - soft * jnp.sum(scaled, axis=-1, keepdims=True)).astype(BF16)
            found[0].append((dot_nn(grad_scores, key_rows[:, columns]) * scale).astype(BF16))
            found[1].append((dot_tn(grad_scores, queries[:, columns]) * scale).astype(BF16))
        for at in range(3):
            joined = jnp.concatenate(found[at], axis=1)
            out_ref[at] = joined.reshape(2, 1, half_len, lanes)
            if at != 1:
                sum_ref[0, at // 2 : at // 2 + 1] = column_sum(joined.astype(F32))

    heads = width // HDIM
    block = pl.BlockSpec((3, 2, 1, half_len, lanes), lambda i, j: (0, 0, i, 0, j))
    return call(
        kernel,
        (images, width // lanes),
        [
            block,
            pl.BlockSpec((2, 1, half_len, lanes), lambda i, j: (0, i, 0, j)),
            pl.BlockSpec((1, per_step, length, length), lambda i, j: (i, j, 0, 0)),
        ],
        [block, pl.BlockSpec((1, 2, lanes), lambda i, j: (i, 0, j))],
        [struct(projected.shape), struct((images, 2, width), F32)],
        24 * images * heads * length * length * HDIM,
        images * heads * length * length * 2,
    )(projected, grad_context, probs)


def add_branch(context, rows, pieces, bias, gain, shift, tile=288):
    count, width = rows.shape
    half = width // 2

    def kernel(context_ref, rows_ref, bias_ref, gain_ref, shift_ref, *refs):
        parts, middle_ref, norm_ref = refs[:8], refs[8], refs[9]
        found = []
        for at in range(4):
            weight = jnp.concatenate([parts[2 * at][...], parts[2 * at + 1][...]], axis=1)
            found.append(dot_nt(context_ref[...], weight))
        middle = rows_ref[...].astype(F32) + (jnp.concatenate(found, axis=1) + bias_ref[...])
        middle_ref[...] = middle
        unit, _ = normal_parts(middle)
        norm_ref[...] = (unit * gain_ref[...] + shift_ref[...]).astype(BF16)

    block = pl.BlockSpec((tile, width), lambda i: (i, 0))
    return call(
        kernel,
        (count // tile,),
        [block, block] + [fixed(1, width)] * 3 + [fixed(PART, half, at=(0, 3))] * 8,
        [block, block],
        [struct((count, width), F32), struct((count, width))],
        2 * count * width * width,
        10 * count * width + 2 * width * width,
    )(context, rows, bias, gain, shift, *pieces)


def feed_up(second, pieces, bias, tile=512):
    count, width = second.shape
    columns = pieces[0].shape[1]

    def kernel(second_ref, bias_ref, *refs):
        parts, active_ref, slope_ref = refs[:8], refs[8], refs[9]
        for x_at in range(2):
            weight = jnp.concatenate([parts[2 * at + x_at][...] for at in range(4)], axis=0)
            hidden = dot_nn(second_ref[...], weight) + bias_ref[x_at]
            gate = 0.5 + 0.5 * jnp.tanh(0.851 * hidden)
            active_ref[x_at] = (hidden * gate).astype(BF16)
            slope_ref[x_at] = (gate * (1.0 + 1.702 * hidden * (1.0 - gate))).astype(BF16)

    block = pl.BlockSpec((2, count, tile), lambda j: (0, 0, j))
    return call(
        kernel,
        (columns // tile,),
        [fixed(count, width), pl.BlockSpec((2, 1, tile), lambda j: (0, 0, j))]
        + [pl.BlockSpec((PART, tile), lambda j: (0, j))] * 8,
        [block, block],
        [struct((2, count, columns))] * 2,
        4 * count * width * columns,
        4 * count * (width + 2 * columns) + 4 * width * columns,
    )(second, bias, *pieces)


def feed_down(active, middle, keep, pieces, bias, order, tile=288):
    _, count, columns = active.shape
    width = middle.shape[1]

    def kernel(active_ref, middle_ref, keep_ref, bias_ref, order_ref, *refs):
        parts, out_ref = refs[:8], refs[8]
        found = []
        for at in range(4):
            found.append(
                dot_nt(active_ref[0], parts[2 * at][...]) + dot_nt(active_ref[1], parts[2 * at + 1][...])
            )
        feed = jnp.concatenate(found, axis=1) + bias_ref[...]
        out = ((middle_ref[...] + feed) * keep_ref[...]).astype(BF16)
        out_ref[...] = dot_nt(out, order_ref[...]).astype(BF16)

    block = pl.BlockSpec((tile, width), lambda i: (i, 0))
    return call(
        kernel,
        (count // tile,),
        [
            pl.BlockSpec((2, tile, columns), lambda i: (0, i, 0)),
            block,
            pl.BlockSpec((tile, 1), lambda i: (i, 0)),
            fixed(1, width),
            fixed(width, width),
        ]
        + [fixed(PART, columns)] * 8,
        block,
        struct((count, width)),
        4 * count * width * columns + 2 * count * width * width,
        4 * count * columns + 6 * count * width + 4 * width * columns,
    )(active, middle, keep, bias, order, *pieces)


def gate_back(final, slope, pieces, tile=512):
    count, width = final.shape
    columns = pieces[0].shape[1]

    def kernel(final_ref, slope_ref, *refs):
        parts, out_ref, sum_ref = refs[:8], refs[8], refs[9]
        for x_at in range(2):
            weight = jnp.concatenate([parts[2 * at + x_at][...] for at in range(4)], axis=0)
            grad = (dot_nn(final_ref[...], weight) * slope_ref[x_at].astype(F32)).astype(BF16)
            out_ref[x_at] = grad
            sum_ref[x_at] = column_sum(grad.astype(F32))

    block = pl.BlockSpec((2, count, tile), lambda j: (0, 0, j))
    return call(
        kernel,
        (columns // tile,),
        [fixed(count, width), block] + [pl.BlockSpec((PART, tile), lambda j: (0, j))] * 8,
        [block, pl.BlockSpec((2, 1, tile), lambda j: (0, 0, j))],
        [struct((2, count, columns)), struct((2, 1, columns), F32)],
        4 * count * width * columns,
        4 * count * (width + 2 * columns) + 4 * width * columns,
    )(final, slope, *pieces)


def weight_half(left, rights, far, received=None, tile=512):
    count, width = left.shape
    right, right_spec, pick, columns = rights
    half = width // 2

    def kernel(left_ref, right_ref, *refs):
        for y_at in range(2):
            for x_at in range(2):
                at = 2 * y_at + x_at
                part = dot_tn(left_ref[:, y_at * PART : (y_at + 1) * PART], pick(right_ref, x_at))
                if received is None:
                    refs[at][...] = part.astype(BF16)
                else:
                    refs[4 + at][...] = (part + refs[at][...].astype(F32)).astype(BF16)

    block = pl.BlockSpec((PART, tile), lambda j: (0, j))
    extra = [] if received is None else list(received)
    return call(
        kernel,
        (columns // tile,),
        [fixed(count, half, at=(0, far)), right_spec] + [block] * len(extra),
        [block] * 4,
        [struct((PART, columns))] * 4,
        2 * count * half * 2 * columns,
        4 * count * columns + count * width + width * columns * (4 if extra else 2),
    )(left, right, *extra)


def weight_sum(left, rights, x_first, tile=512):
    far = weight_half(left, rights, 1, None, tile)
    received = [over_core(piece) for piece in far]
    near = weight_half(left, rights, 0, received, tile)
    return scatter_near(near, x_first)


def second_back(grad_hidden, up_pieces, first_pieces, middle, final, gain, tile=288):
    _, count, columns = grad_hidden.shape
    width = middle.shape[1]
    half = width // 2

    def kernel(hidden_ref, middle_ref, final_ref, gain_ref, *refs):
        ups, outs = refs[:8], refs[8:16]
        grad_ref, branch_ref, context_ref, sum_ref = refs[16:]
        found = []
        for at in range(4):
            found.append(
                dot_nt(hidden_ref[0], ups[2 * at][...]) + dot_nt(hidden_ref[1], ups[2 * at + 1][...])
            )
        grad_second = jnp.concatenate(found, axis=1)
        unit, inv_std = normal_parts(middle_ref[...])
        grad_middle = final_ref[...].astype(F32) + normalize_back(
            grad_second, unit, inv_std, gain_ref[...]
        )
        branch = grad_middle.astype(BF16)
        grad_ref[...] = grad_middle
        branch_ref[...] = branch
        for x_at in range(2):
            weight = jnp.concatenate([outs[2 * at + x_at][...] for at in range(4)], axis=0)
            context_ref[:, x_at * half : (x_at + 1) * half] = dot_nn(branch, weight).astype(BF16)

        @pl.when(pl.program_id(0) == 0)
        def _():
            sum_ref[...] = jnp.zeros_like(sum_ref)

        sum_ref[0:1] += column_sum(grad_second * unit)
        sum_ref[1:2] += column_sum(grad_second)
        sum_ref[2:3] += column_sum(branch.astype(F32))

    block = pl.BlockSpec((tile, width), lambda i: (i, 0))
    return call(
        kernel,
        (count // tile,),
        [pl.BlockSpec((2, tile, columns), lambda i: (0, i, 0)), block, block, fixed(1, width)]
        + [fixed(PART, columns)] * 8
        + [fixed(PART, half, at=(0, 3))] * 8,
        [block, block, block, fixed(8, width)],
        [struct((count, width), F32), struct((count, width)), struct((count, width)), struct((8, width), F32)],
        4 * count * width * columns + 2 * count * width * width,
        4 * count * columns + 14 * count * width + 4 * width * columns,
    )(grad_hidden, middle, final, gain, *up_pieces, *first_pieces)


def first_back(grad_projected, pieces, rows, grad_middle, gain, order, tile=288):
    _, count, width = grad_projected.shape
    half = width // 2

    def kernel(grad_ref, rows_ref, middle_ref, gain_ref, order_ref, *refs):
        parts, out_ref, sum_ref = refs[:8], refs[8], refs[9]
        lefts = [
            jnp.concatenate([grad_ref[at, :, x_at * half : (x_at + 1) * half] for at in range(3)], axis=1)
            for x_at in range(2)
        ]
        found = []
        for at in range(4):
            found.append(
                dot_nt(lefts[0], parts[2 * at][...]) + dot_nt(lefts[1], parts[2 * at + 1][...])
            )
        grad_normed = jnp.concatenate(found, axis=1)
        unit, inv_std = normal_parts(rows_ref[...].astype(F32))
        out = middle_ref[...] + normalize_back(grad_normed, unit, inv_std, gain_ref[...])
        out_ref[...] = dot_nt(out.astype(BF16), order_ref[...]).astype(BF16)

        @pl.when(pl.program_id(0) == 0)
        def _():
            sum_ref[...] = jnp.zeros_like(sum_ref)

        sum_ref[0:1] += column_sum(grad_normed * unit)
        sum_ref[1:2] += column_sum(grad_normed)

    block = pl.BlockSpec((tile, width), lambda i: (i, 0))
    return call(
        kernel,
        (count // tile,),
        [pl.BlockSpec((3, tile, width), lambda i: (0, i, 0)), block, block, fixed(1, width), fixed(width, width)]
        + [fixed(PART, 3 * half)] * 8,
        [block, fixed(8, width)],
        [struct((count, width)), struct((8, width), F32)],
        6 * count * width * width + 2 * count * width * width,
        16 * count * width + 6 * width * width,
    )(grad_projected, rows, grad_middle, gain, order, *pieces)


def fast_shards(
    tokens,
    image_mask,
    out_grad,
    norm1_gain,
    norm1_shift,
    qkv_weight,
    qv_bias,
    out_weight,
    out_bias,
    norm2_gain,
    norm2_shift,
    up_weight,
    up_bias,
    down_weight,
    down_bias,
):
    images, half_len, width = tokens.shape
    mine = images // 2
    half = qkv_weight.shape[2]
    half_hidden = up_weight.shape[1]
    count = 2 * mine * half_len
    me = lax.axis_index("dp")
    side = lax.axis_index("tensor")
    block = jnp.arange(width) // ROWS
    core_rel, y_rel, z_rel = block // 8, (block // 4) % 2, block % 4
    source = ((z_rel * 4 + y_rel * 2 + core_rel) ^ me) * ROWS + jnp.arange(width) % ROWS
    order = (jnp.arange(width)[:, None] == source[None, :]).astype(BF16)

    def exchange(values):
        keep_part = lax.dynamic_slice_in_dim(values, side * mine, mine, 0)
        send_part = lax.dynamic_slice_in_dim(values, (1 - side) * mine, mine, 0)
        return jnp.stack([keep_part, over_x(send_part)]).reshape(count, width)

    def give_back(values):
        values = values.reshape(2, mine, half_len, width)
        own, other = values[0], over_x(values[1])
        low_part = jnp.where(side == 0, own, other)
        high_part = jnp.where(side == 0, other, own)
        return jnp.concatenate([low_part, high_part], axis=0)

    first = jnp.concatenate([qkv_weight.reshape(ROWS, 3 * half), out_weight], axis=1)
    first_pieces = gather_pieces(first, True)
    raw = exchange(tokens)
    raw_grad = exchange(out_grad)
    up_pieces = gather_pieces(up_weight, False)
    down_pieces = gather_pieces(down_weight, True)
    biases = jnp.concatenate([qv_bias.reshape(-1), up_bias])
    biases = jnp.stack([biases, over_x(biases)]).astype(F32)
    bias_q = biases[:, :half].reshape(1, width)
    bias_v = biases[:, half : 2 * half].reshape(1, width)
    bias_qkv = jnp.stack([bias_q, jnp.zeros_like(bias_q), bias_v])
    bias_up = biases[:, 2 * half :].reshape(2, 1, half_hidden)
    vectors = jnp.stack([norm1_gain, norm1_shift, norm2_gain, norm2_shift, out_bias, down_bias])
    vectors = jnp.matmul(vectors, order, preferred_element_type=F32)
    gain_one, shift_one, gain_two, shift_two, bias_out, bias_down = (
        vectors[at : at + 1] for at in range(6)
    )
    keep = lax.dynamic_slice_in_dim(image_mask.astype(F32), side * mine, mine, 0)
    keep = jnp.broadcast_to(keep[None, :, None], (2, mine, half_len)).reshape(count, 1)

    rows, normed, final, sum_final = prepare(raw, order, gain_one, shift_one, keep, raw_grad)
    projected = project(normed, first_pieces, bias_qkv)
    projected = projected.reshape(3, 2, mine, half_len, width)
    context, probs = attend(projected)
    context = context.reshape(count, width)
    middle, second = add_branch(context, rows, first_pieces, bias_out, gain_two, shift_two)
    active, slope = feed_up(second, up_pieces, bias_up)

    def hidden_right(values, tile=512):
        spec = pl.BlockSpec((2, count, tile), lambda j: (0, 0, j))
        return (values, spec, lambda ref, x_at: ref[x_at], half_hidden)

    grad_down = weight_sum(final, hidden_right(active), True)
    grad_hidden, sum_hidden = gate_back(final, slope, down_pieces)
    grad_up = weight_sum(second, hidden_right(grad_hidden), False)
    block_out = feed_down(active, middle, keep, down_pieces, bias_down, order)
    block_out = give_back(block_out)
    grad_middle, grad_branch, grad_context, sums_two = second_back(
        grad_hidden, up_pieces, first_pieces, middle, final, gain_two
    )

    def whole_right(values):
        spec = pl.BlockSpec((count, width), lambda j: (0, 0))
        return (values, spec, lambda ref, x_at: ref[:, x_at * half : (x_at + 1) * half], half)

    grad_out = weight_sum(grad_branch, whole_right(context), True)
    grad_context = grad_context.reshape(2, mine, half_len, width)
    grad_projected, sums_pair = attend_back(projected, grad_context, probs)
    grad_projected = grad_projected.reshape(3, count, width)
    spec = pl.BlockSpec((1, count, width), lambda j: (j, 0, 0))
    grad_qkv = weight_sum(
        normed,
        (grad_projected, spec, lambda ref, x_at: ref[0, :, x_at * half : (x_at + 1) * half], 3 * half),
        False,
    )
    tokens_grad, sums_one = first_back(
        grad_projected, first_pieces, rows, grad_middle, gain_one, order
    )
    tokens_grad = give_back(tokens_grad)

    sums = jnp.concatenate([sums_one[:2], sums_two[2:3], sums_two[:2], sum_final], axis=0)
    sums = jnp.zeros_like(sums).at[:, source].set(sums)
    sums_pair = jnp.sum(sums_pair, axis=0)
    halves = jnp.concatenate(
        [sums_pair[0].reshape(2, half), sums_pair[1].reshape(2, half), sum_hidden.reshape(2, half_hidden)],
        axis=1,
    )
    sums = sums + over_x(sums)
    halves = halves[0] + over_x(halves[1])
    small = jnp.concatenate([sums.reshape(-1), halves])
    small = small + over_core(small)
    small = small + over_y(small)
    small = (small + over_z(small, 1)) + (over_z(small, 2) + over_z(small, 3))
    sums = small[: 6 * width].reshape(6, width)
    halves = small[6 * width :]
    return (
        block_out,
        tokens_grad,
        sums[0],
        sums[1],
        grad_qkv.reshape(ROWS, 3, half),
        halves[: 2 * half].reshape(2, half),
        grad_out,
        sums[2],
        sums[3],
        sums[4],
        grad_up,
        halves[2 * half :],
        grad_down,
        sums[5],
    )


def solution(mesh):
    in_specs = (
        P("dp", "tensor", None),
        P("dp"),
        P("dp", "tensor", None),
        P(),
        P(),
        P("dp", None, "tensor"),
        P(None, "tensor"),
        P("dp", "tensor"),
        P(),
        P(),
        P(),
        P("dp", "tensor"),
        P("tensor"),
        P("dp", "tensor"),
        P(),
    )
    out_specs = (
        P("dp", "tensor", None),
        P("dp", "tensor", None),
        P(),
        P(),
        P("dp", None, "tensor"),
        P(None, "tensor"),
        P("dp", "tensor"),
        P(),
        P(),
        P(),
        P("dp", "tensor"),
        P("tensor"),
        P("dp", "tensor"),
        P(),
    )
    small_slice = mesh.shape["dp"] == 16 and mesh.shape["tensor"] == 2
    shards = fast_shards if small_slice else general_shards
    return jax.shard_map(shards, mesh=mesh, in_specs=in_specs, out_specs=out_specs, check_vma=False)
```

```python
import jax
import jax.numpy as jnp
from jax import lax
from jax.experimental import pallas as pl
from jax.experimental.pallas import tpu as pltpu
from jax.sharding import PartitionSpec as P

HDIM = 64
MICRO = 2


def mixed(form, left, right):
    return jnp.einsum(form, left, right, preferred_element_type=jnp.float32)


def normalize(values, gain, shift):
    mean_val = jnp.mean(values, axis=-1, keepdims=True)
    centered = values - mean_val
    inv_std = lax.rsqrt(jnp.mean(centered * centered, axis=-1, keepdims=True) + 1e-05)
    unit_val = centered * inv_std
    return (unit_val * gain + shift, unit_val, inv_std)


def normalize_back(grad_in, unit_val, inv_std, gain):
    scaled = grad_in * gain
    return inv_std * (
        scaled
        - jnp.mean(scaled, axis=-1, keepdims=True)
        - unit_val * jnp.mean(scaled * unit_val, axis=-1, keepdims=True)
    )


def token_sum(values):
    return jnp.sum(values, axis=(0, 1))


def general_shards(
    tokens,
    image_mask,
    out_grad,
    norm1_gain,
    norm1_shift,
    qkv_weight,
    qv_bias,
    out_weight,
    out_bias,
    norm2_gain,
    norm2_shift,
    up_weight,
    up_bias,
    down_weight,
    down_bias,
):
    images_here = tokens.shape[0] // MICRO
    full_width = norm1_gain.shape[0]
    local_width = qkv_weight.shape[2]
    local_hidden = up_weight.shape[1]
    local_heads = local_width // HDIM
    score_scale = HDIM ** (-0.5)
    gain_one = norm1_gain.astype(jnp.float32)
    shift_one = norm1_shift.astype(jnp.float32)
    gain_two = norm2_gain.astype(jnp.float32)
    shift_two = norm2_shift.astype(jnp.float32)
    bias_pair = qv_bias.astype(jnp.float32)
    grad_qkv = jnp.zeros((full_width, 3, local_width), jnp.float32)
    grad_out = jnp.zeros((full_width, local_width), jnp.float32)
    grad_up = jnp.zeros((full_width, local_hidden), jnp.float32)
    grad_down = jnp.zeros((full_width, local_hidden), jnp.float32)
    grad_gain_one = jnp.zeros((full_width,), jnp.float32)
    grad_shift_one = jnp.zeros((full_width,), jnp.float32)
    grad_gain_two = jnp.zeros((full_width,), jnp.float32)
    grad_shift_two = jnp.zeros((full_width,), jnp.float32)
    grad_out_bias = jnp.zeros((full_width,), jnp.float32)
    grad_down_bias = jnp.zeros((full_width,), jnp.float32)
    grad_pair = jnp.zeros((2, local_width), jnp.float32)
    grad_up_bias = jnp.zeros((local_hidden,), jnp.float32)
    outputs = []
    input_grads = []
    for micro_index in range(MICRO):
        first_image = micro_index * images_here
        block_rows = tokens[first_image : first_image + images_here].astype(jnp.float32)
        keep_mask = image_mask[first_image : first_image + images_here].astype(jnp.float32)[
            :, None, None
        ]
        fwd_weights = (
            lax.all_gather(qkv_weight, "dp", axis=0, tiled=True),
            lax.all_gather(out_weight, "dp", axis=0, tiled=True),
            lax.all_gather(up_weight, "dp", axis=0, tiled=True),
            lax.all_gather(down_weight, "dp", axis=0, tiled=True),
        )
        qkv_full, out_full, up_full, down_full = fwd_weights
        normed, unit_one, inv_one = normalize(block_rows, gain_one, shift_one)
        normed_full = lax.all_gather(normed.astype(jnp.bfloat16), "tensor", axis=1, tiled=True)
        seq_len = normed_full.shape[1]
        head_shape = (images_here, seq_len, local_heads, HDIM)
        projected = mixed("isd,dcf->iscf", normed_full, qkv_full)
        queries = (projected[:, :, 0] + bias_pair[0]).astype(jnp.bfloat16).reshape(head_shape)
        key_rows = projected[:, :, 1].astype(jnp.bfloat16).reshape(head_shape)
        value_rows = (projected[:, :, 2] + bias_pair[1]).astype(jnp.bfloat16).reshape(head_shape)
        scores = mixed("iqhe,ikhe->ihqk", queries, key_rows) * score_scale
        row_top = jnp.max(scores, axis=-1, keepdims=True)
        raw_weights = jnp.exp(scores - row_top)
        row_total = jnp.sum(raw_weights, axis=-1, keepdims=True)
        log_total = row_top + jnp.log(row_total)
        probs = (raw_weights / row_total).astype(jnp.bfloat16)
        context = mixed("ihqk,ikhe->iqhe", probs, value_rows).astype(jnp.bfloat16)
        context = context.reshape(images_here, seq_len, local_width)
        attn_terms = mixed("isf,of->iso", context, out_full)
        branch = lax.psum_scatter(
            attn_terms, "tensor", scatter_dimension=1, tiled=True
        ) + out_bias.astype(jnp.float32)
        middle = block_rows + branch
        second, unit_two, inv_two = normalize(middle, gain_two, shift_two)
        second_full = lax.all_gather(second.astype(jnp.bfloat16), "tensor", axis=1, tiled=True)
        hidden = mixed("isd,df->isf", second_full, up_full) + up_bias.astype(jnp.float32)
        gate_sig = jax.nn.sigmoid(1.702 * hidden)
        active = (hidden * gate_sig).astype(jnp.bfloat16)
        feed_terms = mixed("isf,of->iso", active, down_full)
        feed_out = lax.psum_scatter(
            feed_terms.astype(jnp.bfloat16), "tensor", scatter_dimension=1, tiled=True
        ).astype(jnp.float32) + down_bias.astype(jnp.float32)
        outputs.append(((middle + feed_out) * keep_mask).astype(jnp.bfloat16))
        back_weights = (
            lax.all_gather(qkv_weight, "dp", axis=0, tiled=True),
            lax.all_gather(out_weight, "dp", axis=0, tiled=True),
            lax.all_gather(up_weight, "dp", axis=0, tiled=True),
            lax.all_gather(down_weight, "dp", axis=0, tiled=True),
        )
        qkv_back, out_back, up_back, down_back = back_weights
        grad_final = (
            out_grad[first_image : first_image + images_here].astype(jnp.float32) * keep_mask
        )
        grad_down_bias = grad_down_bias + token_sum(grad_final)
        final_full = lax.all_gather(grad_final.astype(jnp.bfloat16), "tensor", axis=1, tiled=True)
        grad_down = grad_down + mixed("iso,isf->of", final_full, active)
        grad_active = mixed("iso,of->isf", final_full, down_back)
        grad_hidden = (
            grad_active * (gate_sig + 1.702 * hidden * gate_sig * (1.0 - gate_sig))
        ).astype(jnp.bfloat16)
        grad_up_bias = grad_up_bias + token_sum(grad_hidden.astype(jnp.float32))
        grad_up = grad_up + mixed("isd,isf->df", second_full, grad_hidden)
        second_terms = mixed("isf,df->isd", grad_hidden, up_back)
        grad_second = lax.psum_scatter(second_terms, "tensor", scatter_dimension=1, tiled=True)
        grad_gain_two = grad_gain_two + token_sum(grad_second * unit_two)
        grad_shift_two = grad_shift_two + token_sum(grad_second)
        grad_middle = grad_final + normalize_back(grad_second, unit_two, inv_two, gain_two)
        grad_branch = grad_middle.astype(jnp.bfloat16)
        grad_out_bias = grad_out_bias + token_sum(grad_branch.astype(jnp.float32))
        branch_full = lax.all_gather(grad_branch, "tensor", axis=1, tiled=True)
        grad_out = grad_out + mixed("iso,isf->of", branch_full, context)
        grad_context = (
            mixed("iso,of->isf", branch_full, out_back).astype(jnp.bfloat16).reshape(head_shape)
        )
        again = mixed("iqhe,ikhe->ihqk", queries, key_rows) * score_scale
        soft_again = jnp.exp(again - log_total)
        probs_again = soft_again.astype(jnp.bfloat16)
        grad_values = mixed("ihqk,iqhe->ikhe", probs_again, grad_context)
        grad_soft = mixed("iqhe,ikhe->ihqk", grad_context, value_rows)
        grad_scores = (
            soft_again * (grad_soft - jnp.sum(grad_soft * soft_again, axis=-1, keepdims=True))
        ).astype(jnp.bfloat16)
        grad_queries = mixed("ihqk,ikhe->iqhe", grad_scores, key_rows) * score_scale
        grad_keys = mixed("ihqk,iqhe->ikhe", grad_scores, queries) * score_scale
        flat_shape = (images_here, seq_len, local_width)
        grad_projected = jnp.stack(
            (
                grad_queries.reshape(flat_shape),
                grad_keys.reshape(flat_shape),
                grad_values.reshape(flat_shape),
            ),
            axis=2,
        ).astype(jnp.bfloat16)
        pair_terms = grad_projected.astype(jnp.float32)
        grad_pair = grad_pair + jnp.stack(
            (token_sum(pair_terms[:, :, 0]), token_sum(pair_terms[:, :, 2])), axis=0
        )
        grad_qkv = grad_qkv + mixed("isd,iscf->dcf", normed_full, grad_projected)
        normed_terms = mixed("iscf,dcf->isd", grad_projected, qkv_back)
        grad_normed = lax.psum_scatter(
            normed_terms.astype(jnp.bfloat16), "tensor", scatter_dimension=1, tiled=True
        ).astype(jnp.float32)
        grad_gain_one = grad_gain_one + token_sum(grad_normed * unit_one)
        grad_shift_one = grad_shift_one + token_sum(grad_normed)
        grad_tokens = grad_middle + normalize_back(grad_normed, unit_one, inv_one, gain_one)
        input_grads.append(grad_tokens.astype(jnp.bfloat16))
    grad_qkv, grad_out, grad_up, grad_down = (
        lax.psum_scatter(
            grad_qkv.astype(jnp.bfloat16), "dp", scatter_dimension=0, tiled=True
        ).astype(jnp.float32),
        lax.psum_scatter(
            grad_out.astype(jnp.bfloat16), "dp", scatter_dimension=0, tiled=True
        ).astype(jnp.float32),
        lax.psum_scatter(
            grad_up.astype(jnp.bfloat16), "dp", scatter_dimension=0, tiled=True
        ).astype(jnp.float32),
        lax.psum_scatter(
            grad_down.astype(jnp.bfloat16), "dp", scatter_dimension=0, tiled=True
        ).astype(jnp.float32),
    )
    grad_gain_one, grad_shift_one, grad_gain_two, grad_shift_two, grad_out_bias, grad_down_bias = (
        lax.psum(
            (
                grad_gain_one,
                grad_shift_one,
                grad_gain_two,
                grad_shift_two,
                grad_out_bias,
                grad_down_bias,
            ),
            ("dp", "tensor"),
        )
    )
    grad_pair, grad_up_bias = lax.psum((grad_pair, grad_up_bias), "dp")
    block_out = jnp.concatenate(outputs, axis=0)
    tokens_grad = jnp.concatenate(input_grads, axis=0)
    return (
        block_out,
        tokens_grad,
        grad_gain_one,
        grad_shift_one,
        grad_qkv,
        grad_pair,
        grad_out,
        grad_out_bias,
        grad_gain_two,
        grad_shift_two,
        grad_up,
        grad_up_bias,
        grad_down,
        grad_down_bias,
    )


ROWS = 64
PART = 256
VMEM_BYTES = 60 * 1024 * 1024
COST_PART = 0.6
FORWARD_PART = 0.8
LOG2_E = 1.4426950408889634
BF16 = jnp.bfloat16
F32 = jnp.float32


def swap(values, axis_name, flip):
    count = lax.axis_size(axis_name)
    return lax.ppermute(values, axis_name, [(place, place ^ flip) for place in range(count)])


def over_core(values):
    return swap(values, "dp", 1)


def over_y(values):
    return swap(values, "dp", 2)


def over_z(values, step):
    return swap(values, "dp", 4 * step)


def over_x(values):
    return swap(values, "tensor", 1)


def late(values, *marks):
    return lax.optimization_barrier((values, *marks))[0]


def dot_nn(left, right):
    return lax.dot_general(left, right, (((1,), (0,)), ((), ())), preferred_element_type=F32)


def dot_nt(left, right):
    return lax.dot_general(left, right, (((1,), (1,)), ((), ())), preferred_element_type=F32)


def dot_tn(left, right):
    return lax.dot_general(left, right, (((0,), (0,)), ((), ())), preferred_element_type=F32)


def call(
    kernel, grid, in_specs, out_specs, out_shape, flops, moved, after=(), aliases=None, scalars=0, part=None
):
    given, waits = scalars + len(in_specs), len(after)
    part = COST_PART if part is None else part

    def run(*refs):
        kernel(*refs[:given], *refs[given + waits :])

    function = pl.pallas_call(
        run,
        grid_spec=pltpu.PrefetchScalarGridSpec(
            num_scalar_prefetch=scalars,
            grid=grid,
            in_specs=list(in_specs) + [pl.BlockSpec(memory_space=pl.ANY)] * waits,
            out_specs=out_specs,
        ),
        out_shape=out_shape,
        input_output_aliases=aliases or {},
        compiler_params=pltpu.CompilerParams(vmem_limit_bytes=VMEM_BYTES),
        cost_estimate=pl.CostEstimate(
            flops=int(flops * part), bytes_accessed=int(moved * part), transcendentals=0
        ),
    )
    return lambda *arrays: function(*arrays, *after)


def fixed(*shape, at=None):
    place = at or (0,) * len(shape)
    return pl.BlockSpec(shape, lambda *_: place, pipeline_mode=pl.Buffered(1))


def far_list(near, far):
    return list(near) + [far[last].at[y_at] for y_at in range(2) for last in range(2)]


def piece_specs(columns, at=0):
    return [fixed(PART, columns, at=(0, at))] * 4 + [fixed(2, PART, columns, at=(0, 0, at))] * 2


def piece_tiles(tile, near=4, far=2):
    return [pl.BlockSpec((PART, tile), lambda j: (0, j))] * near + [
        pl.BlockSpec((2, PART, tile), lambda j: (0, 0, j))
    ] * far


def struct(shape, dtype=BF16):
    return jax.ShapeDtypeStruct(shape, dtype)


ANYWHERE = pl.BlockSpec(memory_space=pl.ANY)


def normal_parts(values):
    mean_val = jnp.mean(values, axis=-1, keepdims=True)
    centered = values - mean_val
    inv_std = lax.rsqrt(jnp.mean(centered * centered, axis=-1, keepdims=True) + 1e-05)
    return centered * inv_std, inv_std


def column_sum(values):
    return jnp.sum(values, axis=0, keepdims=True)


def combine(arrays, pieces, dtype=BF16, tile=1024, after=()):
    columns = arrays[0].shape[-1]
    rows = arrays[0].size // columns // pieces
    arrays = [values.reshape(pieces, rows, columns) for values in arrays]
    given = len(arrays)

    def kernel(*refs):
        for at in range(pieces):
            parts = [ref[at].astype(F32) for ref in refs[:given]]
            while len(parts) > 1:
                parts = [sum(parts[start : start + 2]) for start in range(0, len(parts), 2)]
            refs[given + at][...] = parts[0].astype(dtype)

    return call(
        kernel,
        (columns // tile,),
        [pl.BlockSpec((pieces, rows, tile), lambda j: (0, 0, j))] * given,
        [pl.BlockSpec((rows, tile), lambda j: (0, j))] * pieces,
        [struct((rows, columns), dtype)] * pieces,
        0,
        2 * pieces * rows * columns * (given + 1),
        after,
    )(*arrays)


def first_step():
    return pl.program_id(0) == 0


def setup(places, vectors, after=()):
    width = vectors[0].shape[1]
    given = len(vectors)

    def kernel(place_ref, *refs):
        order_ref = refs[given]
        source = lax.broadcasted_iota(jnp.int32, (width, width), 0)
        target = lax.broadcasted_iota(jnp.int32, (width, width), 1)
        at = target // ROWS
        z_rel, y_rel, core_rel = at % 4, (at // 4) % 2, at // 8
        place = (z_rel * 4 + y_rel * 2 + core_rel) ^ place_ref[1]
        hit = source == place * ROWS + target % ROWS
        order = jnp.where(hit, 1.0, 0.0).astype(BF16)
        order_ref[...] = order
        rows = jnp.concatenate([ref[...].astype(F32) for ref in refs[:given]] + [jnp.zeros((8 - given, width), F32)], axis=0)
        moved = dot_nn(rows.astype(BF16), order)
        for vector_at in range(given):
            refs[given + 1 + vector_at][...] = moved[vector_at : vector_at + 1]

    row = fixed(1, width)
    return call(
        kernel,
        (1,),
        [row] * given,
        [fixed(width, width)] + [row] * given,
        [struct((width, width))] + [struct((1, width), F32)] * given,
        16 * width * width,
        2 * width * width,
        after,
        None,
        1,
        part=FORWARD_PART,
    )(places, *vectors)


def image_block(height, width, offset):
    return pl.BlockSpec((1, height, width), lambda i, side: (offset(side) + i, 0, 0))


def prepare(side, images, order, gain, shift, half_at, before=None, after=()):
    _, height, width = images.shape
    mine = 2

    def kernel(side_ref, raw_ref, order_ref, gain_ref, shift_ref, *refs):
        rows_ref, norm_ref = refs[-2:]
        rows = dot_nn(raw_ref[0], order_ref[...])
        rows_ref[...] = rows.astype(BF16)
        unit, _ = normal_parts(rows)
        norm_ref[...] = (unit * gain_ref[...] + shift_ref[...]).astype(BF16)

    offset = (lambda side_ref: side_ref[0] * mine) if half_at == 0 else (lambda side_ref: 0)
    out = pl.BlockSpec((height, width), lambda i, _: (half_at * mine + i, 0))
    old = () if before is None else before
    return call(
        kernel,
        (mine,),
        [image_block(height, width, offset), fixed(width, width), fixed(1, width), fixed(1, width)]
        + [ANYWHERE] * len(old),
        [out, out],
        [struct((2 * mine * height, width))] * 2,
        2 * mine * height * width * width,
        6 * mine * height * width,
        after,
        {5: 0, 6: 1} if old else None,
        1,
        part=FORWARD_PART,
    )(side, images, order, gain, shift, *old)


def mask_grad(side, images, order, half_at, before=None, after=()):
    _, height, width = images.shape
    mine = 2

    def kernel(side_ref, raw_ref, order_ref, *refs):
        final_ref, plain_ref, sum_ref = refs[-3:]
        keep = side_ref[2 + side_ref[0] * mine + pl.program_id(0)].astype(F32)
        plain = (raw_ref[0].astype(F32) * keep).astype(BF16)
        plain_ref[...] = plain
        final = dot_nn(plain, order_ref[...])
        final_ref[...] = final.astype(BF16)

        @pl.when(first_step())
        def _():
            sum_ref[...] = jnp.zeros_like(sum_ref)

        sum_ref[...] += column_sum(final)

    offset = (lambda side_ref: side_ref[0] * mine) if half_at == 0 else (lambda side_ref: 0)
    old = () if before is None else before
    out = pl.BlockSpec((height, width), lambda i, _: (half_at * mine + i, 0))
    return call(
        kernel,
        (mine,),
        [image_block(height, width, offset), fixed(width, width)] + [ANYWHERE] * len(old),
        [out, out, fixed(1, width)],
        [struct((2 * mine * height, width))] * 2 + [struct((1, width), F32)],
        2 * mine * height * width * width,
        6 * mine * height * width,
        after,
        {3: 0, 4: 1} if old else None,
        1,
        part=FORWARD_PART,
    )(side, images, order, *old)


def project(normed, parts, bias, after=()):
    count, width = normed.shape
    half = bias.shape[-1]

    def kernel(norm_ref, bias_ref, *refs):
        weight = jnp.concatenate([refs[0][...], refs[1][...], refs[2][0], refs[2][1]], axis=0)
        refs[3][0] = (dot_nn(norm_ref[...], weight) + bias_ref[0]).astype(BF16)

    return call(
        kernel,
        (3,),
        [fixed(count, width), pl.BlockSpec((1, 1, half), lambda j: (j, 0, 0))]
        + piece_tiles(half, 2, 1),
        pl.BlockSpec((1, count, half), lambda j: (j, 0, 0)),
        struct((3, count, half)),
        6 * count * width * half,
        2 * count * (width + 3 * half) + 6 * width * half,
        after,
        part=FORWARD_PART,
    )(normed, bias, *parts)


def attend(projected, first_image, last_image, before=None, lanes=256, after=()):
    _, _, images, half_len, half = projected.shape
    length = 2 * half_len
    per_step = lanes // HDIM

    def kernel(proj_ref, *refs):
        out_ref, probs_ref = refs[-2:]
        queries, key_rows, value_rows = (proj_ref[at].reshape(length, lanes) for at in range(3))
        outs = []
        for head in range(per_step):
            columns = slice(head * HDIM, (head + 1) * HDIM)
            scores = dot_nt(queries[:, columns], key_rows[:, columns])
            top = jnp.max(scores, axis=-1, keepdims=True)
            raw = jnp.exp2((scores - top) * (LOG2_E * HDIM**-0.5))
            probs = (raw * (1.0 / jnp.sum(raw, axis=-1, keepdims=True))).astype(BF16)
            probs_ref[0, head] = probs
            outs.append(dot_nn(probs, value_rows[:, columns]).astype(BF16))
        out_ref[...] = jnp.concatenate(outs, axis=1).reshape(out_ref.shape)

    heads = half // HDIM
    old = () if before is None else before
    return call(
        kernel,
        (last_image - first_image, half // lanes),
        [pl.BlockSpec((3, 2, 1, half_len, lanes), lambda i, j: (0, 0, first_image + i, 0, j))]
        + [ANYWHERE] * len(old),
        [
            pl.BlockSpec((2, 1, half_len, lanes), lambda i, j: (0, first_image + i, 0, j)),
            pl.BlockSpec((1, per_step, length, length), lambda i, j: (first_image + i, j, 0, 0)),
        ],
        [struct((2, images, half_len, half)), struct((images, heads, length, length))],
        24 * (last_image - first_image) * heads * length * length * HDIM,
        (last_image - first_image) * heads * length * length * 2,
        after,
        {1: 0, 2: 1} if old else None,
        part=FORWARD_PART,
    )(projected, *old)


def attend_back(projected, grad_context, probs, lanes=256, after=()):
    _, _, images, half_len, half = projected.shape
    length = 2 * half_len
    per_step = lanes // HDIM
    scale = HDIM**-0.5

    def kernel(proj_ref, grad_ref, probs_ref, out_ref, sum_ref):
        queries, key_rows, value_rows = (proj_ref[at].reshape(length, lanes) for at in range(3))
        grads = grad_ref[...].reshape(length, lanes)
        found = ([], [], [])
        for head in range(per_step):
            columns = slice(head * HDIM, (head + 1) * HDIM)
            low = probs_ref[0, head]
            found[2].append(dot_tn(low, grads[:, columns]).astype(BF16))
            grad_soft = dot_nt(grads[:, columns], value_rows[:, columns])
            soft = low.astype(F32)
            scaled = soft * grad_soft
            grad_scores = (scaled - soft * jnp.sum(scaled, axis=-1, keepdims=True)).astype(BF16)
            found[0].append((dot_nn(grad_scores, key_rows[:, columns]) * scale).astype(BF16))
            found[1].append((dot_tn(grad_scores, queries[:, columns]) * scale).astype(BF16))
        for at in range(3):
            joined = jnp.concatenate(found[at], axis=1)
            out_ref[at] = joined.reshape(2, 1, half_len, lanes)
            if at != 1:
                sum_ref[0, at // 2 : at // 2 + 1] = column_sum(joined.astype(F32))

    heads = half // HDIM
    block = pl.BlockSpec((3, 2, 1, half_len, lanes), lambda i, j: (0, 0, i, 0, j))
    return call(
        kernel,
        (images, half // lanes),
        [
            block,
            pl.BlockSpec((2, 1, half_len, lanes), lambda i, j: (0, i, 0, j)),
            pl.BlockSpec((1, per_step, length, length), lambda i, j: (i, j, 0, 0)),
        ],
        [block, pl.BlockSpec((1, 2, lanes), lambda i, j: (i, 0, j))],
        [struct(projected.shape), struct((images, 2, half), F32)],
        32 * images * heads * length * length * HDIM,
        images * heads * length * length * 2,
        after,
    )(projected, grad_context, probs)


def add_branch(contexts, rows, pieces, bias, gain, shift, tile=288, after=()):
    count, width = rows.shape
    half = width // 2

    def kernel(low_ref, high_ref, rows_ref, bias_ref, gain_ref, shift_ref, *refs):
        parts, (middle_ref, norm_ref) = far_list(refs[:4], refs[4:6]), refs[6:]
        found = []
        for at in range(4):
            found.append(dot_nt(low_ref[...], parts[2 * at][...]) + dot_nt(high_ref[...], parts[2 * at + 1][...]))
        middle = rows_ref[...].astype(F32) + (jnp.concatenate(found, axis=1) + bias_ref[...])
        middle_ref[...] = middle
        unit, _ = normal_parts(middle)
        norm_ref[...] = (unit * gain_ref[...] + shift_ref[...]).astype(BF16)

    block = pl.BlockSpec((tile, width), lambda i: (i, 0))
    half_block = pl.BlockSpec((tile, half), lambda i: (i, 0))
    return call(
        kernel,
        (count // tile,),
        [half_block, half_block, block] + [fixed(1, width)] * 3 + piece_specs(half, 3),
        [block, block],
        [struct((count, width), F32), struct((count, width))],
        2 * count * width * width,
        10 * count * width + 2 * width * width,
        after,
        part=FORWARD_PART,
    )(*contexts, rows, bias, gain, shift, *pieces)


def feed_up(second, parts, bias, tile=512, after=()):
    count, width = second.shape
    columns = parts[0].shape[1]

    def kernel(second_ref, bias_ref, *refs):
        weight = jnp.concatenate([refs[0][...], refs[1][...], refs[2][0], refs[2][1]], axis=0)
        hidden = dot_nn(second_ref[...], weight) + bias_ref[...]
        gate = 0.5 + 0.5 * jnp.tanh(0.851 * hidden)
        refs[3][...] = (hidden * gate).astype(BF16)
        refs[4][...] = (gate * (1.0 + 1.702 * hidden * (1.0 - gate))).astype(BF16)

    block = pl.BlockSpec((count, tile), lambda j: (0, j))
    return call(
        kernel,
        (columns // tile,),
        [fixed(count, width), pl.BlockSpec((1, tile), lambda j: (0, j))] + piece_tiles(tile, 2, 1),
        [block, block],
        [struct((count, columns))] * 2,
        2 * count * width * columns,
        2 * count * (width + 2 * columns) + 2 * width * columns,
        after,
        part=FORWARD_PART,
    )(second, bias, *parts)


def feed_down(side, first_tile, last_tile, actives, middle, gathered, bias, order, before=None, tile=288, after=()):
    count, columns = actives[0].shape
    width = middle.shape[1]
    mine = count // tile // 2
    slices = gathered.shape[0]
    half_at = first_tile // mine
    old = () if before is None else (before,)

    def kernel(side_ref, low_ref, high_ref, middle_ref, bias_ref, order_ref, *refs):
        keep = side_ref[2 + side_ref[0] * mine + first_tile % mine + pl.program_id(0)].astype(F32)
        parts, out_ref = refs[:2], refs[-1]
        feed = dot_nt(low_ref[...], parts[0][...].reshape(width, columns))
        feed = feed + dot_nt(high_ref[...], parts[1][...].reshape(width, columns))
        middle = middle_ref[...]
        top = middle.astype(BF16)
        rest = (middle - top.astype(F32)).astype(BF16)
        middle = dot_nt(top, order_ref[...]) + dot_nt(rest, order_ref[...])
        out_ref[0] = ((middle + (feed + bias_ref[...])) * keep).astype(BF16)

    hidden = pl.BlockSpec((tile, columns), lambda i, _: (first_tile + i, 0))
    offset = (lambda ref: ref[0] * mine + first_tile) if half_at == 0 else (lambda ref: first_tile - mine)

    def weight(x_at):
        return pl.BlockSpec(
            (slices, 1, ROWS, columns),
            lambda i, ref: (0, jnp.bitwise_xor(ref[0], x_at), 0, 0),
            pipeline_mode=pl.Buffered(1),
        )

    return call(
        kernel,
        (last_tile - first_tile,),
        [
            hidden,
            hidden,
            pl.BlockSpec((tile, width), lambda i, _: (first_tile + i, 0)),
            fixed(1, width),
            fixed(width, width),
            weight(0),
            weight(1),
        ]
        + [ANYWHERE] * len(old),
        image_block(tile, width, offset),
        struct(((2 - half_at) * mine, tile, width)),
        2 * count * width * columns + count * width * width,
        2 * count * columns + 3 * count * width + 4 * width * columns,
        after,
        {8: 0} if old else None,
        1,
    )(side, *actives, middle, bias, order, gathered, gathered, *old)


def gate_back(side, plain, slopes, gathered, tile=512, after=()):
    count, width = plain.shape
    slices, _, _, columns = gathered.shape

    def kernel(side_ref, plain_ref, low_ref, high_ref, *refs):
        parts, outs, sums = refs[:2], refs[2:4], refs[4:6]
        for x_at, slope_ref in enumerate((low_ref, high_ref)):
            weight = parts[x_at][...].reshape(width, tile)
            grad = (dot_nn(plain_ref[...], weight) * slope_ref[...].astype(F32)).astype(BF16)
            outs[x_at][...] = grad
            sums[x_at][...] = column_sum(grad.astype(F32))

    block = pl.BlockSpec((count, tile), lambda j, _: (0, j))
    sum_block = pl.BlockSpec((1, tile), lambda j, _: (0, j))

    def weight(x_at):
        return pl.BlockSpec((slices, 1, ROWS, tile), lambda j, ref: (0, jnp.bitwise_xor(ref[0], x_at), 0, j))

    return call(
        kernel,
        (columns // tile,),
        [fixed(count, width), block, block, weight(0), weight(1)],
        [block, block, sum_block, sum_block],
        [struct((count, columns))] * 2 + [struct((1, columns), F32)] * 2,
        4 * count * width * columns,
        4 * count * (width + 2 * columns) + 4 * width * columns,
        after,
        None,
        1,
    )(side, plain, *slopes, gathered, gathered)


def sums_down(final, actives, tile=512, after=()):
    count, width = final.shape
    columns = actives[0].shape[1]

    def kernel(final_ref, low_ref, high_ref, *outs):
        for x_at, right_ref in enumerate((low_ref, high_ref)):
            for core in range(2):
                for y_at in range(2):
                    start = (2 * core + y_at) * PART
                    part = dot_tn(final_ref[:, start : start + PART], right_ref[...]).astype(BF16)
                    for z_at in range(4):
                        row = (2 * (z_at % 2) + x_at) * ROWS
                        outs[core][y_at, z_at // 2, row : row + ROWS, :] = part[z_at * ROWS : (z_at + 1) * ROWS]

    right = pl.BlockSpec((count, tile), lambda j: (0, j))
    return call(
        kernel,
        (columns // tile,),
        [fixed(count, width), right, right],
        [pl.BlockSpec((2, 2, PART, tile), lambda j: (0, 0, 0, j))] * 2,
        [struct((2, 2, PART, columns))] * 2,
        4 * count * width * columns,
        4 * count * columns + 2 * count * width + 4 * width * columns,
        after,
    )(final, *actives)


def sums_up(second, grads, tile=512, after=()):
    count, width = second.shape
    columns = grads[0].shape[1]

    def kernel(second_ref, low_ref, high_ref, *outs):
        for x_at, right_ref in enumerate((low_ref, high_ref)):
            for core in range(2):
                for y_at in range(2):
                    start = (2 * core + y_at) * PART
                    part = dot_tn(second_ref[:, start : start + PART], right_ref[...])
                    outs[core][x_at, y_at] = part.astype(BF16)

    right = pl.BlockSpec((count, tile), lambda j: (0, j))
    return call(
        kernel,
        (columns // tile,),
        [fixed(count, width), right, right],
        [pl.BlockSpec((2, 2, PART, tile), lambda j: (0, 0, 0, j))] * 2,
        [struct((2, 2, PART, columns))] * 2,
        4 * count * width * columns,
        4 * count * columns + 2 * count * width + 4 * width * columns,
        after,
    )(second, *grads)


def sums_first(normed, branch, grad_projected, context, after=()):
    count, width = normed.shape
    half = context.shape[1]

    def kernel(norm_ref, branch_ref, grad_ref, context_ref, *outs):
        def work(left_ref, right):
            for core in range(2):
                for y_at in range(2):
                    start = (2 * core + y_at) * PART
                    outs[core][y_at] = dot_tn(left_ref[:, start : start + PART], right).astype(BF16)

        @pl.when(pl.program_id(0) < 3)
        def _():
            work(norm_ref, grad_ref[0])

        @pl.when(pl.program_id(0) == 3)
        def _():
            work(branch_ref, context_ref[...])

    left = fixed(count, width)
    return call(
        kernel,
        (4,),
        [left, left, pl.BlockSpec((1, count, half), lambda j: (jnp.minimum(j, 2), 0, 0)), fixed(count, half)],
        [pl.BlockSpec((2, PART, half), lambda j: (0, 0, j))] * 2,
        [struct((2, PART, 4 * half))] * 2,
        8 * count * width * half,
        2 * count * (2 * width + 4 * half) + 8 * width * half,
        after,
    )(normed, branch, grad_projected, context)


def second_back(grads, up_pieces, first_pieces, middle, final, gain, tile=288, after=()):
    count, columns = grads[0].shape
    width = middle.shape[1]
    half = width // 2

    def kernel(low_ref, high_ref, middle_ref, final_ref, gain_ref, *refs):
        ups, outs = far_list(refs[:4], refs[4:6]), far_list(refs[6:10], refs[10:12])
        grad_ref, branch_ref, context_low_ref, context_high_ref, sum_ref = refs[12:]
        found = []
        for at in range(4):
            found.append(dot_nt(low_ref[...], ups[2 * at][...]) + dot_nt(high_ref[...], ups[2 * at + 1][...]))
        grad_second = jnp.concatenate(found, axis=1)
        unit, inv_std = normal_parts(middle_ref[...])
        grad_middle = final_ref[...].astype(F32) + normalize_back(
            grad_second, unit, inv_std, gain_ref[...]
        )
        branch = grad_middle.astype(BF16)
        grad_ref[...] = grad_middle
        branch_ref[...] = branch
        for x_at, context_ref in enumerate((context_low_ref, context_high_ref)):
            weight = jnp.concatenate([outs[2 * at + x_at][...] for at in range(4)], axis=0)
            context_ref[...] = dot_nn(branch, weight).astype(BF16)

        @pl.when(first_step())
        def _():
            sum_ref[...] = jnp.zeros_like(sum_ref)

        sum_ref[0:1] += column_sum(grad_second * unit)
        sum_ref[1:2] += column_sum(grad_second)
        sum_ref[2:3] += column_sum(branch.astype(F32))

    block = pl.BlockSpec((tile, width), lambda i: (i, 0))
    half_block = pl.BlockSpec((tile, half), lambda i: (i, 0))
    hidden = pl.BlockSpec((tile, columns), lambda i: (i, 0))
    return call(
        kernel,
        (count // tile,),
        [hidden, hidden, block, block, fixed(1, width)]
        + piece_specs(columns)
        + piece_specs(half, 3),
        [block, block, half_block, half_block, fixed(8, width)],
        [struct((count, width), F32), struct((count, width))]
        + [struct((count, half))] * 2
        + [struct((8, width), F32)],
        4 * count * width * columns + 2 * count * width * width,
        4 * count * columns + 14 * count * width + 4 * width * columns,
        after,
    )(*grads, middle, final, gain, *up_pieces, *first_pieces)


def first_back(side, half_at, grads, pieces, rows, grad_middle, gain, order, tile=288, after=()):
    _, count, half = grads[0].shape
    width = rows.shape[1]
    mine = count // tile // 2

    def kernel(side_ref, low_ref, high_ref, rows_ref, middle_ref, gain_ref, order_ref, *refs):
        parts, (out_ref, sum_ref) = far_list(refs[:4], refs[4:6]), refs[6:]
        lefts = [jnp.concatenate([ref[at] for at in range(3)], axis=1) for ref in (low_ref, high_ref)]
        found = []
        for at in range(4):
            found.append(
                dot_nt(lefts[0], parts[2 * at][...]) + dot_nt(lefts[1], parts[2 * at + 1][...])
            )
        grad_normed = jnp.concatenate(found, axis=1)
        unit, inv_std = normal_parts(rows_ref[...].astype(F32))
        out = middle_ref[...] + normalize_back(grad_normed, unit, inv_std, gain_ref[...])
        out_ref[0] = dot_nt(out.astype(BF16), order_ref[...]).astype(BF16)

        @pl.when(first_step())
        def _():
            sum_ref[...] = jnp.zeros_like(sum_ref)

        sum_ref[0:1] += column_sum(grad_normed * unit)
        sum_ref[1:2] += column_sum(grad_normed)

    start = half_at * mine
    block = pl.BlockSpec((tile, width), lambda i, _: (start + i, 0))
    grad_block = pl.BlockSpec((3, tile, half), lambda i, _: (0, start + i, 0))
    offset = (lambda ref: ref[0] * mine) if half_at == 0 else (lambda ref: 0)
    return call(
        kernel,
        (mine,),
        [grad_block, grad_block, block, block, fixed(1, width), fixed(width, width)]
        + piece_specs(3 * half),
        [image_block(tile, width, offset), fixed(8, width)],
        [struct(((2 - half_at) * mine, tile, width)), struct((8, width), F32)],
        4 * count * width * width,
        8 * count * width + 6 * width * width,
        after,
        None,
        1,
    )(side, *grads, rows, grad_middle, gain, order, *pieces)


def fast_shards(
    tokens,
    image_mask,
    out_grad,
    norm1_gain,
    norm1_shift,
    qkv_weight,
    qv_bias,
    out_weight,
    out_bias,
    norm2_gain,
    norm2_shift,
    up_weight,
    up_bias,
    down_weight,
    down_bias,
):
    images, half_len, width = tokens.shape
    mine = images // 2
    half = qkv_weight.shape[2]
    half_hidden = up_weight.shape[1]
    count = 2 * mine * half_len
    me = lax.axis_index("dp")
    side = lax.axis_index("tensor")
    side_array = jnp.concatenate([jnp.stack([side, me]).astype(jnp.int32), image_mask])
    biases = jnp.concatenate([qv_bias.reshape(-1), up_bias])
    bias_rows = jnp.pad(biases, (0, 16 * half_hidden - biases.size)).reshape(16, half_hidden)

    def split_bias(bias):
        bias = bias.astype(F32)
        parts = jnp.stack([bias[:half], jnp.zeros((half,), F32), bias[half : 2 * half]])
        return parts[:, None], bias[None, 2 * half :]

    vectors = (norm1_gain, norm1_shift, norm2_gain, norm2_shift, out_bias)
    bias_down = down_bias.astype(F32).reshape(1, width)
    order, gain_one, shift_one, gain_two, shift_two, bias_out = setup(
        side_array, [vector.reshape(1, width) for vector in vectors]
    )

    def for_partner(values):
        return over_x(lax.dynamic_slice_in_dim(values, (1 - side) * mine, mine, 0))

    def from_partner(values, send):
        return lax.dynamic_update_slice_in_dim(values, over_x(send), (1 - side) * mine, 0)

    def z_all(values):
        return jnp.concatenate([values] + [over_z(values, step) for step in (1, 2, 3)], axis=0)

    own = prepare(side_array, tokens, order, gain_one, shift_one, 0)
    *final, sum_own = mask_grad(side_array, out_grad, order, 0, after=own[:1])
    tokens_partner = for_partner(tokens)
    first = jnp.concatenate([qkv_weight.reshape(ROWS, 3 * half), out_weight], axis=1)
    first_base = late(z_all(first), final[0])
    down_all = lax.all_gather(late(down_weight, first_base), ("dp", "tensor"))
    down_all = down_all.reshape(-1, 2, ROWS, half_hidden)
    first_x = over_x(jnp.concatenate([late(first_base, tokens_partner), bias_rows], axis=0))
    rows, normed = prepare(
        side_array, tokens_partner, order, gain_one, shift_one, 1, own, after=[first_base]
    )
    first_y = over_y(late(first_base, normed))
    up_base = z_all(late(up_weight, first_base))
    first_xy = over_y(late(first_x, first_y))
    first_far = [over_core(jnp.stack(late([first_base, first_y], first_x, up_base)))]
    up_x = over_x(late(up_base, first_x))
    grad_partner = for_partner(late(out_grad, up_x))

    biases = [split_bias(biases), split_bias(first_x[4 * ROWS :].reshape(-1)[: biases.size])]
    heads_shape = (3, 2, mine, half_len, half)
    projected, contexts, probs = [None, None], [None, None], [None, None]
    projected[0] = project(
        normed, [first_base, first_y] + first_far, biases[0][0]
    ).reshape(heads_shape)
    begun = attend(projected[0], 0, 1, lanes=128)
    first_far += [over_core(jnp.stack(late([first_x, first_xy], begun[0])))]
    first_pieces = [first_base, first_x, first_y, first_xy] + first_far
    up_y = over_y(late(up_base, first_xy))
    contexts[0], probs[0] = attend(projected[0], 1, 2, begun, lanes=128)
    projected[1] = project(
        normed, [first_x, first_xy] + first_far[1:], biases[1][0], after=[contexts[0], up_x]
    ).reshape(heads_shape)
    contexts[1], probs[1] = attend(projected[1], 0, 2, after=[up_y])
    contexts = [values.reshape(count, half) for values in contexts]

    up_xy = over_y(late(up_x, up_y, contexts[1]))
    up_far = [over_core(jnp.stack(late([up_base, up_y], contexts[1])))]
    middle, second = add_branch(
        contexts, rows, first_pieces, bias_out, gain_two, shift_two
    )
    actives, slopes = [None, None], [None, None]
    actives[0], slopes[0] = feed_up(second, [up_base, up_y] + up_far, biases[0][1], after=[grad_partner])
    *final, sum_partner = mask_grad(side_array, grad_partner, order, 1, final, after=[actives[0]])
    up_far += [over_core(jnp.stack(late([up_x, up_xy], actives[0])))]
    up_pieces = [up_base, up_x, up_y, up_xy] + up_far
    actives[1], slopes[1] = feed_up(second, [up_x, up_xy] + up_far[1:], biases[1][1], after=final[:1])

    final, plain = final
    down_sums, down_sent = sums_down(final, actives)
    down_sent = over_core(down_sent)
    grads_sums = gate_back(side_array, plain, slopes, down_all, after=[down_sums])
    grads, sum_hidden = grads_sums[:2], grads_sums[2:]
    down_sums = combine([down_sums, down_sent], 2, after=grads[:1])
    down_sent = over_y(down_sums[1])
    up_sums, up_sent = sums_up(second, grads, after=down_sums[:1])
    up_sent = over_core(up_sent)
    grad_middle, branch, *grad_contexts, sums_two = second_back(
        grads, up_pieces, first_pieces, middle, final, gain_two, after=[up_sums]
    )
    up_sums = combine([up_sums, up_sent], 2, after=[branch])
    up_sent = over_x(up_sums[1])

    def heads_back(x_at, after):
        grad_context = grad_contexts[x_at].reshape(2, mine, half_len, half)
        grad, sums = attend_back(projected[x_at], grad_context, probs[x_at], after=after)
        return grad.reshape(3, count, half), jnp.sum(sums, axis=0)

    grads_qkv, sums_qkv = [None, None], [None, None]
    grads_qkv[1], sums_qkv[1] = heads_back(1, up_sums[:1])
    down_sums = combine([down_sums[0], down_sent], 2, after=[grads_qkv[1]])
    down_sent = over_z(down_sums[1], 2)
    high, high_sent = sums_first(normed, branch, grads_qkv[1], contexts[1], after=down_sums[:1])
    high_sent = over_core(high_sent)
    out_send = feed_down(side_array, 2, 4, actives, middle, down_all, bias_down, order, after=[high])
    high = combine([high, high_sent], 2, after=[out_send])
    high_sent = over_y(high[1])
    grads_qkv[0], sums_qkv[0] = heads_back(0, high[:1])
    up_sums = combine([up_sums[0], up_sent], 2, after=[grads_qkv[0]])
    up_sent = over_y(up_sums[1])
    (high,) = combine([high[0], high_sent], 1, after=up_sums[:1])
    high_sent = over_x(high)
    down_sums = combine([down_sums[0], down_sent], 2, after=[high])
    down_sent = over_z(down_sums[1], 1)
    low, low_sent = sums_first(normed, branch, grads_qkv[0], contexts[0], after=down_sums[:1])
    low = combine([low, over_core(low_sent)], 2)
    low_sent = over_y(low[1])
    send, sums_partner = first_back(
        side_array, 1, grads_qkv, first_pieces, rows, grad_middle, gain_one, order, after=low[:1]
    )
    full, sums_own = first_back(
        side_array, 0, grads_qkv, first_pieces, rows, grad_middle, gain_one, order, after=[send]
    )
    up_sums = combine([up_sums[0], up_sent], 2, after=[full])
    up_sent = over_z(up_sums[1], 2)
    low = combine([low[0], low_sent, high_sent], 4, after=up_sums[:1])
    low_sent = [over_z(low[step], step) for step in (1, 2, 3)]
    down_sums = combine([down_sums[0], down_sent], 2, after=low[:1])
    down_sent = over_x(down_sums[1])
    out_begun = feed_down(
        side_array, 0, 1, actives, middle, down_all, bias_down, order, after=down_sums[:1]
    )
    tokens_grad = from_partner(full, send)
    up_sums = combine([up_sums[0], up_sent], 2, after=[out_begun])
    up_sent = over_z(up_sums[1], 1)
    out_full = feed_down(
        side_array, 1, 2, actives, middle, down_all, bias_down, order, out_begun, after=[tokens_grad, up_sums[0]]
    )
    (grad_down,) = combine([down_sums[0], down_sent], 1, F32, after=[out_full])
    block_out = from_partner(out_full, out_send)
    (grad_up,) = combine([up_sums[0], up_sent], 1, F32, after=[grad_down])
    (grad_first,) = combine([low[0]] + low_sent, 1, F32, after=[grad_up, tokens_grad])

    sums = jnp.concatenate(
        [(sums_own + sums_partner)[:2], sums_two[2:3], sums_two[:2], sum_own + sum_partner], axis=0
    )
    sums = jnp.einsum("td,od->to", sums, order.astype(F32), precision=lax.Precision.HIGHEST)
    halves = [
        jnp.concatenate([sums_qkv[x_at].reshape(-1), sum_hidden[x_at][0]]) for x_at in range(2)
    ]
    small = jnp.concatenate([halves[0], sums.reshape(-1), halves[1]])
    small = small + over_core(small)
    small = late(small, out_begun)
    small = small + over_y(small)
    small = late(small, out_full)
    small = (small + over_z(small, 1)) + (over_z(small, 2) + over_z(small, 3))
    halves_size = 2 * half + half_hidden
    small = late(small, grad_first)
    small = small[:-halves_size] + over_x(
        jnp.concatenate([small[-halves_size:], small[halves_size:-halves_size]])
    )
    halves = small[:halves_size]
    sums = small[halves_size:].reshape(6, width)
    return (
        block_out,
        tokens_grad,
        sums[0],
        sums[1],
        grad_first[:, : 3 * half].reshape(ROWS, 3, half),
        halves[: 2 * half].reshape(2, half),
        grad_first[:, 3 * half :],
        sums[2],
        sums[3],
        sums[4],
        grad_up,
        halves[2 * half :],
        grad_down,
        sums[5],
    )


def solution(mesh):
    in_specs = (
        P("dp", "tensor", None),
        P("dp"),
        P("dp", "tensor", None),
        P(),
        P(),
        P("dp", None, "tensor"),
        P(None, "tensor"),
        P("dp", "tensor"),
        P(),
        P(),
        P(),
        P("dp", "tensor"),
        P("tensor"),
        P("dp", "tensor"),
        P(),
    )
    out_specs = (
        P("dp", "tensor", None),
        P("dp", "tensor", None),
        P(),
        P(),
        P("dp", None, "tensor"),
        P(None, "tensor"),
        P("dp", "tensor"),
        P(),
        P(),
        P(),
        P("dp", "tensor"),
        P("tensor"),
        P("dp", "tensor"),
        P(),
    )
    small_slice = mesh.shape["dp"] == 16 and mesh.shape["tensor"] == 2
    shards = fast_shards if small_slice else general_shards
    return jax.shard_map(shards, mesh=mesh, in_specs=in_specs, out_specs=out_specs, check_vma=False)
```

```python
import jax
import jax.numpy as jnp
from jax import lax
from jax.experimental import pallas as pl
from jax.experimental.pallas import tpu as pltpu
from jax.sharding import PartitionSpec as P

HDIM = 64
MICRO = 2


def mixed(form, left, right):
    return jnp.einsum(form, left, right, preferred_element_type=jnp.float32)


def normalize(values, gain, shift):
    mean_val = jnp.mean(values, axis=-1, keepdims=True)
    centered = values - mean_val
    inv_std = lax.rsqrt(jnp.mean(centered * centered, axis=-1, keepdims=True) + 1e-05)
    unit_val = centered * inv_std
    return (unit_val * gain + shift, unit_val, inv_std)


def normalize_back(grad_in, unit_val, inv_std, gain):
    scaled = grad_in * gain
    return inv_std * (
        scaled
        - jnp.mean(scaled, axis=-1, keepdims=True)
        - unit_val * jnp.mean(scaled * unit_val, axis=-1, keepdims=True)
    )


def token_sum(values):
    return jnp.sum(values, axis=(0, 1))


def general_shards(
    tokens,
    image_mask,
    out_grad,
    norm1_gain,
    norm1_shift,
    qkv_weight,
    qv_bias,
    out_weight,
    out_bias,
    norm2_gain,
    norm2_shift,
    up_weight,
    up_bias,
    down_weight,
    down_bias,
):
    images_here = tokens.shape[0] // MICRO
    full_width = norm1_gain.shape[0]
    local_width = qkv_weight.shape[2]
    local_hidden = up_weight.shape[1]
    local_heads = local_width // HDIM
    score_scale = HDIM ** (-0.5)
    gain_one = norm1_gain.astype(jnp.float32)
    shift_one = norm1_shift.astype(jnp.float32)
    gain_two = norm2_gain.astype(jnp.float32)
    shift_two = norm2_shift.astype(jnp.float32)
    bias_pair = qv_bias.astype(jnp.float32)
    grad_qkv = jnp.zeros((full_width, 3, local_width), jnp.float32)
    grad_out = jnp.zeros((full_width, local_width), jnp.float32)
    grad_up = jnp.zeros((full_width, local_hidden), jnp.float32)
    grad_down = jnp.zeros((full_width, local_hidden), jnp.float32)
    grad_gain_one = jnp.zeros((full_width,), jnp.float32)
    grad_shift_one = jnp.zeros((full_width,), jnp.float32)
    grad_gain_two = jnp.zeros((full_width,), jnp.float32)
    grad_shift_two = jnp.zeros((full_width,), jnp.float32)
    grad_out_bias = jnp.zeros((full_width,), jnp.float32)
    grad_down_bias = jnp.zeros((full_width,), jnp.float32)
    grad_pair = jnp.zeros((2, local_width), jnp.float32)
    grad_up_bias = jnp.zeros((local_hidden,), jnp.float32)
    outputs = []
    input_grads = []
    for micro_index in range(MICRO):
        first_image = micro_index * images_here
        block_rows = tokens[first_image : first_image + images_here].astype(jnp.float32)
        keep_mask = image_mask[first_image : first_image + images_here].astype(jnp.float32)[
            :, None, None
        ]
        fwd_weights = (
            lax.all_gather(qkv_weight, "dp", axis=0, tiled=True),
            lax.all_gather(out_weight, "dp", axis=0, tiled=True),
            lax.all_gather(up_weight, "dp", axis=0, tiled=True),
            lax.all_gather(down_weight, "dp", axis=0, tiled=True),
        )
        qkv_full, out_full, up_full, down_full = fwd_weights
        normed, unit_one, inv_one = normalize(block_rows, gain_one, shift_one)
        normed_full = lax.all_gather(normed.astype(jnp.bfloat16), "tensor", axis=1, tiled=True)
        seq_len = normed_full.shape[1]
        head_shape = (images_here, seq_len, local_heads, HDIM)
        projected = mixed("isd,dcf->iscf", normed_full, qkv_full)
        queries = (projected[:, :, 0] + bias_pair[0]).astype(jnp.bfloat16).reshape(head_shape)
        key_rows = projected[:, :, 1].astype(jnp.bfloat16).reshape(head_shape)
        value_rows = (projected[:, :, 2] + bias_pair[1]).astype(jnp.bfloat16).reshape(head_shape)
        scores = mixed("iqhe,ikhe->ihqk", queries, key_rows) * score_scale
        row_top = jnp.max(scores, axis=-1, keepdims=True)
        raw_weights = jnp.exp(scores - row_top)
        row_total = jnp.sum(raw_weights, axis=-1, keepdims=True)
        log_total = row_top + jnp.log(row_total)
        probs = (raw_weights / row_total).astype(jnp.bfloat16)
        context = mixed("ihqk,ikhe->iqhe", probs, value_rows).astype(jnp.bfloat16)
        context = context.reshape(images_here, seq_len, local_width)
        attn_terms = mixed("isf,of->iso", context, out_full)
        branch = lax.psum_scatter(
            attn_terms, "tensor", scatter_dimension=1, tiled=True
        ) + out_bias.astype(jnp.float32)
        middle = block_rows + branch
        second, unit_two, inv_two = normalize(middle, gain_two, shift_two)
        second_full = lax.all_gather(second.astype(jnp.bfloat16), "tensor", axis=1, tiled=True)
        hidden = mixed("isd,df->isf", second_full, up_full) + up_bias.astype(jnp.float32)
        gate_sig = jax.nn.sigmoid(1.702 * hidden)
        active = (hidden * gate_sig).astype(jnp.bfloat16)
        feed_terms = mixed("isf,of->iso", active, down_full)
        feed_out = lax.psum_scatter(
            feed_terms.astype(jnp.bfloat16), "tensor", scatter_dimension=1, tiled=True
        ).astype(jnp.float32) + down_bias.astype(jnp.float32)
        outputs.append(((middle + feed_out) * keep_mask).astype(jnp.bfloat16))
        back_weights = (
            lax.all_gather(qkv_weight, "dp", axis=0, tiled=True),
            lax.all_gather(out_weight, "dp", axis=0, tiled=True),
            lax.all_gather(up_weight, "dp", axis=0, tiled=True),
            lax.all_gather(down_weight, "dp", axis=0, tiled=True),
        )
        qkv_back, out_back, up_back, down_back = back_weights
        grad_final = (
            out_grad[first_image : first_image + images_here].astype(jnp.float32) * keep_mask
        )
        grad_down_bias = grad_down_bias + token_sum(grad_final)
        final_full = lax.all_gather(grad_final.astype(jnp.bfloat16), "tensor", axis=1, tiled=True)
        grad_down = grad_down + mixed("iso,isf->of", final_full, active)
        grad_active = mixed("iso,of->isf", final_full, down_back)
        grad_hidden = (
            grad_active * (gate_sig + 1.702 * hidden * gate_sig * (1.0 - gate_sig))
        ).astype(jnp.bfloat16)
        grad_up_bias = grad_up_bias + token_sum(grad_hidden.astype(jnp.float32))
        grad_up = grad_up + mixed("isd,isf->df", second_full, grad_hidden)
        second_terms = mixed("isf,df->isd", grad_hidden, up_back)
        grad_second = lax.psum_scatter(second_terms, "tensor", scatter_dimension=1, tiled=True)
        grad_gain_two = grad_gain_two + token_sum(grad_second * unit_two)
        grad_shift_two = grad_shift_two + token_sum(grad_second)
        grad_middle = grad_final + normalize_back(grad_second, unit_two, inv_two, gain_two)
        grad_branch = grad_middle.astype(jnp.bfloat16)
        grad_out_bias = grad_out_bias + token_sum(grad_branch.astype(jnp.float32))
        branch_full = lax.all_gather(grad_branch, "tensor", axis=1, tiled=True)
        grad_out = grad_out + mixed("iso,isf->of", branch_full, context)
        grad_context = (
            mixed("iso,of->isf", branch_full, out_back).astype(jnp.bfloat16).reshape(head_shape)
        )
        again = mixed("iqhe,ikhe->ihqk", queries, key_rows) * score_scale
        soft_again = jnp.exp(again - log_total)
        probs_again = soft_again.astype(jnp.bfloat16)
        grad_values = mixed("ihqk,iqhe->ikhe", probs_again, grad_context)
        grad_soft = mixed("iqhe,ikhe->ihqk", grad_context, value_rows)
        grad_scores = (
            soft_again * (grad_soft - jnp.sum(grad_soft * soft_again, axis=-1, keepdims=True))
        ).astype(jnp.bfloat16)
        grad_queries = mixed("ihqk,ikhe->iqhe", grad_scores, key_rows) * score_scale
        grad_keys = mixed("ihqk,iqhe->ikhe", grad_scores, queries) * score_scale
        flat_shape = (images_here, seq_len, local_width)
        grad_projected = jnp.stack(
            (
                grad_queries.reshape(flat_shape),
                grad_keys.reshape(flat_shape),
                grad_values.reshape(flat_shape),
            ),
            axis=2,
        ).astype(jnp.bfloat16)
        pair_terms = grad_projected.astype(jnp.float32)
        grad_pair = grad_pair + jnp.stack(
            (token_sum(pair_terms[:, :, 0]), token_sum(pair_terms[:, :, 2])), axis=0
        )
        grad_qkv = grad_qkv + mixed("isd,iscf->dcf", normed_full, grad_projected)
        normed_terms = mixed("iscf,dcf->isd", grad_projected, qkv_back)
        grad_normed = lax.psum_scatter(
            normed_terms.astype(jnp.bfloat16), "tensor", scatter_dimension=1, tiled=True
        ).astype(jnp.float32)
        grad_gain_one = grad_gain_one + token_sum(grad_normed * unit_one)
        grad_shift_one = grad_shift_one + token_sum(grad_normed)
        grad_tokens = grad_middle + normalize_back(grad_normed, unit_one, inv_one, gain_one)
        input_grads.append(grad_tokens.astype(jnp.bfloat16))
    grad_qkv, grad_out, grad_up, grad_down = (
        lax.psum_scatter(
            grad_qkv.astype(jnp.bfloat16), "dp", scatter_dimension=0, tiled=True
        ).astype(jnp.float32),
        lax.psum_scatter(
            grad_out.astype(jnp.bfloat16), "dp", scatter_dimension=0, tiled=True
        ).astype(jnp.float32),
        lax.psum_scatter(
            grad_up.astype(jnp.bfloat16), "dp", scatter_dimension=0, tiled=True
        ).astype(jnp.float32),
        lax.psum_scatter(
            grad_down.astype(jnp.bfloat16), "dp", scatter_dimension=0, tiled=True
        ).astype(jnp.float32),
    )
    grad_gain_one, grad_shift_one, grad_gain_two, grad_shift_two, grad_out_bias, grad_down_bias = (
        lax.psum(
            (
                grad_gain_one,
                grad_shift_one,
                grad_gain_two,
                grad_shift_two,
                grad_out_bias,
                grad_down_bias,
            ),
            ("dp", "tensor"),
        )
    )
    grad_pair, grad_up_bias = lax.psum((grad_pair, grad_up_bias), "dp")
    block_out = jnp.concatenate(outputs, axis=0)
    tokens_grad = jnp.concatenate(input_grads, axis=0)
    return (
        block_out,
        tokens_grad,
        grad_gain_one,
        grad_shift_one,
        grad_qkv,
        grad_pair,
        grad_out,
        grad_out_bias,
        grad_gain_two,
        grad_shift_two,
        grad_up,
        grad_up_bias,
        grad_down,
        grad_down_bias,
    )


ROWS = 64
PART = 256
VMEM_BYTES = 60 * 1024 * 1024
COST_PART = 0.6
FORWARD_PART = 0.8
LOG2_E = 1.4426950408889634
BF16 = jnp.bfloat16
F32 = jnp.float32


def swap(values, axis_name, flip):
    count = lax.axis_size(axis_name)
    return lax.ppermute(values, axis_name, [(place, place ^ flip) for place in range(count)])


def over_core(values):
    return swap(values, "dp", 1)


def over_y(values):
    return swap(values, "dp", 2)


def over_z(values, step):
    return swap(values, "dp", 4 * step)


def over_x(values):
    return swap(values, "tensor", 1)


def late(values, *marks):
    return lax.optimization_barrier((values, *marks))[0]


def dot_nn(left, right):
    return lax.dot_general(left, right, (((1,), (0,)), ((), ())), preferred_element_type=F32)


def dot_nt(left, right):
    return lax.dot_general(left, right, (((1,), (1,)), ((), ())), preferred_element_type=F32)


def dot_tn(left, right):
    return lax.dot_general(left, right, (((0,), (0,)), ((), ())), preferred_element_type=F32)


def call(
    kernel, grid, in_specs, out_specs, out_shape, flops, moved, after=(), aliases=None, scalars=0, part=None
):
    given, waits = scalars + len(in_specs), len(after)
    part = COST_PART if part is None else part

    def run(*refs):
        kernel(*refs[:given], *refs[given + waits :])

    function = pl.pallas_call(
        run,
        grid_spec=pltpu.PrefetchScalarGridSpec(
            num_scalar_prefetch=scalars,
            grid=grid,
            in_specs=list(in_specs) + [pl.BlockSpec(memory_space=pl.ANY)] * waits,
            out_specs=out_specs,
        ),
        out_shape=out_shape,
        input_output_aliases=aliases or {},
        compiler_params=pltpu.CompilerParams(vmem_limit_bytes=VMEM_BYTES),
        cost_estimate=pl.CostEstimate(
            flops=int(flops * part), bytes_accessed=int(moved * part), transcendentals=0
        ),
    )
    return lambda *arrays: function(*arrays, *after)


def fixed(*shape, at=None):
    place = at or (0,) * len(shape)
    return pl.BlockSpec(shape, lambda *_: place, pipeline_mode=pl.Buffered(1))


def far_list(near, far):
    return list(near) + [far[last].at[y_at] for y_at in range(2) for last in range(2)]


def piece_specs(columns, at=0):
    return [fixed(PART, columns, at=(0, at))] * 4 + [fixed(2, PART, columns, at=(0, 0, at))] * 2


def piece_tiles(tile, near=4, far=2):
    return [pl.BlockSpec((PART, tile), lambda j: (0, j))] * near + [
        pl.BlockSpec((2, PART, tile), lambda j: (0, 0, j))
    ] * far


def gathered_specs(columns, halves=(0, 1), at=None):
    def spec(block, x_at):
        core, y_at, z_at = block // 8, (block // 4) % 2, block % 4
        slab = z_at * 4 + y_at * 2 + core

        def place(j, *refs):
            where = refs[-1]
            row = jnp.bitwise_xor(where[1], slab), jnp.bitwise_xor(where[0], x_at)
            return (*row, 0, j if at is None else at)

        mode = {} if at is None else {"pipeline_mode": pl.Buffered(1)}
        return pl.BlockSpec((1, 1, ROWS, columns), place, **mode)

    return [spec(block, x_at) for block in range(16) for x_at in halves]


def joined(refs, first, last, step=1, offset=0):
    return jnp.concatenate([refs[step * block + offset][0, 0] for block in range(first, last)], axis=0)


def struct(shape, dtype=BF16):
    return jax.ShapeDtypeStruct(shape, dtype)


ANYWHERE = pl.BlockSpec(memory_space=pl.ANY)


def normal_parts(values):
    mean_val = jnp.mean(values, axis=-1, keepdims=True)
    centered = values - mean_val
    inv_std = lax.rsqrt(jnp.mean(centered * centered, axis=-1, keepdims=True) + 1e-05)
    return centered * inv_std, inv_std


def column_sum(values):
    return jnp.sum(values, axis=0, keepdims=True)


def combine(arrays, pieces, dtype=BF16, tile=1024, after=()):
    columns = arrays[0].shape[-1]
    rows = arrays[0].size // columns // pieces
    arrays = [values.reshape(pieces, rows, columns) for values in arrays]
    given = len(arrays)

    def kernel(*refs):
        for at in range(pieces):
            parts = [ref[at].astype(F32) for ref in refs[:given]]
            while len(parts) > 1:
                parts = [sum(parts[start : start + 2]) for start in range(0, len(parts), 2)]
            refs[given + at][...] = parts[0].astype(dtype)

    return call(
        kernel,
        (columns // tile,),
        [pl.BlockSpec((pieces, rows, tile), lambda j: (0, 0, j))] * given,
        [pl.BlockSpec((rows, tile), lambda j: (0, j))] * pieces,
        [struct((rows, columns), dtype)] * pieces,
        0,
        2 * pieces * rows * columns * (given + 1),
        after,
    )(*arrays)


def first_step():
    return pl.program_id(0) == 0


def setup(places, vectors, after=()):
    width = vectors[0].shape[1]
    given = len(vectors)

    def kernel(place_ref, *refs):
        order_ref = refs[given]
        source = lax.broadcasted_iota(jnp.int32, (width, width), 0)
        target = lax.broadcasted_iota(jnp.int32, (width, width), 1)
        at = target // ROWS
        z_rel, y_rel, core_rel = at % 4, (at // 4) % 2, at // 8
        place = (z_rel * 4 + y_rel * 2 + core_rel) ^ place_ref[1]
        hit = source == place * ROWS + target % ROWS
        order = jnp.where(hit, 1.0, 0.0).astype(BF16)
        order_ref[...] = order
        rows = jnp.concatenate([ref[...].astype(F32) for ref in refs[:given]] + [jnp.zeros((8 - given, width), F32)], axis=0)
        moved = dot_nn(rows.astype(BF16), order)
        for vector_at in range(given):
            refs[given + 1 + vector_at][...] = moved[vector_at : vector_at + 1]

    row = fixed(1, width)
    return call(
        kernel,
        (1,),
        [row] * given,
        [fixed(width, width)] + [row] * given,
        [struct((width, width))] + [struct((1, width), F32)] * given,
        16 * width * width,
        2 * width * width,
        after,
        None,
        1,
        part=FORWARD_PART,
    )(places, *vectors)


def image_block(height, width, offset):
    return pl.BlockSpec((1, height, width), lambda i, side: (offset(side) + i, 0, 0))


def prepare(side, images, order, gain, shift, half_at, before=None, after=()):
    _, height, width = images.shape
    mine = 2

    def kernel(side_ref, raw_ref, order_ref, gain_ref, shift_ref, *refs):
        rows_ref, norm_ref = refs[-2:]
        rows = dot_nn(raw_ref[0], order_ref[...])
        rows_ref[...] = rows.astype(BF16)
        unit, _ = normal_parts(rows)
        norm_ref[...] = (unit * gain_ref[...] + shift_ref[...]).astype(BF16)

    offset = (lambda side_ref: side_ref[0] * mine) if half_at == 0 else (lambda side_ref: 0)
    out = pl.BlockSpec((height, width), lambda i, _: (half_at * mine + i, 0))
    old = () if before is None else before
    return call(
        kernel,
        (mine,),
        [image_block(height, width, offset), fixed(width, width), fixed(1, width), fixed(1, width)]
        + [ANYWHERE] * len(old),
        [out, out],
        [struct((2 * mine * height, width))] * 2,
        2 * mine * height * width * width,
        6 * mine * height * width,
        after,
        {5: 0, 6: 1} if old else None,
        1,
        part=FORWARD_PART,
    )(side, images, order, gain, shift, *old)


def mask_grad(side, images, order, half_at, before=None, after=()):
    _, height, width = images.shape
    mine = 2

    def kernel(side_ref, raw_ref, order_ref, *refs):
        final_ref, sum_ref = refs[-2:]
        keep = side_ref[2 + side_ref[0] * mine + pl.program_id(0)].astype(F32)
        final = dot_nn(raw_ref[0], order_ref[...]) * keep
        final_ref[...] = final.astype(BF16)

        @pl.when(first_step())
        def _():
            sum_ref[...] = jnp.zeros_like(sum_ref)

        sum_ref[...] += column_sum(final)

    offset = (lambda side_ref: side_ref[0] * mine) if half_at == 0 else (lambda side_ref: 0)
    old = () if before is None else (before,)
    out = pl.BlockSpec((height, width), lambda i, _: (half_at * mine + i, 0))
    return call(
        kernel,
        (mine,),
        [image_block(height, width, offset), fixed(width, width)] + [ANYWHERE] * len(old),
        [out, fixed(1, width)],
        [struct((2 * mine * height, width)), struct((1, width), F32)],
        2 * mine * height * width * width,
        6 * mine * height * width,
        after,
        {3: 0} if old else None,
        1,
        part=FORWARD_PART,
    )(side, images, order, *old)


def project(normed, parts, bias, after=()):
    count, width = normed.shape
    half = bias.shape[-1]

    def kernel(norm_ref, bias_ref, *refs):
        weight = jnp.concatenate([refs[0][...], refs[1][...], refs[2][0], refs[2][1]], axis=0)
        refs[3][0] = (dot_nn(norm_ref[...], weight) + bias_ref[0]).astype(BF16)

    return call(
        kernel,
        (3,),
        [fixed(count, width), pl.BlockSpec((1, 1, half), lambda j: (j, 0, 0))]
        + piece_tiles(half, 2, 1),
        pl.BlockSpec((1, count, half), lambda j: (j, 0, 0)),
        struct((3, count, half)),
        6 * count * width * half,
        2 * count * (width + 3 * half) + 6 * width * half,
        after,
        part=FORWARD_PART,
    )(normed, bias, *parts)


def attend(projected, first_image, last_image, before=None, lanes=256, after=()):
    _, _, images, half_len, half = projected.shape
    length = 2 * half_len
    per_step = lanes // HDIM

    def kernel(proj_ref, *refs):
        out_ref, probs_ref = refs[-2:]
        queries, key_rows, value_rows = (proj_ref[at].reshape(length, lanes) for at in range(3))
        outs = []
        for head in range(per_step):
            columns = slice(head * HDIM, (head + 1) * HDIM)
            scores = dot_nt(queries[:, columns], key_rows[:, columns])
            top = jnp.max(scores, axis=-1, keepdims=True)
            raw = jnp.exp2((scores - top) * (LOG2_E * HDIM**-0.5))
            probs = (raw * (1.0 / jnp.sum(raw, axis=-1, keepdims=True))).astype(BF16)
            probs_ref[0, head] = probs
            outs.append(dot_nn(probs, value_rows[:, columns]).astype(BF16))
        out_ref[...] = jnp.concatenate(outs, axis=1).reshape(out_ref.shape)

    heads = half // HDIM
    old = () if before is None else before
    return call(
        kernel,
        (last_image - first_image, half // lanes),
        [pl.BlockSpec((3, 2, 1, half_len, lanes), lambda i, j: (0, 0, first_image + i, 0, j))]
        + [ANYWHERE] * len(old),
        [
            pl.BlockSpec((2, 1, half_len, lanes), lambda i, j: (0, first_image + i, 0, j)),
            pl.BlockSpec((1, per_step, length, length), lambda i, j: (first_image + i, j, 0, 0)),
        ],
        [struct((2, images, half_len, half)), struct((images, heads, length, length))],
        24 * (last_image - first_image) * heads * length * length * HDIM,
        (last_image - first_image) * heads * length * length * 2,
        after,
        {1: 0, 2: 1} if old else None,
        part=FORWARD_PART,
    )(projected, *old)


def attend_back(projected, grad_context, probs, lanes=256, after=()):
    _, _, images, half_len, half = projected.shape
    length = 2 * half_len
    per_step = lanes // HDIM
    scale = HDIM**-0.5

    def kernel(proj_ref, grad_ref, probs_ref, out_ref, sum_ref):
        queries, key_rows, value_rows = (proj_ref[at].reshape(length, lanes) for at in range(3))
        grads = grad_ref[...].reshape(length, lanes)
        found = ([], [], [])
        for head in range(per_step):
            columns = slice(head * HDIM, (head + 1) * HDIM)
            low = probs_ref[0, head]
            found[2].append(dot_tn(low, grads[:, columns]).astype(BF16))
            grad_soft = dot_nt(grads[:, columns], value_rows[:, columns])
            soft = low.astype(F32)
            scaled = soft * grad_soft
            grad_scores = (scaled - soft * jnp.sum(scaled, axis=-1, keepdims=True)).astype(BF16)
            found[0].append((dot_nn(grad_scores, key_rows[:, columns]) * scale).astype(BF16))
            found[1].append((dot_tn(grad_scores, queries[:, columns]) * scale).astype(BF16))
        for at in range(3):
            joined = jnp.concatenate(found[at], axis=1)
            out_ref[at] = joined.reshape(2, 1, half_len, lanes)
            if at != 1:
                sum_ref[0, at // 2 : at // 2 + 1] = column_sum(joined.astype(F32))

    heads = half // HDIM
    block = pl.BlockSpec((3, 2, 1, half_len, lanes), lambda i, j: (0, 0, i, 0, j))
    return call(
        kernel,
        (images, half // lanes),
        [
            block,
            pl.BlockSpec((2, 1, half_len, lanes), lambda i, j: (0, i, 0, j)),
            pl.BlockSpec((1, per_step, length, length), lambda i, j: (i, j, 0, 0)),
        ],
        [block, pl.BlockSpec((1, 2, lanes), lambda i, j: (i, 0, j))],
        [struct(projected.shape), struct((images, 2, half), F32)],
        32 * images * heads * length * length * HDIM,
        images * heads * length * length * 2,
        after,
    )(projected, grad_context, probs)


def add_branch(contexts, rows, pieces, bias, gain, shift, tile=288, after=()):
    count, width = rows.shape
    half = width // 2

    def kernel(low_ref, high_ref, rows_ref, bias_ref, gain_ref, shift_ref, *refs):
        parts, (middle_ref, norm_ref) = far_list(refs[:4], refs[4:6]), refs[6:]
        found = []
        for at in range(4):
            found.append(dot_nt(low_ref[...], parts[2 * at][...]) + dot_nt(high_ref[...], parts[2 * at + 1][...]))
        middle = rows_ref[...].astype(F32) + (jnp.concatenate(found, axis=1) + bias_ref[...])
        middle_ref[...] = middle
        unit, _ = normal_parts(middle)
        norm_ref[...] = (unit * gain_ref[...] + shift_ref[...]).astype(BF16)

    block = pl.BlockSpec((tile, width), lambda i: (i, 0))
    half_block = pl.BlockSpec((tile, half), lambda i: (i, 0))
    return call(
        kernel,
        (count // tile,),
        [half_block, half_block, block] + [fixed(1, width)] * 3 + piece_specs(half, 3),
        [block, block],
        [struct((count, width), F32), struct((count, width))],
        2 * count * width * width,
        10 * count * width + 2 * width * width,
        after,
        part=FORWARD_PART,
    )(*contexts, rows, bias, gain, shift, *pieces)


def feed_up(places, x_at, second, gathered, bias, tile=512, after=()):
    count, width = second.shape
    columns = gathered.shape[-1]

    def kernel(place_ref, second_ref, bias_ref, *refs):
        hidden = dot_nn(second_ref[...], joined(refs, 0, 16)) + bias_ref[...]
        gate = 0.5 + 0.5 * jnp.tanh(0.851 * hidden)
        refs[16][...] = (hidden * gate).astype(BF16)
        refs[17][...] = (gate * (1.0 + 1.702 * hidden * (1.0 - gate))).astype(BF16)

    block = pl.BlockSpec((count, tile), lambda j, _: (0, j))
    return call(
        kernel,
        (columns // tile,),
        [fixed(count, width), pl.BlockSpec((1, tile), lambda j, _: (0, j))] + gathered_specs(tile, (x_at,)),
        [block, block],
        [struct((count, columns))] * 2,
        2 * count * width * columns,
        2 * count * (width + 2 * columns) + 2 * width * columns,
        after,
        None,
        1,
        part=FORWARD_PART,
    )(places, second, bias, *[gathered] * 16)


def feed_down(side, first_tile, last_tile, actives, middle, gathered, bias, order, before=None, tile=288, after=()):
    count, columns = actives[0].shape
    width = middle.shape[1]
    mine = count // tile // 2
    half_at = first_tile // mine
    old = () if before is None else (before,)

    def kernel(side_ref, low_ref, high_ref, middle_ref, bias_ref, order_ref, *refs):
        keep = side_ref[2 + side_ref[0] * mine + first_tile % mine + pl.program_id(0)].astype(F32)
        out_ref = refs[-1]
        feed = dot_nt(low_ref[...], joined(refs, 0, 16, 2, 0)) + dot_nt(high_ref[...], joined(refs, 0, 16, 2, 1))
        out = ((middle_ref[...] + (feed + bias_ref[...])) * keep).astype(BF16)
        out_ref[0] = dot_nt(out, order_ref[...]).astype(BF16)

    hidden = pl.BlockSpec((tile, columns), lambda i, _: (first_tile + i, 0))
    offset = (lambda ref: ref[0] * mine + first_tile) if half_at == 0 else (lambda ref: first_tile - mine)

    return call(
        kernel,
        (last_tile - first_tile,),
        [
            hidden,
            hidden,
            pl.BlockSpec((tile, width), lambda i, _: (first_tile + i, 0)),
            fixed(1, width),
            fixed(width, width),
        ]
        + gathered_specs(columns, at=0)
        + [ANYWHERE] * len(old),
        image_block(tile, width, offset),
        struct(((2 - half_at) * mine, tile, width)),
        2 * count * width * columns + count * width * width,
        2 * count * columns + 3 * count * width + 4 * width * columns,
        after,
        {38: 0} if old else None,
        1,
    )(side, *actives, middle, bias, order, *[gathered] * 32, *old)


def gate_back(side, final, slopes, gathered, tile=512, after=()):
    count, width = final.shape
    columns = gathered.shape[-1]

    def kernel(side_ref, final_ref, low_ref, high_ref, *refs):
        outs, sums = refs[32:34], refs[34:36]
        for x_at, slope_ref in enumerate((low_ref, high_ref)):
            weight = joined(refs, 0, 16, 2, x_at)
            grad = (dot_nn(final_ref[...], weight) * slope_ref[...].astype(F32)).astype(BF16)
            outs[x_at][...] = grad
            sums[x_at][...] = column_sum(grad.astype(F32))

    block = pl.BlockSpec((count, tile), lambda j, _: (0, j))
    sum_block = pl.BlockSpec((1, tile), lambda j, _: (0, j))
    return call(
        kernel,
        (columns // tile,),
        [fixed(count, width), block, block] + gathered_specs(tile),
        [block, block, sum_block, sum_block],
        [struct((count, columns))] * 2 + [struct((1, columns), F32)] * 2,
        4 * count * width * columns,
        4 * count * (width + 2 * columns) + 4 * width * columns,
        after,
        None,
        1,
    )(side, final, *slopes, *[gathered] * 32)


def sums_down(final, actives, tile=512, after=()):
    count, width = final.shape
    columns = actives[0].shape[1]

    def kernel(final_ref, low_ref, high_ref, *outs):
        for x_at, right_ref in enumerate((low_ref, high_ref)):
            for core in range(2):
                for y_at in range(2):
                    start = (2 * core + y_at) * PART
                    part = dot_tn(final_ref[:, start : start + PART], right_ref[...])
                    outs[2 * core + y_at][x_at] = part.astype(BF16)

    right = pl.BlockSpec((count, tile), lambda j: (0, j))
    return call(
        kernel,
        (columns // tile,),
        [fixed(count, width), right, right],
        [pl.BlockSpec((2, PART, tile), lambda j: (0, 0, j))] * 4,
        [struct((2, PART, columns))] * 4,
        4 * count * width * columns,
        4 * count * columns + 2 * count * width + 4 * width * columns,
        after,
    )(final, *actives)


def sums_up(second, grads, tile=512, after=()):
    count, width = second.shape
    columns = grads[0].shape[1]

    def kernel(second_ref, low_ref, high_ref, *outs):
        for x_at, right_ref in enumerate((low_ref, high_ref)):
            for core in range(2):
                for y_at in range(2):
                    start = (2 * core + y_at) * PART
                    part = dot_tn(second_ref[:, start : start + PART], right_ref[...])
                    outs[2 * core + x_at][y_at] = part.astype(BF16)

    right = pl.BlockSpec((count, tile), lambda j: (0, j))
    return call(
        kernel,
        (columns // tile,),
        [fixed(count, width), right, right],
        [pl.BlockSpec((2, PART, tile), lambda j: (0, 0, j))] * 4,
        [struct((2, PART, columns))] * 4,
        4 * count * width * columns,
        4 * count * columns + 2 * count * width + 4 * width * columns,
        after,
    )(second, *grads)


def sums_first(normed, branch, grad_projected, context, after=()):
    count, width = normed.shape
    half = context.shape[1]

    def kernel(norm_ref, branch_ref, grad_ref, context_ref, *outs):
        def work(left_ref, right):
            for core in range(2):
                for y_at in range(2):
                    start = (2 * core + y_at) * PART
                    outs[2 * core + y_at][...] = dot_tn(left_ref[:, start : start + PART], right).astype(BF16)

        @pl.when(pl.program_id(0) < 3)
        def _():
            work(norm_ref, grad_ref[0])

        @pl.when(pl.program_id(0) == 3)
        def _():
            work(branch_ref, context_ref[...])

    left = fixed(count, width)
    return call(
        kernel,
        (4,),
        [left, left, pl.BlockSpec((1, count, half), lambda j: (jnp.minimum(j, 2), 0, 0)), fixed(count, half)],
        [pl.BlockSpec((PART, half), lambda j: (0, j))] * 4,
        [struct((PART, 4 * half))] * 4,
        8 * count * width * half,
        2 * count * (2 * width + 4 * half) + 8 * width * half,
        after,
    )(normed, branch, grad_projected, context)


def second_back(places, grads, gathered, first_pieces, middle, final, gain, tile=288, after=()):
    count, columns = grads[0].shape
    width = middle.shape[1]
    half = width // 2

    def kernel(place_ref, low_ref, high_ref, middle_ref, final_ref, gain_ref, *refs):
        ups, outs = refs[:32], far_list(refs[32:36], refs[36:38])
        grad_ref, branch_ref, context_low_ref, context_high_ref, sum_ref = refs[38:]
        grad_second = dot_nt(low_ref[...], joined(ups, 0, 16, 2, 0)) + dot_nt(high_ref[...], joined(ups, 0, 16, 2, 1))
        unit, inv_std = normal_parts(middle_ref[...])
        grad_middle = final_ref[...].astype(F32) + normalize_back(
            grad_second, unit, inv_std, gain_ref[...]
        )
        branch = grad_middle.astype(BF16)
        grad_ref[...] = grad_middle
        branch_ref[...] = branch
        for x_at, context_ref in enumerate((context_low_ref, context_high_ref)):
            weight = jnp.concatenate([outs[2 * at + x_at][...] for at in range(4)], axis=0)
            context_ref[...] = dot_nn(branch, weight).astype(BF16)

        @pl.when(first_step())
        def _():
            sum_ref[...] = jnp.zeros_like(sum_ref)

        sum_ref[0:1] += column_sum(grad_second * unit)
        sum_ref[1:2] += column_sum(grad_second)
        sum_ref[2:3] += column_sum(branch.astype(F32))

    block = pl.BlockSpec((tile, width), lambda i, _: (i, 0))
    half_block = pl.BlockSpec((tile, half), lambda i, _: (i, 0))
    hidden = pl.BlockSpec((tile, columns), lambda i, _: (i, 0))
    return call(
        kernel,
        (count // tile,),
        [hidden, hidden, block, block, fixed(1, width)]
        + gathered_specs(columns, at=0)
        + piece_specs(half, 3),
        [block, block, half_block, half_block, fixed(8, width)],
        [struct((count, width), F32), struct((count, width))]
        + [struct((count, half))] * 2
        + [struct((8, width), F32)],
        4 * count * width * columns + 2 * count * width * width,
        4 * count * columns + 14 * count * width + 4 * width * columns,
        after,
        None,
        1,
    )(places, *grads, middle, final, gain, *[gathered] * 32, *first_pieces)


def first_back(side, half_at, grads, pieces, rows, grad_middle, gain, order, tile=288, after=()):
    _, count, half = grads[0].shape
    width = rows.shape[1]
    mine = count // tile // 2

    def kernel(side_ref, low_ref, high_ref, rows_ref, middle_ref, gain_ref, order_ref, *refs):
        parts, (out_ref, sum_ref) = far_list(refs[:4], refs[4:6]), refs[6:]
        lefts = [jnp.concatenate([ref[at] for at in range(3)], axis=1) for ref in (low_ref, high_ref)]
        found = []
        for at in range(4):
            found.append(
                dot_nt(lefts[0], parts[2 * at][...]) + dot_nt(lefts[1], parts[2 * at + 1][...])
            )
        grad_normed = jnp.concatenate(found, axis=1)
        unit, inv_std = normal_parts(rows_ref[...].astype(F32))
        out = middle_ref[...] + normalize_back(grad_normed, unit, inv_std, gain_ref[...])
        out_ref[0] = dot_nt(out.astype(BF16), order_ref[...]).astype(BF16)

        @pl.when(first_step())
        def _():
            sum_ref[...] = jnp.zeros_like(sum_ref)

        sum_ref[0:1] += column_sum(grad_normed * unit)
        sum_ref[1:2] += column_sum(grad_normed)

    start = half_at * mine
    block = pl.BlockSpec((tile, width), lambda i, _: (start + i, 0))
    grad_block = pl.BlockSpec((3, tile, half), lambda i, _: (0, start + i, 0))
    offset = (lambda ref: ref[0] * mine) if half_at == 0 else (lambda ref: 0)
    return call(
        kernel,
        (mine,),
        [grad_block, grad_block, block, block, fixed(1, width), fixed(width, width)]
        + piece_specs(3 * half),
        [image_block(tile, width, offset), fixed(8, width)],
        [struct(((2 - half_at) * mine, tile, width)), struct((8, width), F32)],
        4 * count * width * width,
        8 * count * width + 6 * width * width,
        after,
        None,
        1,
        part=0.3,
    )(side, *grads, rows, grad_middle, gain, order, *pieces)


def fast_shards(
    tokens,
    image_mask,
    out_grad,
    norm1_gain,
    norm1_shift,
    qkv_weight,
    qv_bias,
    out_weight,
    out_bias,
    norm2_gain,
    norm2_shift,
    up_weight,
    up_bias,
    down_weight,
    down_bias,
):
    images, half_len, width = tokens.shape
    mine = images // 2
    half = qkv_weight.shape[2]
    half_hidden = up_weight.shape[1]
    count = 2 * mine * half_len
    me = lax.axis_index("dp")
    side = lax.axis_index("tensor")
    side_array = jnp.concatenate([jnp.stack([side, me]).astype(jnp.int32), image_mask])
    vectors = (norm1_gain, norm1_shift, norm2_gain, norm2_shift, out_bias, down_bias)
    order, gain_one, shift_one, gain_two, shift_two, bias_out, bias_down = setup(
        side_array, [vector.reshape(1, width) for vector in vectors]
    )

    def for_partner(values):
        return over_x(lax.dynamic_slice_in_dim(values, (1 - side) * mine, mine, 0))

    def z_all(values):
        return jnp.concatenate([values] + [over_z(values, step) for step in (1, 2, 3)], axis=0)

    up_all = lax.all_gather(up_weight, ("dp", "tensor")).reshape(-1, 2, ROWS, half_hidden)
    own = prepare(side_array, tokens, order, gain_one, shift_one, 0)
    final, sum_own = mask_grad(side_array, out_grad, order, 0, after=own[:1])
    tokens_partner = for_partner(tokens)
    first = jnp.concatenate([qkv_weight.reshape(ROWS, 3 * half), out_weight], axis=1)
    first_base = late(z_all(first), final)
    biases = jnp.concatenate([qv_bias.reshape(-1), up_bias])
    bias_rows = jnp.pad(biases, (0, 16 * half_hidden - biases.size)).reshape(16, half_hidden)

    def split_bias(bias):
        bias = bias.astype(F32)
        parts = jnp.stack([bias[:half], jnp.zeros((half,), F32), bias[half : 2 * half]])
        return parts[:, None], bias[None, 2 * half :]

    rows, normed = prepare(
        side_array, tokens_partner, order, gain_one, shift_one, 1, own, after=[first_base]
    )
    first_x = over_x(jnp.concatenate([late(first_base, normed), bias_rows], axis=0))
    first_y = over_y(late(first_base, normed))
    first_xy = over_y(late(first_x, first_y))
    first_far = [over_core(jnp.stack(late([first_base, first_y], first_x)))]
    biases = [split_bias(biases), split_bias(first_x[4 * ROWS :].reshape(-1)[: biases.size])]
    heads_shape = (3, 2, mine, half_len, half)
    projected, contexts, probs = [None, None], [None, None], [None, None]
    projected[0] = project(normed, [first_base, first_y] + first_far, biases[0][0]).reshape(heads_shape)
    begun = attend(projected[0], 0, 1, lanes=128)
    first_far += [over_core(jnp.stack(late([first_x, first_xy], begun[0])))]
    first_pieces = [first_base, first_x, first_y, first_xy] + first_far
    contexts[0], probs[0] = attend(projected[0], 1, 2, begun, lanes=128)
    grad_partner = for_partner(late(out_grad, first_x))
    projected[1] = project(
        normed, [first_x, first_xy] + first_far[1:], biases[1][0], after=[contexts[0]]
    ).reshape(heads_shape)
    down_all = lax.all_gather(late(down_weight, up_all, contexts[0]), ("dp", "tensor"))
    down_all = down_all.reshape(-1, 2, ROWS, half_hidden)
    contexts[1], probs[1] = attend(projected[1], 0, 2)
    contexts = [values.reshape(count, half) for values in contexts]
    middle, second = add_branch(contexts, rows, first_pieces, bias_out, gain_two, shift_two)
    actives, slopes = [None, None], [None, None]
    actives[0], slopes[0] = feed_up(side_array, 0, second, up_all, biases[0][1])
    final, sum_partner = mask_grad(side_array, grad_partner, order, 1, final, after=[actives[0]])
    actives[1], slopes[1] = feed_up(side_array, 1, second, up_all, biases[1][1], after=[final])

    down_near, down_next, down_far, down_last = sums_down(final, actives)
    grads_sums = gate_back(side_array, final, slopes, down_all, after=[down_near])
    grads, sum_hidden = grads_sums[:2], grads_sums[2:]
    (down_sent,) = combine([down_next, over_core(down_last)], 1, after=grads[:1])
    down_sent_y = over_y(down_sent)
    up_near, up_next, up_far_sums, up_last = sums_up(second, grads, after=[down_sent])
    grad_middle, branch, *grad_contexts, sums_two = second_back(
        side_array, grads, up_all, first_pieces, middle, final, gain_two, after=[up_near]
    )
    (up_sent,) = combine([up_next, over_core(up_last)], 1, after=[branch])
    up_sent_x = over_x(up_sent)
    down_far = over_core(late(down_far, up_sent))

    def heads_back(x_at, after):
        grad_context = grad_contexts[x_at].reshape(2, mine, half_len, half)
        grad, sums = attend_back(projected[x_at], grad_context, probs[x_at], after=after)
        return grad.reshape(3, count, half), jnp.sum(sums, axis=0)

    grads_qkv, sums_qkv = [None, None], [None, None]
    grads_qkv[1], sums_qkv[1] = heads_back(1, [up_sent])
    down_sums = combine([down_near, down_far, down_sent_y], 2, after=[grads_qkv[1]])
    down_sent_x = over_x(down_sums[1])
    high_near, high_next, high_far, high_last = sums_first(
        normed, branch, grads_qkv[1], contexts[1], after=down_sums[:1]
    )
    up_far_sums = over_core(late(up_far_sums, high_near))
    out_send = feed_down(side_array, 2, 4, actives, middle, down_all, bias_down, order, after=[high_near])
    (high_sent,) = combine([high_next, over_core(high_last)], 1, after=[out_send])
    high_sent_y = over_y(high_sent)
    up_sums = combine([up_near, up_far_sums, up_sent_x], 2, after=[high_sent])
    up_sent_y = over_y(up_sums[1])
    high_far = over_core(late(high_far, up_sums[0]))
    out_partner = over_x(late(out_send, up_sums[0]))
    grads_qkv[0], sums_qkv[0] = heads_back(0, up_sums[:1])
    low_near, low_next, low_far, low_last = sums_first(
        normed, branch, grads_qkv[0], contexts[0], after=[high_far]
    )
    (high,) = combine([high_near, high_far, high_sent_y], 1, after=[low_near])
    high_x = over_x(high)
    down_sums = combine([down_sums[0], down_sent_x], 2, after=[high])
    down_sent_z = over_z(down_sums[1], 2)
    (low_sent,) = combine([low_next, over_core(low_last)], 1, after=down_sums[:1])
    low_sent_y = over_y(low_sent)
    send, sums_partner = first_back(
        side_array, 1, grads_qkv, first_pieces, rows, grad_middle, gain_one, order, after=[low_sent]
    )
    up_sums = combine([up_sums[0], up_sent_y], 2, after=[send])
    up_sent_z = over_z(up_sums[1], 2)
    down_sums = combine([down_sums[0], down_sent_z], 2, after=[up_sums[0], out_partner])
    down_sent_z = over_z(down_sums[1], 1)
    low_far = over_core(late(low_far, up_sums[0]))
    full, sums_own = first_back(
        side_array, 0, grads_qkv, first_pieces, rows, grad_middle, gain_one, order, after=down_sums[:1]
    )
    up_sums = combine([up_sums[0], up_sent_z], 2, after=[full])
    up_sent_z = over_z(up_sums[1], 1)
    (grad_down,) = combine([down_sums[0], down_sent_z], 1, F32, after=up_sums[:1])

    sums = jnp.concatenate(
        [(sums_own + sums_partner)[:2], sums_two[2:3], sums_two[:2], sum_own + sum_partner], axis=0
    )
    sums = jnp.einsum("td,od->to", sums, order.astype(F32), precision=lax.Precision.HIGHEST)
    halves = [
        jnp.concatenate([sums_qkv[x_at].reshape(-1), sum_hidden[x_at][0]]) for x_at in range(2)
    ]
    small = late(jnp.concatenate([halves[0], sums.reshape(-1), halves[1]]), up_sums[0])
    small = small + over_core(small)
    small = small + over_y(small)
    small = (small + over_z(small, 1)) + (over_z(small, 2) + over_z(small, 3))
    halves_size = 2 * half + half_hidden
    small_x = over_x(jnp.concatenate([small[-halves_size:], small[halves_size:-halves_size]]))

    low = combine([low_near, low_far, low_sent_y, high_x], 4, after=[grad_down])
    low_z = [over_z(low[step], step) for step in (1, 2, 3)]
    send_x = over_x(late(send, low[0]))
    out_full = feed_down(
        side_array, 0, 2, actives, middle, down_all, bias_down, order, after=[low[0], small]
    )
    block_out = lax.dynamic_update_slice_in_dim(out_full, out_partner, (1 - side) * mine, 0)
    (grad_up,) = combine([up_sums[0], up_sent_z], 1, F32, after=[out_full])
    tokens_grad = lax.dynamic_update_slice_in_dim(full, send_x, (1 - side) * mine, 0)
    (grad_first,) = combine([low[0]] + low_z, 1, F32, after=[grad_up, tokens_grad])

    small = small[:-halves_size] + small_x
    halves = small[:halves_size]
    sums = small[halves_size:].reshape(6, width)
    return (
        block_out,
        tokens_grad,
        sums[0],
        sums[1],
        grad_first[:, : 3 * half].reshape(ROWS, 3, half),
        halves[: 2 * half].reshape(2, half),
        grad_first[:, 3 * half :],
        sums[2],
        sums[3],
        sums[4],
        grad_up,
        halves[2 * half :],
        grad_down,
        sums[5],
    )


def solution(mesh):
    in_specs = (
        P("dp", "tensor", None),
        P("dp"),
        P("dp", "tensor", None),
        P(),
        P(),
        P("dp", None, "tensor"),
        P(None, "tensor"),
        P("dp", "tensor"),
        P(),
        P(),
        P(),
        P("dp", "tensor"),
        P("tensor"),
        P("dp", "tensor"),
        P(),
    )
    out_specs = (
        P("dp", "tensor", None),
        P("dp", "tensor", None),
        P(),
        P(),
        P("dp", None, "tensor"),
        P(None, "tensor"),
        P("dp", "tensor"),
        P(),
        P(),
        P(),
        P("dp", "tensor"),
        P("tensor"),
        P("dp", "tensor"),
        P(),
    )
    small_slice = mesh.shape["dp"] == 16 and mesh.shape["tensor"] == 2
    shards = fast_shards if small_slice else general_shards
    return jax.shard_map(shards, mesh=mesh, in_specs=in_specs, out_specs=out_specs, check_vma=False)
```

```python
import jax
import jax.numpy as jnp
from jax import lax
from jax.experimental import pallas as pl
from jax.experimental.pallas import tpu as pltpu
from jax.sharding import PartitionSpec as P

HDIM = 64
MICRO = 2


def mixed(form, left, right):
    return jnp.einsum(form, left, right, preferred_element_type=jnp.float32)


def normalize(values, gain, shift):
    mean_val = jnp.mean(values, axis=-1, keepdims=True)
    centered = values - mean_val
    inv_std = lax.rsqrt(jnp.mean(centered * centered, axis=-1, keepdims=True) + 1e-05)
    unit_val = centered * inv_std
    return (unit_val * gain + shift, unit_val, inv_std)


def normalize_back(grad_in, unit_val, inv_std, gain):
    scaled = grad_in * gain
    return inv_std * (
        scaled
        - jnp.mean(scaled, axis=-1, keepdims=True)
        - unit_val * jnp.mean(scaled * unit_val, axis=-1, keepdims=True)
    )


def token_sum(values):
    return jnp.sum(values, axis=(0, 1))


def general_shards(
    tokens,
    image_mask,
    out_grad,
    norm1_gain,
    norm1_shift,
    qkv_weight,
    qv_bias,
    out_weight,
    out_bias,
    norm2_gain,
    norm2_shift,
    up_weight,
    up_bias,
    down_weight,
    down_bias,
):
    images_here = tokens.shape[0] // MICRO
    full_width = norm1_gain.shape[0]
    local_width = qkv_weight.shape[2]
    local_hidden = up_weight.shape[1]
    local_heads = local_width // HDIM
    score_scale = HDIM ** (-0.5)
    gain_one = norm1_gain.astype(jnp.float32)
    shift_one = norm1_shift.astype(jnp.float32)
    gain_two = norm2_gain.astype(jnp.float32)
    shift_two = norm2_shift.astype(jnp.float32)
    bias_pair = qv_bias.astype(jnp.float32)
    grad_qkv = jnp.zeros((full_width, 3, local_width), jnp.float32)
    grad_out = jnp.zeros((full_width, local_width), jnp.float32)
    grad_up = jnp.zeros((full_width, local_hidden), jnp.float32)
    grad_down = jnp.zeros((full_width, local_hidden), jnp.float32)
    grad_gain_one = jnp.zeros((full_width,), jnp.float32)
    grad_shift_one = jnp.zeros((full_width,), jnp.float32)
    grad_gain_two = jnp.zeros((full_width,), jnp.float32)
    grad_shift_two = jnp.zeros((full_width,), jnp.float32)
    grad_out_bias = jnp.zeros((full_width,), jnp.float32)
    grad_down_bias = jnp.zeros((full_width,), jnp.float32)
    grad_pair = jnp.zeros((2, local_width), jnp.float32)
    grad_up_bias = jnp.zeros((local_hidden,), jnp.float32)
    outputs = []
    input_grads = []
    for micro_index in range(MICRO):
        first_image = micro_index * images_here
        block_rows = tokens[first_image : first_image + images_here].astype(jnp.float32)
        keep_mask = image_mask[first_image : first_image + images_here].astype(jnp.float32)[
            :, None, None
        ]
        fwd_weights = (
            lax.all_gather(qkv_weight, "dp", axis=0, tiled=True),
            lax.all_gather(out_weight, "dp", axis=0, tiled=True),
            lax.all_gather(up_weight, "dp", axis=0, tiled=True),
            lax.all_gather(down_weight, "dp", axis=0, tiled=True),
        )
        qkv_full, out_full, up_full, down_full = fwd_weights
        normed, unit_one, inv_one = normalize(block_rows, gain_one, shift_one)
        normed_full = lax.all_gather(normed.astype(jnp.bfloat16), "tensor", axis=1, tiled=True)
        seq_len = normed_full.shape[1]
        head_shape = (images_here, seq_len, local_heads, HDIM)
        projected = mixed("isd,dcf->iscf", normed_full, qkv_full)
        queries = (projected[:, :, 0] + bias_pair[0]).astype(jnp.bfloat16).reshape(head_shape)
        key_rows = projected[:, :, 1].astype(jnp.bfloat16).reshape(head_shape)
        value_rows = (projected[:, :, 2] + bias_pair[1]).astype(jnp.bfloat16).reshape(head_shape)
        scores = mixed("iqhe,ikhe->ihqk", queries, key_rows) * score_scale
        row_top = jnp.max(scores, axis=-1, keepdims=True)
        raw_weights = jnp.exp(scores - row_top)
        row_total = jnp.sum(raw_weights, axis=-1, keepdims=True)
        log_total = row_top + jnp.log(row_total)
        probs = (raw_weights / row_total).astype(jnp.bfloat16)
        context = mixed("ihqk,ikhe->iqhe", probs, value_rows).astype(jnp.bfloat16)
        context = context.reshape(images_here, seq_len, local_width)
        attn_terms = mixed("isf,of->iso", context, out_full)
        branch = lax.psum_scatter(
            attn_terms, "tensor", scatter_dimension=1, tiled=True
        ) + out_bias.astype(jnp.float32)
        middle = block_rows + branch
        second, unit_two, inv_two = normalize(middle, gain_two, shift_two)
        second_full = lax.all_gather(second.astype(jnp.bfloat16), "tensor", axis=1, tiled=True)
        hidden = mixed("isd,df->isf", second_full, up_full) + up_bias.astype(jnp.float32)
        gate_sig = jax.nn.sigmoid(1.702 * hidden)
        active = (hidden * gate_sig).astype(jnp.bfloat16)
        feed_terms = mixed("isf,of->iso", active, down_full)
        feed_out = lax.psum_scatter(
            feed_terms.astype(jnp.bfloat16), "tensor", scatter_dimension=1, tiled=True
        ).astype(jnp.float32) + down_bias.astype(jnp.float32)
        outputs.append(((middle + feed_out) * keep_mask).astype(jnp.bfloat16))
        back_weights = (
            lax.all_gather(qkv_weight, "dp", axis=0, tiled=True),
            lax.all_gather(out_weight, "dp", axis=0, tiled=True),
            lax.all_gather(up_weight, "dp", axis=0, tiled=True),
            lax.all_gather(down_weight, "dp", axis=0, tiled=True),
        )
        qkv_back, out_back, up_back, down_back = back_weights
        grad_final = (
            out_grad[first_image : first_image + images_here].astype(jnp.float32) * keep_mask
        )
        grad_down_bias = grad_down_bias + token_sum(grad_final)
        final_full = lax.all_gather(grad_final.astype(jnp.bfloat16), "tensor", axis=1, tiled=True)
        grad_down = grad_down + mixed("iso,isf->of", final_full, active)
        grad_active = mixed("iso,of->isf", final_full, down_back)
        grad_hidden = (
            grad_active * (gate_sig + 1.702 * hidden * gate_sig * (1.0 - gate_sig))
        ).astype(jnp.bfloat16)
        grad_up_bias = grad_up_bias + token_sum(grad_hidden.astype(jnp.float32))
        grad_up = grad_up + mixed("isd,isf->df", second_full, grad_hidden)
        second_terms = mixed("isf,df->isd", grad_hidden, up_back)
        grad_second = lax.psum_scatter(second_terms, "tensor", scatter_dimension=1, tiled=True)
        grad_gain_two = grad_gain_two + token_sum(grad_second * unit_two)
        grad_shift_two = grad_shift_two + token_sum(grad_second)
        grad_middle = grad_final + normalize_back(grad_second, unit_two, inv_two, gain_two)
        grad_branch = grad_middle.astype(jnp.bfloat16)
        grad_out_bias = grad_out_bias + token_sum(grad_branch.astype(jnp.float32))
        branch_full = lax.all_gather(grad_branch, "tensor", axis=1, tiled=True)
        grad_out = grad_out + mixed("iso,isf->of", branch_full, context)
        grad_context = (
            mixed("iso,of->isf", branch_full, out_back).astype(jnp.bfloat16).reshape(head_shape)
        )
        again = mixed("iqhe,ikhe->ihqk", queries, key_rows) * score_scale
        soft_again = jnp.exp(again - log_total)
        probs_again = soft_again.astype(jnp.bfloat16)
        grad_values = mixed("ihqk,iqhe->ikhe", probs_again, grad_context)
        grad_soft = mixed("iqhe,ikhe->ihqk", grad_context, value_rows)
        grad_scores = (
            soft_again * (grad_soft - jnp.sum(grad_soft * soft_again, axis=-1, keepdims=True))
        ).astype(jnp.bfloat16)
        grad_queries = mixed("ihqk,ikhe->iqhe", grad_scores, key_rows) * score_scale
        grad_keys = mixed("ihqk,iqhe->ikhe", grad_scores, queries) * score_scale
        flat_shape = (images_here, seq_len, local_width)
        grad_projected = jnp.stack(
            (
                grad_queries.reshape(flat_shape),
                grad_keys.reshape(flat_shape),
                grad_values.reshape(flat_shape),
            ),
            axis=2,
        ).astype(jnp.bfloat16)
        pair_terms = grad_projected.astype(jnp.float32)
        grad_pair = grad_pair + jnp.stack(
            (token_sum(pair_terms[:, :, 0]), token_sum(pair_terms[:, :, 2])), axis=0
        )
        grad_qkv = grad_qkv + mixed("isd,iscf->dcf", normed_full, grad_projected)
        normed_terms = mixed("iscf,dcf->isd", grad_projected, qkv_back)
        grad_normed = lax.psum_scatter(
            normed_terms.astype(jnp.bfloat16), "tensor", scatter_dimension=1, tiled=True
        ).astype(jnp.float32)
        grad_gain_one = grad_gain_one + token_sum(grad_normed * unit_one)
        grad_shift_one = grad_shift_one + token_sum(grad_normed)
        grad_tokens = grad_middle + normalize_back(grad_normed, unit_one, inv_one, gain_one)
        input_grads.append(grad_tokens.astype(jnp.bfloat16))
    grad_qkv, grad_out, grad_up, grad_down = (
        lax.psum_scatter(
            grad_qkv.astype(jnp.bfloat16), "dp", scatter_dimension=0, tiled=True
        ).astype(jnp.float32),
        lax.psum_scatter(
            grad_out.astype(jnp.bfloat16), "dp", scatter_dimension=0, tiled=True
        ).astype(jnp.float32),
        lax.psum_scatter(
            grad_up.astype(jnp.bfloat16), "dp", scatter_dimension=0, tiled=True
        ).astype(jnp.float32),
        lax.psum_scatter(
            grad_down.astype(jnp.bfloat16), "dp", scatter_dimension=0, tiled=True
        ).astype(jnp.float32),
    )
    grad_gain_one, grad_shift_one, grad_gain_two, grad_shift_two, grad_out_bias, grad_down_bias = (
        lax.psum(
            (
                grad_gain_one,
                grad_shift_one,
                grad_gain_two,
                grad_shift_two,
                grad_out_bias,
                grad_down_bias,
            ),
            ("dp", "tensor"),
        )
    )
    grad_pair, grad_up_bias = lax.psum((grad_pair, grad_up_bias), "dp")
    block_out = jnp.concatenate(outputs, axis=0)
    tokens_grad = jnp.concatenate(input_grads, axis=0)
    return (
        block_out,
        tokens_grad,
        grad_gain_one,
        grad_shift_one,
        grad_qkv,
        grad_pair,
        grad_out,
        grad_out_bias,
        grad_gain_two,
        grad_shift_two,
        grad_up,
        grad_up_bias,
        grad_down,
        grad_down_bias,
    )


ROWS = 64
PART = 256
VMEM_BYTES = 24 * 1024 * 1024
COST_PART = 0.6
FORWARD_PART = 0.8
LOG2_E = 1.4426950408889634
BF16 = jnp.bfloat16
F32 = jnp.float32


def swap(values, axis_name, flip):
    count = lax.axis_size(axis_name)
    return lax.ppermute(values, axis_name, [(place, place ^ flip) for place in range(count)])


def over_core(values):
    return swap(values, "dp", 1)


def over_y(values):
    return swap(values, "dp", 2)


def over_z(values, step):
    return swap(values, "dp", 4 * step)


def over_x(values):
    return swap(values, "tensor", 1)


def late(values, *marks):
    return lax.optimization_barrier((values, *marks))[0]


def dot_nn(left, right):
    return lax.dot_general(left, right, (((1,), (0,)), ((), ())), preferred_element_type=F32)


def dot_nt(left, right):
    return lax.dot_general(left, right, (((1,), (1,)), ((), ())), preferred_element_type=F32)


def dot_tn(left, right):
    return lax.dot_general(left, right, (((0,), (0,)), ((), ())), preferred_element_type=F32)


def call(
    kernel, grid, in_specs, out_specs, out_shape, flops, moved, after=(), aliases=None, scalars=0, part=None
):
    given, waits = scalars + len(in_specs), len(after)
    part = COST_PART if part is None else part

    def run(*refs):
        kernel(*refs[:given], *refs[given + waits :])

    function = pl.pallas_call(
        run,
        grid_spec=pltpu.PrefetchScalarGridSpec(
            num_scalar_prefetch=scalars,
            grid=grid,
            in_specs=list(in_specs) + [pl.BlockSpec(memory_space=pl.ANY)] * waits,
            out_specs=out_specs,
        ),
        out_shape=out_shape,
        input_output_aliases=aliases or {},
        compiler_params=pltpu.CompilerParams(vmem_limit_bytes=VMEM_BYTES),
        cost_estimate=pl.CostEstimate(
            flops=int(flops * part), bytes_accessed=int(moved * part), transcendentals=0
        ),
    )
    return lambda *arrays: function(*arrays, *after)


def fixed(*shape, at=None):
    place = at or (0,) * len(shape)
    return pl.BlockSpec(shape, lambda *_: place, pipeline_mode=pl.Buffered(1))


def far_list(near, far):
    return list(near) + [far[last].at[y_at] for y_at in range(2) for last in range(2)]


def piece_specs(columns, at=0):
    return [fixed(PART, columns, at=(0, at))] * 4 + [fixed(2, PART, columns, at=(0, 0, at))] * 2


def piece_tiles(tile, near=4, far=2):
    return [pl.BlockSpec((PART, tile), lambda j: (0, j))] * near + [
        pl.BlockSpec((2, PART, tile), lambda j: (0, 0, j))
    ] * far


def gathered_specs(columns, halves=(0, 1), at=None):
    def spec(block, x_at):
        core, y_at, z_at = block // 8, (block // 4) % 2, block % 4
        slab = z_at * 4 + y_at * 2 + core

        def place(j, *refs):
            where = refs[-1]
            row = jnp.bitwise_xor(where[1], slab), jnp.bitwise_xor(where[0], x_at)
            return (*row, 0, j if at is None else at)

        mode = {} if at is None else {"pipeline_mode": pl.Buffered(1)}
        return pl.BlockSpec((1, 1, ROWS, columns), place, **mode)

    return [spec(block, x_at) for block in range(16) for x_at in halves]


def joined(refs, first, last, step=1, offset=0):
    return jnp.concatenate([refs[step * block + offset][0, 0] for block in range(first, last)], axis=0)


def struct(shape, dtype=BF16):
    return jax.ShapeDtypeStruct(shape, dtype)


def outer(shape, dtype=BF16):
    return pltpu.HBM(shape, dtype)


def in_hbm(values):
    if isinstance(values, (list, tuple)):
        return [in_hbm(part) for part in values]
    return pltpu.with_memory_space_constraint(values, pltpu.HBM)


ANYWHERE = pl.BlockSpec(memory_space=pl.ANY)


def normal_parts(values):
    mean_val = jnp.mean(values, axis=-1, keepdims=True)
    centered = values - mean_val
    inv_std = lax.rsqrt(jnp.mean(centered * centered, axis=-1, keepdims=True) + 1e-05)
    return centered * inv_std, inv_std


def column_sum(values):
    return jnp.sum(values, axis=0, keepdims=True)


def combine(arrays, pieces, dtype=BF16, tile=1024, after=()):
    columns = arrays[0].shape[-1]
    rows = arrays[0].size // columns // pieces
    arrays = [values.reshape(pieces, rows, columns) for values in arrays]
    given = len(arrays)

    def kernel(*refs):
        for at in range(pieces):
            parts = [ref[at].astype(F32) for ref in refs[:given]]
            while len(parts) > 1:
                parts = [sum(parts[start : start + 2]) for start in range(0, len(parts), 2)]
            refs[given + at][...] = parts[0].astype(dtype)

    return call(
        kernel,
        (columns // tile,),
        [pl.BlockSpec((pieces, rows, tile), lambda j: (0, 0, j))] * given,
        [pl.BlockSpec((rows, tile), lambda j: (0, j))] * pieces,
        [outer((rows, columns), dtype)] * pieces,
        0,
        2 * pieces * rows * columns * (given + 1),
        after,
    )(*arrays)


def finish(low_near, up_near, small, near, middle, far, after=()):
    rows, columns = low_near.shape
    split = columns * 3 // 4
    height = small.shape[0] // 2

    def kernel(low_ref, up_ref, small_ref, near_ref, middle_ref, far_ref, qkv_ref, out_ref, up_out_ref, sum_ref):
        def rows_of(ref, start):
            return ref[start : start + rows, :].astype(F32)

        def vectors_of(ref, start):
            values = ref[start : start + 2 * height, :].astype(F32)
            return values[:height] + values[height:]

        low = (rows_of(low_ref, 0) + rows_of(near_ref, 0)) + (rows_of(middle_ref, 0) + rows_of(far_ref, 0))
        qkv_ref[...] = low[:, :split]
        out_ref[...] = low[:, split:]
        up_out_ref[...] = rows_of(up_ref, 0) + rows_of(near_ref, rows)
        sum_ref[...] = (vectors_of(small_ref, 0) + vectors_of(near_ref, 2 * rows)) + (
            vectors_of(middle_ref, rows) + vectors_of(far_ref, rows)
        )

    given = [low_near, up_near, small, near, middle, far]
    return call(
        kernel,
        (1,),
        [fixed(*values.shape) for values in given],
        [fixed(rows, split), fixed(rows, columns - split), fixed(rows, columns), fixed(height, columns)],
        [
            struct((rows, split), F32),
            struct((rows, columns - split), F32),
            struct((rows, columns), F32),
            struct((height, columns), F32),
        ],
        0,
        20 * rows * columns,
        after,
    )(*given)


def first_step():
    return pl.program_id(0) == 0


def setup(places, vectors, after=()):
    width = vectors[0].shape[1]
    given = len(vectors)

    def kernel(place_ref, *refs):
        order_ref = refs[given]
        source = lax.broadcasted_iota(jnp.int32, (width, width), 0)
        target = lax.broadcasted_iota(jnp.int32, (width, width), 1)
        at = target // ROWS
        z_rel, y_rel, core_rel = at % 4, (at // 4) % 2, at // 8
        place = (z_rel * 4 + y_rel * 2 + core_rel) ^ place_ref[1]
        hit = source == place * ROWS + target % ROWS
        order = jnp.where(hit, 1.0, 0.0).astype(BF16)
        order_ref[...] = order
        rows = jnp.concatenate([ref[...].astype(F32) for ref in refs[:given]] + [jnp.zeros((8 - given, width), F32)], axis=0)
        moved = dot_nn(rows.astype(BF16), order)
        for vector_at in range(given):
            refs[given + 1 + vector_at][...] = moved[vector_at : vector_at + 1]

    row = fixed(1, width)
    return call(
        kernel,
        (1,),
        [row] * given,
        [fixed(width, width)] + [row] * given,
        [struct((width, width))] + [struct((1, width), F32)] * given,
        16 * width * width,
        2 * width * width,
        after,
        None,
        1,
        part=FORWARD_PART,
    )(places, *vectors)


def image_block(height, width, offset):
    return pl.BlockSpec((1, height, width), lambda i, side: (offset(side) + i, 0, 0))


def prepare(side, images, order, gain, shift, half_at, before=None, after=()):
    _, height, width = images.shape
    mine = 2

    def kernel(side_ref, raw_ref, order_ref, gain_ref, shift_ref, *refs):
        rows_ref, norm_ref = refs[-2:]
        rows = dot_nn(raw_ref[0], order_ref[...])
        rows_ref[...] = rows.astype(BF16)
        unit, _ = normal_parts(rows)
        norm_ref[...] = (unit * gain_ref[...] + shift_ref[...]).astype(BF16)

    offset = (lambda side_ref: side_ref[0] * mine) if half_at == 0 else (lambda side_ref: 0)
    out = pl.BlockSpec((height, width), lambda i, _: (half_at * mine + i, 0))
    old = () if before is None else before
    return call(
        kernel,
        (mine,),
        [image_block(height, width, offset), fixed(width, width), fixed(1, width), fixed(1, width)]
        + [ANYWHERE] * len(old),
        [out, out],
        [outer((2 * mine * height, width))] * 2,
        2 * mine * height * width * width,
        6 * mine * height * width,
        after,
        {5: 0, 6: 1} if old else None,
        1,
        part=FORWARD_PART,
    )(side, images, order, gain, shift, *old)


def mask_grad(side, images, order, half_at, before=None, after=()):
    _, height, width = images.shape
    mine = 2

    def kernel(side_ref, raw_ref, order_ref, *refs):
        final_ref, sum_ref = refs[-2:]
        keep = side_ref[2 + side_ref[0] * mine + pl.program_id(0)].astype(F32)
        final = dot_nn(raw_ref[0], order_ref[...]) * keep
        final_ref[...] = final.astype(BF16)

        @pl.when(first_step())
        def _():
            sum_ref[...] = jnp.zeros_like(sum_ref)

        sum_ref[...] += column_sum(final)

    offset = (lambda side_ref: side_ref[0] * mine) if half_at == 0 else (lambda side_ref: 0)
    old = () if before is None else (before,)
    out = pl.BlockSpec((height, width), lambda i, _: (half_at * mine + i, 0))
    return call(
        kernel,
        (mine,),
        [image_block(height, width, offset), fixed(width, width)] + [ANYWHERE] * len(old),
        [out, fixed(1, width)],
        [struct((2 * mine * height, width)), struct((1, width), F32)],
        2 * mine * height * width * width,
        6 * mine * height * width,
        after,
        {3: 0} if old else None,
        1,
        part=FORWARD_PART,
    )(side, images, order, *old)


def project(normed, parts, bias, after=()):
    count, width = normed.shape
    half = bias.shape[-1]

    def kernel(norm_ref, bias_ref, *refs):
        weight = jnp.concatenate([refs[0][...], refs[1][...], refs[2][0], refs[2][1]], axis=0)
        refs[3][0] = (dot_nn(norm_ref[...], weight) + bias_ref[0]).astype(BF16)

    return call(
        kernel,
        (3,),
        [fixed(count, width), pl.BlockSpec((1, 1, half), lambda j: (j, 0, 0))]
        + piece_tiles(half, 2, 1),
        pl.BlockSpec((1, count, half), lambda j: (j, 0, 0)),
        outer((3, count, half)),
        6 * count * width * half,
        2 * count * (width + 3 * half) + 6 * width * half,
        after,
        part=FORWARD_PART,
    )(normed, bias, *parts)


def attend(projected, first_image, last_image, before=None, lanes=256, after=()):
    _, _, images, half_len, half = projected.shape
    length = 2 * half_len
    per_step = lanes // HDIM

    def kernel(proj_ref, *refs):
        out_ref, probs_ref = refs[-2:]
        queries, key_rows, value_rows = (proj_ref[at].reshape(length, lanes) for at in range(3))
        outs = []
        for head in range(per_step):
            columns = slice(head * HDIM, (head + 1) * HDIM)
            scores = dot_nt(queries[:, columns], key_rows[:, columns])
            top = jnp.max(scores, axis=-1, keepdims=True)
            raw = jnp.exp2((scores - top) * (LOG2_E * HDIM**-0.5))
            probs = (raw * (1.0 / jnp.sum(raw, axis=-1, keepdims=True))).astype(BF16)
            probs_ref[0, head] = probs
            outs.append(dot_nn(probs, value_rows[:, columns]).astype(BF16))
        out_ref[...] = jnp.concatenate(outs, axis=1).reshape(out_ref.shape)

    heads = half // HDIM
    old = () if before is None else before
    return call(
        kernel,
        (last_image - first_image, half // lanes),
        [pl.BlockSpec((3, 2, 1, half_len, lanes), lambda i, j: (0, 0, first_image + i, 0, j))]
        + [ANYWHERE] * len(old),
        [
            pl.BlockSpec((2, 1, half_len, lanes), lambda i, j: (0, first_image + i, 0, j)),
            pl.BlockSpec((1, per_step, length, length), lambda i, j: (first_image + i, j, 0, 0)),
        ],
        [struct((2, images, half_len, half)), outer((images, heads, length, length))],
        24 * (last_image - first_image) * heads * length * length * HDIM,
        (last_image - first_image) * heads * length * length * 2,
        after,
        {1: 0, 2: 1} if old else None,
        part=FORWARD_PART,
    )(in_hbm(projected), *old)


def attend_back(projected, grad_context, probs, lanes=256, after=()):
    _, _, images, half_len, half = projected.shape
    length = 2 * half_len
    per_step = lanes // HDIM
    scale = HDIM**-0.5

    def kernel(proj_ref, grad_ref, probs_ref, out_ref, sum_ref):
        queries, key_rows, value_rows = (proj_ref[at].reshape(length, lanes) for at in range(3))
        grads = grad_ref[...].reshape(length, lanes)
        found = ([], [], [])
        for head in range(per_step):
            columns = slice(head * HDIM, (head + 1) * HDIM)
            low = probs_ref[0, head]
            found[2].append(dot_tn(low, grads[:, columns]).astype(BF16))
            grad_soft = dot_nt(grads[:, columns], value_rows[:, columns])
            soft = low.astype(F32)
            scaled = soft * grad_soft
            grad_scores = (scaled - soft * jnp.sum(scaled, axis=-1, keepdims=True)).astype(BF16)
            found[0].append((dot_nn(grad_scores, key_rows[:, columns]) * scale).astype(BF16))
            found[1].append((dot_tn(grad_scores, queries[:, columns]) * scale).astype(BF16))
        for at in range(3):
            joined = jnp.concatenate(found[at], axis=1)
            out_ref[at] = joined.reshape(2, 1, half_len, lanes)
            if at != 1:
                sum_ref[0, at // 2 : at // 2 + 1] = column_sum(joined.astype(F32))

    heads = half // HDIM
    block = pl.BlockSpec((3, 2, 1, half_len, lanes), lambda i, j: (0, 0, i, 0, j))
    return call(
        kernel,
        (images, half // lanes),
        [
            block,
            pl.BlockSpec((2, 1, half_len, lanes), lambda i, j: (0, i, 0, j)),
            pl.BlockSpec((1, per_step, length, length), lambda i, j: (i, j, 0, 0)),
        ],
        [block, pl.BlockSpec((1, 2, lanes), lambda i, j: (i, 0, j))],
        [struct(projected.shape), struct((images, 2, half), F32)],
        32 * images * heads * length * length * HDIM,
        images * heads * length * length * 2,
        after,
    )(in_hbm(projected), grad_context, in_hbm(probs))


def add_branch(places, contexts, rows, gathered, bias, gain, shift, tile=288, after=()):
    count, width = rows.shape
    half = width // 2

    def kernel(place_ref, low_ref, high_ref, rows_ref, bias_ref, gain_ref, shift_ref, *refs):
        middle_ref, norm_ref = refs[32:]
        branch = dot_nt(low_ref[...], joined(refs, 0, 16, 2, 0)) + dot_nt(high_ref[...], joined(refs, 0, 16, 2, 1))
        middle = rows_ref[...].astype(F32) + (branch + bias_ref[...])
        middle_ref[...] = middle
        unit, _ = normal_parts(middle)
        norm_ref[...] = (unit * gain_ref[...] + shift_ref[...]).astype(BF16)

    block = pl.BlockSpec((tile, width), lambda i, _: (i, 0))
    half_block = pl.BlockSpec((tile, half), lambda i, _: (i, 0))
    return call(
        kernel,
        (count // tile,),
        [half_block, half_block, block] + [fixed(1, width)] * 3 + gathered_specs(half, at=4),
        [block, block],
        [outer((count, width), F32), struct((count, width))],
        2 * count * width * width,
        10 * count * width + 2 * width * width,
        after,
        None,
        1,
        part=FORWARD_PART,
    )(places, *contexts, rows, bias, gain, shift, *[gathered] * 32)


def feed_up(places, x_at, second, gathered, bias, tile=512, after=()):
    count, width = second.shape
    columns = bias.shape[-1]

    def kernel(place_ref, second_ref, bias_ref, *refs):
        hidden = dot_nn(second_ref[...], joined(refs, 0, 16)) + bias_ref[...]
        gate = 0.5 + 0.5 * jnp.tanh(0.851 * hidden)
        refs[16][...] = (hidden * gate).astype(BF16)
        refs[17][...] = (gate * (1.0 + 1.702 * hidden * (1.0 - gate))).astype(BF16)

    block = pl.BlockSpec((count, tile), lambda j, _: (0, j))
    return call(
        kernel,
        (columns // tile,),
        [fixed(count, width), pl.BlockSpec((1, tile), lambda j, _: (0, j))] + gathered_specs(tile, (x_at,)),
        [block, block],
        [outer((count, columns))] * 2,
        2 * count * width * columns,
        2 * count * (width + 2 * columns) + 2 * width * columns,
        after,
        None,
        1,
        part=FORWARD_PART,
    )(places, second, bias, *[gathered] * 16)


def feed_down(side, first_tile, last_tile, actives, middle, gathered, bias, order, before=None, tile=288, after=()):
    count, columns = actives[0].shape
    width = middle.shape[1]
    mine = count // tile // 2
    half_at = first_tile // mine
    old = () if before is None else (before,)

    def kernel(side_ref, low_ref, high_ref, middle_ref, bias_ref, order_ref, *refs):
        keep = side_ref[2 + side_ref[0] * mine + first_tile % mine + pl.program_id(0)].astype(F32)
        out_ref = refs[-1]
        feed = dot_nt(low_ref[...], joined(refs, 0, 16, 2, 0)) + dot_nt(high_ref[...], joined(refs, 0, 16, 2, 1))
        out = ((middle_ref[...] + (feed + bias_ref[...])) * keep).astype(BF16)
        out_ref[0] = dot_nt(out, order_ref[...]).astype(BF16)

    hidden = pl.BlockSpec((tile, columns), lambda i, _: (first_tile + i, 0))
    offset = (lambda ref: ref[0] * mine + first_tile) if half_at == 0 else (lambda ref: first_tile - mine)

    return call(
        kernel,
        (last_tile - first_tile,),
        [
            hidden,
            hidden,
            pl.BlockSpec((tile, width), lambda i, _: (first_tile + i, 0)),
            fixed(1, width),
            fixed(width, width),
        ]
        + gathered_specs(columns, at=0)
        + [ANYWHERE] * len(old),
        image_block(tile, width, offset),
        struct(((2 - half_at) * mine, tile, width)),
        2 * count * width * columns + count * width * width,
        2 * count * columns + 3 * count * width + 4 * width * columns,
        after,
        {38: 0} if old else None,
        1,
    )(side, *[in_hbm(values) for values in actives], in_hbm(middle), bias, order, *[gathered] * 32, *old)


def gate_back(side, final, slopes, gathered, tile=512, after=()):
    count, width = final.shape
    columns = gathered.shape[-1]

    def kernel(side_ref, final_ref, low_ref, high_ref, *refs):
        outs, sums = refs[32:34], refs[34:36]
        for x_at, slope_ref in enumerate((low_ref, high_ref)):
            weight = joined(refs, 0, 16, 2, x_at)
            grad = (dot_nn(final_ref[...], weight) * slope_ref[...].astype(F32)).astype(BF16)
            outs[x_at][...] = grad
            sums[x_at][...] = column_sum(grad.astype(F32))

    block = pl.BlockSpec((count, tile), lambda j, _: (0, j))
    sum_block = pl.BlockSpec((1, tile), lambda j, _: (0, j))
    return call(
        kernel,
        (columns // tile,),
        [fixed(count, width), block, block] + gathered_specs(tile),
        [block, block, sum_block, sum_block],
        [struct((count, columns))] * 2 + [struct((1, columns), F32)] * 2,
        4 * count * width * columns,
        4 * count * (width + 2 * columns) + 4 * width * columns,
        after,
        None,
        1,
    )(side, in_hbm(final), *in_hbm(slopes), *[gathered] * 32)


def sums_down(final, actives, tile=512, after=()):
    count, width = final.shape
    columns = actives[0].shape[1]

    def kernel(final_ref, low_ref, high_ref, *outs):
        for x_at, right_ref in enumerate((low_ref, high_ref)):
            for core in range(2):
                for y_at in range(2):
                    start = (2 * core + y_at) * PART
                    part = dot_tn(final_ref[:, start : start + PART], right_ref[...])
                    outs[2 * core + y_at][x_at] = part.astype(BF16)

    right = pl.BlockSpec((count, tile), lambda j: (0, j))
    return call(
        kernel,
        (columns // tile,),
        [fixed(count, width), right, right],
        [pl.BlockSpec((2, PART, tile), lambda j: (0, 0, j))] * 4,
        [outer((2, PART, columns))] * 4,
        4 * count * width * columns,
        4 * count * columns + 2 * count * width + 4 * width * columns,
        after,
    )(final, *[in_hbm(values) for values in actives])


def sums_up(second, grads, tile=512, after=()):
    count, width = second.shape
    columns = grads[0].shape[1]

    def kernel(second_ref, low_ref, high_ref, *outs):
        for x_at, right_ref in enumerate((low_ref, high_ref)):
            for core in range(2):
                for y_at in range(2):
                    start = (2 * core + y_at) * PART
                    part = dot_tn(second_ref[:, start : start + PART], right_ref[...])
                    outs[2 * core + x_at][y_at] = part.astype(BF16)

    right = pl.BlockSpec((count, tile), lambda j: (0, j))
    return call(
        kernel,
        (columns // tile,),
        [fixed(count, width), right, right],
        [pl.BlockSpec((2, PART, tile), lambda j: (0, 0, j))] * 4,
        [outer((2, PART, columns))] * 4,
        4 * count * width * columns,
        4 * count * columns + 2 * count * width + 4 * width * columns,
        after,
    )(second, *grads)


def sums_first(normed, branch, grad_projected, context, after=()):
    count, width = normed.shape
    half = context.shape[1]

    def kernel(norm_ref, branch_ref, grad_ref, context_ref, *outs):
        def work(left_ref, right):
            for core in range(2):
                for y_at in range(2):
                    start = (2 * core + y_at) * PART
                    outs[2 * core + y_at][...] = dot_tn(left_ref[:, start : start + PART], right).astype(BF16)

        @pl.when(pl.program_id(0) < 3)
        def _():
            work(norm_ref, grad_ref[0])

        @pl.when(pl.program_id(0) == 3)
        def _():
            work(branch_ref, context_ref[...])

    left = fixed(count, width)
    return call(
        kernel,
        (4,),
        [left, left, pl.BlockSpec((1, count, half), lambda j: (jnp.minimum(j, 2), 0, 0)), fixed(count, half)],
        [pl.BlockSpec((PART, half), lambda j: (0, j))] * 4,
        [outer((PART, 4 * half))] * 4,
        8 * count * width * half,
        2 * count * (2 * width + 4 * half) + 8 * width * half,
        after,
    )(normed, branch, grad_projected, context)


def second_back(places, grads, gathered, middle, final, gain, tile=288, after=()):
    count, columns = grads[0].shape
    width = middle.shape[1]
    half = width // 2

    def kernel(place_ref, low_ref, high_ref, middle_ref, final_ref, gain_ref, *refs):
        ups, outs = refs[:32], refs[32:64]
        grad_ref, branch_ref, context_low_ref, context_high_ref, sum_ref = refs[64:]
        grad_second = dot_nt(low_ref[...], joined(ups, 0, 16, 2, 0)) + dot_nt(high_ref[...], joined(ups, 0, 16, 2, 1))
        unit, inv_std = normal_parts(middle_ref[...])
        grad_middle = final_ref[...].astype(F32) + normalize_back(
            grad_second, unit, inv_std, gain_ref[...]
        )
        branch = grad_middle.astype(BF16)
        grad_ref[...] = grad_middle
        branch_ref[...] = branch
        for x_at, context_ref in enumerate((context_low_ref, context_high_ref)):
            context_ref[...] = dot_nn(branch, joined(outs, 0, 16, 2, x_at)).astype(BF16)

        @pl.when(first_step())
        def _():
            sum_ref[...] = jnp.zeros_like(sum_ref)

        sum_ref[0:1] += column_sum(grad_second * unit)
        sum_ref[1:2] += column_sum(grad_second)
        sum_ref[2:3] += column_sum(branch.astype(F32))

    block = pl.BlockSpec((tile, width), lambda i, _: (i, 0))
    half_block = pl.BlockSpec((tile, half), lambda i, _: (i, 0))
    hidden = pl.BlockSpec((tile, columns), lambda i, _: (i, 0))
    return call(
        kernel,
        (count // tile,),
        [hidden, hidden, block, block, fixed(1, width)]
        + gathered_specs(columns, at=0)
        + gathered_specs(half, at=4),
        [block, block, half_block, half_block, fixed(8, width)],
        [outer((count, width), F32), struct((count, width))]
        + [struct((count, half))] * 2
        + [struct((8, width), F32)],
        4 * count * width * columns + 2 * count * width * width,
        4 * count * columns + 14 * count * width + 4 * width * columns,
        after,
        None,
        1,
    )(places, *grads, middle, final, gain, *[gathered] * 64)


def first_back(side, half_at, grads, pieces, rows, grad_middle, gain, order, tile=288, after=()):
    _, count, half = grads[0].shape
    width = rows.shape[1]
    mine = count // tile // 2

    def kernel(side_ref, low_ref, high_ref, rows_ref, middle_ref, gain_ref, order_ref, *refs):
        parts, (out_ref, sum_ref) = far_list(refs[:4], refs[4:6]), refs[6:]
        lefts = [jnp.concatenate([ref[at] for at in range(3)], axis=1) for ref in (low_ref, high_ref)]
        found = []
        for at in range(4):
            found.append(
                dot_nt(lefts[0], parts[2 * at][...]) + dot_nt(lefts[1], parts[2 * at + 1][...])
            )
        grad_normed = jnp.concatenate(found, axis=1)
        unit, inv_std = normal_parts(rows_ref[...].astype(F32))
        out = middle_ref[...] + normalize_back(grad_normed, unit, inv_std, gain_ref[...])
        out_ref[0] = dot_nt(out.astype(BF16), order_ref[...]).astype(BF16)

        @pl.when(first_step())
        def _():
            sum_ref[...] = jnp.zeros_like(sum_ref)

        sum_ref[0:1] += column_sum(grad_normed * unit)
        sum_ref[1:2] += column_sum(grad_normed)

    start = half_at * mine
    block = pl.BlockSpec((tile, width), lambda i, _: (start + i, 0))
    grad_block = pl.BlockSpec((3, tile, half), lambda i, _: (0, start + i, 0))
    offset = (lambda ref: ref[0] * mine) if half_at == 0 else (lambda ref: 0)
    return call(
        kernel,
        (mine,),
        [grad_block, grad_block, block, block, fixed(1, width), fixed(width, width)]
        + piece_specs(3 * half),
        [image_block(tile, width, offset), fixed(8, width)],
        [struct(((2 - half_at) * mine, tile, width)), struct((8, width), F32)],
        4 * count * width * width,
        8 * count * width + 6 * width * width,
        after,
        None,
        1,
        part=0.3,
    )(side, *in_hbm(grads), in_hbm(rows), in_hbm(grad_middle), gain, order, *in_hbm(pieces))


def fast_shards(
    tokens,
    image_mask,
    out_grad,
    norm1_gain,
    norm1_shift,
    qkv_weight,
    qv_bias,
    out_weight,
    out_bias,
    norm2_gain,
    norm2_shift,
    up_weight,
    up_bias,
    down_weight,
    down_bias,
):
    images, half_len, width = tokens.shape
    mine = images // 2
    half = qkv_weight.shape[2]
    half_hidden = up_weight.shape[1]
    count = 2 * mine * half_len
    me = lax.axis_index("dp")
    side = lax.axis_index("tensor")
    side_array = jnp.concatenate([jnp.stack([side, me]).astype(jnp.int32), image_mask])
    vectors = (norm1_gain, norm1_shift, norm2_gain, norm2_shift, out_bias, down_bias)
    order, gain_one, shift_one, gain_two, shift_two, bias_out, bias_down = setup(
        side_array, [vector.reshape(1, width) for vector in vectors]
    )

    def for_partner(values):
        return over_x(lax.dynamic_slice_in_dim(values, (1 - side) * mine, mine, 0))

    def z_all(values):
        return jnp.concatenate([values] + [over_z(values, step) for step in (1, 2, 3)], axis=0)

    second_group = jnp.concatenate([up_weight, out_weight], axis=1)
    up_all = lax.all_gather(second_group, ("dp", "tensor")).reshape(-1, 2, ROWS, half_hidden + half)
    own = prepare(side_array, tokens, order, gain_one, shift_one, 0)
    final, sum_own = mask_grad(side_array, out_grad, order, 0, after=own[:1])
    tokens_partner = for_partner(tokens)
    first = qkv_weight.reshape(ROWS, 3 * half)
    first_base = late(z_all(first), final)
    biases = jnp.concatenate([qv_bias.reshape(-1), up_bias])
    bias_rows = jnp.pad(biases, (0, 16 * 3 * half - biases.size)).reshape(16, 3 * half)

    def split_bias(bias):
        bias = bias.astype(F32)
        parts = jnp.stack([bias[:half], jnp.zeros((half,), F32), bias[half : 2 * half]])
        return parts[:, None], bias[None, 2 * half :]

    rows, normed = prepare(
        side_array, tokens_partner, order, gain_one, shift_one, 1, own, after=[first_base]
    )
    first_x = over_x(jnp.concatenate([first_base, bias_rows], axis=0))
    first_y = over_y(first_base)
    first_xy = over_y(late(first_x, first_y))
    first_far = [over_core(jnp.stack(late([first_base, first_y], first_x, normed)))]
    biases = [split_bias(biases), split_bias(first_x[4 * ROWS :].reshape(-1)[: biases.size])]
    heads_shape = (3, 2, mine, half_len, half)
    projected, contexts, probs = [None, None], [None, None], [None, None]
    projected[0] = project(normed, [first_base, first_y] + first_far, biases[0][0]).reshape(heads_shape)
    begun = attend(projected[0], 0, 1, lanes=128)
    first_far += [over_core(jnp.stack(late([first_x, first_xy], begun[0])))]
    first_pieces = [first_base, first_x, first_y, first_xy] + first_far
    contexts[0], probs[0] = attend(projected[0], 1, 2, begun, lanes=128)
    grad_partner = for_partner(late(out_grad, first_x))
    projected[1] = project(
        normed, [first_x, first_xy] + first_far[1:], biases[1][0], after=[contexts[0]]
    ).reshape(heads_shape)
    down_all = lax.all_gather(late(down_weight, up_all, contexts[0]), ("dp", "tensor"))
    down_all = down_all.reshape(-1, 2, ROWS, half_hidden)
    contexts[1], probs[1] = attend(projected[1], 0, 2)
    contexts = [values.reshape(count, half) for values in contexts]
    middle, second = add_branch(side_array, contexts, rows, up_all, bias_out, gain_two, shift_two)
    actives, slopes = [None, None], [None, None]
    actives[0], slopes[0] = feed_up(side_array, 0, second, up_all, biases[0][1])
    final, sum_partner = mask_grad(side_array, grad_partner, order, 1, final, after=[actives[0]])
    actives[1], slopes[1] = feed_up(side_array, 1, second, up_all, biases[1][1], after=[final])

    down_near, down_next, down_far, down_last = sums_down(final, actives)
    grads_sums = gate_back(side_array, final, slopes, down_all, after=[down_near])
    grads, sum_hidden = grads_sums[:2], grads_sums[2:]
    (down_sent,) = combine([down_next, over_core(down_last)], 1, after=grads[:1])
    down_sent_y = over_y(down_sent)
    up_near, up_next, up_far_sums, up_last = sums_up(second, grads, after=[down_sent])
    grad_middle, branch, *grad_contexts, sums_two = second_back(
        side_array, grads, up_all, middle, final, gain_two, after=[up_near]
    )
    (up_sent,) = combine([up_next, over_core(up_last)], 1, after=[branch])
    up_sent_x = over_x(up_sent)
    down_far = over_core(late(down_far, up_sent))

    def heads_back(x_at, after):
        grad_context = grad_contexts[x_at].reshape(2, mine, half_len, half)
        grad, sums = attend_back(projected[x_at], grad_context, probs[x_at], after=after)
        return grad.reshape(3, count, half), jnp.sum(sums, axis=0)

    grads_qkv, sums_qkv = [None, None], [None, None]
    grads_qkv[1], sums_qkv[1] = heads_back(1, [up_sent])
    down_sums = combine([down_near, down_far, down_sent_y], 2, after=[grads_qkv[1]])
    down_sent_x = over_x(down_sums[1])
    high_near, high_next, high_far, high_last = sums_first(
        normed, branch, grads_qkv[1], contexts[1], after=down_sums[:1]
    )
    up_far_sums = over_core(late(up_far_sums, high_near))
    out_send = feed_down(side_array, 2, 4, actives, middle, down_all, bias_down, order, after=[high_near])
    (high_sent,) = combine([high_next, over_core(high_last)], 1, after=[out_send])
    high_sent_y = over_y(high_sent)
    up_sums = combine([up_near, up_far_sums, up_sent_x], 2, after=[high_sent])
    up_sent_y = over_y(up_sums[1])
    high_far = over_core(late(high_far, up_sums[0]))
    out_partner = over_x(late(out_send, up_sums[0]))
    grads_qkv[0], sums_qkv[0] = heads_back(0, up_sums[:1])
    down_sums = combine([down_sums[0], down_sent_x], 2, after=[high_far, grads_qkv[0]])
    down_sent_z = over_z(down_sums[1], 2)
    low_near, low_next, low_far, low_last = sums_first(
        normed, branch, grads_qkv[0], contexts[0], after=down_sums[:1]
    )
    (high,) = combine([high_near, high_far, high_sent_y], 1, after=[low_near])
    high_x = over_x(high)
    (low_sent,) = combine([low_next, over_core(low_last)], 1, after=[high])
    low_sent_y = over_y(low_sent)
    send, sums_partner = first_back(
        side_array, 1, grads_qkv, first_pieces, rows, grad_middle, gain_one, order, after=[low_sent]
    )
    up_sums = combine([up_sums[0], up_sent_y], 2, after=[send])
    up_sent_z = over_z(up_sums[1], 2)
    down_sums = combine([down_sums[0], down_sent_z], 2, after=[up_sums[0], out_partner])
    down_sent_z = over_z(down_sums[1], 1)
    low_far = over_core(late(low_far, up_sums[0]))
    full, sums_own = first_back(
        side_array, 0, grads_qkv, first_pieces, rows, grad_middle, gain_one, order, after=down_sums[:1]
    )
    up_sums = combine([up_sums[0], up_sent_z], 2, after=[full])
    sums = jnp.concatenate(
        [(sums_own + sums_partner)[:2], sums_two[2:3], sums_two[:2], sum_own + sum_partner], axis=0
    )
    sums = jnp.einsum("td,od->to", sums, order.astype(F32), precision=lax.Precision.HIGHEST)
    halves = [
        jnp.concatenate([sums_qkv[x_at].reshape(-1), sum_hidden[x_at][0]]) for x_at in range(2)
    ]
    small = jnp.concatenate([halves[0], sums.reshape(-1), halves[1]])
    small = late(small + over_core(small), up_sums[0])
    small = small + over_y(small)
    halves_size = 2 * half + half_hidden
    small_x = over_x(jnp.concatenate([small[-halves_size:], small[halves_size:-halves_size]]))
    small = small[:-halves_size] + small_x
    height = 8
    small_rows = jnp.pad(small, (0, height * half_hidden - small.size)).reshape(height, half_hidden)
    small_top = small_rows.astype(BF16)
    small_rows = jnp.concatenate([small_top, (small_rows - small_top.astype(F32)).astype(BF16)], axis=0)

    low = combine([low_near, low_far, low_sent_y, high_x], 4, after=up_sums[:1])
    near_z = over_z(jnp.concatenate([low[1], up_sums[1], small_rows], axis=0), 1)
    middle_z = over_z(jnp.concatenate([low[2], small_rows], axis=0), 2)
    far_z = over_z(jnp.concatenate([low[3], small_rows], axis=0), 3)
    send_x = over_x(late(send, low[0]))
    out_full = feed_down(
        side_array, 0, 2, actives, middle, down_all, bias_down, order, after=[low[0], small_rows]
    )
    (grad_down,) = combine([down_sums[0], down_sent_z], 1, F32, after=[out_full])
    block_out = lax.dynamic_update_slice_in_dim(out_full, out_partner, (1 - side) * mine, 0)
    tokens_grad = lax.dynamic_update_slice_in_dim(full, send_x, (1 - side) * mine, 0)
    grad_qkv, grad_out, grad_up, sums = finish(
        low[0], up_sums[0], small_rows, near_z, middle_z, far_z, after=[out_full, tokens_grad]
    )
    sums = sums.reshape(-1)
    halves = sums[:halves_size]
    sums = sums[halves_size : halves_size + 6 * width].reshape(6, width)
    return (
        block_out,
        tokens_grad,
        sums[0],
        sums[1],
        grad_qkv.reshape(ROWS, 3, half),
        halves[: 2 * half].reshape(2, half),
        grad_out,
        sums[2],
        sums[3],
        sums[4],
        grad_up,
        halves[2 * half :],
        grad_down,
        sums[5],
    )


def solution(mesh):
    in_specs = (
        P("dp", "tensor", None),
        P("dp"),
        P("dp", "tensor", None),
        P(),
        P(),
        P("dp", None, "tensor"),
        P(None, "tensor"),
        P("dp", "tensor"),
        P(),
        P(),
        P(),
        P("dp", "tensor"),
        P("tensor"),
        P("dp", "tensor"),
        P(),
    )
    out_specs = (
        P("dp", "tensor", None),
        P("dp", "tensor", None),
        P(),
        P(),
        P("dp", None, "tensor"),
        P(None, "tensor"),
        P("dp", "tensor"),
        P(),
        P(),
        P(),
        P("dp", "tensor"),
        P("tensor"),
        P("dp", "tensor"),
        P(),
    )
    small_slice = mesh.shape["dp"] == 16 and mesh.shape["tensor"] == 2
    shards = fast_shards if small_slice else general_shards
    return jax.shard_map(shards, mesh=mesh, in_specs=in_specs, out_specs=out_specs, check_vma=False)
```

```python
import jax
import jax.numpy as jnp
from jax import lax
from jax.experimental import pallas as pl
from jax.experimental.pallas import tpu as pltpu
from jax.sharding import PartitionSpec as P

HDIM = 64
MICRO = 2


def mixed(form, left, right):
    return jnp.einsum(form, left, right, preferred_element_type=jnp.float32)


def normalize(values, gain, shift):
    mean_val = jnp.mean(values, axis=-1, keepdims=True)
    centered = values - mean_val
    inv_std = lax.rsqrt(jnp.mean(centered * centered, axis=-1, keepdims=True) + 1e-05)
    unit_val = centered * inv_std
    return (unit_val * gain + shift, unit_val, inv_std)


def normalize_back(grad_in, unit_val, inv_std, gain):
    scaled = grad_in * gain
    return inv_std * (
        scaled
        - jnp.mean(scaled, axis=-1, keepdims=True)
        - unit_val * jnp.mean(scaled * unit_val, axis=-1, keepdims=True)
    )


def token_sum(values):
    return jnp.sum(values, axis=(0, 1))


def general_shards(
    tokens,
    image_mask,
    out_grad,
    norm1_gain,
    norm1_shift,
    qkv_weight,
    qv_bias,
    out_weight,
    out_bias,
    norm2_gain,
    norm2_shift,
    up_weight,
    up_bias,
    down_weight,
    down_bias,
):
    images_here = tokens.shape[0] // MICRO
    full_width = norm1_gain.shape[0]
    local_width = qkv_weight.shape[2]
    local_hidden = up_weight.shape[1]
    local_heads = local_width // HDIM
    score_scale = HDIM ** (-0.5)
    gain_one = norm1_gain.astype(jnp.float32)
    shift_one = norm1_shift.astype(jnp.float32)
    gain_two = norm2_gain.astype(jnp.float32)
    shift_two = norm2_shift.astype(jnp.float32)
    bias_pair = qv_bias.astype(jnp.float32)
    grad_qkv = jnp.zeros((full_width, 3, local_width), jnp.float32)
    grad_out = jnp.zeros((full_width, local_width), jnp.float32)
    grad_up = jnp.zeros((full_width, local_hidden), jnp.float32)
    grad_down = jnp.zeros((full_width, local_hidden), jnp.float32)
    grad_gain_one = jnp.zeros((full_width,), jnp.float32)
    grad_shift_one = jnp.zeros((full_width,), jnp.float32)
    grad_gain_two = jnp.zeros((full_width,), jnp.float32)
    grad_shift_two = jnp.zeros((full_width,), jnp.float32)
    grad_out_bias = jnp.zeros((full_width,), jnp.float32)
    grad_down_bias = jnp.zeros((full_width,), jnp.float32)
    grad_pair = jnp.zeros((2, local_width), jnp.float32)
    grad_up_bias = jnp.zeros((local_hidden,), jnp.float32)
    outputs = []
    input_grads = []
    for micro_index in range(MICRO):
        first_image = micro_index * images_here
        block_rows = tokens[first_image : first_image + images_here].astype(jnp.float32)
        keep_mask = image_mask[first_image : first_image + images_here].astype(jnp.float32)[
            :, None, None
        ]
        fwd_weights = (
            lax.all_gather(qkv_weight, "dp", axis=0, tiled=True),
            lax.all_gather(out_weight, "dp", axis=0, tiled=True),
            lax.all_gather(up_weight, "dp", axis=0, tiled=True),
            lax.all_gather(down_weight, "dp", axis=0, tiled=True),
        )
        qkv_full, out_full, up_full, down_full = fwd_weights
        normed, unit_one, inv_one = normalize(block_rows, gain_one, shift_one)
        normed_full = lax.all_gather(normed.astype(jnp.bfloat16), "tensor", axis=1, tiled=True)
        seq_len = normed_full.shape[1]
        head_shape = (images_here, seq_len, local_heads, HDIM)
        projected = mixed("isd,dcf->iscf", normed_full, qkv_full)
        queries = (projected[:, :, 0] + bias_pair[0]).astype(jnp.bfloat16).reshape(head_shape)
        key_rows = projected[:, :, 1].astype(jnp.bfloat16).reshape(head_shape)
        value_rows = (projected[:, :, 2] + bias_pair[1]).astype(jnp.bfloat16).reshape(head_shape)
        scores = mixed("iqhe,ikhe->ihqk", queries, key_rows) * score_scale
        row_top = jnp.max(scores, axis=-1, keepdims=True)
        raw_weights = jnp.exp(scores - row_top)
        row_total = jnp.sum(raw_weights, axis=-1, keepdims=True)
        log_total = row_top + jnp.log(row_total)
        probs = (raw_weights / row_total).astype(jnp.bfloat16)
        context = mixed("ihqk,ikhe->iqhe", probs, value_rows).astype(jnp.bfloat16)
        context = context.reshape(images_here, seq_len, local_width)
        attn_terms = mixed("isf,of->iso", context, out_full)
        branch = lax.psum_scatter(
            attn_terms, "tensor", scatter_dimension=1, tiled=True
        ) + out_bias.astype(jnp.float32)
        middle = block_rows + branch
        second, unit_two, inv_two = normalize(middle, gain_two, shift_two)
        second_full = lax.all_gather(second.astype(jnp.bfloat16), "tensor", axis=1, tiled=True)
        hidden = mixed("isd,df->isf", second_full, up_full) + up_bias.astype(jnp.float32)
        gate_sig = jax.nn.sigmoid(1.702 * hidden)
        active = (hidden * gate_sig).astype(jnp.bfloat16)
        feed_terms = mixed("isf,of->iso", active, down_full)
        feed_out = lax.psum_scatter(
            feed_terms.astype(jnp.bfloat16), "tensor", scatter_dimension=1, tiled=True
        ).astype(jnp.float32) + down_bias.astype(jnp.float32)
        outputs.append(((middle + feed_out) * keep_mask).astype(jnp.bfloat16))
        back_weights = (
            lax.all_gather(qkv_weight, "dp", axis=0, tiled=True),
            lax.all_gather(out_weight, "dp", axis=0, tiled=True),
            lax.all_gather(up_weight, "dp", axis=0, tiled=True),
            lax.all_gather(down_weight, "dp", axis=0, tiled=True),
        )
        qkv_back, out_back, up_back, down_back = back_weights
        grad_final = (
            out_grad[first_image : first_image + images_here].astype(jnp.float32) * keep_mask
        )
        grad_down_bias = grad_down_bias + token_sum(grad_final)
        final_full = lax.all_gather(grad_final.astype(jnp.bfloat16), "tensor", axis=1, tiled=True)
        grad_down = grad_down + mixed("iso,isf->of", final_full, active)
        grad_active = mixed("iso,of->isf", final_full, down_back)
        grad_hidden = (
            grad_active * (gate_sig + 1.702 * hidden * gate_sig * (1.0 - gate_sig))
        ).astype(jnp.bfloat16)
        grad_up_bias = grad_up_bias + token_sum(grad_hidden.astype(jnp.float32))
        grad_up = grad_up + mixed("isd,isf->df", second_full, grad_hidden)
        second_terms = mixed("isf,df->isd", grad_hidden, up_back)
        grad_second = lax.psum_scatter(second_terms, "tensor", scatter_dimension=1, tiled=True)
        grad_gain_two = grad_gain_two + token_sum(grad_second * unit_two)
        grad_shift_two = grad_shift_two + token_sum(grad_second)
        grad_middle = grad_final + normalize_back(grad_second, unit_two, inv_two, gain_two)
        grad_branch = grad_middle.astype(jnp.bfloat16)
        grad_out_bias = grad_out_bias + token_sum(grad_branch.astype(jnp.float32))
        branch_full = lax.all_gather(grad_branch, "tensor", axis=1, tiled=True)
        grad_out = grad_out + mixed("iso,isf->of", branch_full, context)
        grad_context = (
            mixed("iso,of->isf", branch_full, out_back).astype(jnp.bfloat16).reshape(head_shape)
        )
        again = mixed("iqhe,ikhe->ihqk", queries, key_rows) * score_scale
        soft_again = jnp.exp(again - log_total)
        probs_again = soft_again.astype(jnp.bfloat16)
        grad_values = mixed("ihqk,iqhe->ikhe", probs_again, grad_context)
        grad_soft = mixed("iqhe,ikhe->ihqk", grad_context, value_rows)
        grad_scores = (
            soft_again * (grad_soft - jnp.sum(grad_soft * soft_again, axis=-1, keepdims=True))
        ).astype(jnp.bfloat16)
        grad_queries = mixed("ihqk,ikhe->iqhe", grad_scores, key_rows) * score_scale
        grad_keys = mixed("ihqk,iqhe->ikhe", grad_scores, queries) * score_scale
        flat_shape = (images_here, seq_len, local_width)
        grad_projected = jnp.stack(
            (
                grad_queries.reshape(flat_shape),
                grad_keys.reshape(flat_shape),
                grad_values.reshape(flat_shape),
            ),
            axis=2,
        ).astype(jnp.bfloat16)
        pair_terms = grad_projected.astype(jnp.float32)
        grad_pair = grad_pair + jnp.stack(
            (token_sum(pair_terms[:, :, 0]), token_sum(pair_terms[:, :, 2])), axis=0
        )
        grad_qkv = grad_qkv + mixed("isd,iscf->dcf", normed_full, grad_projected)
        normed_terms = mixed("iscf,dcf->isd", grad_projected, qkv_back)
        grad_normed = lax.psum_scatter(
            normed_terms.astype(jnp.bfloat16), "tensor", scatter_dimension=1, tiled=True
        ).astype(jnp.float32)
        grad_gain_one = grad_gain_one + token_sum(grad_normed * unit_one)
        grad_shift_one = grad_shift_one + token_sum(grad_normed)
        grad_tokens = grad_middle + normalize_back(grad_normed, unit_one, inv_one, gain_one)
        input_grads.append(grad_tokens.astype(jnp.bfloat16))
    grad_qkv, grad_out, grad_up, grad_down = (
        lax.psum_scatter(
            grad_qkv.astype(jnp.bfloat16), "dp", scatter_dimension=0, tiled=True
        ).astype(jnp.float32),
        lax.psum_scatter(
            grad_out.astype(jnp.bfloat16), "dp", scatter_dimension=0, tiled=True
        ).astype(jnp.float32),
        lax.psum_scatter(
            grad_up.astype(jnp.bfloat16), "dp", scatter_dimension=0, tiled=True
        ).astype(jnp.float32),
        lax.psum_scatter(
            grad_down.astype(jnp.bfloat16), "dp", scatter_dimension=0, tiled=True
        ).astype(jnp.float32),
    )
    grad_gain_one, grad_shift_one, grad_gain_two, grad_shift_two, grad_out_bias, grad_down_bias = (
        lax.psum(
            (
                grad_gain_one,
                grad_shift_one,
                grad_gain_two,
                grad_shift_two,
                grad_out_bias,
                grad_down_bias,
            ),
            ("dp", "tensor"),
        )
    )
    grad_pair, grad_up_bias = lax.psum((grad_pair, grad_up_bias), "dp")
    block_out = jnp.concatenate(outputs, axis=0)
    tokens_grad = jnp.concatenate(input_grads, axis=0)
    return (
        block_out,
        tokens_grad,
        grad_gain_one,
        grad_shift_one,
        grad_qkv,
        grad_pair,
        grad_out,
        grad_out_bias,
        grad_gain_two,
        grad_shift_two,
        grad_up,
        grad_up_bias,
        grad_down,
        grad_down_bias,
    )


ROWS = 64
PART = 256
VMEM_BYTES = 24 * 1024 * 1024
COST_PART = 0.6
FORWARD_PART = 0.8
LOG2_E = 1.4426950408889634
BF16 = jnp.bfloat16
F32 = jnp.float32


def swap(values, axis_name, flip):
    count = lax.axis_size(axis_name)
    return lax.ppermute(values, axis_name, [(place, place ^ flip) for place in range(count)])


def over_core(values):
    return swap(values, "dp", 1)


def over_y(values):
    return swap(values, "dp", 2)


def over_z(values, step):
    return swap(values, "dp", 4 * step)


def over_x(values):
    return swap(values, "tensor", 1)


def late(values, *marks):
    return lax.optimization_barrier((values, *marks))[0]


def dot_nn(left, right):
    return lax.dot_general(left, right, (((1,), (0,)), ((), ())), preferred_element_type=F32)


def dot_nt(left, right):
    return lax.dot_general(left, right, (((1,), (1,)), ((), ())), preferred_element_type=F32)


def dot_tn(left, right):
    return lax.dot_general(left, right, (((0,), (0,)), ((), ())), preferred_element_type=F32)


def call(
    kernel, grid, in_specs, out_specs, out_shape, flops, moved, after=(), aliases=None, scalars=0, part=None
):
    given, waits = scalars + len(in_specs), len(after)
    part = COST_PART if part is None else part

    def run(*refs):
        kernel(*refs[:given], *refs[given + waits :])

    function = pl.pallas_call(
        run,
        grid_spec=pltpu.PrefetchScalarGridSpec(
            num_scalar_prefetch=scalars,
            grid=grid,
            in_specs=list(in_specs) + [pl.BlockSpec(memory_space=pl.ANY)] * waits,
            out_specs=out_specs,
        ),
        out_shape=out_shape,
        input_output_aliases=aliases or {},
        compiler_params=pltpu.CompilerParams(vmem_limit_bytes=VMEM_BYTES),
        cost_estimate=pl.CostEstimate(
            flops=int(flops * part), bytes_accessed=int(moved * part), transcendentals=0
        ),
    )
    return lambda *arrays: function(*arrays, *after)


def fixed(*shape, at=None):
    place = at or (0,) * len(shape)
    return pl.BlockSpec(shape, lambda *_: place, pipeline_mode=pl.Buffered(1))


def far_list(near, far):
    return list(near) + [far[last].at[y_at] for y_at in range(2) for last in range(2)]


def piece_specs(columns, at=0):
    return [fixed(PART, columns, at=(0, at))] * 4 + [fixed(2, PART, columns, at=(0, 0, at))] * 2


def piece_tiles(tile, near=4, far=2):
    return [pl.BlockSpec((PART, tile), lambda j: (0, j))] * near + [
        pl.BlockSpec((2, PART, tile), lambda j: (0, 0, j))
    ] * far


def gathered_specs(columns, halves=(0, 1), at=None):
    def spec(block, x_at):
        core, y_at, z_at = block // 8, (block // 4) % 2, block % 4
        slab = z_at * 4 + y_at * 2 + core

        def place(j, *refs):
            where = refs[-1]
            row = jnp.bitwise_xor(where[1], slab), jnp.bitwise_xor(where[0], x_at)
            return (*row, 0, j if at is None else at)

        mode = {} if at is None else {"pipeline_mode": pl.Buffered(1)}
        return pl.BlockSpec((1, 1, ROWS, columns), place, **mode)

    return [spec(block, x_at) for block in range(16) for x_at in halves]


def joined(refs, first, last, step=1, offset=0):
    return jnp.concatenate([refs[step * block + offset][0, 0] for block in range(first, last)], axis=0)


def struct(shape, dtype=BF16):
    return jax.ShapeDtypeStruct(shape, dtype)


def outer(shape, dtype=BF16):
    return pltpu.HBM(shape, dtype)


def in_hbm(values):
    if isinstance(values, (list, tuple)):
        return [in_hbm(part) for part in values]
    return pltpu.with_memory_space_constraint(values, pltpu.HBM)


ANYWHERE = pl.BlockSpec(memory_space=pl.ANY)


def normal_parts(values):
    mean_val = jnp.mean(values, axis=-1, keepdims=True)
    centered = values - mean_val
    inv_std = lax.rsqrt(jnp.mean(centered * centered, axis=-1, keepdims=True) + 1e-05)
    return centered * inv_std, inv_std


def column_sum(values):
    return jnp.sum(values, axis=0, keepdims=True)


def combine(arrays, pieces, dtype=BF16, tile=1024, after=()):
    columns = arrays[0].shape[-1]
    rows = arrays[0].size // columns // pieces
    arrays = [values.reshape(pieces, rows, columns) for values in arrays]
    given = len(arrays)

    def kernel(*refs):
        for at in range(pieces):
            parts = [ref[at].astype(F32) for ref in refs[:given]]
            while len(parts) > 1:
                parts = [sum(parts[start : start + 2]) for start in range(0, len(parts), 2)]
            refs[given + at][...] = parts[0].astype(dtype)

    return call(
        kernel,
        (columns // tile,),
        [pl.BlockSpec((pieces, rows, tile), lambda j: (0, 0, j))] * given,
        [pl.BlockSpec((rows, tile), lambda j: (0, j))] * pieces,
        [outer((rows, columns), dtype)] * pieces,
        0,
        2 * pieces * rows * columns * (given + 1),
        after,
    )(*arrays)


def finish(low_near, up_near, small, near, middle, far, after=()):
    rows, columns = low_near.shape
    split = columns * 3 // 4
    height = small.shape[0] // 2

    def kernel(low_ref, up_ref, small_ref, near_ref, middle_ref, far_ref, qkv_ref, out_ref, up_out_ref, sum_ref):
        def rows_of(ref, start):
            return ref[start : start + rows, :].astype(F32)

        def vectors_of(ref, start):
            values = ref[start : start + 2 * height, :].astype(F32)
            return values[:height] + values[height:]

        low = (rows_of(low_ref, 0) + rows_of(near_ref, 0)) + (rows_of(middle_ref, 0) + rows_of(far_ref, 0))
        qkv_ref[...] = low[:, :split]
        out_ref[...] = low[:, split:]
        up_out_ref[...] = rows_of(up_ref, 0) + rows_of(near_ref, rows)
        sum_ref[...] = (vectors_of(small_ref, 0) + vectors_of(near_ref, 2 * rows)) + (
            vectors_of(middle_ref, rows) + vectors_of(far_ref, rows)
        )

    given = [low_near, up_near, small, near, middle, far]
    return call(
        kernel,
        (1,),
        [fixed(*values.shape) for values in given],
        [fixed(rows, split), fixed(rows, columns - split), fixed(rows, columns), fixed(height, columns)],
        [
            struct((rows, split), F32),
            struct((rows, columns - split), F32),
            struct((rows, columns), F32),
            struct((height, columns), F32),
        ],
        0,
        20 * rows * columns,
        after,
    )(*given)


def first_step():
    return pl.program_id(0) == 0


def setup(places, vectors, after=()):
    width = vectors[0].shape[1]
    given = len(vectors)

    def kernel(place_ref, *refs):
        order_ref = refs[given]
        source = lax.broadcasted_iota(jnp.int32, (width, width), 0)
        target = lax.broadcasted_iota(jnp.int32, (width, width), 1)
        at = target // ROWS
        z_rel, y_rel, core_rel = at % 4, (at // 4) % 2, at // 8
        place = (z_rel * 4 + y_rel * 2 + core_rel) ^ place_ref[1]
        hit = source == place * ROWS + target % ROWS
        order = jnp.where(hit, 1.0, 0.0).astype(BF16)
        order_ref[...] = order
        rows = jnp.concatenate([ref[...].astype(F32) for ref in refs[:given]] + [jnp.zeros((8 - given, width), F32)], axis=0)
        moved = dot_nn(rows.astype(BF16), order)
        for vector_at in range(given):
            refs[given + 1 + vector_at][...] = moved[vector_at : vector_at + 1]

    row = fixed(1, width)
    return call(
        kernel,
        (1,),
        [row] * given,
        [fixed(width, width)] + [row] * given,
        [struct((width, width))] + [struct((1, width), F32)] * given,
        16 * width * width,
        2 * width * width,
        after,
        None,
        1,
        part=FORWARD_PART,
    )(places, *vectors)


def image_block(height, width, offset):
    return pl.BlockSpec((1, height, width), lambda i, side: (offset(side) + i, 0, 0))


def prepare(side, images, order, gain, shift, half_at, before=None, after=()):
    _, height, width = images.shape
    mine = 2

    def kernel(side_ref, raw_ref, order_ref, gain_ref, shift_ref, *refs):
        rows_ref, norm_ref = refs[-2:]
        rows = dot_nn(raw_ref[0], order_ref[...])
        rows_ref[...] = rows.astype(BF16)
        unit, _ = normal_parts(rows)
        norm_ref[...] = (unit * gain_ref[...] + shift_ref[...]).astype(BF16)

    offset = (lambda side_ref: side_ref[0] * mine) if half_at == 0 else (lambda side_ref: 0)
    out = pl.BlockSpec((height, width), lambda i, _: (half_at * mine + i, 0))
    old = () if before is None else before
    return call(
        kernel,
        (mine,),
        [image_block(height, width, offset), fixed(width, width), fixed(1, width), fixed(1, width)]
        + [ANYWHERE] * len(old),
        [out, out],
        [outer((2 * mine * height, width))] * 2,
        2 * mine * height * width * width,
        6 * mine * height * width,
        after,
        {5: 0, 6: 1} if old else None,
        1,
        part=FORWARD_PART,
    )(side, images, order, gain, shift, *old)


def mask_grad(side, images, order, half_at, before=None, after=()):
    _, height, width = images.shape
    mine = 2

    def kernel(side_ref, raw_ref, order_ref, *refs):
        final_ref, sum_ref = refs[-2:]
        keep = side_ref[2 + side_ref[0] * mine + pl.program_id(0)].astype(F32)
        final = dot_nn(raw_ref[0], order_ref[...]) * keep
        final_ref[...] = final.astype(BF16)

        @pl.when(first_step())
        def _():
            sum_ref[...] = jnp.zeros_like(sum_ref)

        sum_ref[...] += column_sum(final)

    offset = (lambda side_ref: side_ref[0] * mine) if half_at == 0 else (lambda side_ref: 0)
    old = () if before is None else (before,)
    out = pl.BlockSpec((height, width), lambda i, _: (half_at * mine + i, 0))
    return call(
        kernel,
        (mine,),
        [image_block(height, width, offset), fixed(width, width)] + [ANYWHERE] * len(old),
        [out, fixed(1, width)],
        [struct((2 * mine * height, width)), struct((1, width), F32)],
        2 * mine * height * width * width,
        6 * mine * height * width,
        after,
        {3: 0} if old else None,
        1,
        part=FORWARD_PART,
    )(side, images, order, *old)


def project(normed, parts, bias, after=()):
    count, width = normed.shape
    half = bias.shape[-1]

    def kernel(norm_ref, bias_ref, *refs):
        weight = jnp.concatenate([refs[0][...], refs[1][...], refs[2][0], refs[2][1]], axis=0)
        refs[3][0] = (dot_nn(norm_ref[...], weight) + bias_ref[0]).astype(BF16)

    return call(
        kernel,
        (3,),
        [fixed(count, width), pl.BlockSpec((1, 1, half), lambda j: (j, 0, 0))]
        + piece_tiles(half, 2, 1),
        pl.BlockSpec((1, count, half), lambda j: (j, 0, 0)),
        outer((3, count, half)),
        6 * count * width * half,
        2 * count * (width + 3 * half) + 6 * width * half,
        after,
        part=FORWARD_PART,
    )(normed, bias, *parts)


def attend(projected, first_image, last_image, before=None, lanes=256, after=()):
    _, _, images, half_len, half = projected.shape
    length = 2 * half_len
    per_step = lanes // HDIM
    steps = half // lanes

    def kernel(proj_ref, *refs):
        out_ref, weights_ref, inverse_ref = refs[-3:]
        queries, key_rows, value_rows = (proj_ref[at].reshape(length, lanes) for at in range(3))
        queries, value_rows = queries.T, value_rows.T
        outs, inverses = [], []
        for head in range(per_step):
            part = slice(head * HDIM, (head + 1) * HDIM)
            scores = dot_nn(key_rows[:, part], queries[part])
            top = jnp.max(scores, axis=0, keepdims=True)
            weights = jnp.exp2((scores - top) * (LOG2_E * HDIM**-0.5)).astype(BF16)
            weights_ref[0, head] = weights
            ones = jnp.ones((16, length), BF16)
            sums = dot_nn(jnp.concatenate([value_rows[part], ones], axis=0), weights)
            inverse = 1.0 / sums[HDIM : HDIM + 1]
            outs.append((sums[:HDIM] * inverse).astype(BF16))
            inverses.append(inverse)
        out_ref[...] = jnp.concatenate(outs, axis=0).T.reshape(out_ref.shape)
        inverse_ref[0] = jnp.concatenate(inverses + [jnp.zeros((8 - per_step, length), F32)], axis=0)

    heads = half // HDIM
    old = () if before is None else before
    return call(
        kernel,
        (last_image - first_image, steps),
        [pl.BlockSpec((3, 2, 1, half_len, lanes), lambda i, j: (0, 0, first_image + i, 0, j))]
        + [ANYWHERE] * len(old),
        [
            pl.BlockSpec((2, 1, half_len, lanes), lambda i, j: (0, first_image + i, 0, j)),
            pl.BlockSpec((1, per_step, length, length), lambda i, j: (first_image + i, j, 0, 0)),
            pl.BlockSpec((1, 8, length), lambda i, j: (first_image + i, j, 0)),
        ],
        [
            struct((2, images, half_len, half)),
            outer((images, heads, length, length)),
            struct((images, 8 * steps, length), F32),
        ],
        24 * (last_image - first_image) * heads * length * length * HDIM,
        (last_image - first_image) * heads * length * length * 2,
        after,
        {1: 0, 2: 1, 3: 2} if old else None,
        part=FORWARD_PART,
    )(in_hbm(projected), *old)


def attend_back(projected, grad_context, context, weights, inverse, after=()):
    _, _, images, half_len, half = projected.shape
    length = 2 * half_len
    steps = inverse.shape[1] // 8
    lanes = half // steps
    per_step = lanes // HDIM
    scale = HDIM**-0.5

    def kernel(proj_ref, grad_ref, context_ref, weights_ref, inverse_ref, out_ref, sum_ref):
        queries, key_rows, value_rows = (proj_ref[at].reshape(length, lanes) for at in range(3))
        queries, key_rows = queries.T, key_rows.T
        grads = grad_ref[...].reshape(length, lanes).T.astype(F32)
        contexts = context_ref[...].reshape(length, lanes).T.astype(F32)
        found = ([], [], [])
        for head in range(per_step):
            part = slice(head * HDIM, (head + 1) * HDIM)
            weights = weights_ref[0, head]
            grad = grads[part] * inverse_ref[0, head : head + 1]
            level = jnp.sum(grad * contexts[part], axis=0, keepdims=True)
            grad = grad.astype(BF16)
            found[2].append(dot_nt(grad, weights).astype(BF16))
            grad_soft = dot_nn(value_rows[:, part], grad)
            grad_scores = (weights.astype(F32) * (grad_soft - level)).astype(BF16)
            found[0].append((dot_nn(key_rows[part], grad_scores) * scale).astype(BF16))
            found[1].append((dot_nt(queries[part], grad_scores) * scale).astype(BF16))
        for at in range(3):
            joined = jnp.concatenate(found[at], axis=0).T
            out_ref[at] = joined.reshape(2, 1, half_len, lanes)
            if at != 1:
                sum_ref[0, at // 2 : at // 2 + 1] = column_sum(joined.astype(F32))

    heads = half // HDIM
    block = pl.BlockSpec((3, 2, 1, half_len, lanes), lambda i, j: (0, 0, i, 0, j))
    rows = pl.BlockSpec((2, 1, half_len, lanes), lambda i, j: (0, i, 0, j))
    return call(
        kernel,
        (images, steps),
        [
            block,
            rows,
            rows,
            pl.BlockSpec((1, per_step, length, length), lambda i, j: (i, j, 0, 0)),
            pl.BlockSpec((1, 8, length), lambda i, j: (i, j, 0)),
        ],
        [block, pl.BlockSpec((1, 2, lanes), lambda i, j: (i, 0, j))],
        [struct(projected.shape), struct((images, 2, half), F32)],
        32 * images * heads * length * length * HDIM,
        images * heads * length * length * 2,
        after,
    )(in_hbm(projected), grad_context, context, in_hbm(weights), inverse)


def add_branch(places, contexts, rows, gathered, bias, gain, shift, tile=576, after=()):
    count, width = rows.shape
    half = width // 2

    def kernel(place_ref, low_ref, high_ref, rows_ref, bias_ref, gain_ref, shift_ref, *refs):
        middle_ref, norm_ref = refs[32:]
        branch = dot_nt(low_ref[...], joined(refs, 0, 16, 2, 0)) + dot_nt(high_ref[...], joined(refs, 0, 16, 2, 1))
        middle = rows_ref[...].astype(F32) + (branch + bias_ref[...])
        middle_ref[...] = middle
        unit, _ = normal_parts(middle)
        norm_ref[...] = (unit * gain_ref[...] + shift_ref[...]).astype(BF16)

    block = pl.BlockSpec((tile, width), lambda i, _: (i, 0))
    half_block = pl.BlockSpec((tile, half), lambda i, _: (i, 0))
    return call(
        kernel,
        (count // tile,),
        [half_block, half_block, block] + [fixed(1, width)] * 3 + gathered_specs(half, at=4),
        [block, block],
        [outer((count, width), F32), struct((count, width))],
        2 * count * width * width,
        10 * count * width + 2 * width * width,
        after,
        None,
        1,
        part=FORWARD_PART,
    )(places, *contexts, rows, bias, gain, shift, *[gathered] * 32)


def feed_up(places, x_at, second, gathered, bias, tile=512, after=()):
    count, width = second.shape
    columns = bias.shape[-1]

    def kernel(place_ref, second_ref, bias_ref, *refs):
        hidden = dot_nn(second_ref[...], joined(refs, 0, 16)) + bias_ref[...]
        gate = 0.5 + 0.5 * jnp.tanh(0.851 * hidden)
        refs[16][...] = (hidden * gate).astype(BF16)
        refs[17][...] = (gate * (1.0 + 1.702 * hidden * (1.0 - gate))).astype(BF16)

    block = pl.BlockSpec((count, tile), lambda j, _: (0, j))
    return call(
        kernel,
        (columns // tile,),
        [fixed(count, width), pl.BlockSpec((1, tile), lambda j, _: (0, j))] + gathered_specs(tile, (x_at,)),
        [block, block],
        [outer((count, columns))] * 2,
        2 * count * width * columns,
        2 * count * (width + 2 * columns) + 2 * width * columns,
        after,
        None,
        1,
        part=FORWARD_PART,
    )(places, second, bias, *[gathered] * 16)


def feed_down(side, first_tile, last_tile, actives, middle, gathered, bias, order, before=None, tile=288, after=()):
    count, columns = actives[0].shape
    width = middle.shape[1]
    mine = count // tile // 2
    half_at = first_tile // mine
    old = () if before is None else (before,)

    def kernel(side_ref, low_ref, high_ref, middle_ref, bias_ref, order_ref, *refs):
        keep = side_ref[2 + side_ref[0] * mine + first_tile % mine + pl.program_id(0)].astype(F32)
        out_ref = refs[-1]
        feed = dot_nt(low_ref[...], joined(refs, 0, 16, 2, 0)) + dot_nt(high_ref[...], joined(refs, 0, 16, 2, 1))
        out = ((middle_ref[...] + (feed + bias_ref[...])) * keep).astype(BF16)
        out_ref[0] = dot_nt(out, order_ref[...]).astype(BF16)

    hidden = pl.BlockSpec((tile, columns), lambda i, _: (first_tile + i, 0))
    offset = (lambda ref: ref[0] * mine + first_tile) if half_at == 0 else (lambda ref: first_tile - mine)

    return call(
        kernel,
        (last_tile - first_tile,),
        [
            hidden,
            hidden,
            pl.BlockSpec((tile, width), lambda i, _: (first_tile + i, 0)),
            fixed(1, width),
            fixed(width, width),
        ]
        + gathered_specs(columns, at=0)
        + [ANYWHERE] * len(old),
        image_block(tile, width, offset),
        struct(((2 - half_at) * mine, tile, width)),
        2 * count * width * columns + count * width * width,
        2 * count * columns + 3 * count * width + 4 * width * columns,
        after,
        {38: 0} if old else None,
        1,
    )(side, *[in_hbm(values) for values in actives], in_hbm(middle), bias, order, *[gathered] * 32, *old)


def gate_back(side, final, slopes, gathered, tile=512, after=()):
    count, width = final.shape
    columns = gathered.shape[-1]

    def kernel(side_ref, final_ref, low_ref, high_ref, *refs):
        outs, sums = refs[32:34], refs[34:36]
        for x_at, slope_ref in enumerate((low_ref, high_ref)):
            weight = joined(refs, 0, 16, 2, x_at)
            grad = (dot_nn(final_ref[...], weight) * slope_ref[...].astype(F32)).astype(BF16)
            outs[x_at][...] = grad
            sums[x_at][...] = column_sum(grad.astype(F32))

    block = pl.BlockSpec((count, tile), lambda j, _: (0, j))
    sum_block = pl.BlockSpec((1, tile), lambda j, _: (0, j))
    return call(
        kernel,
        (columns // tile,),
        [fixed(count, width), block, block] + gathered_specs(tile),
        [block, block, sum_block, sum_block],
        [struct((count, columns))] * 2 + [struct((1, columns), F32)] * 2,
        4 * count * width * columns,
        4 * count * (width + 2 * columns) + 4 * width * columns,
        after,
        None,
        1,
    )(side, in_hbm(final), *in_hbm(slopes), *[gathered] * 32)


def sums_down(final, actives, tile=512, after=()):
    count, width = final.shape
    columns = actives[0].shape[1]

    def kernel(final_ref, low_ref, high_ref, *outs):
        for x_at, right_ref in enumerate((low_ref, high_ref)):
            for core in range(2):
                for y_at in range(2):
                    start = (2 * core + y_at) * PART
                    part = dot_tn(final_ref[:, start : start + PART], right_ref[...])
                    outs[2 * core + y_at][x_at] = part.astype(BF16)

    right = pl.BlockSpec((count, tile), lambda j: (0, j))
    return call(
        kernel,
        (columns // tile,),
        [fixed(count, width), right, right],
        [pl.BlockSpec((2, PART, tile), lambda j: (0, 0, j))] * 4,
        [outer((2, PART, columns))] * 4,
        4 * count * width * columns,
        4 * count * columns + 2 * count * width + 4 * width * columns,
        after,
    )(final, *[in_hbm(values) for values in actives])


def sums_up(second, grads, tile=512, after=()):
    count, width = second.shape
    columns = grads[0].shape[1]

    def kernel(second_ref, low_ref, high_ref, *outs):
        for x_at, right_ref in enumerate((low_ref, high_ref)):
            for core in range(2):
                for y_at in range(2):
                    start = (2 * core + y_at) * PART
                    part = dot_tn(second_ref[:, start : start + PART], right_ref[...])
                    outs[2 * core + x_at][y_at] = part.astype(BF16)

    right = pl.BlockSpec((count, tile), lambda j: (0, j))
    return call(
        kernel,
        (columns // tile,),
        [fixed(count, width), right, right],
        [pl.BlockSpec((2, PART, tile), lambda j: (0, 0, j))] * 4,
        [outer((2, PART, columns))] * 4,
        4 * count * width * columns,
        4 * count * columns + 2 * count * width + 4 * width * columns,
        after,
    )(second, *grads)


def sums_first(normed, branch, grad_projected, context, after=()):
    count, width = normed.shape
    half = context.shape[1]

    def kernel(norm_ref, branch_ref, grad_ref, context_ref, *outs):
        def work(left_ref, right):
            for core in range(2):
                for y_at in range(2):
                    start = (2 * core + y_at) * PART
                    outs[2 * core + y_at][...] = dot_tn(left_ref[:, start : start + PART], right).astype(BF16)

        @pl.when(pl.program_id(0) < 3)
        def _():
            work(norm_ref, grad_ref[0])

        @pl.when(pl.program_id(0) == 3)
        def _():
            work(branch_ref, context_ref[...])

    left = fixed(count, width)
    return call(
        kernel,
        (4,),
        [left, left, pl.BlockSpec((1, count, half), lambda j: (jnp.minimum(j, 2), 0, 0)), fixed(count, half)],
        [pl.BlockSpec((PART, half), lambda j: (0, j))] * 4,
        [outer((PART, 4 * half))] * 4,
        8 * count * width * half,
        2 * count * (2 * width + 4 * half) + 8 * width * half,
        after,
    )(normed, branch, grad_projected, context)


def second_back(places, grads, gathered, middle, final, gain, tile=576, after=()):
    count, columns = grads[0].shape
    width = middle.shape[1]
    half = width // 2

    def kernel(place_ref, low_ref, high_ref, middle_ref, final_ref, gain_ref, *refs):
        ups, outs = refs[:32], refs[32:64]
        grad_ref, branch_ref, context_low_ref, context_high_ref, sum_ref = refs[64:]
        grad_second = dot_nt(low_ref[...], joined(ups, 0, 16, 2, 0)) + dot_nt(high_ref[...], joined(ups, 0, 16, 2, 1))
        unit, inv_std = normal_parts(middle_ref[...])
        grad_middle = final_ref[...].astype(F32) + normalize_back(
            grad_second, unit, inv_std, gain_ref[...]
        )
        branch = grad_middle.astype(BF16)
        grad_ref[...] = grad_middle
        branch_ref[...] = branch
        for x_at, context_ref in enumerate((context_low_ref, context_high_ref)):
            context_ref[...] = dot_nn(branch, joined(outs, 0, 16, 2, x_at)).astype(BF16)

        @pl.when(first_step())
        def _():
            sum_ref[...] = jnp.zeros_like(sum_ref)

        sum_ref[0:1] += column_sum(grad_second * unit)
        sum_ref[1:2] += column_sum(grad_second)
        sum_ref[2:3] += column_sum(branch.astype(F32))

    block = pl.BlockSpec((tile, width), lambda i, _: (i, 0))
    half_block = pl.BlockSpec((tile, half), lambda i, _: (i, 0))
    hidden = pl.BlockSpec((tile, columns), lambda i, _: (i, 0))
    return call(
        kernel,
        (count // tile,),
        [hidden, hidden, block, block, fixed(1, width)]
        + gathered_specs(columns, at=0)
        + gathered_specs(half, at=4),
        [block, block, half_block, half_block, fixed(8, width)],
        [outer((count, width), F32), struct((count, width))]
        + [struct((count, half))] * 2
        + [struct((8, width), F32)],
        4 * count * width * columns + 2 * count * width * width,
        4 * count * columns + 14 * count * width + 4 * width * columns,
        after,
        None,
        1,
    )(places, *grads, middle, final, gain, *[gathered] * 64)


def first_back(side, half_at, grads, pieces, rows, grad_middle, gain, order, tile=288, after=()):
    _, count, half = grads[0].shape
    width = rows.shape[1]
    mine = count // tile // 2

    def kernel(side_ref, low_ref, high_ref, rows_ref, middle_ref, gain_ref, order_ref, *refs):
        parts, (out_ref, sum_ref) = far_list(refs[:4], refs[4:6]), refs[6:]
        lefts = [jnp.concatenate([ref[at] for at in range(3)], axis=1) for ref in (low_ref, high_ref)]
        found = []
        for at in range(4):
            found.append(
                dot_nt(lefts[0], parts[2 * at][...]) + dot_nt(lefts[1], parts[2 * at + 1][...])
            )
        grad_normed = jnp.concatenate(found, axis=1)
        unit, inv_std = normal_parts(rows_ref[...].astype(F32))
        out = middle_ref[...] + normalize_back(grad_normed, unit, inv_std, gain_ref[...])
        out_ref[0] = dot_nt(out.astype(BF16), order_ref[...]).astype(BF16)

        @pl.when(first_step())
        def _():
            sum_ref[...] = jnp.zeros_like(sum_ref)

        sum_ref[0:1] += column_sum(grad_normed * unit)
        sum_ref[1:2] += column_sum(grad_normed)

    start = half_at * mine
    block = pl.BlockSpec((tile, width), lambda i, _: (start + i, 0))
    grad_block = pl.BlockSpec((3, tile, half), lambda i, _: (0, start + i, 0))
    offset = (lambda ref: ref[0] * mine) if half_at == 0 else (lambda ref: 0)
    return call(
        kernel,
        (mine,),
        [grad_block, grad_block, block, block, fixed(1, width), fixed(width, width)]
        + piece_specs(3 * half),
        [image_block(tile, width, offset), fixed(8, width)],
        [struct(((2 - half_at) * mine, tile, width)), struct((8, width), F32)],
        4 * count * width * width,
        8 * count * width + 6 * width * width,
        after,
        None,
        1,
        part=0.3,
    )(side, *in_hbm(grads), in_hbm(rows), in_hbm(grad_middle), gain, order, *in_hbm(pieces))


def fast_shards(
    tokens,
    image_mask,
    out_grad,
    norm1_gain,
    norm1_shift,
    qkv_weight,
    qv_bias,
    out_weight,
    out_bias,
    norm2_gain,
    norm2_shift,
    up_weight,
    up_bias,
    down_weight,
    down_bias,
):
    images, half_len, width = tokens.shape
    mine = images // 2
    half = qkv_weight.shape[2]
    half_hidden = up_weight.shape[1]
    count = 2 * mine * half_len
    me = lax.axis_index("dp")
    side = lax.axis_index("tensor")
    side_array = jnp.concatenate([jnp.stack([side, me]).astype(jnp.int32), image_mask])
    vectors = (norm1_gain, norm1_shift, norm2_gain, norm2_shift, out_bias, down_bias)
    order, gain_one, shift_one, gain_two, shift_two, bias_out, bias_down = setup(
        side_array, [vector.reshape(1, width) for vector in vectors]
    )

    def for_partner(values):
        return over_x(lax.dynamic_slice_in_dim(values, (1 - side) * mine, mine, 0))

    def z_all(values):
        return jnp.concatenate([values] + [over_z(values, step) for step in (1, 2, 3)], axis=0)

    second_group = jnp.concatenate([up_weight, out_weight], axis=1)
    up_all = lax.all_gather(second_group, ("dp", "tensor")).reshape(-1, 2, ROWS, half_hidden + half)
    own = prepare(side_array, tokens, order, gain_one, shift_one, 0)
    final, sum_own = mask_grad(side_array, out_grad, order, 0, after=own[:1])
    tokens_partner = for_partner(tokens)
    first = qkv_weight.reshape(ROWS, 3 * half)
    first_base = late(z_all(first), final)
    biases = jnp.concatenate([qv_bias.reshape(-1), up_bias])
    bias_rows = jnp.pad(biases, (0, 16 * 3 * half - biases.size)).reshape(16, 3 * half)

    def split_bias(bias):
        bias = bias.astype(F32)
        parts = jnp.stack([bias[:half], jnp.zeros((half,), F32), bias[half : 2 * half]])
        return parts[:, None], bias[None, 2 * half :]

    rows, normed = prepare(
        side_array, tokens_partner, order, gain_one, shift_one, 1, own, after=[first_base]
    )
    first_x = over_x(jnp.concatenate([first_base, bias_rows], axis=0))
    first_y = over_y(first_base)
    first_xy = over_y(late(first_x, first_y))
    first_far = [over_core(jnp.stack(late([first_base, first_y], first_x, normed)))]
    biases = [split_bias(biases), split_bias(first_x[4 * ROWS :].reshape(-1)[: biases.size])]
    heads_shape = (3, 2, mine, half_len, half)
    projected, contexts, kept = [None, None], [None, None], [None, None]
    projected[0] = project(normed, [first_base, first_y] + first_far, biases[0][0]).reshape(heads_shape)
    begun = attend(projected[0], 0, 1, lanes=128)
    first_far += [over_core(jnp.stack(late([first_x, first_xy], begun[0])))]
    first_pieces = [first_base, first_x, first_y, first_xy] + first_far
    contexts[0], *kept[0] = attend(projected[0], 1, 2, begun, lanes=128)
    grad_partner = for_partner(late(out_grad, first_x))
    projected[1] = project(
        normed, [first_x, first_xy] + first_far[1:], biases[1][0], after=[contexts[0]]
    ).reshape(heads_shape)
    down_all = lax.all_gather(late(down_weight, up_all, contexts[0]), ("dp", "tensor"))
    down_all = down_all.reshape(-1, 2, ROWS, half_hidden)
    contexts[1], *kept[1] = attend(projected[1], 0, 2)
    contexts = [values.reshape(count, half) for values in contexts]
    middle, second = add_branch(side_array, contexts, rows, up_all, bias_out, gain_two, shift_two)
    actives, slopes = [None, None], [None, None]
    actives[0], slopes[0] = feed_up(side_array, 0, second, up_all, biases[0][1])
    final, sum_partner = mask_grad(side_array, grad_partner, order, 1, final, after=[actives[0]])
    actives[1], slopes[1] = feed_up(side_array, 1, second, up_all, biases[1][1], after=[final])

    down_near, down_next, down_far, down_last = sums_down(final, actives)
    grads_sums = gate_back(side_array, final, slopes, down_all, after=[down_near])
    grads, sum_hidden = grads_sums[:2], grads_sums[2:]
    (down_sent,) = combine([down_next, over_core(down_last)], 1, after=grads[:1])
    down_sent_y = over_y(down_sent)
    up_near, up_next, up_far_sums, up_last = sums_up(second, grads, after=[down_sent])
    grad_middle, branch, *grad_contexts, sums_two = second_back(
        side_array, grads, up_all, middle, final, gain_two, after=[up_near]
    )
    (up_sent,) = combine([up_next, over_core(up_last)], 1, after=[branch])
    up_sent_x = over_x(up_sent)
    down_far = over_core(late(down_far, up_sent))

    def heads_back(x_at, after):
        grad_context = grad_contexts[x_at].reshape(2, mine, half_len, half)
        grad, sums = attend_back(
            projected[x_at], grad_context, contexts[x_at].reshape(grad_context.shape), *kept[x_at], after=after
        )
        return grad.reshape(3, count, half), jnp.sum(sums, axis=0)

    grads_qkv, sums_qkv = [None, None], [None, None]
    grads_qkv[1], sums_qkv[1] = heads_back(1, [up_sent])
    down_sums = combine([down_near, down_far, down_sent_y], 2, after=[grads_qkv[1]])
    down_sent_x = over_x(down_sums[1])
    high_near, high_next, high_far, high_last = sums_first(
        normed, branch, grads_qkv[1], contexts[1], after=down_sums[:1]
    )
    up_far_sums = over_core(late(up_far_sums, high_near))
    out_send = feed_down(side_array, 2, 4, actives, middle, down_all, bias_down, order, after=[high_near])
    (high_sent,) = combine([high_next, over_core(high_last)], 1, after=[out_send])
    high_sent_y = over_y(high_sent)
    up_sums = combine([up_near, up_far_sums, up_sent_x], 2, after=[high_sent])
    up_sent_y = over_y(up_sums[1])
    high_far = over_core(late(high_far, up_sums[0]))
    out_partner = over_x(late(out_send, up_sums[0]))
    grads_qkv[0], sums_qkv[0] = heads_back(0, up_sums[:1])
    down_sums = combine([down_sums[0], down_sent_x], 2, after=[high_far, grads_qkv[0]])
    down_sent_z = over_z(down_sums[1], 2)
    low_near, low_next, low_far, low_last = sums_first(
        normed, branch, grads_qkv[0], contexts[0], after=down_sums[:1]
    )
    (high,) = combine([high_near, high_far, high_sent_y], 1, after=[low_near])
    high_x = over_x(high)
    (low_sent,) = combine([low_next, over_core(low_last)], 1, after=[high])
    low_sent_y = over_y(low_sent)
    send, sums_partner = first_back(
        side_array, 1, grads_qkv, first_pieces, rows, grad_middle, gain_one, order, after=[low_sent]
    )
    up_sums = combine([up_sums[0], up_sent_y], 2, after=[send])
    up_sent_z = over_z(up_sums[1], 2)
    down_sums = combine([down_sums[0], down_sent_z], 2, after=[up_sums[0], out_partner])
    down_sent_z = over_z(down_sums[1], 1)
    low_far = over_core(late(low_far, up_sums[0]))
    full, sums_own = first_back(
        side_array, 0, grads_qkv, first_pieces, rows, grad_middle, gain_one, order, after=down_sums[:1]
    )
    up_sums = combine([up_sums[0], up_sent_z], 2, after=[full])
    sums = jnp.concatenate(
        [(sums_own + sums_partner)[:2], sums_two[2:3], sums_two[:2], sum_own + sum_partner], axis=0
    )
    sums = jnp.einsum("td,od->to", sums, order.astype(F32), precision=lax.Precision.HIGHEST)
    halves = [
        jnp.concatenate([sums_qkv[x_at].reshape(-1), sum_hidden[x_at][0]]) for x_at in range(2)
    ]
    small = jnp.concatenate([halves[0], sums.reshape(-1), halves[1]])
    small = late(small + over_core(small), up_sums[0])
    small = small + over_y(small)
    halves_size = 2 * half + half_hidden
    small_x = over_x(jnp.concatenate([small[-halves_size:], small[halves_size:-halves_size]]))
    small = small[:-halves_size] + small_x
    height = 8
    small_rows = jnp.pad(small, (0, height * half_hidden - small.size)).reshape(height, half_hidden)
    small_top = small_rows.astype(BF16)
    small_rows = jnp.concatenate([small_top, (small_rows - small_top.astype(F32)).astype(BF16)], axis=0)

    low = combine([low_near, low_far, low_sent_y, high_x], 4, after=up_sums[:1])
    near_z = over_z(jnp.concatenate([low[1], up_sums[1], small_rows], axis=0), 1)
    middle_z = over_z(jnp.concatenate([low[2], small_rows], axis=0), 2)
    far_z = over_z(jnp.concatenate([low[3], small_rows], axis=0), 3)
    send_x = over_x(late(send, low[0]))
    out_full = feed_down(
        side_array, 0, 2, actives, middle, down_all, bias_down, order, after=[low[0], small_rows]
    )
    (grad_down,) = combine([down_sums[0], down_sent_z], 1, F32, after=[out_full])
    block_out = lax.dynamic_update_slice_in_dim(out_full, out_partner, (1 - side) * mine, 0)
    tokens_grad = lax.dynamic_update_slice_in_dim(full, send_x, (1 - side) * mine, 0)
    grad_qkv, grad_out, grad_up, sums = finish(
        low[0], up_sums[0], small_rows, near_z, middle_z, far_z, after=[out_full, tokens_grad]
    )
    sums = sums.reshape(-1)
    halves = sums[:halves_size]
    sums = sums[halves_size : halves_size + 6 * width].reshape(6, width)
    return (
        block_out,
        tokens_grad,
        sums[0],
        sums[1],
        grad_qkv.reshape(ROWS, 3, half),
        halves[: 2 * half].reshape(2, half),
        grad_out,
        sums[2],
        sums[3],
        sums[4],
        grad_up,
        halves[2 * half :],
        grad_down,
        sums[5],
    )


def solution(mesh):
    in_specs = (
        P("dp", "tensor", None),
        P("dp"),
        P("dp", "tensor", None),
        P(),
        P(),
        P("dp", None, "tensor"),
        P(None, "tensor"),
        P("dp", "tensor"),
        P(),
        P(),
        P(),
        P("dp", "tensor"),
        P("tensor"),
        P("dp", "tensor"),
        P(),
    )
    out_specs = (
        P("dp", "tensor", None),
        P("dp", "tensor", None),
        P(),
        P(),
        P("dp", None, "tensor"),
        P(None, "tensor"),
        P("dp", "tensor"),
        P(),
        P(),
        P(),
        P("dp", "tensor"),
        P("tensor"),
        P("dp", "tensor"),
        P(),
    )
    small_slice = mesh.shape["dp"] == 16 and mesh.shape["tensor"] == 2
    shards = fast_shards if small_slice else general_shards
    return jax.shard_map(shards, mesh=mesh, in_specs=in_specs, out_specs=out_specs, check_vma=False)
```

```python
import jax
import jax.numpy as jnp
from jax import lax
from jax.experimental import pallas as pl
from jax.experimental.pallas import tpu as pltpu
from jax.sharding import PartitionSpec as P

HDIM = 64
MICRO = 2


def mixed(form, left, right):
    return jnp.einsum(form, left, right, preferred_element_type=jnp.float32)


def normalize(values, gain, shift):
    mean_val = jnp.mean(values, axis=-1, keepdims=True)
    centered = values - mean_val
    inv_std = lax.rsqrt(jnp.mean(centered * centered, axis=-1, keepdims=True) + 1e-05)
    unit_val = centered * inv_std
    return (unit_val * gain + shift, unit_val, inv_std)


def normalize_back(grad_in, unit_val, inv_std, gain):
    scaled = grad_in * gain
    return inv_std * (
        scaled
        - jnp.mean(scaled, axis=-1, keepdims=True)
        - unit_val * jnp.mean(scaled * unit_val, axis=-1, keepdims=True)
    )


def token_sum(values):
    return jnp.sum(values, axis=(0, 1))


def general_shards(
    tokens,
    image_mask,
    out_grad,
    norm1_gain,
    norm1_shift,
    qkv_weight,
    qv_bias,
    out_weight,
    out_bias,
    norm2_gain,
    norm2_shift,
    up_weight,
    up_bias,
    down_weight,
    down_bias,
):
    images_here = tokens.shape[0] // MICRO
    full_width = norm1_gain.shape[0]
    local_width = qkv_weight.shape[2]
    local_hidden = up_weight.shape[1]
    local_heads = local_width // HDIM
    score_scale = HDIM ** (-0.5)
    gain_one = norm1_gain.astype(jnp.float32)
    shift_one = norm1_shift.astype(jnp.float32)
    gain_two = norm2_gain.astype(jnp.float32)
    shift_two = norm2_shift.astype(jnp.float32)
    bias_pair = qv_bias.astype(jnp.float32)
    grad_qkv = jnp.zeros((full_width, 3, local_width), jnp.float32)
    grad_out = jnp.zeros((full_width, local_width), jnp.float32)
    grad_up = jnp.zeros((full_width, local_hidden), jnp.float32)
    grad_down = jnp.zeros((full_width, local_hidden), jnp.float32)
    grad_gain_one = jnp.zeros((full_width,), jnp.float32)
    grad_shift_one = jnp.zeros((full_width,), jnp.float32)
    grad_gain_two = jnp.zeros((full_width,), jnp.float32)
    grad_shift_two = jnp.zeros((full_width,), jnp.float32)
    grad_out_bias = jnp.zeros((full_width,), jnp.float32)
    grad_down_bias = jnp.zeros((full_width,), jnp.float32)
    grad_pair = jnp.zeros((2, local_width), jnp.float32)
    grad_up_bias = jnp.zeros((local_hidden,), jnp.float32)
    outputs = []
    input_grads = []
    for micro_index in range(MICRO):
        first_image = micro_index * images_here
        block_rows = tokens[first_image : first_image + images_here].astype(jnp.float32)
        keep_mask = image_mask[first_image : first_image + images_here].astype(jnp.float32)[
            :, None, None
        ]
        fwd_weights = (
            lax.all_gather(qkv_weight, "dp", axis=0, tiled=True),
            lax.all_gather(out_weight, "dp", axis=0, tiled=True),
            lax.all_gather(up_weight, "dp", axis=0, tiled=True),
            lax.all_gather(down_weight, "dp", axis=0, tiled=True),
        )
        qkv_full, out_full, up_full, down_full = fwd_weights
        normed, unit_one, inv_one = normalize(block_rows, gain_one, shift_one)
        normed_full = lax.all_gather(normed.astype(jnp.bfloat16), "tensor", axis=1, tiled=True)
        seq_len = normed_full.shape[1]
        head_shape = (images_here, seq_len, local_heads, HDIM)
        projected = mixed("isd,dcf->iscf", normed_full, qkv_full)
        queries = (projected[:, :, 0] + bias_pair[0]).astype(jnp.bfloat16).reshape(head_shape)
        key_rows = projected[:, :, 1].astype(jnp.bfloat16).reshape(head_shape)
        value_rows = (projected[:, :, 2] + bias_pair[1]).astype(jnp.bfloat16).reshape(head_shape)
        scores = mixed("iqhe,ikhe->ihqk", queries, key_rows) * score_scale
        row_top = jnp.max(scores, axis=-1, keepdims=True)
        raw_weights = jnp.exp(scores - row_top)
        row_total = jnp.sum(raw_weights, axis=-1, keepdims=True)
        log_total = row_top + jnp.log(row_total)
        probs = (raw_weights / row_total).astype(jnp.bfloat16)
        context = mixed("ihqk,ikhe->iqhe", probs, value_rows).astype(jnp.bfloat16)
        context = context.reshape(images_here, seq_len, local_width)
        attn_terms = mixed("isf,of->iso", context, out_full)
        branch = lax.psum_scatter(
            attn_terms, "tensor", scatter_dimension=1, tiled=True
        ) + out_bias.astype(jnp.float32)
        middle = block_rows + branch
        second, unit_two, inv_two = normalize(middle, gain_two, shift_two)
        second_full = lax.all_gather(second.astype(jnp.bfloat16), "tensor", axis=1, tiled=True)
        hidden = mixed("isd,df->isf", second_full, up_full) + up_bias.astype(jnp.float32)
        gate_sig = jax.nn.sigmoid(1.702 * hidden)
        active = (hidden * gate_sig).astype(jnp.bfloat16)
        feed_terms = mixed("isf,of->iso", active, down_full)
        feed_out = lax.psum_scatter(
            feed_terms.astype(jnp.bfloat16), "tensor", scatter_dimension=1, tiled=True
        ).astype(jnp.float32) + down_bias.astype(jnp.float32)
        outputs.append(((middle + feed_out) * keep_mask).astype(jnp.bfloat16))
        back_weights = (
            lax.all_gather(qkv_weight, "dp", axis=0, tiled=True),
            lax.all_gather(out_weight, "dp", axis=0, tiled=True),
            lax.all_gather(up_weight, "dp", axis=0, tiled=True),
            lax.all_gather(down_weight, "dp", axis=0, tiled=True),
        )
        qkv_back, out_back, up_back, down_back = back_weights
        grad_final = (
            out_grad[first_image : first_image + images_here].astype(jnp.float32) * keep_mask
        )
        grad_down_bias = grad_down_bias + token_sum(grad_final)
        final_full = lax.all_gather(grad_final.astype(jnp.bfloat16), "tensor", axis=1, tiled=True)
        grad_down = grad_down + mixed("iso,isf->of", final_full, active)
        grad_active = mixed("iso,of->isf", final_full, down_back)
        grad_hidden = (
            grad_active * (gate_sig + 1.702 * hidden * gate_sig * (1.0 - gate_sig))
        ).astype(jnp.bfloat16)
        grad_up_bias = grad_up_bias + token_sum(grad_hidden.astype(jnp.float32))
        grad_up = grad_up + mixed("isd,isf->df", second_full, grad_hidden)
        second_terms = mixed("isf,df->isd", grad_hidden, up_back)
        grad_second = lax.psum_scatter(second_terms, "tensor", scatter_dimension=1, tiled=True)
        grad_gain_two = grad_gain_two + token_sum(grad_second * unit_two)
        grad_shift_two = grad_shift_two + token_sum(grad_second)
        grad_middle = grad_final + normalize_back(grad_second, unit_two, inv_two, gain_two)
        grad_branch = grad_middle.astype(jnp.bfloat16)
        grad_out_bias = grad_out_bias + token_sum(grad_branch.astype(jnp.float32))
        branch_full = lax.all_gather(grad_branch, "tensor", axis=1, tiled=True)
        grad_out = grad_out + mixed("iso,isf->of", branch_full, context)
        grad_context = (
            mixed("iso,of->isf", branch_full, out_back).astype(jnp.bfloat16).reshape(head_shape)
        )
        again = mixed("iqhe,ikhe->ihqk", queries, key_rows) * score_scale
        soft_again = jnp.exp(again - log_total)
        probs_again = soft_again.astype(jnp.bfloat16)
        grad_values = mixed("ihqk,iqhe->ikhe", probs_again, grad_context)
        grad_soft = mixed("iqhe,ikhe->ihqk", grad_context, value_rows)
        grad_scores = (
            soft_again * (grad_soft - jnp.sum(grad_soft * soft_again, axis=-1, keepdims=True))
        ).astype(jnp.bfloat16)
        grad_queries = mixed("ihqk,ikhe->iqhe", grad_scores, key_rows) * score_scale
        grad_keys = mixed("ihqk,iqhe->ikhe", grad_scores, queries) * score_scale
        flat_shape = (images_here, seq_len, local_width)
        grad_projected = jnp.stack(
            (
                grad_queries.reshape(flat_shape),
                grad_keys.reshape(flat_shape),
                grad_values.reshape(flat_shape),
            ),
            axis=2,
        ).astype(jnp.bfloat16)
        pair_terms = grad_projected.astype(jnp.float32)
        grad_pair = grad_pair + jnp.stack(
            (token_sum(pair_terms[:, :, 0]), token_sum(pair_terms[:, :, 2])), axis=0
        )
        grad_qkv = grad_qkv + mixed("isd,iscf->dcf", normed_full, grad_projected)
        normed_terms = mixed("iscf,dcf->isd", grad_projected, qkv_back)
        grad_normed = lax.psum_scatter(
            normed_terms.astype(jnp.bfloat16), "tensor", scatter_dimension=1, tiled=True
        ).astype(jnp.float32)
        grad_gain_one = grad_gain_one + token_sum(grad_normed * unit_one)
        grad_shift_one = grad_shift_one + token_sum(grad_normed)
        grad_tokens = grad_middle + normalize_back(grad_normed, unit_one, inv_one, gain_one)
        input_grads.append(grad_tokens.astype(jnp.bfloat16))
    grad_qkv, grad_out, grad_up, grad_down = (
        lax.psum_scatter(
            grad_qkv.astype(jnp.bfloat16), "dp", scatter_dimension=0, tiled=True
        ).astype(jnp.float32),
        lax.psum_scatter(
            grad_out.astype(jnp.bfloat16), "dp", scatter_dimension=0, tiled=True
        ).astype(jnp.float32),
        lax.psum_scatter(
            grad_up.astype(jnp.bfloat16), "dp", scatter_dimension=0, tiled=True
        ).astype(jnp.float32),
        lax.psum_scatter(
            grad_down.astype(jnp.bfloat16), "dp", scatter_dimension=0, tiled=True
        ).astype(jnp.float32),
    )
    grad_gain_one, grad_shift_one, grad_gain_two, grad_shift_two, grad_out_bias, grad_down_bias = (
        lax.psum(
            (
                grad_gain_one,
                grad_shift_one,
                grad_gain_two,
                grad_shift_two,
                grad_out_bias,
                grad_down_bias,
            ),
            ("dp", "tensor"),
        )
    )
    grad_pair, grad_up_bias = lax.psum((grad_pair, grad_up_bias), "dp")
    block_out = jnp.concatenate(outputs, axis=0)
    tokens_grad = jnp.concatenate(input_grads, axis=0)
    return (
        block_out,
        tokens_grad,
        grad_gain_one,
        grad_shift_one,
        grad_qkv,
        grad_pair,
        grad_out,
        grad_out_bias,
        grad_gain_two,
        grad_shift_two,
        grad_up,
        grad_up_bias,
        grad_down,
        grad_down_bias,
    )


ROWS = 64
PART = 256
VMEM_BYTES = 24 * 1024 * 1024
COST_PART = 0.6
FORWARD_PART = 0.8
LOG2_E = 1.4426950408889634
BF16 = jnp.bfloat16
F32 = jnp.float32


def swap(values, axis_name, flip):
    count = lax.axis_size(axis_name)
    return lax.ppermute(values, axis_name, [(place, place ^ flip) for place in range(count)])


def over_core(values):
    return swap(values, "dp", 1)


def over_y(values):
    return swap(values, "dp", 2)


def over_z(values, step):
    return swap(values, "dp", 4 * step)


def over_x(values):
    return swap(values, "tensor", 1)


def late(values, *marks):
    return lax.optimization_barrier((values, *marks))[0]


def dot_nn(left, right):
    return lax.dot_general(left, right, (((1,), (0,)), ((), ())), preferred_element_type=F32)


def dot_nt(left, right):
    return lax.dot_general(left, right, (((1,), (1,)), ((), ())), preferred_element_type=F32)


def dot_tn(left, right):
    return lax.dot_general(left, right, (((0,), (0,)), ((), ())), preferred_element_type=F32)


def call(
    kernel, grid, in_specs, out_specs, out_shape, flops, moved, after=(), aliases=None, scalars=0, part=None
):
    given, waits = scalars + len(in_specs), len(after)
    part = COST_PART if part is None else part

    def run(*refs):
        kernel(*refs[:given], *refs[given + waits :])

    function = pl.pallas_call(
        run,
        grid_spec=pltpu.PrefetchScalarGridSpec(
            num_scalar_prefetch=scalars,
            grid=grid,
            in_specs=list(in_specs) + [pl.BlockSpec(memory_space=pl.ANY)] * waits,
            out_specs=out_specs,
        ),
        out_shape=out_shape,
        input_output_aliases=aliases or {},
        compiler_params=pltpu.CompilerParams(vmem_limit_bytes=VMEM_BYTES),
        cost_estimate=pl.CostEstimate(
            flops=int(flops * part), bytes_accessed=int(moved * part), transcendentals=0
        ),
    )
    return lambda *arrays: function(*arrays, *after)


def fixed(*shape, at=None):
    place = at or (0,) * len(shape)
    return pl.BlockSpec(shape, lambda *_: place, pipeline_mode=pl.Buffered(1))


def far_list(near, far):
    return list(near) + [far[last].at[y_at] for y_at in range(2) for last in range(2)]


def piece_specs(columns, at=0):
    return [fixed(PART, columns, at=(0, at))] * 4 + [fixed(2, PART, columns, at=(0, 0, at))] * 2


def piece_tiles(tile, near=4, far=2):
    return [pl.BlockSpec((PART, tile), lambda j: (0, j))] * near + [
        pl.BlockSpec((2, PART, tile), lambda j: (0, 0, j))
    ] * far


def gathered_specs(columns, halves=(0, 1), at=None):
    def spec(block, x_at):
        core, y_at, z_at = block // 8, (block // 4) % 2, block % 4
        slab = z_at * 4 + y_at * 2 + core

        def place(j, *refs):
            where = refs[-1]
            row = jnp.bitwise_xor(where[1], slab), jnp.bitwise_xor(where[0], x_at)
            return (*row, 0, j if at is None else at)

        mode = {} if at is None else {"pipeline_mode": pl.Buffered(1)}
        return pl.BlockSpec((1, 1, ROWS, columns), place, **mode)

    return [spec(block, x_at) for block in range(16) for x_at in halves]


def joined(refs, first, last, step=1, offset=0):
    return jnp.concatenate([refs[step * block + offset][0, 0] for block in range(first, last)], axis=0)


def struct(shape, dtype=BF16):
    return jax.ShapeDtypeStruct(shape, dtype)


def outer(shape, dtype=BF16):
    return pltpu.HBM(shape, dtype)


def in_hbm(values):
    if isinstance(values, (list, tuple)):
        return [in_hbm(part) for part in values]
    return pltpu.with_memory_space_constraint(values, pltpu.HBM)


ANYWHERE = pl.BlockSpec(memory_space=pl.ANY)


def normal_parts(values):
    mean_val = jnp.mean(values, axis=-1, keepdims=True)
    centered = values - mean_val
    inv_std = lax.rsqrt(jnp.mean(centered * centered, axis=-1, keepdims=True) + 1e-05)
    return centered * inv_std, inv_std


def column_sum(values):
    return jnp.sum(values, axis=0, keepdims=True)


def combine(arrays, pieces, dtype=BF16, tile=1024, after=()):
    columns = arrays[0].shape[-1]
    rows = arrays[0].size // columns // pieces
    arrays = [values.reshape(pieces, rows, columns) for values in arrays]
    given = len(arrays)

    def kernel(*refs):
        for at in range(pieces):
            parts = [ref[at].astype(F32) for ref in refs[:given]]
            while len(parts) > 1:
                parts = [sum(parts[start : start + 2]) for start in range(0, len(parts), 2)]
            refs[given + at][...] = parts[0].astype(dtype)

    return call(
        kernel,
        (columns // tile,),
        [pl.BlockSpec((pieces, rows, tile), lambda j: (0, 0, j))] * given,
        [pl.BlockSpec((rows, tile), lambda j: (0, j))] * pieces,
        [outer((rows, columns), dtype)] * pieces,
        0,
        2 * pieces * rows * columns * (given + 1),
        after,
    )(*arrays)


def finish(low_near, up_near, small, near, middle, far, after=()):
    rows, columns = low_near.shape
    split = columns * 3 // 4
    height = small.shape[0] // 2

    def kernel(low_ref, up_ref, small_ref, near_ref, middle_ref, far_ref, qkv_ref, out_ref, up_out_ref, sum_ref):
        def rows_of(ref, start):
            return ref[start : start + rows, :].astype(F32)

        def vectors_of(ref, start):
            values = ref[start : start + 2 * height, :].astype(F32)
            return values[:height] + values[height:]

        low = (rows_of(low_ref, 0) + rows_of(near_ref, 0)) + (rows_of(middle_ref, 0) + rows_of(far_ref, 0))
        qkv_ref[...] = low[:, :split]
        out_ref[...] = low[:, split:]
        up_out_ref[...] = rows_of(up_ref, 0) + rows_of(near_ref, rows)
        sum_ref[...] = (vectors_of(small_ref, 0) + vectors_of(near_ref, 2 * rows)) + (
            vectors_of(middle_ref, rows) + vectors_of(far_ref, rows)
        )

    given = [low_near, up_near, small, near, middle, far]
    return call(
        kernel,
        (1,),
        [fixed(*values.shape) for values in given],
        [fixed(rows, split), fixed(rows, columns - split), fixed(rows, columns), fixed(height, columns)],
        [
            struct((rows, split), F32),
            struct((rows, columns - split), F32),
            struct((rows, columns), F32),
            struct((height, columns), F32),
        ],
        0,
        20 * rows * columns,
        after,
    )(*given)


def first_step():
    return pl.program_id(0) == 0


def setup(places, vectors, after=()):
    width = vectors[0].shape[1]
    given = len(vectors)

    def kernel(place_ref, *refs):
        order_ref = refs[given]
        source = lax.broadcasted_iota(jnp.int32, (width, width), 0)
        target = lax.broadcasted_iota(jnp.int32, (width, width), 1)
        at = target // ROWS
        z_rel, y_rel, core_rel = at % 4, (at // 4) % 2, at // 8
        place = (z_rel * 4 + y_rel * 2 + core_rel) ^ place_ref[1]
        hit = source == place * ROWS + target % ROWS
        order = jnp.where(hit, 1.0, 0.0).astype(BF16)
        order_ref[...] = order
        rows = jnp.concatenate([ref[...].astype(F32) for ref in refs[:given]] + [jnp.zeros((8 - given, width), F32)], axis=0)
        moved = dot_nn(rows.astype(BF16), order)
        for vector_at in range(given):
            refs[given + 1 + vector_at][...] = moved[vector_at : vector_at + 1]

    row = fixed(1, width)
    return call(
        kernel,
        (1,),
        [row] * given,
        [fixed(width, width)] + [row] * given,
        [struct((width, width))] + [struct((1, width), F32)] * given,
        16 * width * width,
        2 * width * width,
        after,
        None,
        1,
        part=FORWARD_PART,
    )(places, *vectors)


def image_block(height, width, offset):
    return pl.BlockSpec((1, height, width), lambda i, side: (offset(side) + i, 0, 0))


def prepare(side, images, order, gain, shift, half_at, before=None, after=()):
    _, height, width = images.shape
    mine = 2

    def kernel(side_ref, raw_ref, order_ref, gain_ref, shift_ref, *refs):
        rows_ref, norm_ref = refs[-2:]
        rows = dot_nn(raw_ref[0], order_ref[...])
        rows_ref[...] = rows.astype(BF16)
        unit, _ = normal_parts(rows)
        norm_ref[...] = (unit * gain_ref[...] + shift_ref[...]).astype(BF16)

    offset = (lambda side_ref: side_ref[0] * mine) if half_at == 0 else (lambda side_ref: 0)
    out = pl.BlockSpec((height, width), lambda i, _: (half_at * mine + i, 0))
    old = () if before is None else before
    return call(
        kernel,
        (mine,),
        [image_block(height, width, offset), fixed(width, width), fixed(1, width), fixed(1, width)]
        + [ANYWHERE] * len(old),
        [out, out],
        [outer((2 * mine * height, width))] * 2,
        2 * mine * height * width * width,
        6 * mine * height * width,
        after,
        {5: 0, 6: 1} if old else None,
        1,
        part=FORWARD_PART,
    )(side, images, order, gain, shift, *old)


def mask_grad(side, images, order, half_at, before=None, after=()):
    _, height, width = images.shape
    mine = 2

    def kernel(side_ref, raw_ref, order_ref, *refs):
        final_ref, sum_ref = refs[-2:]
        keep = side_ref[2 + side_ref[0] * mine + pl.program_id(0)].astype(F32)
        final = dot_nn(raw_ref[0], order_ref[...]) * keep
        final_ref[...] = final.astype(BF16)

        @pl.when(first_step())
        def _():
            sum_ref[...] = jnp.zeros_like(sum_ref)

        sum_ref[...] += column_sum(final)

    offset = (lambda side_ref: side_ref[0] * mine) if half_at == 0 else (lambda side_ref: 0)
    old = () if before is None else (before,)
    out = pl.BlockSpec((height, width), lambda i, _: (half_at * mine + i, 0))
    return call(
        kernel,
        (mine,),
        [image_block(height, width, offset), fixed(width, width)] + [ANYWHERE] * len(old),
        [out, fixed(1, width)],
        [struct((2 * mine * height, width)), struct((1, width), F32)],
        2 * mine * height * width * width,
        6 * mine * height * width,
        after,
        {3: 0} if old else None,
        1,
        part=FORWARD_PART,
    )(side, images, order, *old)


def project(normed, parts, bias, after=()):
    count, width = normed.shape
    half = bias.shape[-1]

    def kernel(norm_ref, bias_ref, *refs):
        weight = jnp.concatenate([refs[0][...], refs[1][...], refs[2][0], refs[2][1]], axis=0)
        refs[3][0] = (dot_nn(norm_ref[...], weight) + bias_ref[0]).astype(BF16)

    return call(
        kernel,
        (3,),
        [fixed(count, width), pl.BlockSpec((1, 1, half), lambda j: (j, 0, 0))]
        + piece_tiles(half, 2, 1),
        pl.BlockSpec((1, count, half), lambda j: (j, 0, 0)),
        outer((3, count, half)),
        6 * count * width * half,
        2 * count * (width + 3 * half) + 6 * width * half,
        after,
        part=FORWARD_PART,
    )(normed, bias, *parts)


def attend(projected, first_image, last_image, before=None, lanes=256, after=()):
    _, _, images, half_len, half = projected.shape
    length = 2 * half_len
    per_step = lanes // HDIM
    steps = half // lanes

    def kernel(proj_ref, *refs):
        out_ref, weights_ref, inverse_ref = refs[-3:]
        queries, key_rows, value_rows = (proj_ref[at].reshape(length, lanes) for at in range(3))
        queries, value_rows = queries.T, value_rows.T
        outs, inverses = [], []
        for head in range(per_step):
            part = slice(head * HDIM, (head + 1) * HDIM)
            scores = dot_nn(key_rows[:, part], queries[part])
            top = jnp.max(scores, axis=0, keepdims=True)
            weights = jnp.exp2((scores - top) * (LOG2_E * HDIM**-0.5)).astype(BF16)
            weights_ref[0, head] = weights
            ones = jnp.ones((16, length), BF16)
            sums = dot_nn(jnp.concatenate([value_rows[part], ones], axis=0), weights)
            inverse = 1.0 / sums[HDIM : HDIM + 1]
            outs.append((sums[:HDIM] * inverse).astype(BF16))
            inverses.append(inverse)
        out_ref[...] = jnp.concatenate(outs, axis=0).T.reshape(out_ref.shape)
        inverse_ref[0] = jnp.concatenate(inverses + [jnp.zeros((8 - per_step, length), F32)], axis=0)

    heads = half // HDIM
    old = () if before is None else before
    return call(
        kernel,
        (last_image - first_image, steps),
        [pl.BlockSpec((3, 2, 1, half_len, lanes), lambda i, j: (0, 0, first_image + i, 0, j))]
        + [ANYWHERE] * len(old),
        [
            pl.BlockSpec((2, 1, half_len, lanes), lambda i, j: (0, first_image + i, 0, j)),
            pl.BlockSpec((1, per_step, length, length), lambda i, j: (first_image + i, j, 0, 0)),
            pl.BlockSpec((1, 8, length), lambda i, j: (first_image + i, j, 0)),
        ],
        [
            struct((2, images, half_len, half)),
            outer((images, heads, length, length)),
            struct((images, 8 * steps, length), F32),
        ],
        24 * (last_image - first_image) * heads * length * length * HDIM,
        (last_image - first_image) * heads * length * length * 2,
        after,
        {1: 0, 2: 1, 3: 2} if old else None,
        part=FORWARD_PART,
    )(in_hbm(projected), *old)


def attend_back(projected, grad_context, context, weights, inverse, after=()):
    _, _, images, half_len, half = projected.shape
    length = 2 * half_len
    steps = inverse.shape[1] // 8
    lanes = half // steps
    per_step = lanes // HDIM
    scale = HDIM**-0.5

    def kernel(proj_ref, grad_ref, context_ref, weights_ref, inverse_ref, out_ref, sum_ref):
        queries, key_rows, value_rows = (proj_ref[at].reshape(length, lanes) for at in range(3))
        queries, key_rows = queries.T, key_rows.T
        grads = grad_ref[...].reshape(length, lanes).T.astype(F32)
        contexts = context_ref[...].reshape(length, lanes).T.astype(F32)
        found = ([], [], [])
        for head in range(per_step):
            part = slice(head * HDIM, (head + 1) * HDIM)
            weights = weights_ref[0, head]
            grad = grads[part] * inverse_ref[0, head : head + 1]
            level = jnp.sum(grad * contexts[part], axis=0, keepdims=True)
            grad = grad.astype(BF16)
            found[2].append(dot_nt(grad, weights).astype(BF16))
            grad_soft = dot_nn(value_rows[:, part], grad)
            grad_scores = (weights.astype(F32) * (grad_soft - level)).astype(BF16)
            found[0].append((dot_nn(key_rows[part], grad_scores) * scale).astype(BF16))
            found[1].append((dot_nt(queries[part], grad_scores) * scale).astype(BF16))
        for at in range(3):
            joined = jnp.concatenate(found[at], axis=0).T
            out_ref[at] = joined.reshape(2, 1, half_len, lanes)
            if at != 1:
                sum_ref[0, at // 2 : at // 2 + 1] = column_sum(joined.astype(F32))

    heads = half // HDIM
    block = pl.BlockSpec((3, 2, 1, half_len, lanes), lambda i, j: (0, 0, i, 0, j))
    rows = pl.BlockSpec((2, 1, half_len, lanes), lambda i, j: (0, i, 0, j))
    return call(
        kernel,
        (images, steps),
        [
            block,
            rows,
            rows,
            pl.BlockSpec((1, per_step, length, length), lambda i, j: (i, j, 0, 0)),
            pl.BlockSpec((1, 8, length), lambda i, j: (i, j, 0)),
        ],
        [block, pl.BlockSpec((1, 2, lanes), lambda i, j: (i, 0, j))],
        [struct(projected.shape), struct((images, 2, half), F32)],
        32 * images * heads * length * length * HDIM,
        images * heads * length * length * 2,
        after,
    )(in_hbm(projected), grad_context, context, in_hbm(weights), inverse)


def add_branch(places, contexts, rows, gathered, bias, gain, shift, tile=576, after=()):
    count, width = rows.shape
    half = width // 2

    def kernel(place_ref, low_ref, high_ref, rows_ref, bias_ref, gain_ref, shift_ref, *refs):
        middle_ref, norm_ref = refs[32:]
        branch = dot_nt(low_ref[...], joined(refs, 0, 16, 2, 0)) + dot_nt(high_ref[...], joined(refs, 0, 16, 2, 1))
        middle = rows_ref[...].astype(F32) + (branch + bias_ref[...])
        middle_ref[...] = middle
        unit, _ = normal_parts(middle)
        norm_ref[...] = (unit * gain_ref[...] + shift_ref[...]).astype(BF16)

    block = pl.BlockSpec((tile, width), lambda i, _: (i, 0))
    half_block = pl.BlockSpec((tile, half), lambda i, _: (i, 0))
    return call(
        kernel,
        (count // tile,),
        [half_block, half_block, block] + [fixed(1, width)] * 3 + gathered_specs(half, at=4),
        [block, block],
        [outer((count, width), F32), struct((count, width))],
        2 * count * width * width,
        10 * count * width + 2 * width * width,
        after,
        None,
        1,
        part=FORWARD_PART,
    )(places, *contexts, rows, bias, gain, shift, *[gathered] * 32)


def feed_up(places, x_at, second, gathered, bias, tile=512, after=()):
    count, width = second.shape
    columns = bias.shape[-1]

    def kernel(place_ref, second_ref, bias_ref, *refs):
        hidden = dot_nn(second_ref[...], joined(refs, 0, 16)) + bias_ref[...]
        gate = 0.5 + 0.5 * jnp.tanh(0.851 * hidden)
        refs[16][...] = (hidden * gate).astype(BF16)
        refs[17][...] = (gate * (1.0 + 1.702 * hidden * (1.0 - gate))).astype(BF16)

    block = pl.BlockSpec((count, tile), lambda j, _: (0, j))
    return call(
        kernel,
        (columns // tile,),
        [fixed(count, width), pl.BlockSpec((1, tile), lambda j, _: (0, j))] + gathered_specs(tile, (x_at,)),
        [block, block],
        [outer((count, columns))] * 2,
        2 * count * width * columns,
        2 * count * (width + 2 * columns) + 2 * width * columns,
        after,
        None,
        1,
        part=FORWARD_PART,
    )(places, second, bias, *[gathered] * 16)


def feed_down(side, first_tile, last_tile, actives, middle, gathered, bias, order, before=None, tile=288, after=()):
    count, columns = actives[0].shape
    width = middle.shape[1]
    mine = count // tile // 2
    half_at = first_tile // mine
    old = () if before is None else (before,)

    def kernel(side_ref, low_ref, high_ref, middle_ref, bias_ref, order_ref, *refs):
        keep = side_ref[2 + side_ref[0] * mine + first_tile % mine + pl.program_id(0)].astype(F32)
        out_ref = refs[-1]
        feed = dot_nt(low_ref[...], joined(refs, 0, 16, 2, 0)) + dot_nt(high_ref[...], joined(refs, 0, 16, 2, 1))
        out = ((middle_ref[...] + (feed + bias_ref[...])) * keep).astype(BF16)
        out_ref[0] = dot_nt(out, order_ref[...]).astype(BF16)

    hidden = pl.BlockSpec((tile, columns), lambda i, _: (first_tile + i, 0))
    offset = (lambda ref: ref[0] * mine + first_tile) if half_at == 0 else (lambda ref: first_tile - mine)

    return call(
        kernel,
        (last_tile - first_tile,),
        [
            hidden,
            hidden,
            pl.BlockSpec((tile, width), lambda i, _: (first_tile + i, 0)),
            fixed(1, width),
            fixed(width, width),
        ]
        + gathered_specs(columns, at=0)
        + [ANYWHERE] * len(old),
        image_block(tile, width, offset),
        struct(((2 - half_at) * mine, tile, width)),
        2 * count * width * columns + count * width * width,
        2 * count * columns + 3 * count * width + 4 * width * columns,
        after,
        {38: 0} if old else None,
        1,
    )(side, *[in_hbm(values) for values in actives], in_hbm(middle), bias, order, *[gathered] * 32, *old)


def gate_back(side, final, slopes, gathered, tile=512, after=()):
    count, width = final.shape
    columns = gathered.shape[-1]

    def kernel(side_ref, final_ref, low_ref, high_ref, *refs):
        outs, sums = refs[32:34], refs[34:36]
        for x_at, slope_ref in enumerate((low_ref, high_ref)):
            weight = joined(refs, 0, 16, 2, x_at)
            grad = (dot_nn(final_ref[...], weight) * slope_ref[...].astype(F32)).astype(BF16)
            outs[x_at][...] = grad
            sums[x_at][...] = column_sum(grad.astype(F32))

    block = pl.BlockSpec((count, tile), lambda j, _: (0, j))
    sum_block = pl.BlockSpec((1, tile), lambda j, _: (0, j))
    return call(
        kernel,
        (columns // tile,),
        [fixed(count, width), block, block] + gathered_specs(tile),
        [block, block, sum_block, sum_block],
        [struct((count, columns))] * 2 + [struct((1, columns), F32)] * 2,
        4 * count * width * columns,
        4 * count * (width + 2 * columns) + 4 * width * columns,
        after,
        None,
        1,
    )(side, in_hbm(final), *in_hbm(slopes), *[gathered] * 32)


def sums_down(final, actives, tile=512, after=()):
    count, width = final.shape
    columns = actives[0].shape[1]

    def kernel(final_ref, low_ref, high_ref, *outs):
        for x_at, right_ref in enumerate((low_ref, high_ref)):
            for core in range(2):
                for y_at in range(2):
                    start = (2 * core + y_at) * PART
                    part = dot_tn(final_ref[:, start : start + PART], right_ref[...])
                    outs[2 * core + y_at][x_at] = part.astype(BF16)

    right = pl.BlockSpec((count, tile), lambda j: (0, j))
    return call(
        kernel,
        (columns // tile,),
        [fixed(count, width), right, right],
        [pl.BlockSpec((2, PART, tile), lambda j: (0, 0, j))] * 4,
        [outer((2, PART, columns))] * 4,
        4 * count * width * columns,
        4 * count * columns + 2 * count * width + 4 * width * columns,
        after,
    )(final, *[in_hbm(values) for values in actives])


def sums_up(second, grads, tile=512, after=()):
    count, width = second.shape
    columns = grads[0].shape[1]

    def kernel(second_ref, low_ref, high_ref, *outs):
        for x_at, right_ref in enumerate((low_ref, high_ref)):
            for core in range(2):
                for y_at in range(2):
                    start = (2 * core + y_at) * PART
                    part = dot_tn(second_ref[:, start : start + PART], right_ref[...])
                    outs[2 * core + x_at][y_at] = part.astype(BF16)

    right = pl.BlockSpec((count, tile), lambda j: (0, j))
    return call(
        kernel,
        (columns // tile,),
        [fixed(count, width), right, right],
        [pl.BlockSpec((2, PART, tile), lambda j: (0, 0, j))] * 4,
        [outer((2, PART, columns))] * 4,
        4 * count * width * columns,
        4 * count * columns + 2 * count * width + 4 * width * columns,
        after,
    )(second, *grads)


def sums_first(normed, branch, grad_projected, context, after=()):
    count, width = normed.shape
    half = context.shape[1]

    def kernel(norm_ref, branch_ref, grad_ref, context_ref, *outs):
        def work(left_ref, right):
            for core in range(2):
                for y_at in range(2):
                    start = (2 * core + y_at) * PART
                    outs[2 * core + y_at][...] = dot_tn(left_ref[:, start : start + PART], right).astype(BF16)

        @pl.when(pl.program_id(0) < 3)
        def _():
            work(norm_ref, grad_ref[0])

        @pl.when(pl.program_id(0) == 3)
        def _():
            work(branch_ref, context_ref[...])

    left = fixed(count, width)
    return call(
        kernel,
        (4,),
        [left, left, pl.BlockSpec((1, count, half), lambda j: (jnp.minimum(j, 2), 0, 0)), fixed(count, half)],
        [pl.BlockSpec((PART, half), lambda j: (0, j))] * 4,
        [outer((PART, 4 * half))] * 4,
        8 * count * width * half,
        2 * count * (2 * width + 4 * half) + 8 * width * half,
        after,
    )(normed, branch, grad_projected, context)


def second_back(places, grads, gathered, middle, final, gain, tile=576, after=()):
    count, columns = grads[0].shape
    width = middle.shape[1]
    half = width // 2

    def kernel(place_ref, low_ref, high_ref, middle_ref, final_ref, gain_ref, *refs):
        ups, outs = refs[:32], refs[32:64]
        grad_ref, branch_ref, context_low_ref, context_high_ref, sum_ref = refs[64:]
        grad_second = dot_nt(low_ref[...], joined(ups, 0, 16, 2, 0)) + dot_nt(high_ref[...], joined(ups, 0, 16, 2, 1))
        unit, inv_std = normal_parts(middle_ref[...])
        grad_middle = final_ref[...].astype(F32) + normalize_back(
            grad_second, unit, inv_std, gain_ref[...]
        )
        branch = grad_middle.astype(BF16)
        grad_ref[...] = grad_middle
        branch_ref[...] = branch
        for x_at, context_ref in enumerate((context_low_ref, context_high_ref)):
            context_ref[...] = dot_nn(branch, joined(outs, 0, 16, 2, x_at)).astype(BF16)

        @pl.when(first_step())
        def _():
            sum_ref[...] = jnp.zeros_like(sum_ref)

        sum_ref[0:1] += column_sum(grad_second * unit)
        sum_ref[1:2] += column_sum(grad_second)
        sum_ref[2:3] += column_sum(branch.astype(F32))

    block = pl.BlockSpec((tile, width), lambda i, _: (i, 0))
    half_block = pl.BlockSpec((tile, half), lambda i, _: (i, 0))
    hidden = pl.BlockSpec((tile, columns), lambda i, _: (i, 0))
    return call(
        kernel,
        (count // tile,),
        [hidden, hidden, block, block, fixed(1, width)]
        + gathered_specs(columns, at=0)
        + gathered_specs(half, at=4),
        [block, block, half_block, half_block, fixed(8, width)],
        [outer((count, width), F32), struct((count, width))]
        + [struct((count, half))] * 2
        + [struct((8, width), F32)],
        4 * count * width * columns + 2 * count * width * width,
        4 * count * columns + 14 * count * width + 4 * width * columns,
        after,
        None,
        1,
    )(places, *grads, middle, final, gain, *[gathered] * 64)


def first_back(side, half_at, grads, pieces, rows, grad_middle, gain, order, tile=288, after=()):
    _, count, half = grads[0].shape
    width = rows.shape[1]
    mine = count // tile // 2

    def kernel(side_ref, low_ref, high_ref, rows_ref, middle_ref, gain_ref, order_ref, *refs):
        parts, (out_ref, sum_ref) = far_list(refs[:4], refs[4:6]), refs[6:]
        lefts = [jnp.concatenate([ref[at] for at in range(3)], axis=1) for ref in (low_ref, high_ref)]
        found = []
        for at in range(4):
            found.append(
                dot_nt(lefts[0], parts[2 * at][...]) + dot_nt(lefts[1], parts[2 * at + 1][...])
            )
        grad_normed = jnp.concatenate(found, axis=1)
        unit, inv_std = normal_parts(rows_ref[...].astype(F32))
        out = middle_ref[...] + normalize_back(grad_normed, unit, inv_std, gain_ref[...])
        out_ref[0] = dot_nt(out.astype(BF16), order_ref[...]).astype(BF16)

        @pl.when(first_step())
        def _():
            sum_ref[...] = jnp.zeros_like(sum_ref)

        sum_ref[0:1] += column_sum(grad_normed * unit)
        sum_ref[1:2] += column_sum(grad_normed)

    start = half_at * mine
    block = pl.BlockSpec((tile, width), lambda i, _: (start + i, 0))
    grad_block = pl.BlockSpec((3, tile, half), lambda i, _: (0, start + i, 0))
    offset = (lambda ref: ref[0] * mine) if half_at == 0 else (lambda ref: 0)
    return call(
        kernel,
        (mine,),
        [grad_block, grad_block, block, block, fixed(1, width), fixed(width, width)]
        + piece_specs(3 * half),
        [image_block(tile, width, offset), fixed(8, width)],
        [struct(((2 - half_at) * mine, tile, width)), struct((8, width), F32)],
        4 * count * width * width,
        8 * count * width + 6 * width * width,
        after,
        None,
        1,
        part=0.3,
    )(side, *in_hbm(grads), in_hbm(rows), in_hbm(grad_middle), gain, order, *in_hbm(pieces))


def fast_shards(
    tokens,
    image_mask,
    out_grad,
    norm1_gain,
    norm1_shift,
    qkv_weight,
    qv_bias,
    out_weight,
    out_bias,
    norm2_gain,
    norm2_shift,
    up_weight,
    up_bias,
    down_weight,
    down_bias,
):
    images, half_len, width = tokens.shape
    mine = images // 2
    half = qkv_weight.shape[2]
    half_hidden = up_weight.shape[1]
    count = 2 * mine * half_len
    me = lax.axis_index("dp")
    side = lax.axis_index("tensor")
    side_array = jnp.concatenate([jnp.stack([side, me]).astype(jnp.int32), image_mask])
    vectors = (norm1_gain, norm1_shift, norm2_gain, norm2_shift, out_bias, down_bias)
    order, gain_one, shift_one, gain_two, shift_two, bias_out, bias_down = setup(
        side_array, [vector.reshape(1, width) for vector in vectors]
    )

    def for_partner(values):
        return over_x(lax.dynamic_slice_in_dim(values, (1 - side) * mine, mine, 0))

    def z_all(values):
        return jnp.concatenate([values] + [over_z(values, step) for step in (1, 2, 3)], axis=0)

    second_group = jnp.concatenate([up_weight, out_weight], axis=1)
    up_all = lax.all_gather(second_group, ("dp", "tensor")).reshape(-1, 2, ROWS, half_hidden + half)
    own = prepare(side_array, tokens, order, gain_one, shift_one, 0)
    final, sum_own = mask_grad(side_array, out_grad, order, 0, after=own[:1])
    tokens_partner = for_partner(tokens)
    first = qkv_weight.reshape(ROWS, 3 * half)
    first_base = late(z_all(first), final)
    biases = jnp.concatenate([qv_bias.reshape(-1), up_bias])
    bias_rows = jnp.pad(biases, (0, 16 * 3 * half - biases.size)).reshape(16, 3 * half)

    def split_bias(bias):
        bias = bias.astype(F32)
        parts = jnp.stack([bias[:half], jnp.zeros((half,), F32), bias[half : 2 * half]])
        return parts[:, None], bias[None, 2 * half :]

    rows, normed = prepare(
        side_array, tokens_partner, order, gain_one, shift_one, 1, own, after=[first_base]
    )
    first_x = over_x(jnp.concatenate([first_base, bias_rows], axis=0))
    first_y = over_y(first_base)
    first_xy = over_y(late(first_x, first_y))
    first_far = [over_core(jnp.stack(late([first_base, first_y], first_x, normed)))]
    biases = [split_bias(biases), split_bias(first_x[4 * ROWS :].reshape(-1)[: biases.size])]
    heads_shape = (3, 2, mine, half_len, half)
    projected, contexts, kept = [None, None], [None, None], [None, None]
    projected[0] = project(normed, [first_base, first_y] + first_far, biases[0][0]).reshape(heads_shape)
    begun = attend(projected[0], 0, 1, lanes=128)
    first_far += [over_core(jnp.stack(late([first_x, first_xy], begun[0])))]
    first_pieces = [first_base, first_x, first_y, first_xy] + first_far
    contexts[0], *kept[0] = attend(projected[0], 1, 2, begun, lanes=128)
    grad_partner = for_partner(late(out_grad, first_x))
    projected[1] = project(
        normed, [first_x, first_xy] + first_far[1:], biases[1][0], after=[contexts[0]]
    ).reshape(heads_shape)
    down_all = lax.all_gather(late(down_weight, up_all, contexts[0]), ("dp", "tensor"))
    down_all = down_all.reshape(-1, 2, ROWS, half_hidden)
    contexts[1], *kept[1] = attend(projected[1], 0, 2)
    contexts = [values.reshape(count, half) for values in contexts]
    middle, second = add_branch(side_array, contexts, rows, up_all, bias_out, gain_two, shift_two)
    actives, slopes = [None, None], [None, None]
    actives[0], slopes[0] = feed_up(side_array, 0, second, up_all, biases[0][1])
    final, sum_partner = mask_grad(side_array, grad_partner, order, 1, final, after=[actives[0]])
    actives[1], slopes[1] = feed_up(side_array, 1, second, up_all, biases[1][1], after=[final])

    down_near, down_next, down_far, down_last = sums_down(final, actives)
    grads_sums = gate_back(side_array, final, slopes, down_all, after=[down_near])
    grads, sum_hidden = grads_sums[:2], grads_sums[2:]
    (down_sent,) = combine([down_next, over_core(down_last)], 1, after=grads[:1])
    down_sent_y = over_y(down_sent)
    up_near, up_next, up_far_sums, up_last = sums_up(second, grads, after=[down_sent])
    grad_middle, branch, *grad_contexts, sums_two = second_back(
        side_array, grads, up_all, middle, final, gain_two, after=[up_near]
    )
    (up_sent,) = combine([up_next, over_core(up_last)], 1, after=[branch])
    up_sent_x = over_x(up_sent)
    down_far = over_core(late(down_far, up_sent))

    def heads_back(x_at, after):
        grad_context = grad_contexts[x_at].reshape(2, mine, half_len, half)
        grad, sums = attend_back(
            projected[x_at], grad_context, contexts[x_at].reshape(grad_context.shape), *kept[x_at], after=after
        )
        return grad.reshape(3, count, half), jnp.sum(sums, axis=0)

    grads_qkv, sums_qkv = [None, None], [None, None]
    grads_qkv[1], sums_qkv[1] = heads_back(1, [up_sent])
    down_sums = combine([down_near, down_far, down_sent_y], 2, after=[grads_qkv[1]])
    down_sent_x = over_x(down_sums[1])
    high_near, high_next, high_far, high_last = sums_first(
        normed, branch, grads_qkv[1], contexts[1], after=down_sums[:1]
    )
    up_far_sums = over_core(late(up_far_sums, high_near))
    out_send = feed_down(side_array, 2, 4, actives, middle, down_all, bias_down, order, after=[high_near])
    (high_sent,) = combine([high_next, over_core(high_last)], 1, after=[out_send])
    high_sent_y = over_y(high_sent)
    up_sums = combine([up_near, up_far_sums, up_sent_x], 2, after=[high_sent])
    up_sent_y = over_y(up_sums[1])
    high_far = over_core(late(high_far, up_sums[0]))
    out_partner = over_x(late(out_send, up_sums[0]))
    grads_qkv[0], sums_qkv[0] = heads_back(0, up_sums[:1])
    down_sums = combine([down_sums[0], down_sent_x], 2, after=[high_far, grads_qkv[0]])
    down_sent_z = over_z(down_sums[1], 2)
    low_near, low_next, low_far, low_last = sums_first(
        normed, branch, grads_qkv[0], contexts[0], after=down_sums[:1]
    )
    (high,) = combine([high_near, high_far, high_sent_y], 1, after=[low_near])
    high_x = over_x(high)
    (low_sent,) = combine([low_next, over_core(low_last)], 1, after=[high])
    low_sent_y = over_y(low_sent)
    send, sums_partner = first_back(
        side_array, 1, grads_qkv, first_pieces, rows, grad_middle, gain_one, order, after=[low_sent]
    )
    up_sums = combine([up_sums[0], up_sent_y], 2, after=[send])
    up_sent_z = over_z(up_sums[1], 2)
    down_sums = combine([down_sums[0], down_sent_z], 2, after=[up_sums[0], out_partner])
    down_sent_z = over_z(down_sums[1], 1)
    low_far = over_core(late(low_far, up_sums[0]))
    full, sums_own = first_back(
        side_array, 0, grads_qkv, first_pieces, rows, grad_middle, gain_one, order, after=down_sums[:1]
    )
    low = combine([low_near, low_far, low_sent_y, high_x], 4, after=[full])
    up_sums = combine([up_sums[0], up_sent_z], 2, after=low[:1])
    sums = jnp.concatenate(
        [(sums_own + sums_partner)[:2], sums_two[2:3], sums_two[:2], sum_own + sum_partner], axis=0
    )
    sums = jnp.einsum("td,od->to", sums, order.astype(F32), precision=lax.Precision.HIGHEST)
    halves = [
        jnp.concatenate([sums_qkv[x_at].reshape(-1), sum_hidden[x_at][0]]) for x_at in range(2)
    ]
    small = late(jnp.concatenate([halves[0], sums.reshape(-1), halves[1]]), low[0])
    small = small + over_core(small)
    small = late(small + over_y(small), up_sums[0])
    halves_size = 2 * half + half_hidden
    small_x = over_x(jnp.concatenate([small[-halves_size:], small[halves_size:-halves_size]]))
    small = small[:-halves_size] + small_x
    height = 8
    small_rows = jnp.pad(small, (0, height * half_hidden - small.size)).reshape(height, half_hidden)
    small_top = small_rows.astype(BF16)
    small_rows = jnp.concatenate([small_top, (small_rows - small_top.astype(F32)).astype(BF16)], axis=0)

    near_z = over_z(jnp.concatenate([low[1], up_sums[1], small_rows], axis=0), 1)
    middle_z = over_z(jnp.concatenate([low[2], small_rows], axis=0), 2)
    far_z = over_z(jnp.concatenate([low[3], small_rows], axis=0), 3)
    send_x = over_x(late(send, low[0]))
    out_full = feed_down(
        side_array, 0, 2, actives, middle, down_all, bias_down, order, after=[low[0], small_rows]
    )
    (grad_down,) = combine([down_sums[0], down_sent_z], 1, F32, after=[out_full])
    block_out = lax.dynamic_update_slice_in_dim(out_full, out_partner, (1 - side) * mine, 0)
    tokens_grad = lax.dynamic_update_slice_in_dim(full, send_x, (1 - side) * mine, 0)
    grad_qkv, grad_out, grad_up, sums = finish(
        low[0], up_sums[0], small_rows, near_z, middle_z, far_z, after=[block_out, tokens_grad]
    )
    sums = sums.reshape(-1)
    halves = sums[:halves_size]
    sums = sums[halves_size : halves_size + 6 * width].reshape(6, width)
    return (
        block_out,
        tokens_grad,
        sums[0],
        sums[1],
        grad_qkv.reshape(ROWS, 3, half),
        halves[: 2 * half].reshape(2, half),
        grad_out,
        sums[2],
        sums[3],
        sums[4],
        grad_up,
        halves[2 * half :],
        grad_down,
        sums[5],
    )


def solution(mesh):
    in_specs = (
        P("dp", "tensor", None),
        P("dp"),
        P("dp", "tensor", None),
        P(),
        P(),
        P("dp", None, "tensor"),
        P(None, "tensor"),
        P("dp", "tensor"),
        P(),
        P(),
        P(),
        P("dp", "tensor"),
        P("tensor"),
        P("dp", "tensor"),
        P(),
    )
    out_specs = (
        P("dp", "tensor", None),
        P("dp", "tensor", None),
        P(),
        P(),
        P("dp", None, "tensor"),
        P(None, "tensor"),
        P("dp", "tensor"),
        P(),
        P(),
        P(),
        P("dp", "tensor"),
        P("tensor"),
        P("dp", "tensor"),
        P(),
    )
    small_slice = mesh.shape["dp"] == 16 and mesh.shape["tensor"] == 2
    shards = fast_shards if small_slice else general_shards
    return jax.shard_map(shards, mesh=mesh, in_specs=in_specs, out_specs=out_specs, check_vma=False)
```

```python
import jax
import jax.numpy as jnp
from jax import lax
from jax.experimental import pallas as pl
from jax.experimental.pallas import tpu as pltpu
from jax.sharding import PartitionSpec as P

HDIM = 64
MICRO = 2


def mixed(form, left, right):
    return jnp.einsum(form, left, right, preferred_element_type=jnp.float32)


def normalize(values, gain, shift):
    mean_val = jnp.mean(values, axis=-1, keepdims=True)
    centered = values - mean_val
    inv_std = lax.rsqrt(jnp.mean(centered * centered, axis=-1, keepdims=True) + 1e-05)
    unit_val = centered * inv_std
    return (unit_val * gain + shift, unit_val, inv_std)


def normalize_back(grad_in, unit_val, inv_std, gain):
    scaled = grad_in * gain
    return inv_std * (
        scaled
        - jnp.mean(scaled, axis=-1, keepdims=True)
        - unit_val * jnp.mean(scaled * unit_val, axis=-1, keepdims=True)
    )


def token_sum(values):
    return jnp.sum(values, axis=(0, 1))


def general_shards(
    tokens,
    image_mask,
    out_grad,
    norm1_gain,
    norm1_shift,
    qkv_weight,
    qv_bias,
    out_weight,
    out_bias,
    norm2_gain,
    norm2_shift,
    up_weight,
    up_bias,
    down_weight,
    down_bias,
):
    images_here = tokens.shape[0] // MICRO
    full_width = norm1_gain.shape[0]
    local_width = qkv_weight.shape[2]
    local_hidden = up_weight.shape[1]
    local_heads = local_width // HDIM
    score_scale = HDIM ** (-0.5)
    gain_one = norm1_gain.astype(jnp.float32)
    shift_one = norm1_shift.astype(jnp.float32)
    gain_two = norm2_gain.astype(jnp.float32)
    shift_two = norm2_shift.astype(jnp.float32)
    bias_pair = qv_bias.astype(jnp.float32)
    grad_qkv = jnp.zeros((full_width, 3, local_width), jnp.float32)
    grad_out = jnp.zeros((full_width, local_width), jnp.float32)
    grad_up = jnp.zeros((full_width, local_hidden), jnp.float32)
    grad_down = jnp.zeros((full_width, local_hidden), jnp.float32)
    grad_gain_one = jnp.zeros((full_width,), jnp.float32)
    grad_shift_one = jnp.zeros((full_width,), jnp.float32)
    grad_gain_two = jnp.zeros((full_width,), jnp.float32)
    grad_shift_two = jnp.zeros((full_width,), jnp.float32)
    grad_out_bias = jnp.zeros((full_width,), jnp.float32)
    grad_down_bias = jnp.zeros((full_width,), jnp.float32)
    grad_pair = jnp.zeros((2, local_width), jnp.float32)
    grad_up_bias = jnp.zeros((local_hidden,), jnp.float32)
    outputs = []
    input_grads = []
    for micro_index in range(MICRO):
        first_image = micro_index * images_here
        block_rows = tokens[first_image : first_image + images_here].astype(jnp.float32)
        keep_mask = image_mask[first_image : first_image + images_here].astype(jnp.float32)[
            :, None, None
        ]
        fwd_weights = (
            lax.all_gather(qkv_weight, "dp", axis=0, tiled=True),
            lax.all_gather(out_weight, "dp", axis=0, tiled=True),
            lax.all_gather(up_weight, "dp", axis=0, tiled=True),
            lax.all_gather(down_weight, "dp", axis=0, tiled=True),
        )
        qkv_full, out_full, up_full, down_full = fwd_weights
        normed, unit_one, inv_one = normalize(block_rows, gain_one, shift_one)
        normed_full = lax.all_gather(normed.astype(jnp.bfloat16), "tensor", axis=1, tiled=True)
        seq_len = normed_full.shape[1]
        head_shape = (images_here, seq_len, local_heads, HDIM)
        projected = mixed("isd,dcf->iscf", normed_full, qkv_full)
        queries = (projected[:, :, 0] + bias_pair[0]).astype(jnp.bfloat16).reshape(head_shape)
        key_rows = projected[:, :, 1].astype(jnp.bfloat16).reshape(head_shape)
        value_rows = (projected[:, :, 2] + bias_pair[1]).astype(jnp.bfloat16).reshape(head_shape)
        scores = mixed("iqhe,ikhe->ihqk", queries, key_rows) * score_scale
        row_top = jnp.max(scores, axis=-1, keepdims=True)
        raw_weights = jnp.exp(scores - row_top)
        row_total = jnp.sum(raw_weights, axis=-1, keepdims=True)
        log_total = row_top + jnp.log(row_total)
        probs = (raw_weights / row_total).astype(jnp.bfloat16)
        context = mixed("ihqk,ikhe->iqhe", probs, value_rows).astype(jnp.bfloat16)
        context = context.reshape(images_here, seq_len, local_width)
        attn_terms = mixed("isf,of->iso", context, out_full)
        branch = lax.psum_scatter(
            attn_terms, "tensor", scatter_dimension=1, tiled=True
        ) + out_bias.astype(jnp.float32)
        middle = block_rows + branch
        second, unit_two, inv_two = normalize(middle, gain_two, shift_two)
        second_full = lax.all_gather(second.astype(jnp.bfloat16), "tensor", axis=1, tiled=True)
        hidden = mixed("isd,df->isf", second_full, up_full) + up_bias.astype(jnp.float32)
        gate_sig = jax.nn.sigmoid(1.702 * hidden)
        active = (hidden * gate_sig).astype(jnp.bfloat16)
        feed_terms = mixed("isf,of->iso", active, down_full)
        feed_out = lax.psum_scatter(
            feed_terms.astype(jnp.bfloat16), "tensor", scatter_dimension=1, tiled=True
        ).astype(jnp.float32) + down_bias.astype(jnp.float32)
        outputs.append(((middle + feed_out) * keep_mask).astype(jnp.bfloat16))
        back_weights = (
            lax.all_gather(qkv_weight, "dp", axis=0, tiled=True),
            lax.all_gather(out_weight, "dp", axis=0, tiled=True),
            lax.all_gather(up_weight, "dp", axis=0, tiled=True),
            lax.all_gather(down_weight, "dp", axis=0, tiled=True),
        )
        qkv_back, out_back, up_back, down_back = back_weights
        grad_final = (
            out_grad[first_image : first_image + images_here].astype(jnp.float32) * keep_mask
        )
        grad_down_bias = grad_down_bias + token_sum(grad_final)
        final_full = lax.all_gather(grad_final.astype(jnp.bfloat16), "tensor", axis=1, tiled=True)
        grad_down = grad_down + mixed("iso,isf->of", final_full, active)
        grad_active = mixed("iso,of->isf", final_full, down_back)
        grad_hidden = (
            grad_active * (gate_sig + 1.702 * hidden * gate_sig * (1.0 - gate_sig))
        ).astype(jnp.bfloat16)
        grad_up_bias = grad_up_bias + token_sum(grad_hidden.astype(jnp.float32))
        grad_up = grad_up + mixed("isd,isf->df", second_full, grad_hidden)
        second_terms = mixed("isf,df->isd", grad_hidden, up_back)
        grad_second = lax.psum_scatter(second_terms, "tensor", scatter_dimension=1, tiled=True)
        grad_gain_two = grad_gain_two + token_sum(grad_second * unit_two)
        grad_shift_two = grad_shift_two + token_sum(grad_second)
        grad_middle = grad_final + normalize_back(grad_second, unit_two, inv_two, gain_two)
        grad_branch = grad_middle.astype(jnp.bfloat16)
        grad_out_bias = grad_out_bias + token_sum(grad_branch.astype(jnp.float32))
        branch_full = lax.all_gather(grad_branch, "tensor", axis=1, tiled=True)
        grad_out = grad_out + mixed("iso,isf->of", branch_full, context)
        grad_context = (
            mixed("iso,of->isf", branch_full, out_back).astype(jnp.bfloat16).reshape(head_shape)
        )
        again = mixed("iqhe,ikhe->ihqk", queries, key_rows) * score_scale
        soft_again = jnp.exp(again - log_total)
        probs_again = soft_again.astype(jnp.bfloat16)
        grad_values = mixed("ihqk,iqhe->ikhe", probs_again, grad_context)
        grad_soft = mixed("iqhe,ikhe->ihqk", grad_context, value_rows)
        grad_scores = (
            soft_again * (grad_soft - jnp.sum(grad_soft * soft_again, axis=-1, keepdims=True))
        ).astype(jnp.bfloat16)
        grad_queries = mixed("ihqk,ikhe->iqhe", grad_scores, key_rows) * score_scale
        grad_keys = mixed("ihqk,iqhe->ikhe", grad_scores, queries) * score_scale
        flat_shape = (images_here, seq_len, local_width)
        grad_projected = jnp.stack(
            (
                grad_queries.reshape(flat_shape),
                grad_keys.reshape(flat_shape),
                grad_values.reshape(flat_shape),
            ),
            axis=2,
        ).astype(jnp.bfloat16)
        pair_terms = grad_projected.astype(jnp.float32)
        grad_pair = grad_pair + jnp.stack(
            (token_sum(pair_terms[:, :, 0]), token_sum(pair_terms[:, :, 2])), axis=0
        )
        grad_qkv = grad_qkv + mixed("isd,iscf->dcf", normed_full, grad_projected)
        normed_terms = mixed("iscf,dcf->isd", grad_projected, qkv_back)
        grad_normed = lax.psum_scatter(
            normed_terms.astype(jnp.bfloat16), "tensor", scatter_dimension=1, tiled=True
        ).astype(jnp.float32)
        grad_gain_one = grad_gain_one + token_sum(grad_normed * unit_one)
        grad_shift_one = grad_shift_one + token_sum(grad_normed)
        grad_tokens = grad_middle + normalize_back(grad_normed, unit_one, inv_one, gain_one)
        input_grads.append(grad_tokens.astype(jnp.bfloat16))
    grad_qkv, grad_out, grad_up, grad_down = (
        lax.psum_scatter(
            grad_qkv.astype(jnp.bfloat16), "dp", scatter_dimension=0, tiled=True
        ).astype(jnp.float32),
        lax.psum_scatter(
            grad_out.astype(jnp.bfloat16), "dp", scatter_dimension=0, tiled=True
        ).astype(jnp.float32),
        lax.psum_scatter(
            grad_up.astype(jnp.bfloat16), "dp", scatter_dimension=0, tiled=True
        ).astype(jnp.float32),
        lax.psum_scatter(
            grad_down.astype(jnp.bfloat16), "dp", scatter_dimension=0, tiled=True
        ).astype(jnp.float32),
    )
    grad_gain_one, grad_shift_one, grad_gain_two, grad_shift_two, grad_out_bias, grad_down_bias = (
        lax.psum(
            (
                grad_gain_one,
                grad_shift_one,
                grad_gain_two,
                grad_shift_two,
                grad_out_bias,
                grad_down_bias,
            ),
            ("dp", "tensor"),
        )
    )
    grad_pair, grad_up_bias = lax.psum((grad_pair, grad_up_bias), "dp")
    block_out = jnp.concatenate(outputs, axis=0)
    tokens_grad = jnp.concatenate(input_grads, axis=0)
    return (
        block_out,
        tokens_grad,
        grad_gain_one,
        grad_shift_one,
        grad_qkv,
        grad_pair,
        grad_out,
        grad_out_bias,
        grad_gain_two,
        grad_shift_two,
        grad_up,
        grad_up_bias,
        grad_down,
        grad_down_bias,
    )


ROWS = 64
PART = 256
VMEM_BYTES = 27 * 1024 * 1024
COST_PART = 0.6
FORWARD_PART = 1.0
LOG2_E = 1.4426950408889634
BF16 = jnp.bfloat16
F32 = jnp.float32


def swap(values, axis_name, flip):
    count = lax.axis_size(axis_name)
    return lax.ppermute(values, axis_name, [(place, place ^ flip) for place in range(count)])


def over_core(values):
    return swap(values, "dp", 1)


def over_y(values):
    return swap(values, "dp", 2)


def over_z(values, step):
    return swap(values, "dp", 4 * step)


def over_x(values):
    return swap(values, "tensor", 1)


def late(values, *marks):
    return lax.optimization_barrier((values, *marks))[0]


def dot_nn(left, right):
    return lax.dot_general(left, right, (((1,), (0,)), ((), ())), preferred_element_type=F32)


def dot_nt(left, right):
    return lax.dot_general(left, right, (((1,), (1,)), ((), ())), preferred_element_type=F32)


def dot_tn(left, right):
    return lax.dot_general(left, right, (((0,), (0,)), ((), ())), preferred_element_type=F32)


def call(
    kernel, grid, in_specs, out_specs, out_shape, flops, moved, after=(), aliases=None, scalars=0, part=None
):
    given, waits = scalars + len(in_specs), len(after)
    part = COST_PART if part is None else part

    def run(*refs):
        kernel(*refs[:given], *refs[given + waits :])

    function = pl.pallas_call(
        run,
        grid_spec=pltpu.PrefetchScalarGridSpec(
            num_scalar_prefetch=scalars,
            grid=grid,
            in_specs=list(in_specs) + [pl.BlockSpec(memory_space=pl.ANY)] * waits,
            out_specs=out_specs,
        ),
        out_shape=out_shape,
        input_output_aliases=aliases or {},
        compiler_params=pltpu.CompilerParams(vmem_limit_bytes=VMEM_BYTES),
        cost_estimate=pl.CostEstimate(
            flops=int(flops * part), bytes_accessed=int(moved * part), transcendentals=0
        ),
    )
    return lambda *arrays: function(*arrays, *after)


def fixed(*shape, at=None):
    place = at or (0,) * len(shape)
    return pl.BlockSpec(shape, lambda *_: place, pipeline_mode=pl.Buffered(1))


def far_list(near, far):
    return list(near) + [far[last].at[y_at] for y_at in range(2) for last in range(2)]


def piece_specs(columns, at=0):
    return [fixed(PART, columns, at=(0, at))] * 4 + [fixed(2, PART, columns, at=(0, 0, at))] * 2


def piece_tiles(tile, near=4, far=2):
    return [pl.BlockSpec((PART, tile), lambda j: (0, j))] * near + [
        pl.BlockSpec((2, PART, tile), lambda j: (0, 0, j))
    ] * far


def gathered_specs(columns, halves=(0, 1), at=None):
    def spec(block, x_at):
        core, y_at, z_at = block // 8, (block // 4) % 2, block % 4
        slab = z_at * 4 + y_at * 2 + core

        def place(j, *refs):
            where = refs[-1]
            row = jnp.bitwise_xor(where[1], slab), jnp.bitwise_xor(where[0], x_at)
            return (*row, 0, j if at is None else at)

        mode = {} if at is None else {"pipeline_mode": pl.Buffered(1)}
        return pl.BlockSpec((1, 1, ROWS, columns), place, **mode)

    return [spec(block, x_at) for block in range(16) for x_at in halves]


def joined(refs, first, last, step=1, offset=0):
    return jnp.concatenate([refs[step * block + offset][0, 0] for block in range(first, last)], axis=0)


def struct(shape, dtype=BF16):
    return jax.ShapeDtypeStruct(shape, dtype)


def outer(shape, dtype=BF16):
    return pltpu.HBM(shape, dtype)


def in_hbm(values):
    if isinstance(values, (list, tuple)):
        return [in_hbm(part) for part in values]
    return pltpu.with_memory_space_constraint(values, pltpu.HBM)


ANYWHERE = pl.BlockSpec(memory_space=pl.ANY)


def normal_parts(values):
    mean_val = jnp.mean(values, axis=-1, keepdims=True)
    centered = values - mean_val
    inv_std = lax.rsqrt(jnp.mean(centered * centered, axis=-1, keepdims=True) + 1e-05)
    return centered * inv_std, inv_std


def column_sum(values):
    return jnp.sum(values, axis=0, keepdims=True)


def combine(arrays, pieces, dtype=BF16, tile=1024, after=()):
    columns = arrays[0].shape[-1]
    rows = arrays[0].size // columns // pieces
    arrays = [values.reshape(pieces, rows, columns) for values in arrays]
    given = len(arrays)

    def kernel(*refs):
        for at in range(pieces):
            parts = [ref[at].astype(F32) for ref in refs[:given]]
            while len(parts) > 1:
                parts = [sum(parts[start : start + 2]) for start in range(0, len(parts), 2)]
            refs[given + at][...] = parts[0].astype(dtype)

    return call(
        kernel,
        (columns // tile,),
        [pl.BlockSpec((pieces, rows, tile), lambda j: (0, 0, j))] * given,
        [pl.BlockSpec((rows, tile), lambda j: (0, j))] * pieces,
        [outer((rows, columns), dtype)] * pieces,
        0,
        2 * pieces * rows * columns * (given + 1),
        after,
    )(*arrays)


def finish(low_near, up_near, small, near, middle, far, after=()):
    rows, columns = low_near.shape
    split = columns * 3 // 4
    height = small.shape[0] // 2

    def kernel(low_ref, up_ref, small_ref, near_ref, middle_ref, far_ref, qkv_ref, out_ref, up_out_ref, sum_ref):
        def rows_of(ref, start):
            return ref[start : start + rows, :].astype(F32)

        def vectors_of(ref, start):
            values = ref[start : start + 2 * height, :].astype(F32)
            return values[:height] + values[height:]

        low = (rows_of(low_ref, 0) + rows_of(near_ref, 0)) + (rows_of(middle_ref, 0) + rows_of(far_ref, 0))
        qkv_ref[...] = low[:, :split]
        out_ref[...] = low[:, split:]
        up_out_ref[...] = rows_of(up_ref, 0) + rows_of(near_ref, rows)
        sum_ref[...] = (vectors_of(small_ref, 0) + vectors_of(near_ref, 2 * rows)) + (
            vectors_of(middle_ref, rows) + vectors_of(far_ref, rows)
        )

    given = [low_near, up_near, small, near, middle, far]
    return call(
        kernel,
        (1,),
        [fixed(*values.shape) for values in given],
        [fixed(rows, split), fixed(rows, columns - split), fixed(rows, columns), fixed(height, columns)],
        [
            struct((rows, split), F32),
            struct((rows, columns - split), F32),
            struct((rows, columns), F32),
            struct((height, columns), F32),
        ],
        0,
        20 * rows * columns,
        after,
    )(*given)


def first_step():
    return pl.program_id(0) == 0


def setup(places, vectors, after=()):
    width = vectors[0].shape[1]
    given = len(vectors)

    def kernel(place_ref, *refs):
        order_ref = refs[given]
        source = lax.broadcasted_iota(jnp.int32, (width, width), 0)
        target = lax.broadcasted_iota(jnp.int32, (width, width), 1)
        at = target // ROWS
        z_rel, y_rel, core_rel = at % 4, (at // 4) % 2, at // 8
        place = (z_rel * 4 + y_rel * 2 + core_rel) ^ place_ref[1]
        hit = source == place * ROWS + target % ROWS
        order = jnp.where(hit, 1.0, 0.0).astype(BF16)
        order_ref[...] = order
        rows = jnp.concatenate([ref[...].astype(F32) for ref in refs[:given]] + [jnp.zeros((8 - given, width), F32)], axis=0)
        moved = dot_nn(rows.astype(BF16), order)
        for vector_at in range(given):
            refs[given + 1 + vector_at][...] = moved[vector_at : vector_at + 1]

    row = fixed(1, width)
    return call(
        kernel,
        (1,),
        [row] * given,
        [fixed(width, width)] + [row] * given,
        [struct((width, width))] + [struct((1, width), F32)] * given,
        16 * width * width,
        2 * width * width,
        after,
        None,
        1,
        part=FORWARD_PART,
    )(places, *vectors)


def image_block(height, width, offset):
    return pl.BlockSpec((1, height, width), lambda i, side: (offset(side) + i, 0, 0))


def prepare(side, images, order, gain, shift, half_at, before=None, after=()):
    _, height, width = images.shape
    mine = 2

    def kernel(side_ref, raw_ref, order_ref, gain_ref, shift_ref, *refs):
        rows_ref, norm_ref = refs[-2:]
        rows = dot_nn(raw_ref[0], order_ref[...])
        rows_ref[...] = rows.astype(BF16)
        unit, _ = normal_parts(rows)
        norm_ref[...] = (unit * gain_ref[...] + shift_ref[...]).astype(BF16)

    offset = (lambda side_ref: side_ref[0] * mine) if half_at == 0 else (lambda side_ref: 0)
    out = pl.BlockSpec((height, width), lambda i, _: (half_at * mine + i, 0))
    old = () if before is None else before
    return call(
        kernel,
        (mine,),
        [image_block(height, width, offset), fixed(width, width), fixed(1, width), fixed(1, width)]
        + [ANYWHERE] * len(old),
        [out, out],
        [outer((2 * mine * height, width))] * 2,
        2 * mine * height * width * width,
        6 * mine * height * width,
        after,
        {5: 0, 6: 1} if old else None,
        1,
        part=FORWARD_PART,
    )(side, images, order, gain, shift, *old)


def mask_grad(side, images, order, half_at, before=None, after=()):
    _, height, width = images.shape
    mine = 2

    def kernel(side_ref, raw_ref, order_ref, *refs):
        final_ref, sum_ref = refs[-2:]
        keep = side_ref[2 + side_ref[0] * mine + pl.program_id(0)].astype(F32)
        final = dot_nn(raw_ref[0], order_ref[...]) * keep
        final_ref[...] = final.astype(BF16)

        @pl.when(first_step())
        def _():
            sum_ref[...] = jnp.zeros_like(sum_ref)

        sum_ref[...] += column_sum(final)

    offset = (lambda side_ref: side_ref[0] * mine) if half_at == 0 else (lambda side_ref: 0)
    old = () if before is None else (before,)
    out = pl.BlockSpec((height, width), lambda i, _: (half_at * mine + i, 0))
    return call(
        kernel,
        (mine,),
        [image_block(height, width, offset), fixed(width, width)] + [ANYWHERE] * len(old),
        [out, fixed(1, width)],
        [struct((2 * mine * height, width)), struct((1, width), F32)],
        2 * mine * height * width * width,
        6 * mine * height * width,
        after,
        {3: 0} if old else None,
        1,
        part=FORWARD_PART,
    )(side, images, order, *old)


def project(normed, parts, bias, after=()):
    count, width = normed.shape
    half = bias.shape[-1]

    def kernel(norm_ref, bias_ref, *refs):
        weight = jnp.concatenate([refs[0][...], refs[1][...], refs[2][0], refs[2][1]], axis=0)
        refs[3][0] = (dot_nn(norm_ref[...], weight) + bias_ref[0]).astype(BF16)

    return call(
        kernel,
        (3,),
        [fixed(count, width), pl.BlockSpec((1, 1, half), lambda j: (j, 0, 0))]
        + piece_tiles(half, 2, 1),
        pl.BlockSpec((1, count, half), lambda j: (j, 0, 0)),
        outer((3, count, half)),
        6 * count * width * half,
        2 * count * (width + 3 * half) + 6 * width * half,
        after,
        part=FORWARD_PART,
    )(normed, bias, *parts)


def attend(projected, first_image, last_image, before=None, lanes=256, after=()):
    _, _, images, half_len, half = projected.shape
    length = 2 * half_len
    per_step = lanes // HDIM
    steps = half // lanes

    def kernel(proj_ref, *refs):
        out_ref, weights_ref, inverse_ref = refs[-3:]
        queries, key_rows, value_rows = (proj_ref[at].reshape(length, lanes) for at in range(3))
        queries, value_rows = queries.T, value_rows.T
        outs, inverses = [], []
        for head in range(per_step):
            part = slice(head * HDIM, (head + 1) * HDIM)
            scores = dot_nn(key_rows[:, part], queries[part])
            top = jnp.max(scores, axis=0, keepdims=True)
            weights = jnp.exp2((scores - top) * (LOG2_E * HDIM**-0.5)).astype(BF16)
            weights_ref[0, head] = weights
            ones = jnp.ones((16, length), BF16)
            sums = dot_nn(jnp.concatenate([value_rows[part], ones], axis=0), weights)
            inverse = 1.0 / sums[HDIM : HDIM + 1]
            outs.append((sums[:HDIM] * inverse).astype(BF16))
            inverses.append(inverse)
        out_ref[...] = jnp.concatenate(outs, axis=0).T.reshape(out_ref.shape)
        inverse_ref[0] = jnp.concatenate(inverses + [jnp.zeros((8 - per_step, length), F32)], axis=0)

    heads = half // HDIM
    old = () if before is None else before
    return call(
        kernel,
        (last_image - first_image, steps),
        [pl.BlockSpec((3, 2, 1, half_len, lanes), lambda i, j: (0, 0, first_image + i, 0, j))]
        + [ANYWHERE] * len(old),
        [
            pl.BlockSpec((2, 1, half_len, lanes), lambda i, j: (0, first_image + i, 0, j)),
            pl.BlockSpec((1, per_step, length, length), lambda i, j: (first_image + i, j, 0, 0)),
            pl.BlockSpec((1, 8, length), lambda i, j: (first_image + i, j, 0)),
        ],
        [
            struct((2, images, half_len, half)),
            outer((images, heads, length, length)),
            struct((images, 8 * steps, length), F32),
        ],
        24 * (last_image - first_image) * heads * length * length * HDIM,
        (last_image - first_image) * heads * length * length * 2,
        after,
        {1: 0, 2: 1, 3: 2} if old else None,
        part=FORWARD_PART,
    )(in_hbm(projected), *old)


def attend_back(projected, grad_context, context, weights, inverse, after=()):
    _, _, images, half_len, half = projected.shape
    length = 2 * half_len
    steps = inverse.shape[1] // 8
    lanes = half // steps
    per_step = lanes // HDIM
    scale = HDIM**-0.5

    def kernel(proj_ref, grad_ref, context_ref, weights_ref, inverse_ref, out_ref, sum_ref):
        queries, key_rows, value_rows = (proj_ref[at].reshape(length, lanes) for at in range(3))
        queries, key_rows = queries.T, key_rows.T
        grads = grad_ref[...].reshape(length, lanes).T.astype(F32)
        contexts = context_ref[...].reshape(length, lanes).T.astype(F32)
        found = ([], [], [])
        for head in range(per_step):
            part = slice(head * HDIM, (head + 1) * HDIM)
            weights = weights_ref[0, head]
            grad = grads[part] * inverse_ref[0, head : head + 1]
            level = jnp.sum(grad * contexts[part], axis=0, keepdims=True)
            grad = grad.astype(BF16)
            found[2].append(dot_nt(grad, weights).astype(BF16))
            grad_soft = dot_nn(value_rows[:, part], grad)
            grad_scores = (weights.astype(F32) * (grad_soft - level)).astype(BF16)
            found[0].append((dot_nn(key_rows[part], grad_scores) * scale).astype(BF16))
            found[1].append((dot_nt(queries[part], grad_scores) * scale).astype(BF16))
        for at in range(3):
            joined = jnp.concatenate(found[at], axis=0).T
            out_ref[at] = joined.reshape(2, 1, half_len, lanes)
            if at != 1:
                sum_ref[0, at // 2 : at // 2 + 1] = column_sum(joined.astype(F32))

    heads = half // HDIM
    block = pl.BlockSpec((3, 2, 1, half_len, lanes), lambda i, j: (0, 0, i, 0, j))
    rows = pl.BlockSpec((2, 1, half_len, lanes), lambda i, j: (0, i, 0, j))
    return call(
        kernel,
        (images, steps),
        [
            block,
            rows,
            rows,
            pl.BlockSpec((1, per_step, length, length), lambda i, j: (i, j, 0, 0)),
            pl.BlockSpec((1, 8, length), lambda i, j: (i, j, 0)),
        ],
        [block, pl.BlockSpec((1, 2, lanes), lambda i, j: (i, 0, j))],
        [struct(projected.shape), struct((images, 2, half), F32)],
        32 * images * heads * length * length * HDIM,
        images * heads * length * length * 2,
        after,
    )(in_hbm(projected), grad_context, context, in_hbm(weights), inverse)


def add_branch(contexts, rows, pieces, bias, gain, shift, tile=576, after=()):
    count, width = rows.shape
    half = width // 2

    def kernel(low_ref, high_ref, rows_ref, bias_ref, gain_ref, shift_ref, *refs):
        parts, (middle_ref, norm_ref) = far_list(refs[:4], refs[4:6]), refs[6:]
        found = []
        for at in range(4):
            found.append(dot_nt(low_ref[...], parts[2 * at][...]) + dot_nt(high_ref[...], parts[2 * at + 1][...]))
        middle = rows_ref[...].astype(F32) + (jnp.concatenate(found, axis=1) + bias_ref[...])
        middle_ref[...] = middle
        unit, _ = normal_parts(middle)
        norm_ref[...] = (unit * gain_ref[...] + shift_ref[...]).astype(BF16)

    block = pl.BlockSpec((tile, width), lambda i: (i, 0))
    half_block = pl.BlockSpec((tile, half), lambda i: (i, 0))
    return call(
        kernel,
        (count // tile,),
        [half_block, half_block, block] + [fixed(1, width)] * 3 + piece_specs(half, 3),
        [block, block],
        [outer((count, width), F32), struct((count, width))],
        2 * count * width * width,
        10 * count * width + 2 * width * width,
        after,
        part=FORWARD_PART,
    )(*contexts, rows, bias, gain, shift, *pieces)


def feed_up(places, x_at, second, gathered, bias, tile=512, after=()):
    count, width = second.shape
    columns = bias.shape[-1]

    def kernel(place_ref, second_ref, bias_ref, *refs):
        hidden = dot_nn(second_ref[...], joined(refs, 0, 16)) + bias_ref[...]
        gate = 0.5 + 0.5 * jnp.tanh(0.851 * hidden)
        refs[16][...] = (hidden * gate).astype(BF16)
        refs[17][...] = (gate * (1.0 + 1.702 * hidden * (1.0 - gate))).astype(BF16)

    block = pl.BlockSpec((count, tile), lambda j, _: (0, j))
    return call(
        kernel,
        (columns // tile,),
        [fixed(count, width), pl.BlockSpec((1, tile), lambda j, _: (0, j))] + gathered_specs(tile, (x_at,)),
        [block, block],
        [outer((count, columns))] * 2,
        2 * count * width * columns,
        2 * count * (width + 2 * columns) + 2 * width * columns,
        after,
        None,
        1,
        part=FORWARD_PART,
    )(places, second, bias, *[gathered] * 16)


def feed_down(side, first_tile, last_tile, actives, middle, gathered, bias, order, before=None, tile=288, after=()):
    count, columns = actives[0].shape
    width = middle.shape[1]
    mine = count // tile // 2
    half_at = first_tile // mine
    old = () if before is None else (before,)

    def kernel(side_ref, low_ref, high_ref, middle_ref, bias_ref, order_ref, *refs):
        keep = side_ref[2 + side_ref[0] * mine + first_tile % mine + pl.program_id(0)].astype(F32)
        out_ref = refs[-1]
        feed = dot_nt(low_ref[...], joined(refs, 0, 16, 2, 0)) + dot_nt(high_ref[...], joined(refs, 0, 16, 2, 1))
        out = ((middle_ref[...] + (feed + bias_ref[...])) * keep).astype(BF16)
        out_ref[0] = dot_nt(out, order_ref[...]).astype(BF16)

    hidden = pl.BlockSpec((tile, columns), lambda i, _: (first_tile + i, 0))
    offset = (lambda ref: ref[0] * mine + first_tile) if half_at == 0 else (lambda ref: first_tile - mine)

    return call(
        kernel,
        (last_tile - first_tile,),
        [
            hidden,
            hidden,
            pl.BlockSpec((tile, width), lambda i, _: (first_tile + i, 0)),
            fixed(1, width),
            fixed(width, width),
        ]
        + gathered_specs(columns, at=0)
        + [ANYWHERE] * len(old),
        image_block(tile, width, offset),
        struct(((2 - half_at) * mine, tile, width)),
        2 * count * width * columns + count * width * width,
        2 * count * columns + 3 * count * width + 4 * width * columns,
        after,
        {38: 0} if old else None,
        1,
    )(side, *[in_hbm(values) for values in actives], in_hbm(middle), bias, order, *[gathered] * 32, *old)


def gate_back(side, final, slopes, gathered, tile=512, after=()):
    count, width = final.shape
    columns = gathered.shape[-1]

    def kernel(side_ref, final_ref, low_ref, high_ref, *refs):
        outs, sums = refs[32:34], refs[34:36]
        for x_at, slope_ref in enumerate((low_ref, high_ref)):
            weight = joined(refs, 0, 16, 2, x_at)
            grad = (dot_nn(final_ref[...], weight) * slope_ref[...].astype(F32)).astype(BF16)
            outs[x_at][...] = grad
            sums[x_at][...] = column_sum(grad.astype(F32))

    block = pl.BlockSpec((count, tile), lambda j, _: (0, j))
    sum_block = pl.BlockSpec((1, tile), lambda j, _: (0, j))
    return call(
        kernel,
        (columns // tile,),
        [fixed(count, width), block, block] + gathered_specs(tile),
        [block, block, sum_block, sum_block],
        [struct((count, columns))] * 2 + [struct((1, columns), F32)] * 2,
        4 * count * width * columns,
        4 * count * (width + 2 * columns) + 4 * width * columns,
        after,
        None,
        1,
    )(side, in_hbm(final), *in_hbm(slopes), *[in_hbm(gathered)] * 32)


def sums_down(final, actives, tile=512, after=()):
    count, width = final.shape
    columns = actives[0].shape[1]

    def kernel(final_ref, low_ref, high_ref, *outs):
        for x_at, right_ref in enumerate((low_ref, high_ref)):
            for core in range(2):
                for y_at in range(2):
                    start = (2 * core + y_at) * PART
                    part = dot_tn(final_ref[:, start : start + PART], right_ref[...])
                    outs[2 * core + y_at][x_at] = part.astype(BF16)

    right = pl.BlockSpec((count, tile), lambda j: (0, j))
    return call(
        kernel,
        (columns // tile,),
        [fixed(count, width), right, right],
        [pl.BlockSpec((2, PART, tile), lambda j: (0, 0, j))] * 4,
        [outer((2, PART, columns))] * 4,
        4 * count * width * columns,
        4 * count * columns + 2 * count * width + 4 * width * columns,
        after,
    )(final, *[in_hbm(values) for values in actives])


def sums_up(second, grads, tile=512, after=()):
    count, width = second.shape
    columns = grads[0].shape[1]

    def kernel(second_ref, low_ref, high_ref, *outs):
        for x_at, right_ref in enumerate((low_ref, high_ref)):
            for core in range(2):
                for y_at in range(2):
                    start = (2 * core + y_at) * PART
                    part = dot_tn(second_ref[:, start : start + PART], right_ref[...])
                    outs[2 * core + x_at][y_at] = part.astype(BF16)

    right = pl.BlockSpec((count, tile), lambda j: (0, j))
    return call(
        kernel,
        (columns // tile,),
        [fixed(count, width), right, right],
        [pl.BlockSpec((2, PART, tile), lambda j: (0, 0, j))] * 4,
        [outer((2, PART, columns))] * 4,
        4 * count * width * columns,
        4 * count * columns + 2 * count * width + 4 * width * columns,
        after,
    )(second, *grads)


def sums_first(normed, branch, grad_projected, context, after=()):
    count, width = normed.shape
    half = context.shape[1]

    def kernel(norm_ref, branch_ref, grad_ref, context_ref, *outs):
        def work(left_ref, right):
            for core in range(2):
                for y_at in range(2):
                    start = (2 * core + y_at) * PART
                    outs[2 * core + y_at][...] = dot_tn(left_ref[:, start : start + PART], right).astype(BF16)

        @pl.when(pl.program_id(0) < 3)
        def _():
            work(norm_ref, grad_ref[0])

        @pl.when(pl.program_id(0) == 3)
        def _():
            work(branch_ref, context_ref[...])

    left = fixed(count, width)
    return call(
        kernel,
        (4,),
        [left, left, pl.BlockSpec((1, count, half), lambda j: (jnp.minimum(j, 2), 0, 0)), fixed(count, half)],
        [pl.BlockSpec((PART, half), lambda j: (0, j))] * 4,
        [outer((PART, 4 * half))] * 4,
        8 * count * width * half,
        2 * count * (2 * width + 4 * half) + 8 * width * half,
        after,
    )(normed, branch, grad_projected, context)


def second_back(places, grads, gathered, first_pieces, middle, final, gain, tile=576, after=()):
    count, columns = grads[0].shape
    width = middle.shape[1]
    half = width // 2

    def kernel(place_ref, low_ref, high_ref, middle_ref, final_ref, gain_ref, *refs):
        ups, outs = refs[:32], far_list(refs[32:36], refs[36:38])
        grad_ref, branch_ref, context_low_ref, context_high_ref, sum_ref = refs[38:]
        grad_second = dot_nt(low_ref[...], joined(ups, 0, 16, 2, 0)) + dot_nt(high_ref[...], joined(ups, 0, 16, 2, 1))
        unit, inv_std = normal_parts(middle_ref[...])
        grad_middle = final_ref[...].astype(F32) + normalize_back(
            grad_second, unit, inv_std, gain_ref[...]
        )
        branch = grad_middle.astype(BF16)
        grad_ref[...] = grad_middle
        branch_ref[...] = branch
        for x_at, context_ref in enumerate((context_low_ref, context_high_ref)):
            weight = jnp.concatenate([outs[2 * at + x_at][...] for at in range(4)], axis=0)
            context_ref[...] = dot_nn(branch, weight).astype(BF16)

        @pl.when(first_step())
        def _():
            sum_ref[...] = jnp.zeros_like(sum_ref)

        sum_ref[0:1] += column_sum(grad_second * unit)
        sum_ref[1:2] += column_sum(grad_second)
        sum_ref[2:3] += column_sum(branch.astype(F32))

    block = pl.BlockSpec((tile, width), lambda i, _: (i, 0))
    half_block = pl.BlockSpec((tile, half), lambda i, _: (i, 0))
    hidden = pl.BlockSpec((tile, columns), lambda i, _: (i, 0))
    return call(
        kernel,
        (count // tile,),
        [hidden, hidden, block, block, fixed(1, width)]
        + gathered_specs(columns, at=0)
        + piece_specs(half, 3),
        [block, block, half_block, half_block, fixed(8, width)],
        [outer((count, width), F32), struct((count, width))]
        + [struct((count, half))] * 2
        + [struct((8, width), F32)],
        4 * count * width * columns + 2 * count * width * width,
        4 * count * columns + 14 * count * width + 4 * width * columns,
        after,
        None,
        1,
    )(places, *grads, middle, final, gain, *[gathered] * 32, *first_pieces)


def first_back(side, half_at, grads, pieces, rows, grad_middle, gain, order, tile=288, after=()):
    _, count, half = grads[0].shape
    width = rows.shape[1]
    mine = count // tile // 2

    def kernel(side_ref, low_ref, high_ref, rows_ref, middle_ref, gain_ref, order_ref, *refs):
        parts, (out_ref, sum_ref) = far_list(refs[:4], refs[4:6]), refs[6:]
        lefts = [jnp.concatenate([ref[at] for at in range(3)], axis=1) for ref in (low_ref, high_ref)]
        found = []
        for at in range(4):
            found.append(
                dot_nt(lefts[0], parts[2 * at][...]) + dot_nt(lefts[1], parts[2 * at + 1][...])
            )
        grad_normed = jnp.concatenate(found, axis=1)
        unit, inv_std = normal_parts(rows_ref[...].astype(F32))
        out = middle_ref[...] + normalize_back(grad_normed, unit, inv_std, gain_ref[...])
        out_ref[0] = dot_nt(out.astype(BF16), order_ref[...]).astype(BF16)

        @pl.when(first_step())
        def _():
            sum_ref[...] = jnp.zeros_like(sum_ref)

        sum_ref[0:1] += column_sum(grad_normed * unit)
        sum_ref[1:2] += column_sum(grad_normed)

    start = half_at * mine
    block = pl.BlockSpec((tile, width), lambda i, _: (start + i, 0))
    grad_block = pl.BlockSpec((3, tile, half), lambda i, _: (0, start + i, 0))
    offset = (lambda ref: ref[0] * mine) if half_at == 0 else (lambda ref: 0)
    return call(
        kernel,
        (mine,),
        [grad_block, grad_block, block, block, fixed(1, width), fixed(width, width)]
        + piece_specs(3 * half),
        [image_block(tile, width, offset), fixed(8, width)],
        [struct(((2 - half_at) * mine, tile, width)), struct((8, width), F32)],
        4 * count * width * width,
        8 * count * width + 6 * width * width,
        after,
        None,
        1,
        part=0.3,
    )(side, *in_hbm(grads), in_hbm(rows), in_hbm(grad_middle), gain, order, *in_hbm(pieces))


def fast_shards(
    tokens,
    image_mask,
    out_grad,
    norm1_gain,
    norm1_shift,
    qkv_weight,
    qv_bias,
    out_weight,
    out_bias,
    norm2_gain,
    norm2_shift,
    up_weight,
    up_bias,
    down_weight,
    down_bias,
):
    images, half_len, width = tokens.shape
    mine = images // 2
    half = qkv_weight.shape[2]
    half_hidden = up_weight.shape[1]
    count = 2 * mine * half_len
    me = lax.axis_index("dp")
    side = lax.axis_index("tensor")
    side_array = jnp.concatenate([jnp.stack([side, me]).astype(jnp.int32), image_mask])
    vectors = (norm1_gain, norm1_shift, norm2_gain, norm2_shift, out_bias, down_bias)
    order, gain_one, shift_one, gain_two, shift_two, bias_out, bias_down = setup(
        side_array, [vector.reshape(1, width) for vector in vectors]
    )

    def for_partner(values):
        return over_x(lax.dynamic_slice_in_dim(values, (1 - side) * mine, mine, 0))

    def z_all(values):
        return jnp.concatenate([values] + [over_z(values, step) for step in (1, 2, 3)], axis=0)

    up_all = lax.all_gather(up_weight, ("dp", "tensor")).reshape(-1, 2, ROWS, half_hidden)
    own = prepare(side_array, tokens, order, gain_one, shift_one, 0)
    final, sum_own = mask_grad(side_array, out_grad, order, 0, after=own[:1])
    tokens_partner = for_partner(tokens)
    first = jnp.concatenate([qkv_weight.reshape(ROWS, 3 * half), out_weight], axis=1)
    first_base = late(z_all(first), final)
    biases = jnp.concatenate([qv_bias.reshape(-1), up_bias])
    bias_rows = jnp.pad(biases, (0, 16 * 4 * half - biases.size)).reshape(16, 4 * half)

    def split_bias(bias):
        bias = bias.astype(F32)
        parts = jnp.stack([bias[:half], jnp.zeros((half,), F32), bias[half : 2 * half]])
        return parts[:, None], bias[None, 2 * half :]

    rows, normed = prepare(
        side_array, tokens_partner, order, gain_one, shift_one, 1, own, after=[first_base]
    )
    first_x = over_x(jnp.concatenate([first_base, bias_rows], axis=0))
    first_y = over_y(first_base)
    first_xy = over_y(late(first_x, first_y))
    first_far = [over_core(jnp.stack(late([first_base, first_y], first_x, normed)))]
    biases = [split_bias(biases), split_bias(first_x[4 * ROWS :].reshape(-1)[: biases.size])]
    heads_shape = (3, 2, mine, half_len, half)
    projected, contexts, kept = [None, None], [None, None], [None, None]
    projected[0] = project(normed, [first_base, first_y] + first_far, biases[0][0]).reshape(heads_shape)
    begun = attend(projected[0], 0, 1, lanes=128)
    first_far += [over_core(jnp.stack(late([first_x, first_xy], begun[0])))]
    first_pieces = [first_base, first_x, first_y, first_xy] + first_far
    contexts[0], *kept[0] = attend(projected[0], 1, 2, begun, lanes=128)
    grad_partner = for_partner(late(out_grad, first_x))
    projected[1] = project(
        normed, [first_x, first_xy] + first_far[1:], biases[1][0], after=[contexts[0]]
    ).reshape(heads_shape)
    down_all = lax.all_gather(late(down_weight, up_all, contexts[0]), ("dp", "tensor"))
    down_all = down_all.reshape(-1, 2, ROWS, half_hidden)
    contexts[1], *kept[1] = attend(projected[1], 0, 2)
    contexts = [values.reshape(count, half) for values in contexts]
    middle, second = add_branch(contexts, rows, first_pieces, bias_out, gain_two, shift_two)
    actives, slopes = [None, None], [None, None]
    actives[0], slopes[0] = feed_up(side_array, 0, second, up_all, biases[0][1])
    final, sum_partner = mask_grad(side_array, grad_partner, order, 1, final, after=[actives[0]])
    actives[1], slopes[1] = feed_up(side_array, 1, second, up_all, biases[1][1], after=[final])

    down_near, down_next, down_far, down_last = sums_down(final, actives)
    grads_sums = gate_back(side_array, final, slopes, down_all, after=[down_near])
    grads, sum_hidden = grads_sums[:2], grads_sums[2:]
    (down_sent,) = combine([down_next, over_core(down_last)], 1, after=grads[:1])
    down_sent_y = over_y(down_sent)
    up_near, up_next, up_far_sums, up_last = sums_up(second, grads, after=[down_sent])
    grad_middle, branch, *grad_contexts, sums_two = second_back(
        side_array, grads, up_all, first_pieces, middle, final, gain_two, after=[up_near]
    )
    (up_sent,) = combine([up_next, over_core(up_last)], 1, after=[branch])
    up_sent_x = over_x(up_sent)
    down_far = over_core(late(down_far, up_sent))

    def heads_back(x_at, after):
        grad_context = grad_contexts[x_at].reshape(2, mine, half_len, half)
        grad, sums = attend_back(
            projected[x_at], grad_context, contexts[x_at].reshape(grad_context.shape), *kept[x_at], after=after
        )
        return grad.reshape(3, count, half), jnp.sum(sums, axis=0)

    grads_qkv, sums_qkv = [None, None], [None, None]
    grads_qkv[1], sums_qkv[1] = heads_back(1, [up_sent])
    down_sums = combine([down_near, down_far, down_sent_y], 2, after=[grads_qkv[1]])
    down_sent_x = over_x(down_sums[1])
    high_near, high_next, high_far, high_last = sums_first(
        normed, branch, grads_qkv[1], contexts[1], after=down_sums[:1]
    )
    up_far_sums = over_core(late(up_far_sums, high_near))
    out_send = feed_down(side_array, 2, 4, actives, middle, down_all, bias_down, order, after=[high_near])
    (high_sent,) = combine([high_next, over_core(high_last)], 1, after=[out_send])
    high_sent_y = over_y(high_sent)
    up_sums = combine([up_near, up_far_sums, up_sent_x], 2, after=[high_sent])
    up_sent_y = over_y(up_sums[1])
    high_far = over_core(late(high_far, up_sums[0]))
    out_partner = over_x(late(out_send, up_sums[0]))
    grads_qkv[0], sums_qkv[0] = heads_back(0, up_sums[:1])
    down_sums = combine([down_sums[0], down_sent_x], 2, after=[high_far, grads_qkv[0]])
    down_sent_z = over_z(down_sums[1], 2)
    low_near, low_next, low_far, low_last = sums_first(
        normed, branch, grads_qkv[0], contexts[0], after=down_sums[:1]
    )
    (high,) = combine([high_near, high_far, high_sent_y], 1, after=[low_near])
    high_x = over_x(high)
    (low_sent,) = combine([low_next, over_core(low_last)], 1, after=[high])
    low_sent_y = over_y(low_sent)
    send, sums_partner = first_back(
        side_array, 1, grads_qkv, first_pieces, rows, grad_middle, gain_one, order, after=[low_sent]
    )
    up_sums = combine([up_sums[0], up_sent_y], 2, after=[send])
    up_sent_z = over_z(up_sums[1], 2)
    down_sums = combine([down_sums[0], down_sent_z], 2, after=[up_sums[0], out_partner])
    down_sent_z = over_z(down_sums[1], 1)
    low_far = over_core(late(low_far, up_sums[0]))
    full, sums_own = first_back(
        side_array, 0, grads_qkv, first_pieces, rows, grad_middle, gain_one, order, after=down_sums[:1]
    )
    low = combine([low_near, low_far, low_sent_y, high_x], 4, after=[full])
    up_sums = combine([up_sums[0], up_sent_z], 2, after=low[:1])
    sums = jnp.concatenate(
        [(sums_own + sums_partner)[:2], sums_two[2:3], sums_two[:2], sum_own + sum_partner], axis=0
    )
    sums = jnp.einsum("td,od->to", sums, order.astype(F32), precision=lax.Precision.HIGHEST)
    halves = [
        jnp.concatenate([sums_qkv[x_at].reshape(-1), sum_hidden[x_at][0]]) for x_at in range(2)
    ]
    small = late(jnp.concatenate([halves[0], sums.reshape(-1), halves[1]]), low[0])
    small = small + over_core(small)
    small = late(small + over_y(small), up_sums[0])
    halves_size = 2 * half + half_hidden
    small_x = over_x(jnp.concatenate([small[-halves_size:], small[halves_size:-halves_size]]))
    small = small[:-halves_size] + small_x
    height = 8
    small_rows = jnp.pad(small, (0, height * half_hidden - small.size)).reshape(height, half_hidden)
    small_top = small_rows.astype(BF16)
    small_rows = jnp.concatenate([small_top, (small_rows - small_top.astype(F32)).astype(BF16)], axis=0)

    near_z = over_z(jnp.concatenate([low[1], up_sums[1], small_rows], axis=0), 1)
    middle_z = over_z(jnp.concatenate([low[2], small_rows], axis=0), 2)
    far_z = over_z(jnp.concatenate([low[3], small_rows], axis=0), 3)
    send_x = over_x(late(send, low[0]))
    out_full = feed_down(
        side_array, 0, 2, actives, middle, down_all, bias_down, order, after=[low[0], small_rows]
    )
    (grad_down,) = combine([down_sums[0], down_sent_z], 1, F32, after=[out_full])
    block_out = lax.dynamic_update_slice_in_dim(out_full, out_partner, (1 - side) * mine, 0)
    tokens_grad = lax.dynamic_update_slice_in_dim(full, send_x, (1 - side) * mine, 0)
    grad_qkv, grad_out, grad_up, sums = finish(
        low[0], up_sums[0], small_rows, near_z, middle_z, far_z, after=[block_out, tokens_grad]
    )
    sums = sums.reshape(-1)
    halves = sums[:halves_size]
    sums = sums[halves_size : halves_size + 6 * width].reshape(6, width)
    return (
        block_out,
        tokens_grad,
        sums[0],
        sums[1],
        grad_qkv.reshape(ROWS, 3, half),
        halves[: 2 * half].reshape(2, half),
        grad_out,
        sums[2],
        sums[3],
        sums[4],
        grad_up,
        halves[2 * half :],
        grad_down,
        sums[5],
    )


def solution(mesh):
    in_specs = (
        P("dp", "tensor", None),
        P("dp"),
        P("dp", "tensor", None),
        P(),
        P(),
        P("dp", None, "tensor"),
        P(None, "tensor"),
        P("dp", "tensor"),
        P(),
        P(),
        P(),
        P("dp", "tensor"),
        P("tensor"),
        P("dp", "tensor"),
        P(),
    )
    out_specs = (
        P("dp", "tensor", None),
        P("dp", "tensor", None),
        P(),
        P(),
        P("dp", None, "tensor"),
        P(None, "tensor"),
        P("dp", "tensor"),
        P(),
        P(),
        P(),
        P("dp", "tensor"),
        P("tensor"),
        P("dp", "tensor"),
        P(),
    )
    small_slice = mesh.shape["dp"] == 16 and mesh.shape["tensor"] == 2
    shards = fast_shards if small_slice else general_shards
    return jax.shard_map(shards, mesh=mesh, in_specs=in_specs, out_specs=out_specs, check_vma=False)
```

```python
import jax
import jax.numpy as jnp
from jax import lax
from jax.experimental import pallas as pl
from jax.experimental.pallas import tpu as pltpu
from jax.sharding import PartitionSpec as P

HDIM = 64
MICRO = 2


def mixed(form, left, right):
    return jnp.einsum(form, left, right, preferred_element_type=jnp.float32)


def normalize(values, gain, shift):
    mean_val = jnp.mean(values, axis=-1, keepdims=True)
    centered = values - mean_val
    inv_std = lax.rsqrt(jnp.mean(centered * centered, axis=-1, keepdims=True) + 1e-05)
    unit_val = centered * inv_std
    return (unit_val * gain + shift, unit_val, inv_std)


def normalize_back(grad_in, unit_val, inv_std, gain):
    scaled = grad_in * gain
    return inv_std * (
        scaled
        - jnp.mean(scaled, axis=-1, keepdims=True)
        - unit_val * jnp.mean(scaled * unit_val, axis=-1, keepdims=True)
    )


def token_sum(values):
    return jnp.sum(values, axis=(0, 1))


def general_shards(
    tokens,
    image_mask,
    out_grad,
    norm1_gain,
    norm1_shift,
    qkv_weight,
    qv_bias,
    out_weight,
    out_bias,
    norm2_gain,
    norm2_shift,
    up_weight,
    up_bias,
    down_weight,
    down_bias,
):
    images_here = tokens.shape[0] // MICRO
    full_width = norm1_gain.shape[0]
    local_width = qkv_weight.shape[2]
    local_hidden = up_weight.shape[1]
    local_heads = local_width // HDIM
    score_scale = HDIM ** (-0.5)
    gain_one = norm1_gain.astype(jnp.float32)
    shift_one = norm1_shift.astype(jnp.float32)
    gain_two = norm2_gain.astype(jnp.float32)
    shift_two = norm2_shift.astype(jnp.float32)
    bias_pair = qv_bias.astype(jnp.float32)
    grad_qkv = jnp.zeros((full_width, 3, local_width), jnp.float32)
    grad_out = jnp.zeros((full_width, local_width), jnp.float32)
    grad_up = jnp.zeros((full_width, local_hidden), jnp.float32)
    grad_down = jnp.zeros((full_width, local_hidden), jnp.float32)
    grad_gain_one = jnp.zeros((full_width,), jnp.float32)
    grad_shift_one = jnp.zeros((full_width,), jnp.float32)
    grad_gain_two = jnp.zeros((full_width,), jnp.float32)
    grad_shift_two = jnp.zeros((full_width,), jnp.float32)
    grad_out_bias = jnp.zeros((full_width,), jnp.float32)
    grad_down_bias = jnp.zeros((full_width,), jnp.float32)
    grad_pair = jnp.zeros((2, local_width), jnp.float32)
    grad_up_bias = jnp.zeros((local_hidden,), jnp.float32)
    outputs = []
    input_grads = []
    for micro_index in range(MICRO):
        first_image = micro_index * images_here
        block_rows = tokens[first_image : first_image + images_here].astype(jnp.float32)
        keep_mask = image_mask[first_image : first_image + images_here].astype(jnp.float32)[
            :, None, None
        ]
        fwd_weights = (
            lax.all_gather(qkv_weight, "dp", axis=0, tiled=True),
            lax.all_gather(out_weight, "dp", axis=0, tiled=True),
            lax.all_gather(up_weight, "dp", axis=0, tiled=True),
            lax.all_gather(down_weight, "dp", axis=0, tiled=True),
        )
        qkv_full, out_full, up_full, down_full = fwd_weights
        normed, unit_one, inv_one = normalize(block_rows, gain_one, shift_one)
        normed_full = lax.all_gather(normed.astype(jnp.bfloat16), "tensor", axis=1, tiled=True)
        seq_len = normed_full.shape[1]
        head_shape = (images_here, seq_len, local_heads, HDIM)
        projected = mixed("isd,dcf->iscf", normed_full, qkv_full)
        queries = (projected[:, :, 0] + bias_pair[0]).astype(jnp.bfloat16).reshape(head_shape)
        key_rows = projected[:, :, 1].astype(jnp.bfloat16).reshape(head_shape)
        value_rows = (projected[:, :, 2] + bias_pair[1]).astype(jnp.bfloat16).reshape(head_shape)
        scores = mixed("iqhe,ikhe->ihqk", queries, key_rows) * score_scale
        row_top = jnp.max(scores, axis=-1, keepdims=True)
        raw_weights = jnp.exp(scores - row_top)
        row_total = jnp.sum(raw_weights, axis=-1, keepdims=True)
        log_total = row_top + jnp.log(row_total)
        probs = (raw_weights / row_total).astype(jnp.bfloat16)
        context = mixed("ihqk,ikhe->iqhe", probs, value_rows).astype(jnp.bfloat16)
        context = context.reshape(images_here, seq_len, local_width)
        attn_terms = mixed("isf,of->iso", context, out_full)
        branch = lax.psum_scatter(
            attn_terms, "tensor", scatter_dimension=1, tiled=True
        ) + out_bias.astype(jnp.float32)
        middle = block_rows + branch
        second, unit_two, inv_two = normalize(middle, gain_two, shift_two)
        second_full = lax.all_gather(second.astype(jnp.bfloat16), "tensor", axis=1, tiled=True)
        hidden = mixed("isd,df->isf", second_full, up_full) + up_bias.astype(jnp.float32)
        gate_sig = jax.nn.sigmoid(1.702 * hidden)
        active = (hidden * gate_sig).astype(jnp.bfloat16)
        feed_terms = mixed("isf,of->iso", active, down_full)
        feed_out = lax.psum_scatter(
            feed_terms.astype(jnp.bfloat16), "tensor", scatter_dimension=1, tiled=True
        ).astype(jnp.float32) + down_bias.astype(jnp.float32)
        outputs.append(((middle + feed_out) * keep_mask).astype(jnp.bfloat16))
        back_weights = (
            lax.all_gather(qkv_weight, "dp", axis=0, tiled=True),
            lax.all_gather(out_weight, "dp", axis=0, tiled=True),
            lax.all_gather(up_weight, "dp", axis=0, tiled=True),
            lax.all_gather(down_weight, "dp", axis=0, tiled=True),
        )
        qkv_back, out_back, up_back, down_back = back_weights
        grad_final = (
            out_grad[first_image : first_image + images_here].astype(jnp.float32) * keep_mask
        )
        grad_down_bias = grad_down_bias + token_sum(grad_final)
        final_full = lax.all_gather(grad_final.astype(jnp.bfloat16), "tensor", axis=1, tiled=True)
        grad_down = grad_down + mixed("iso,isf->of", final_full, active)
        grad_active = mixed("iso,of->isf", final_full, down_back)
        grad_hidden = (
            grad_active * (gate_sig + 1.702 * hidden * gate_sig * (1.0 - gate_sig))
        ).astype(jnp.bfloat16)
        grad_up_bias = grad_up_bias + token_sum(grad_hidden.astype(jnp.float32))
        grad_up = grad_up + mixed("isd,isf->df", second_full, grad_hidden)
        second_terms = mixed("isf,df->isd", grad_hidden, up_back)
        grad_second = lax.psum_scatter(second_terms, "tensor", scatter_dimension=1, tiled=True)
        grad_gain_two = grad_gain_two + token_sum(grad_second * unit_two)
        grad_shift_two = grad_shift_two + token_sum(grad_second)
        grad_middle = grad_final + normalize_back(grad_second, unit_two, inv_two, gain_two)
        grad_branch = grad_middle.astype(jnp.bfloat16)
        grad_out_bias = grad_out_bias + token_sum(grad_branch.astype(jnp.float32))
        branch_full = lax.all_gather(grad_branch, "tensor", axis=1, tiled=True)
        grad_out = grad_out + mixed("iso,isf->of", branch_full, context)
        grad_context = (
            mixed("iso,of->isf", branch_full, out_back).astype(jnp.bfloat16).reshape(head_shape)
        )
        again = mixed("iqhe,ikhe->ihqk", queries, key_rows) * score_scale
        soft_again = jnp.exp(again - log_total)
        probs_again = soft_again.astype(jnp.bfloat16)
        grad_values = mixed("ihqk,iqhe->ikhe", probs_again, grad_context)
        grad_soft = mixed("iqhe,ikhe->ihqk", grad_context, value_rows)
        grad_scores = (
            soft_again * (grad_soft - jnp.sum(grad_soft * soft_again, axis=-1, keepdims=True))
        ).astype(jnp.bfloat16)
        grad_queries = mixed("ihqk,ikhe->iqhe", grad_scores, key_rows) * score_scale
        grad_keys = mixed("ihqk,iqhe->ikhe", grad_scores, queries) * score_scale
        flat_shape = (images_here, seq_len, local_width)
        grad_projected = jnp.stack(
            (
                grad_queries.reshape(flat_shape),
                grad_keys.reshape(flat_shape),
                grad_values.reshape(flat_shape),
            ),
            axis=2,
        ).astype(jnp.bfloat16)
        pair_terms = grad_projected.astype(jnp.float32)
        grad_pair = grad_pair + jnp.stack(
            (token_sum(pair_terms[:, :, 0]), token_sum(pair_terms[:, :, 2])), axis=0
        )
        grad_qkv = grad_qkv + mixed("isd,iscf->dcf", normed_full, grad_projected)
        normed_terms = mixed("iscf,dcf->isd", grad_projected, qkv_back)
        grad_normed = lax.psum_scatter(
            normed_terms.astype(jnp.bfloat16), "tensor", scatter_dimension=1, tiled=True
        ).astype(jnp.float32)
        grad_gain_one = grad_gain_one + token_sum(grad_normed * unit_one)
        grad_shift_one = grad_shift_one + token_sum(grad_normed)
        grad_tokens = grad_middle + normalize_back(grad_normed, unit_one, inv_one, gain_one)
        input_grads.append(grad_tokens.astype(jnp.bfloat16))
    grad_qkv, grad_out, grad_up, grad_down = (
        lax.psum_scatter(
            grad_qkv.astype(jnp.bfloat16), "dp", scatter_dimension=0, tiled=True
        ).astype(jnp.float32),
        lax.psum_scatter(
            grad_out.astype(jnp.bfloat16), "dp", scatter_dimension=0, tiled=True
        ).astype(jnp.float32),
        lax.psum_scatter(
            grad_up.astype(jnp.bfloat16), "dp", scatter_dimension=0, tiled=True
        ).astype(jnp.float32),
        lax.psum_scatter(
            grad_down.astype(jnp.bfloat16), "dp", scatter_dimension=0, tiled=True
        ).astype(jnp.float32),
    )
    grad_gain_one, grad_shift_one, grad_gain_two, grad_shift_two, grad_out_bias, grad_down_bias = (
        lax.psum(
            (
                grad_gain_one,
                grad_shift_one,
                grad_gain_two,
                grad_shift_two,
                grad_out_bias,
                grad_down_bias,
            ),
            ("dp", "tensor"),
        )
    )
    grad_pair, grad_up_bias = lax.psum((grad_pair, grad_up_bias), "dp")
    block_out = jnp.concatenate(outputs, axis=0)
    tokens_grad = jnp.concatenate(input_grads, axis=0)
    return (
        block_out,
        tokens_grad,
        grad_gain_one,
        grad_shift_one,
        grad_qkv,
        grad_pair,
        grad_out,
        grad_out_bias,
        grad_gain_two,
        grad_shift_two,
        grad_up,
        grad_up_bias,
        grad_down,
        grad_down_bias,
    )


ROWS = 64
PART = 256
VMEM_BYTES = 27 * 1024 * 1024
COST_PART = 0.6
FORWARD_PART = 1.0
LOG2_E = 1.4426950408889634
BF16 = jnp.bfloat16
F32 = jnp.float32


def swap(values, axis_name, flip):
    count = lax.axis_size(axis_name)
    return lax.ppermute(values, axis_name, [(place, place ^ flip) for place in range(count)])


def over_core(values):
    return swap(values, "dp", 1)


def over_y(values):
    return swap(values, "dp", 2)


def over_z(values, step):
    return swap(values, "dp", 4 * step)


def over_x(values):
    return swap(values, "tensor", 1)


def late(values, *marks):
    return lax.optimization_barrier((values, *marks))[0]


def dot_nn(left, right):
    return lax.dot_general(left, right, (((1,), (0,)), ((), ())), preferred_element_type=F32)


def dot_nt(left, right):
    return lax.dot_general(left, right, (((1,), (1,)), ((), ())), preferred_element_type=F32)


def dot_tn(left, right):
    return lax.dot_general(left, right, (((0,), (0,)), ((), ())), preferred_element_type=F32)


def call(
    kernel, grid, in_specs, out_specs, out_shape, flops, moved, after=(), aliases=None, scalars=0, part=None
):
    given, waits = scalars + len(in_specs), len(after)
    part = COST_PART if part is None else part

    def run(*refs):
        kernel(*refs[:given], *refs[given + waits :])

    function = pl.pallas_call(
        run,
        grid_spec=pltpu.PrefetchScalarGridSpec(
            num_scalar_prefetch=scalars,
            grid=grid,
            in_specs=list(in_specs) + [pl.BlockSpec(memory_space=pl.ANY)] * waits,
            out_specs=out_specs,
        ),
        out_shape=out_shape,
        input_output_aliases=aliases or {},
        compiler_params=pltpu.CompilerParams(vmem_limit_bytes=VMEM_BYTES),
        cost_estimate=pl.CostEstimate(
            flops=int(flops * part), bytes_accessed=int(moved * part), transcendentals=0
        ),
    )
    return lambda *arrays: function(*arrays, *after)


def fixed(*shape, at=None):
    place = at or (0,) * len(shape)
    return pl.BlockSpec(shape, lambda *_: place, pipeline_mode=pl.Buffered(1))


def far_list(near, far):
    return list(near) + [far[last].at[y_at] for y_at in range(2) for last in range(2)]


def piece_specs(columns, at=0):
    return [fixed(PART, columns, at=(0, at))] * 4 + [fixed(2, PART, columns, at=(0, 0, at))] * 2


def piece_tiles(tile, near=4, far=2):
    return [pl.BlockSpec((PART, tile), lambda j: (0, j))] * near + [
        pl.BlockSpec((2, PART, tile), lambda j: (0, 0, j))
    ] * far


def gathered_specs(columns, halves=(0, 1), at=None):
    def spec(block, x_at):
        core, y_at, z_at = block // 8, (block // 4) % 2, block % 4
        slab = z_at * 4 + y_at * 2 + core

        def place(j, *refs):
            where = refs[-1]
            row = jnp.bitwise_xor(where[1], slab), jnp.bitwise_xor(where[0], x_at)
            return (*row, 0, j if at is None else at)

        mode = {} if at is None else {"pipeline_mode": pl.Buffered(1)}
        return pl.BlockSpec((1, 1, ROWS, columns), place, **mode)

    return [spec(block, x_at) for block in range(16) for x_at in halves]


def joined(refs, first, last, step=1, offset=0):
    return jnp.concatenate([refs[step * block + offset][0, 0] for block in range(first, last)], axis=0)


def struct(shape, dtype=BF16):
    return jax.ShapeDtypeStruct(shape, dtype)


def outer(shape, dtype=BF16):
    return pltpu.HBM(shape, dtype)


def in_hbm(values):
    if isinstance(values, (list, tuple)):
        return [in_hbm(part) for part in values]
    return pltpu.with_memory_space_constraint(values, pltpu.HBM)


ANYWHERE = pl.BlockSpec(memory_space=pl.ANY)


def normal_parts(values):
    mean_val = jnp.mean(values, axis=-1, keepdims=True)
    centered = values - mean_val
    inv_std = lax.rsqrt(jnp.mean(centered * centered, axis=-1, keepdims=True) + 1e-05)
    return centered * inv_std, inv_std


def column_sum(values):
    return jnp.sum(values, axis=0, keepdims=True)


def combine(arrays, pieces, dtype=BF16, tile=1024, after=()):
    columns = arrays[0].shape[-1]
    rows = arrays[0].size // columns // pieces
    arrays = [values.reshape(pieces, rows, columns) for values in arrays]
    given = len(arrays)

    def kernel(*refs):
        for at in range(pieces):
            parts = [ref[at].astype(F32) for ref in refs[:given]]
            while len(parts) > 1:
                parts = [sum(parts[start : start + 2]) for start in range(0, len(parts), 2)]
            refs[given + at][...] = parts[0].astype(dtype)

    return call(
        kernel,
        (columns // tile,),
        [pl.BlockSpec((pieces, rows, tile), lambda j: (0, 0, j))] * given,
        [pl.BlockSpec((rows, tile), lambda j: (0, j))] * pieces,
        [outer((rows, columns), dtype)] * pieces,
        0,
        2 * pieces * rows * columns * (given + 1),
        after,
    )(*arrays)


def finish(low_near, up_near, small, near, middle, far, after=()):
    rows, columns = low_near.shape
    split = columns * 3 // 4
    height = small.shape[0] // 2

    def kernel(low_ref, up_ref, small_ref, near_ref, middle_ref, far_ref, qkv_ref, out_ref, up_out_ref, sum_ref):
        def rows_of(ref, start):
            return ref[start : start + rows, :].astype(F32)

        def vectors_of(ref, start):
            values = ref[start : start + 2 * height, :].astype(F32)
            return values[:height] + values[height:]

        low = (rows_of(low_ref, 0) + rows_of(near_ref, 0)) + (rows_of(middle_ref, 0) + rows_of(far_ref, 0))
        qkv_ref[...] = low[:, :split]
        out_ref[...] = low[:, split:]
        up_out_ref[...] = rows_of(up_ref, 0) + rows_of(near_ref, rows)
        sum_ref[...] = (vectors_of(small_ref, 0) + vectors_of(near_ref, 2 * rows)) + (
            vectors_of(middle_ref, rows) + vectors_of(far_ref, rows)
        )

    given = [low_near, up_near, small, near, middle, far]
    return call(
        kernel,
        (1,),
        [fixed(*values.shape) for values in given],
        [fixed(rows, split), fixed(rows, columns - split), fixed(rows, columns), fixed(height, columns)],
        [
            struct((rows, split), F32),
            struct((rows, columns - split), F32),
            struct((rows, columns), F32),
            struct((height, columns), F32),
        ],
        0,
        20 * rows * columns,
        after,
    )(*given)


def first_step():
    return pl.program_id(0) == 0


def setup(places, vectors, after=()):
    width = vectors[0].shape[1]
    given = len(vectors)

    def kernel(place_ref, *refs):
        order_ref = refs[given]
        source = lax.broadcasted_iota(jnp.int32, (width, width), 0)
        target = lax.broadcasted_iota(jnp.int32, (width, width), 1)
        at = target // ROWS
        z_rel, y_rel, core_rel = at % 4, (at // 4) % 2, at // 8
        place = (z_rel * 4 + y_rel * 2 + core_rel) ^ place_ref[1]
        hit = source == place * ROWS + target % ROWS
        order = jnp.where(hit, 1.0, 0.0).astype(BF16)
        order_ref[...] = order
        rows = jnp.concatenate([ref[...].astype(F32) for ref in refs[:given]] + [jnp.zeros((8 - given, width), F32)], axis=0)
        moved = dot_nn(rows.astype(BF16), order)
        for vector_at in range(given):
            refs[given + 1 + vector_at][...] = moved[vector_at : vector_at + 1]

    row = fixed(1, width)
    return call(
        kernel,
        (1,),
        [row] * given,
        [fixed(width, width)] + [row] * given,
        [struct((width, width))] + [struct((1, width), F32)] * given,
        16 * width * width,
        2 * width * width,
        after,
        None,
        1,
        part=FORWARD_PART,
    )(places, *vectors)


def image_block(height, width, offset):
    return pl.BlockSpec((1, height, width), lambda i, side: (offset(side) + i, 0, 0))


def prepare(side, images, order, gain, shift, half_at, before=None, after=()):
    _, height, width = images.shape
    mine = 2

    def kernel(side_ref, raw_ref, order_ref, gain_ref, shift_ref, *refs):
        rows_ref, norm_ref = refs[-2:]
        rows = dot_nn(raw_ref[0], order_ref[...])
        rows_ref[...] = rows.astype(BF16)
        unit, _ = normal_parts(rows)
        norm_ref[...] = (unit * gain_ref[...] + shift_ref[...]).astype(BF16)

    offset = (lambda side_ref: side_ref[0] * mine) if half_at == 0 else (lambda side_ref: 0)
    out = pl.BlockSpec((height, width), lambda i, _: (half_at * mine + i, 0))
    old = () if before is None else before
    return call(
        kernel,
        (mine,),
        [image_block(height, width, offset), fixed(width, width), fixed(1, width), fixed(1, width)]
        + [ANYWHERE] * len(old),
        [out, out],
        [outer((2 * mine * height, width))] * 2,
        2 * mine * height * width * width,
        6 * mine * height * width,
        after,
        {5: 0, 6: 1} if old else None,
        1,
        part=FORWARD_PART,
    )(side, images, order, gain, shift, *old)


def mask_grad(side, images, order, half_at, before=None, after=()):
    _, height, width = images.shape
    mine = 2

    def kernel(side_ref, raw_ref, order_ref, *refs):
        final_ref, sum_ref = refs[-2:]
        keep = side_ref[2 + side_ref[0] * mine + pl.program_id(0)].astype(F32)
        final = dot_nn(raw_ref[0], order_ref[...]) * keep
        final_ref[...] = final.astype(BF16)

        @pl.when(first_step())
        def _():
            sum_ref[...] = jnp.zeros_like(sum_ref)

        sum_ref[...] += column_sum(final)

    offset = (lambda side_ref: side_ref[0] * mine) if half_at == 0 else (lambda side_ref: 0)
    old = () if before is None else (before,)
    out = pl.BlockSpec((height, width), lambda i, _: (half_at * mine + i, 0))
    return call(
        kernel,
        (mine,),
        [image_block(height, width, offset), fixed(width, width)] + [ANYWHERE] * len(old),
        [out, fixed(1, width)],
        [struct((2 * mine * height, width)), struct((1, width), F32)],
        2 * mine * height * width * width,
        6 * mine * height * width,
        after,
        {3: 0} if old else None,
        1,
        part=FORWARD_PART,
    )(side, images, order, *old)


def project(normed, parts, bias, after=()):
    count, width = normed.shape
    half = bias.shape[-1]

    def kernel(norm_ref, bias_ref, *refs):
        weight = jnp.concatenate([refs[0][...], refs[1][...], refs[2][0], refs[2][1]], axis=0)
        refs[3][0] = (dot_nn(norm_ref[...], weight) + bias_ref[0]).astype(BF16)

    return call(
        kernel,
        (3,),
        [fixed(count, width), pl.BlockSpec((1, 1, half), lambda j: (j, 0, 0))]
        + piece_tiles(half, 2, 1),
        pl.BlockSpec((1, count, half), lambda j: (j, 0, 0)),
        outer((3, count, half)),
        6 * count * width * half,
        2 * count * (width + 3 * half) + 6 * width * half,
        after,
        part=FORWARD_PART,
    )(normed, bias, *parts)


def attend(projected, first_image, last_image, before=None, lanes=256, after=()):
    _, _, images, half_len, half = projected.shape
    length = 2 * half_len
    per_step = lanes // HDIM
    steps = half // lanes

    def kernel(proj_ref, *refs):
        out_ref, weights_ref, inverse_ref = refs[-3:]
        queries, key_rows, value_rows = (proj_ref[at].reshape(length, lanes) for at in range(3))
        queries, value_rows = queries.T, value_rows.T
        outs, inverses = [], []
        for head in range(per_step):
            part = slice(head * HDIM, (head + 1) * HDIM)
            scores = dot_nn(key_rows[:, part], queries[part])
            top = jnp.max(scores, axis=0, keepdims=True)
            weights = jnp.exp2((scores - top) * (LOG2_E * HDIM**-0.5)).astype(BF16)
            weights_ref[0, head] = weights
            ones = jnp.ones((16, length), BF16)
            sums = dot_nn(jnp.concatenate([value_rows[part], ones], axis=0), weights)
            inverse = 1.0 / sums[HDIM : HDIM + 1]
            outs.append((sums[:HDIM] * inverse).astype(BF16))
            inverses.append(inverse)
        out_ref[...] = jnp.concatenate(outs, axis=0).T.reshape(out_ref.shape)
        inverse_ref[0] = jnp.concatenate(inverses + [jnp.zeros((8 - per_step, length), F32)], axis=0)

    heads = half // HDIM
    old = () if before is None else before
    return call(
        kernel,
        (last_image - first_image, steps),
        [pl.BlockSpec((3, 2, 1, half_len, lanes), lambda i, j: (0, 0, first_image + i, 0, j))]
        + [ANYWHERE] * len(old),
        [
            pl.BlockSpec((2, 1, half_len, lanes), lambda i, j: (0, first_image + i, 0, j)),
            pl.BlockSpec((1, per_step, length, length), lambda i, j: (first_image + i, j, 0, 0)),
            pl.BlockSpec((1, 8, length), lambda i, j: (first_image + i, j, 0)),
        ],
        [
            struct((2, images, half_len, half)),
            outer((images, heads, length, length)),
            struct((images, 8 * steps, length), F32),
        ],
        24 * (last_image - first_image) * heads * length * length * HDIM,
        (last_image - first_image) * heads * length * length * 2,
        after,
        {1: 0, 2: 1, 3: 2} if old else None,
        part=FORWARD_PART,
    )(in_hbm(projected), *old)


def attend_back(projected, grad_context, context, weights, inverse, after=()):
    _, _, images, half_len, half = projected.shape
    length = 2 * half_len
    steps = inverse.shape[1] // 8
    lanes = half // steps
    per_step = lanes // HDIM
    scale = HDIM**-0.5

    def kernel(proj_ref, grad_ref, context_ref, weights_ref, inverse_ref, out_ref, sum_ref):
        queries, key_rows, value_rows = (proj_ref[at].reshape(length, lanes) for at in range(3))
        queries, key_rows = queries.T, key_rows.T
        grads = grad_ref[...].reshape(length, lanes).T.astype(F32)
        contexts = context_ref[...].reshape(length, lanes).T.astype(F32)
        found = ([], [], [])
        for head in range(per_step):
            part = slice(head * HDIM, (head + 1) * HDIM)
            weights = weights_ref[0, head]
            grad = grads[part] * inverse_ref[0, head : head + 1]
            level = jnp.sum(grad * contexts[part], axis=0, keepdims=True)
            grad = grad.astype(BF16)
            found[2].append(dot_nt(grad, weights).astype(BF16))
            grad_soft = dot_nn(value_rows[:, part], grad)
            grad_scores = (weights.astype(F32) * (grad_soft - level)).astype(BF16)
            found[0].append((dot_nn(key_rows[part], grad_scores) * scale).astype(BF16))
            found[1].append((dot_nt(queries[part], grad_scores) * scale).astype(BF16))
        for at in range(3):
            joined = jnp.concatenate(found[at], axis=0).T
            out_ref[at] = joined.reshape(2, 1, half_len, lanes)
            if at != 1:
                sum_ref[0, at // 2 : at // 2 + 1] = column_sum(joined.astype(F32))

    heads = half // HDIM
    block = pl.BlockSpec((3, 2, 1, half_len, lanes), lambda i, j: (0, 0, i, 0, j))
    rows = pl.BlockSpec((2, 1, half_len, lanes), lambda i, j: (0, i, 0, j))
    return call(
        kernel,
        (images, steps),
        [
            block,
            rows,
            rows,
            pl.BlockSpec((1, per_step, length, length), lambda i, j: (i, j, 0, 0)),
            pl.BlockSpec((1, 8, length), lambda i, j: (i, j, 0)),
        ],
        [block, pl.BlockSpec((1, 2, lanes), lambda i, j: (i, 0, j))],
        [struct(projected.shape), struct((images, 2, half), F32)],
        32 * images * heads * length * length * HDIM,
        images * heads * length * length * 2,
        after,
    )(in_hbm(projected), grad_context, context, in_hbm(weights), inverse)


def add_branch(contexts, rows, pieces, bias, gain, shift, tile=576, after=()):
    count, width = rows.shape
    half = width // 2

    def kernel(low_ref, high_ref, rows_ref, bias_ref, gain_ref, shift_ref, *refs):
        parts, (middle_ref, norm_ref) = far_list(refs[:4], refs[4:6]), refs[6:]
        found = []
        for at in range(4):
            found.append(dot_nt(low_ref[...], parts[2 * at][...]) + dot_nt(high_ref[...], parts[2 * at + 1][...]))
        middle = rows_ref[...].astype(F32) + (jnp.concatenate(found, axis=1) + bias_ref[...])
        middle_ref[...] = middle
        unit, _ = normal_parts(middle)
        norm_ref[...] = (unit * gain_ref[...] + shift_ref[...]).astype(BF16)

    block = pl.BlockSpec((tile, width), lambda i: (i, 0))
    half_block = pl.BlockSpec((tile, half), lambda i: (i, 0))
    return call(
        kernel,
        (count // tile,),
        [half_block, half_block, block] + [fixed(1, width)] * 3 + piece_specs(half, 3),
        [block, block],
        [outer((count, width), F32), struct((count, width))],
        2 * count * width * width,
        10 * count * width + 2 * width * width,
        after,
        part=FORWARD_PART,
    )(*contexts, rows, bias, gain, shift, *pieces)


def feed_up(places, x_at, second, gathered, bias, tile=512, after=()):
    count, width = second.shape
    columns = bias.shape[-1]

    def kernel(place_ref, second_ref, bias_ref, *refs):
        hidden = dot_nn(second_ref[...], joined(refs, 0, 16)) + bias_ref[...]
        gate = 0.5 + 0.5 * jnp.tanh(0.851 * hidden)
        refs[16][...] = (hidden * gate).astype(BF16)
        refs[17][...] = (gate * (1.0 + 1.702 * hidden * (1.0 - gate))).astype(BF16)

    block = pl.BlockSpec((count, tile), lambda j, _: (0, j))
    return call(
        kernel,
        (columns // tile,),
        [fixed(count, width), pl.BlockSpec((1, tile), lambda j, _: (0, j))] + gathered_specs(tile, (x_at,)),
        [block, block],
        [outer((count, columns))] * 2,
        2 * count * width * columns,
        2 * count * (width + 2 * columns) + 2 * width * columns,
        after,
        None,
        1,
        part=FORWARD_PART,
    )(places, second, bias, *[gathered] * 16)


def feed_down(side, first_tile, last_tile, actives, middle, gathered, bias, order, before=None, tile=288, after=()):
    count, columns = actives[0].shape
    width = middle.shape[1]
    mine = count // tile // 2
    half_at = first_tile // mine
    old = () if before is None else (before,)

    def kernel(side_ref, low_ref, high_ref, middle_ref, bias_ref, order_ref, *refs):
        keep = side_ref[2 + side_ref[0] * mine + first_tile % mine + pl.program_id(0)].astype(F32)
        out_ref = refs[-1]
        feed = dot_nt(low_ref[...], joined(refs, 0, 16, 2, 0)) + dot_nt(high_ref[...], joined(refs, 0, 16, 2, 1))
        out = ((middle_ref[...] + (feed + bias_ref[...])) * keep).astype(BF16)
        out_ref[0] = dot_nt(out, order_ref[...]).astype(BF16)

    hidden = pl.BlockSpec((tile, columns), lambda i, _: (first_tile + i, 0))
    offset = (lambda ref: ref[0] * mine + first_tile) if half_at == 0 else (lambda ref: first_tile - mine)

    return call(
        kernel,
        (last_tile - first_tile,),
        [
            hidden,
            hidden,
            pl.BlockSpec((tile, width), lambda i, _: (first_tile + i, 0)),
            fixed(1, width),
            fixed(width, width),
        ]
        + gathered_specs(columns, at=0)
        + [ANYWHERE] * len(old),
        image_block(tile, width, offset),
        struct(((2 - half_at) * mine, tile, width)),
        2 * count * width * columns + count * width * width,
        2 * count * columns + 3 * count * width + 4 * width * columns,
        after,
        {38: 0} if old else None,
        1,
    )(side, *[in_hbm(values) for values in actives], in_hbm(middle), bias, order, *[gathered] * 32, *old)


def gate_back(side, final, slopes, gathered, tile=512, after=()):
    count, width = final.shape
    columns = gathered.shape[-1]

    def kernel(side_ref, final_ref, low_ref, high_ref, *refs):
        outs, sums = refs[32:34], refs[34:36]
        for x_at, slope_ref in enumerate((low_ref, high_ref)):
            weight = joined(refs, 0, 16, 2, x_at)
            grad = (dot_nn(final_ref[...], weight) * slope_ref[...].astype(F32)).astype(BF16)
            outs[x_at][...] = grad
            sums[x_at][...] = column_sum(grad.astype(F32))

    block = pl.BlockSpec((count, tile), lambda j, _: (0, j))
    sum_block = pl.BlockSpec((1, tile), lambda j, _: (0, j))
    return call(
        kernel,
        (columns // tile,),
        [fixed(count, width), block, block] + gathered_specs(tile),
        [block, block, sum_block, sum_block],
        [struct((count, columns))] * 2 + [struct((1, columns), F32)] * 2,
        4 * count * width * columns,
        4 * count * (width + 2 * columns) + 4 * width * columns,
        after,
        None,
        1,
    )(side, in_hbm(final), *in_hbm(slopes), *[in_hbm(gathered)] * 32)


def sums_down(final, actives, tile=512, after=()):
    count, width = final.shape
    columns = actives[0].shape[1]

    def kernel(final_ref, low_ref, high_ref, *outs):
        for x_at, right_ref in enumerate((low_ref, high_ref)):
            for core in range(2):
                for y_at in range(2):
                    start = (2 * core + y_at) * PART
                    part = dot_tn(final_ref[:, start : start + PART], right_ref[...])
                    outs[2 * core + y_at][x_at] = part.astype(BF16)

    right = pl.BlockSpec((count, tile), lambda j: (0, j))
    return call(
        kernel,
        (columns // tile,),
        [fixed(count, width), right, right],
        [pl.BlockSpec((2, PART, tile), lambda j: (0, 0, j))] * 4,
        [outer((2, PART, columns))] * 4,
        4 * count * width * columns,
        4 * count * columns + 2 * count * width + 4 * width * columns,
        after,
    )(final, *[in_hbm(values) for values in actives])


def sums_up(second, grads, tile=512, after=()):
    count, width = second.shape
    columns = grads[0].shape[1]

    def kernel(second_ref, low_ref, high_ref, *outs):
        for x_at, right_ref in enumerate((low_ref, high_ref)):
            for core in range(2):
                for y_at in range(2):
                    start = (2 * core + y_at) * PART
                    part = dot_tn(second_ref[:, start : start + PART], right_ref[...])
                    outs[2 * core + x_at][y_at] = part.astype(BF16)

    right = pl.BlockSpec((count, tile), lambda j: (0, j))
    return call(
        kernel,
        (columns // tile,),
        [fixed(count, width), right, right],
        [pl.BlockSpec((2, PART, tile), lambda j: (0, 0, j))] * 4,
        [outer((2, PART, columns))] * 4,
        4 * count * width * columns,
        4 * count * columns + 2 * count * width + 4 * width * columns,
        after,
    )(second, *grads)


def sums_first(normed, branch, grad_projected, context, after=()):
    count, width = normed.shape
    half = context.shape[1]

    def kernel(norm_ref, branch_ref, grad_ref, context_ref, *outs):
        def work(left_ref, right):
            for core in range(2):
                for y_at in range(2):
                    start = (2 * core + y_at) * PART
                    outs[2 * core + y_at][...] = dot_tn(left_ref[:, start : start + PART], right).astype(BF16)

        @pl.when(pl.program_id(0) < 3)
        def _():
            work(norm_ref, grad_ref[0])

        @pl.when(pl.program_id(0) == 3)
        def _():
            work(branch_ref, context_ref[...])

    left = fixed(count, width)
    return call(
        kernel,
        (4,),
        [left, left, pl.BlockSpec((1, count, half), lambda j: (jnp.minimum(j, 2), 0, 0)), fixed(count, half)],
        [pl.BlockSpec((PART, half), lambda j: (0, j))] * 4,
        [outer((PART, 4 * half))] * 4,
        8 * count * width * half,
        2 * count * (2 * width + 4 * half) + 8 * width * half,
        after,
    )(normed, branch, grad_projected, context)


def second_back(places, grads, gathered, first_pieces, middle, final, gain, tile=576, after=()):
    count, columns = grads[0].shape
    width = middle.shape[1]
    half = width // 2

    def kernel(place_ref, low_ref, high_ref, middle_ref, final_ref, gain_ref, *refs):
        ups, outs = refs[:32], far_list(refs[32:36], refs[36:38])
        grad_ref, branch_ref, context_low_ref, context_high_ref, sum_ref = refs[38:]
        grad_second = dot_nt(low_ref[...], joined(ups, 0, 16, 2, 0)) + dot_nt(high_ref[...], joined(ups, 0, 16, 2, 1))
        unit, inv_std = normal_parts(middle_ref[...])
        grad_middle = final_ref[...].astype(F32) + normalize_back(
            grad_second, unit, inv_std, gain_ref[...]
        )
        branch = grad_middle.astype(BF16)
        grad_ref[...] = grad_middle
        branch_ref[...] = branch
        for x_at, context_ref in enumerate((context_low_ref, context_high_ref)):
            weight = jnp.concatenate([outs[2 * at + x_at][...] for at in range(4)], axis=0)
            context_ref[...] = dot_nn(branch, weight).astype(BF16)

        @pl.when(first_step())
        def _():
            sum_ref[...] = jnp.zeros_like(sum_ref)

        sum_ref[0:1] += column_sum(grad_second * unit)
        sum_ref[1:2] += column_sum(grad_second)
        sum_ref[2:3] += column_sum(branch.astype(F32))

    block = pl.BlockSpec((tile, width), lambda i, _: (i, 0))
    half_block = pl.BlockSpec((tile, half), lambda i, _: (i, 0))
    hidden = pl.BlockSpec((tile, columns), lambda i, _: (i, 0))
    return call(
        kernel,
        (count // tile,),
        [hidden, hidden, block, block, fixed(1, width)]
        + gathered_specs(columns, at=0)
        + piece_specs(half, 3),
        [block, block, half_block, half_block, fixed(8, width)],
        [outer((count, width), F32), struct((count, width))]
        + [struct((count, half))] * 2
        + [struct((8, width), F32)],
        4 * count * width * columns + 2 * count * width * width,
        4 * count * columns + 14 * count * width + 4 * width * columns,
        after,
        None,
        1,
    )(places, *grads, middle, final, gain, *[gathered] * 32, *first_pieces)


def first_back(side, half_at, grads, pieces, rows, grad_middle, gain, order, tile=288, after=()):
    _, count, half = grads[0].shape
    width = rows.shape[1]
    mine = count // tile // 2

    def kernel(side_ref, low_ref, high_ref, rows_ref, middle_ref, gain_ref, order_ref, *refs):
        parts, (out_ref, sum_ref) = far_list(refs[:4], refs[4:6]), refs[6:]
        lefts = [jnp.concatenate([ref[at] for at in range(3)], axis=1) for ref in (low_ref, high_ref)]
        found = []
        for at in range(4):
            found.append(
                dot_nt(lefts[0], parts[2 * at][...]) + dot_nt(lefts[1], parts[2 * at + 1][...])
            )
        grad_normed = jnp.concatenate(found, axis=1)
        unit, inv_std = normal_parts(rows_ref[...].astype(F32))
        out = middle_ref[...] + normalize_back(grad_normed, unit, inv_std, gain_ref[...])
        out_ref[0] = dot_nt(out.astype(BF16), order_ref[...]).astype(BF16)

        @pl.when(first_step())
        def _():
            sum_ref[...] = jnp.zeros_like(sum_ref)

        sum_ref[0:1] += column_sum(grad_normed * unit)
        sum_ref[1:2] += column_sum(grad_normed)

    start = half_at * mine
    block = pl.BlockSpec((tile, width), lambda i, _: (start + i, 0))
    grad_block = pl.BlockSpec((3, tile, half), lambda i, _: (0, start + i, 0))
    offset = (lambda ref: ref[0] * mine) if half_at == 0 else (lambda ref: 0)
    return call(
        kernel,
        (mine,),
        [grad_block, grad_block, block, block, fixed(1, width), fixed(width, width)]
        + piece_specs(3 * half),
        [image_block(tile, width, offset), fixed(8, width)],
        [struct(((2 - half_at) * mine, tile, width)), struct((8, width), F32)],
        4 * count * width * width,
        8 * count * width + 6 * width * width,
        after,
        None,
        1,
        part=0.3,
    )(side, *in_hbm(grads), in_hbm(rows), in_hbm(grad_middle), gain, order, *in_hbm(pieces))


def fast_shards(
    tokens,
    image_mask,
    out_grad,
    norm1_gain,
    norm1_shift,
    qkv_weight,
    qv_bias,
    out_weight,
    out_bias,
    norm2_gain,
    norm2_shift,
    up_weight,
    up_bias,
    down_weight,
    down_bias,
):
    images, half_len, width = tokens.shape
    mine = images // 2
    half = qkv_weight.shape[2]
    half_hidden = up_weight.shape[1]
    count = 2 * mine * half_len
    me = lax.axis_index("dp")
    side = lax.axis_index("tensor")
    side_array = jnp.concatenate([jnp.stack([side, me]).astype(jnp.int32), image_mask])
    vectors = (norm1_gain, norm1_shift, norm2_gain, norm2_shift, out_bias, down_bias)
    order, gain_one, shift_one, gain_two, shift_two, bias_out, bias_down = setup(
        side_array, [vector.reshape(1, width) for vector in vectors]
    )

    def for_partner(values):
        return over_x(lax.dynamic_slice_in_dim(values, (1 - side) * mine, mine, 0))

    def z_all(values):
        return jnp.concatenate([values] + [over_z(values, step) for step in (1, 2, 3)], axis=0)

    up_all = lax.all_gather(up_weight, ("dp", "tensor")).reshape(-1, 2, ROWS, half_hidden)
    own = prepare(side_array, tokens, order, gain_one, shift_one, 0)
    final, sum_own = mask_grad(side_array, out_grad, order, 0, after=own[:1])
    tokens_partner = for_partner(tokens)
    first = jnp.concatenate([qkv_weight.reshape(ROWS, 3 * half), out_weight], axis=1)
    first_base = late(z_all(first), final)
    biases = jnp.concatenate([qv_bias.reshape(-1), up_bias])
    bias_rows = jnp.pad(biases, (0, 16 * 4 * half - biases.size)).reshape(16, 4 * half)

    def split_bias(bias):
        bias = bias.astype(F32)
        parts = jnp.stack([bias[:half], jnp.zeros((half,), F32), bias[half : 2 * half]])
        return parts[:, None], bias[None, 2 * half :]

    rows, normed = prepare(
        side_array, tokens_partner, order, gain_one, shift_one, 1, own, after=[first_base]
    )
    first_x = over_x(jnp.concatenate([first_base, bias_rows], axis=0))
    first_y = over_y(first_base)
    first_xy = over_y(late(first_x, first_y))
    first_far = [over_core(jnp.stack(late([first_base, first_y], first_x, normed)))]
    biases = [split_bias(biases), split_bias(first_x[4 * ROWS :].reshape(-1)[: biases.size])]
    heads_shape = (3, 2, mine, half_len, half)
    projected, contexts, kept = [None, None], [None, None], [None, None]
    projected[0] = project(normed, [first_base, first_y] + first_far, biases[0][0]).reshape(heads_shape)
    begun = attend(projected[0], 0, 1, lanes=128)
    first_far += [over_core(jnp.stack(late([first_x, first_xy], begun[0])))]
    first_pieces = [first_base, first_x, first_y, first_xy] + first_far
    contexts[0], *kept[0] = attend(projected[0], 1, 2, begun, lanes=128)
    grad_partner = for_partner(late(out_grad, first_x))
    projected[1] = project(
        normed, [first_x, first_xy] + first_far[1:], biases[1][0], after=[contexts[0]]
    ).reshape(heads_shape)
    down_all = lax.all_gather(late(down_weight, up_all, contexts[0]), ("dp", "tensor"))
    down_all = down_all.reshape(-1, 2, ROWS, half_hidden)
    contexts[1], *kept[1] = attend(projected[1], 0, 2)
    contexts = [values.reshape(count, half) for values in contexts]
    middle, second = add_branch(contexts, rows, first_pieces, bias_out, gain_two, shift_two)
    actives, slopes = [None, None], [None, None]
    actives[0], slopes[0] = feed_up(side_array, 0, second, up_all, biases[0][1])
    final, sum_partner = mask_grad(side_array, grad_partner, order, 1, final, after=in_hbm([actives[0]]))
    actives[1], slopes[1] = feed_up(side_array, 1, second, up_all, biases[1][1], after=[final])

    down_near, down_next, down_far, down_last = sums_down(final, actives)
    grads_sums = gate_back(side_array, final, slopes, down_all, after=in_hbm([down_near]))
    grads, sum_hidden = grads_sums[:2], grads_sums[2:]
    (down_sent,) = combine([down_next, over_core(down_last)], 1, after=grads[:1])
    down_sent_y = over_y(down_sent)
    up_near, up_next, up_far_sums, up_last = sums_up(second, grads, after=in_hbm([down_sent]))
    grad_middle, branch, *grad_contexts, sums_two = second_back(
        side_array, grads, up_all, first_pieces, middle, final, gain_two, after=in_hbm([up_near])
    )
    (up_sent,) = combine([up_next, over_core(up_last)], 1, after=[branch])
    up_sent_x = over_x(up_sent)
    down_far = over_core(late(down_far, up_sent))

    def heads_back(x_at, after):
        grad_context = grad_contexts[x_at].reshape(2, mine, half_len, half)
        grad, sums = attend_back(
            projected[x_at], grad_context, contexts[x_at].reshape(grad_context.shape), *kept[x_at], after=after
        )
        return grad.reshape(3, count, half), jnp.sum(sums, axis=0)

    grads_qkv, sums_qkv = [None, None], [None, None]
    grads_qkv[1], sums_qkv[1] = heads_back(1, in_hbm([up_sent]))
    down_sums = combine([down_near, down_far, down_sent_y], 2, after=[grads_qkv[1]])
    down_sent_x = over_x(down_sums[1])
    high_near, high_next, high_far, high_last = sums_first(
        normed, branch, grads_qkv[1], contexts[1], after=in_hbm(down_sums[:1])
    )
    up_far_sums = over_core(late(up_far_sums, high_near))
    out_send = feed_down(side_array, 2, 4, actives, middle, down_all, bias_down, order, after=in_hbm([high_near]))
    (high_sent,) = combine([high_next, over_core(high_last)], 1, after=[out_send])
    high_sent_y = over_y(high_sent)
    up_sums = combine([up_near, up_far_sums, up_sent_x], 2, after=in_hbm([high_sent]))
    up_sent_y = over_y(up_sums[1])
    high_far = over_core(late(high_far, up_sums[0]))
    out_partner = over_x(late(out_send, up_sums[0]))
    grads_qkv[0], sums_qkv[0] = heads_back(0, in_hbm(up_sums[:1]))
    down_sums = combine([down_sums[0], down_sent_x], 2, after=[high_far, grads_qkv[0]])
    down_sent_z = over_z(down_sums[1], 2)
    low_near, low_next, low_far, low_last = sums_first(
        normed, branch, grads_qkv[0], contexts[0], after=in_hbm(down_sums[:1])
    )
    (high,) = combine([high_near, high_far, high_sent_y], 1, after=in_hbm([low_near]))
    high_x = over_x(high)
    (low_sent,) = combine([low_next, over_core(low_last)], 1, after=in_hbm([high]))
    low_sent_y = over_y(low_sent)
    send, sums_partner = first_back(
        side_array, 1, grads_qkv, first_pieces, rows, grad_middle, gain_one, order, after=in_hbm([low_sent])
    )
    up_sums = combine([up_sums[0], up_sent_y], 2, after=[send])
    up_sent_z = over_z(up_sums[1], 2)
    down_sums = combine([down_sums[0], down_sent_z], 2, after=[up_sums[0], out_partner])
    down_sent_z = over_z(down_sums[1], 1)
    low_far = over_core(late(low_far, up_sums[0]))
    full, sums_own = first_back(
        side_array, 0, grads_qkv, first_pieces, rows, grad_middle, gain_one, order, after=in_hbm(down_sums[:1])
    )
    low = combine([low_near, low_far, low_sent_y, high_x], 4, after=[full])
    up_sums = combine([up_sums[0], up_sent_z], 2, after=in_hbm(low[:1]))
    sums = jnp.concatenate(
        [(sums_own + sums_partner)[:2], sums_two[2:3], sums_two[:2], sum_own + sum_partner], axis=0
    )
    sums = jnp.einsum("td,od->to", sums, order.astype(F32), precision=lax.Precision.HIGHEST)
    halves = [
        jnp.concatenate([sums_qkv[x_at].reshape(-1), sum_hidden[x_at][0]]) for x_at in range(2)
    ]
    small = late(jnp.concatenate([halves[0], sums.reshape(-1), halves[1]]), low[0])
    small = small + over_core(small)
    small = late(small + over_y(small), up_sums[0])
    halves_size = 2 * half + half_hidden
    small_x = over_x(jnp.concatenate([small[-halves_size:], small[halves_size:-halves_size]]))
    small = small[:-halves_size] + small_x
    height = 8
    small_rows = jnp.pad(small, (0, height * half_hidden - small.size)).reshape(height, half_hidden)
    small_top = small_rows.astype(BF16)
    small_rows = jnp.concatenate([small_top, (small_rows - small_top.astype(F32)).astype(BF16)], axis=0)

    near_z = over_z(jnp.concatenate([low[1], up_sums[1], small_rows], axis=0), 1)
    middle_z = over_z(jnp.concatenate([low[2], small_rows], axis=0), 2)
    far_z = over_z(jnp.concatenate([low[3], small_rows], axis=0), 3)
    send_x = over_x(late(send, low[0]))
    out_full = feed_down(
        side_array, 0, 2, actives, middle, down_all, bias_down, order, after=[low[0], small_rows]
    )
    (grad_down,) = combine([down_sums[0], down_sent_z], 1, F32, after=[out_full])
    block_out = lax.dynamic_update_slice_in_dim(out_full, out_partner, (1 - side) * mine, 0)
    tokens_grad = lax.dynamic_update_slice_in_dim(full, send_x, (1 - side) * mine, 0)
    grad_qkv, grad_out, grad_up, sums = finish(
        low[0], up_sums[0], small_rows, near_z, middle_z, far_z, after=[block_out, tokens_grad]
    )
    sums = sums.reshape(-1)
    halves = sums[:halves_size]
    sums = sums[halves_size : halves_size + 6 * width].reshape(6, width)
    return (
        block_out,
        tokens_grad,
        sums[0],
        sums[1],
        grad_qkv.reshape(ROWS, 3, half),
        halves[: 2 * half].reshape(2, half),
        grad_out,
        sums[2],
        sums[3],
        sums[4],
        grad_up,
        halves[2 * half :],
        grad_down,
        sums[5],
    )


def solution(mesh):
    in_specs = (
        P("dp", "tensor", None),
        P("dp"),
        P("dp", "tensor", None),
        P(),
        P(),
        P("dp", None, "tensor"),
        P(None, "tensor"),
        P("dp", "tensor"),
        P(),
        P(),
        P(),
        P("dp", "tensor"),
        P("tensor"),
        P("dp", "tensor"),
        P(),
    )
    out_specs = (
        P("dp", "tensor", None),
        P("dp", "tensor", None),
        P(),
        P(),
        P("dp", None, "tensor"),
        P(None, "tensor"),
        P("dp", "tensor"),
        P(),
        P(),
        P(),
        P("dp", "tensor"),
        P("tensor"),
        P("dp", "tensor"),
        P(),
    )
    small_slice = mesh.shape["dp"] == 16 and mesh.shape["tensor"] == 2
    shards = fast_shards if small_slice else general_shards
    return jax.shard_map(shards, mesh=mesh, in_specs=in_specs, out_specs=out_specs, check_vma=False)
```
